128 devices in a mesh: dp: 4 (over y), ep: 8 (over x, core), tp: 4 (over z).
Axes of the slice: x: 4, y: 4, z: 4, core: 2. Of those that a mesh axis runs over, the one named last changes fastest.
Arguments:
- inputs: bfloat16 [8, 1024, 768], P('dp', 'ep'), may hold values from -6 to 6
- lengths: int32 [8], P('dp'), may hold values from 256 to 1024, as said below
- expert_ids: int32 [2, 8, 1024, 2], P(None, 'dp', 'ep'), may hold values from 0 to 15, as said below
- slot_ids: int32 [2, 8, 1024, 2], P(None, 'dp', 'ep'), may hold values from 0 to 32, as said below
- attn_gain: bfloat16 [2, 768], P(None, ('dp', 'ep')), may hold values from 0.5 to 1.5
- query_weight: bfloat16 [2, 768, 768], P(None, ('dp', 'ep'), 'tp'), may hold values from -0.21875 to 0.21875
- key_weight: bfloat16 [2, 768, 768], P(None, ('dp', 'ep'), 'tp'), may hold values from -0.21875 to 0.21875
- value_weight: bfloat16 [2, 768, 768], P(None, ('dp', 'ep'), 'tp'), may hold values from -0.21875 to 0.21875
- out_weight: bfloat16 [2, 768, 768], P(None, ('dp', 'ep'), 'tp'), may hold values from -1.75 to 1.75
- ffn_gain: bfloat16 [2, 768], P(None, ('dp', 'ep')), may hold values from 0.5 to 1.5
- router_weight: bfloat16 [2, 768, 16], P(None, ('dp', 'ep')), may hold values from -0.15625 to 0.15625
- dense_gate: bfloat16 [2, 768, 2048], P(None, ('dp', 'ep'), 'tp'), may hold values from -0.21875 to 0.21875
- dense_up: bfloat16 [2, 768, 2048], P(None, ('dp', 'ep'), 'tp'), may hold values from -0.21875 to 0.21875
- dense_down: bfloat16 [2, 768, 2048], P(None, ('dp', 'ep'), 'tp'), may hold values from -0.125 to 0.125
- expert_gate: bfloat16 [2, 16, 768, 2048], P(None, 'ep', None, 'tp'), may hold values from -0.21875 to 0.21875
- expert_up: bfloat16 [2, 16, 768, 2048], P(None, 'ep', None, 'tp'), may hold values from -0.21875 to 0.21875
- expert_down: bfloat16 [2, 16, 2048, 768], P(None, 'ep', 'tp'), may hold values from -0.125 to 0.125
- cotangent: bfloat16 [8, 1024, 768], P('dp', 'ep'), may hold values from -6 to 6
Outputs:
- outputs: float32 [8, 1024, 768], P('dp', 'ep')
- input_grad: float32 [8, 1024, 768], P('dp', 'ep')
- attn_gain_grad: float32 [2, 768], P(None, ('dp', 'ep'))
- query_grad: float32 [2, 768, 768], P(None, ('dp', 'ep'), 'tp')
- key_grad: float32 [2, 768, 768], P(None, ('dp', 'ep'), 'tp')
- value_grad: float32 [2, 768, 768], P(None, ('dp', 'ep'), 'tp')
- out_grad: float32 [2, 768, 768], P(None, ('dp', 'ep'), 'tp')
- ffn_gain_grad: float32 [2, 768], P(None, ('dp', 'ep'))
- router_grad: float32 [2, 768, 16], P(None, ('dp', 'ep'))
- dense_gate_grad: float32 [2, 768, 2048], P(None, ('dp', 'ep'), 'tp')
- dense_up_grad: float32 [2, 768, 2048], P(None, ('dp', 'ep'), 'tp')
- dense_down_grad: float32 [2, 768, 2048], P(None, ('dp', 'ep'), 'tp')
- expert_gate_grad: float32 [2, 16, 768, 2048], P(None, 'ep', None, 'tp')
- expert_up_grad: float32 [2, 16, 768, 2048], P(None, 'ep', None, 'tp')
- expert_down_grad: float32 [2, 16, 2048, 768], P(None, 'ep', 'tp')
The draws below stay inside these ranges and needn't reach their ends.
Inputs may be any that keep to these rules, and one draw needn't show every extreme that they name: `lengths`: in each group of 2 sequences of one dp index, one sequence, drawn, has length 1024. `expert_ids`: each token names two different experts in each block. `slot_ids`: within one block and one row block (the 256 tokens of one dp and ep index), the pairs (token, choice) of one expert, in order of tokens and then choices, get slots 0, 1, 2 and so on; a pair that finds all 32 slots taken gets 32 and is dropped. In every draw and block some expert fills all 32 slots of every row block of its dp index.
All inputs are finite; a program needn't handle non-finite values.
Results may differ from the reference program's by a relative error of at most 0.038.
Values may be sent and summed in bfloat16 or wider, within the bound.
A program may use at most 256 MiB of HBM per device.

```python
import jax
import jax.numpy as jnp
from jax import lax

D = 768
HEADS = 12
HD = 64
HQ = 768
FF = 2048
FD = 2048
EXPERTS = 16
LAYERS = 2
LEN = 1024
SEQ_GRP = 2
SEQS = 8
SPAN = 128
TOK_DEV = 256
CAP = 32
N_DP = 4
N_EP = 8


def route_table(key):
    key_scores, key_bias, key_hot, key_order = jax.random.split(key, 4)
    row_count = SEQ_GRP * SPAN
    base_scores = jax.random.randint(key_scores, (LAYERS, N_DP, N_EP, row_count, EXPERTS), 0, 65536)
    expert_bias = jax.random.randint(key_bias, (LAYERS, N_DP, N_EP, 1, EXPERTS), 0, 32768)
    hot_expert = jax.random.randint(key_hot, (LAYERS, N_DP, 1, 1, 1), 0, EXPERTS)
    block_keys = jax.random.split(key_order, LAYERS * N_DP * N_EP)
    orders = jax.vmap(lambda block_key: jax.random.permutation(block_key, row_count))(block_keys)
    orders = orders.reshape(LAYERS, N_DP, N_EP, row_count)
    forced = orders < 3 * CAP // 2
    expert_range = jnp.arange(EXPERTS)
    scores = (base_scores + expert_bias) * 32 + expert_range
    boost = jnp.where(forced[..., None] & (expert_range == hot_expert), 8388608, 0)
    scores = (scores + boost).astype(jnp.int32)
    chosen_ids = lax.top_k(scores, 2)[1].astype(jnp.int32)
    pairs = chosen_ids.reshape(LAYERS, N_DP, N_EP, row_count * 2)
    pair_onehot = (pairs[..., None] == expert_range).astype(jnp.int32)
    before = jnp.cumsum(pair_onehot, axis=3) - pair_onehot
    slot_rows = jnp.minimum(jnp.sum(before * pair_onehot, axis=-1), CAP).astype(jnp.int32)
    slot_rows = slot_rows.reshape(LAYERS, N_DP, N_EP, SEQ_GRP, SPAN, 2)
    id_rows = chosen_ids.reshape(LAYERS, N_DP, N_EP, SEQ_GRP, SPAN, 2)
    id_rows = id_rows.transpose(0, 1, 3, 2, 4, 5).reshape(LAYERS, SEQS, LEN, 2)
    slot_rows = slot_rows.transpose(0, 1, 3, 2, 4, 5).reshape(LAYERS, SEQS, LEN, 2)
    return (id_rows, slot_rows)


def draw_lengths(key, part):
    key = jax.random.fold_in(key, 11)
    short_key, choice_key = jax.random.split(key)
    shorter = jax.random.randint(short_key, (N_DP, SEQ_GRP), LEN // 4, LEN + 1)
    longest = jax.random.randint(choice_key, (N_DP, 1), 0, SEQ_GRP)
    full_mask = jnp.arange(SEQ_GRP)[None, :] == longest
    return jnp.where(full_mask, LEN, shorter).reshape(SEQS).astype(jnp.int32)


def draw_expert_ids(key, part):
    id_rows, slot_rows = route_table(key)
    return id_rows


def draw_slot_ids(key, part):
    id_rows, slot_rows = route_table(key)
    return slot_rows


def shard_levels(own_key, shape, shards, smallest, top_value):
    loudness = 1.0
    for axis_at, parts in shards:
        draws = jax.random.uniform(jax.random.fold_in(jax.random.fold_in(own_key, 6), axis_at), (parts,), jnp.float32, smallest / len(shards), top_value / len(shards))
        loudness = loudness * jnp.repeat(jnp.exp(draws), shape[axis_at] // parts).reshape((-1,) + (1,) * (len(shape) - 1 - axis_at))
    return loudness


def noise(stream_key, dims, scale, reach, cuts=(), kind=jnp.bfloat16):
    result = jax.random.normal(stream_key, dims, jnp.float32) * scale
    if len(cuts) > 0:
        result = shard_levels(stream_key, dims, cuts, -0.22, 0.18) * result
    return jnp.clip(result, min=-reach, max=reach).astype(kind)


def setup_inputs(seed: int = 0) -> dict:
    arg_keys = jax.random.split(jax.random.key(seed), 19)
    inputs = noise(arg_keys[0], (SEQS, LEN, D), 1.0, 6.0, ((0, 4), (1, 8)))
    lengths = draw_lengths(jax.random.fold_in(arg_keys[18], 71), 0)
    expert_ids = draw_expert_ids(jax.random.fold_in(arg_keys[18], 71), 0)
    slot_ids = draw_slot_ids(jax.random.fold_in(arg_keys[18], 71), 0)
    attn_gain = jnp.clip(1.0 + 0.1 * jax.random.normal(arg_keys[4], (LAYERS, D), jnp.float32), 0.5, 1.5).astype(jnp.bfloat16)
    query_weight = noise(arg_keys[5], (LAYERS, D, HQ), D ** -0.5, 0.21875, ((1, 32), (2, 4)))
    key_weight = noise(arg_keys[6], (LAYERS, D, HQ), D ** -0.5, 0.21875, ((1, 32), (2, 4)))
    value_weight = noise(arg_keys[7], (LAYERS, D, HQ), D ** -0.5, 0.21875, ((1, 32), (2, 4)))
    out_weight = noise(arg_keys[8], (LAYERS, D, HQ), (max(1, HQ * 16 // LEN)) ** -0.5, 1.75, ((1, 32), (2, 4)))
    ffn_gain = jnp.clip(1.0 + 0.1 * jax.random.normal(arg_keys[9], (LAYERS, D), jnp.float32), 0.5, 1.5).astype(jnp.bfloat16)
    router_weight = noise(arg_keys[10], (LAYERS, D, EXPERTS), (2 * D) ** -0.5, 0.15625, ((1, 32),))
    dense_gate = noise(arg_keys[11], (LAYERS, D, FD), D ** -0.5, 0.21875, ((1, 32), (2, 4)))
    dense_up = noise(arg_keys[12], (LAYERS, D, FD), D ** -0.5, 0.21875, ((1, 32), (2, 4)))
    dense_down = noise(arg_keys[13], (LAYERS, D, FD), FD ** -0.5, 0.125, ((1, 32), (2, 4)))
    expert_gate = noise(arg_keys[14], (LAYERS, EXPERTS, D, FF), D ** -0.5, 0.21875, ((1, 8), (3, 4)))
    expert_up = noise(arg_keys[15], (LAYERS, EXPERTS, D, FF), D ** -0.5, 0.21875, ((1, 8), (3, 4)))
    expert_down = noise(arg_keys[16], (LAYERS, EXPERTS, FF, D), FF ** -0.5, 0.125, ((1, 8), (2, 4)))
    cotangent = noise(arg_keys[17], (SEQS, LEN, D), 1.0, 6.0, ((0, 4), (1, 8)))
    return dict(inputs=inputs, lengths=lengths, expert_ids=expert_ids, slot_ids=slot_ids, attn_gain=attn_gain, query_weight=query_weight, key_weight=key_weight, value_weight=value_weight, out_weight=out_weight, ffn_gain=ffn_gain, router_weight=router_weight, dense_gate=dense_gate, dense_up=dense_up, dense_down=dense_down, expert_gate=expert_gate, expert_up=expert_up, expert_down=expert_down, cotangent=cotangent)


@jax.custom_vjp
def low(v):
    return lax.optimization_barrier(v.astype(jnp.bfloat16)).astype(jnp.float32)

@jax.custom_vjp
def low_back(v):
    return v

def low_keep(v):
    return (low(v), None)

def low_pass(kept, grad):
    return (grad,)

def back_keep(v):
    return (v, None)

def back_low(kept, grad):
    return (low(grad),)
low.defvjp(low_keep, low_pass)
low_back.defvjp(back_keep, back_low)
epsilon = 1e-06
highest = lax.Precision.HIGHEST

def normalize(values, gain):
    return values * lax.rsqrt(lax.optimization_barrier(jnp.mean(values * values, axis=-1, keepdims=True)) + epsilon) * gain

def rotate(values, positions, turn_sign):
    half_dim = values.shape[-1] // 2
    frequency = jnp.exp(-jnp.log(10000.0) * jnp.arange(half_dim).astype(jnp.float32) / half_dim)
    angles = positions[:, None] * frequency[None, :]
    cosine = jnp.cos(angles)[:, None, :]
    sine_part = turn_sign * jnp.sin(angles)[:, None, :]
    front_half = values[..., :half_dim]
    back_half = values[..., half_dim:]
    return jnp.concatenate([front_half * cosine - back_half * sine_part, back_half * cosine + front_half * sine_part], axis=-1)

def attend(pieces):
    queries, keys_rot, values_low, length = pieces
    places = jnp.arange(LEN)
    scores = low_back(jnp.einsum('qhd,khd->hqk', queries, keys_rot, precision=highest) * HD ** (-0.5))
    allowed = (places[None, :] <= places[:, None]) & (places[None, :] < length)
    scores = jnp.where(allowed[None], scores, -1e+30)
    row_max = lax.optimization_barrier(jnp.max(scores, axis=-1, keepdims=True))
    probs = jnp.exp(scores - row_max)
    probs = probs / lax.optimization_barrier(jnp.sum(probs, axis=-1, keepdims=True))
    return jnp.einsum('hqk,khd->qhd', low(probs), values_low, precision=highest)

def blocked(values):
    width = values.shape[-1]
    return values.reshape(N_DP, SEQ_GRP, N_EP, SPAN, width).transpose(0, 2, 1, 3, 4).reshape(N_DP * N_EP, TOK_DEV, width)

def unblock(values):
    width = values.shape[-1]
    return values.reshape(N_DP, N_EP, SEQ_GRP, SPAN, width).transpose(0, 2, 1, 3, 4).reshape(SEQS, LEN, width)

def layer(stream, params, route_now, slot_now, lengths):
    attn_gain, query_weight, key_weight, value_weight, out_weight, ffn_gain, router_weight, dense_gate, dense_up, dense_down, expert_gate, expert_up, expert_down = params
    places = jnp.arange(LEN).astype(jnp.float32)
    normed = low(normalize(stream, attn_gain))
    query_lin = low_back(jnp.dot(normed, query_weight, precision=highest))
    queries = low(rotate(query_lin.reshape(SEQS, LEN, HEADS, HD), places, 1.0))
    key_lin = low_back(jnp.dot(normed, key_weight, precision=highest))
    keys_rot = low(rotate(key_lin.reshape(SEQS, LEN, HEADS, HD), places, 1.0))
    values_low = low(low_back(jnp.dot(normed, value_weight, precision=highest))).reshape(SEQS, LEN, HEADS, HD)
    attended = lax.map(jax.checkpoint(attend), (queries, keys_rot, values_low, lengths))
    attended = low(low_back(attended.reshape(SEQS, LEN, HQ)))
    middle = stream + low_back(jnp.einsum('sth,dh->std', attended, out_weight, precision=highest))
    ffn_in = low(normalize(middle, ffn_gain))
    logits = low_back(jnp.einsum('std,de->ste', ffn_in, router_weight, precision=highest))
    gate_dense = low_back(jnp.einsum('std,df->stf', ffn_in, dense_gate, precision=highest))
    up_dense = low_back(jnp.einsum('std,df->stf', ffn_in, dense_up, precision=highest))
    hidden_dense = low(jax.nn.silu(gate_dense) * up_dense)
    dense_out = jnp.einsum('stf,df->std', hidden_dense, dense_down, precision=highest)
    tokens = blocked(ffn_in)
    logit_rows = blocked(logits)
    route_rows = blocked(route_now)
    slot_rows = blocked(slot_now)
    pick_expert = (route_rows[..., None] == jnp.arange(EXPERTS)).astype(jnp.float32)
    pick_slot = (slot_rows[..., None] == jnp.arange(CAP)).astype(jnp.float32)
    pick_pair = pick_expert[..., :, None] * pick_slot[..., None, :]
    chosen = lax.optimization_barrier(jnp.sum(pick_expert * logit_rows[:, :, None, :], axis=-1))
    shares = jax.nn.softmax(chosen, axis=-1)
    placed = lax.optimization_barrier(jnp.sum(pick_pair, axis=2))
    mixing = lax.optimization_barrier(jnp.sum(shares[..., None, None] * pick_pair, axis=2))
    sent = jnp.einsum('nbec,nbd->necd', placed, tokens, precision=highest)
    gate_exp = low_back(jnp.einsum('necd,edf->necf', sent, expert_gate, precision=highest))
    up_exp = low_back(jnp.einsum('necd,edf->necf', sent, expert_up, precision=highest))
    hidden_exp = low(jax.nn.silu(gate_exp) * up_exp)
    returned = low_back(jnp.einsum('necf,efd->necd', hidden_exp, expert_down, precision=highest))
    moe = unblock(jnp.einsum('nbec,necd->nbd', mixing, returned, precision=highest))
    return middle + low_back(dense_out + moe)

def reference(inputs, lengths, expert_ids, slot_ids, attn_gain, query_weight, key_weight, value_weight, out_weight, ffn_gain, router_weight, dense_gate, dense_up, dense_down, expert_gate, expert_up, expert_down, cotangent):
    params = [weight.astype(jnp.float32) for weight in (attn_gain, query_weight, key_weight, value_weight, out_weight, ffn_gain, router_weight, dense_gate, dense_up, dense_down, expert_gate, expert_up, expert_down)]

    def forward(stream, *weights):
        for depth in range(LAYERS):
            stream = layer(stream, [weight[depth] for weight in weights], expert_ids[depth], slot_ids[depth], lengths)
        return stream
    outputs, pullback = jax.vjp(forward, inputs.astype(jnp.float32), *params)
    grads = pullback(cotangent.astype(jnp.float32))
    return (outputs, grads[0], grads[1], grads[2], grads[3], grads[4], grads[5], grads[6], grads[7], grads[8], grads[9], grads[10], grads[11], grads[12], grads[13])
```

```python
import functools

import jax
import jax.numpy as jnp
from jax import lax
from jax.experimental import pallas as pl
from jax.experimental.pallas import tpu as pltpu
from jax.sharding import PartitionSpec as P

HD = 64
MESH = pl.DeviceIdType.MESH
BF = jnp.bfloat16
F32 = jnp.float32
WIDE = 2432
CHUNK = 48
VM = pl.BlockSpec(memory_space=pltpu.VMEM)


def place():
    y = lax.axis_index("dp")
    e = lax.axis_index("ep")
    z = lax.axis_index("tp")
    return y, e // 2, e % 2, z


def device(y, x, c, z):
    return (y, x * 2 + c, z)


def meet(givers, takers):
    barrier = pltpu.get_barrier_semaphore()
    for who in givers:
        pl.semaphore_signal(barrier, inc=1, device_id=who, device_id_type=MESH)
    pl.semaphore_wait(barrier, takers)


class Line:
    def __init__(self, send_sems, recv_sems):
        self.send_sems, self.recv_sems, self.used, self.open = send_sems, recv_sems, 0, []

    def start(self, src, dst, who):
        at = self.used
        self.used += 1
        copy = pltpu.make_async_remote_copy(
            src_ref=src,
            dst_ref=dst,
            send_sem=self.send_sems.at[at],
            recv_sem=self.recv_sems.at[at],
            device_id=who,
            device_id_type=MESH,
        )
        copy.start()
        self.open.append(copy)
        return copy

    def finish(self):
        for copy in self.open:
            copy.wait_send()


def gather_kernel(src, out, land, send_sems, recv_sems):
    y, x, c, z = place()

    def at(j, d, core=None):
        yy = (y + j * c + d * (1 - c) + 8) % 4
        xx = (x + j * (1 - c) + d * c + 8) % 4
        return yy, xx

    def who(j, d):
        yy, xx = at(j, d)
        return device(yy, xx, c, z)

    def slot(j, d):
        yy, xx = at(j, d)
        return yy * 8 + xx * 2 + c

    sibling = device(y, x, 1 - c, z)
    near = [who(1, 0), who(-1, 0), who(0, 1), who(0, -1), sibling]
    meet(near, 5)
    line = Line(send_sems, recv_sems)
    sib = []

    def spread(ref, j):
        plus = line.start(ref, land.at[slot(j, 0)], who(0, 1))
        minus = line.start(ref, land.at[slot(j, 0)], who(0, -1))
        sib.append(line.start(ref, land.at[slot(j, 0)], sibling))
        return plus, minus

    first_plus = line.start(src, land.at[slot(0, 0)], who(1, 0))
    first_minus = line.start(src, land.at[slot(0, 0)], who(-1, 0))
    second = {0: spread(src, 0)}
    land[slot(0, 0)] = src[...]
    first_plus.wait_recv()
    below = land.at[slot(-1, 0)]
    on_plus = line.start(below.at[pl.ds(0, 32)], below.at[pl.ds(0, 32)], who(1, 0))
    second[-1] = spread(below, -1)
    first_minus.wait_recv()
    above = land.at[slot(1, 0)]
    on_minus = line.start(above.at[pl.ds(32, 16)], above.at[pl.ds(32, 16)], who(-1, 0))
    second[1] = spread(above, 1)
    on_plus.wait_recv()
    on_minus.wait_recv()
    second[2] = spread(land.at[slot(2, 0)], 2)
    far = []
    for j in (0, -1, 1, 2):
        plus, minus = second[j]
        plus.wait_recv()
        got = land.at[slot(j, -1)]
        sib.append(line.start(got, got, sibling))
        if j in (0, -1):
            far.append((j, line.start(got, got, who(0, 1))))
        minus.wait_recv()
        got = land.at[slot(j, 1)]
        sib.append(line.start(got, got, sibling))
        if j in (1, 2):
            far.append((j, line.start(got, got, who(0, -1))))
    for j, copy in far:
        copy.wait_recv()
        got = land.at[slot(j, 2)]
        sib.append(line.start(got, got, sibling))
    for copy in sib:
        copy.wait_recv()
    line.finish()

    def unpack(p, carry):
        one = land[2 * p].astype(F32)
        two = land[2 * p + 1].astype(F32)
        rows = pl.ds(pl.multiple_of(p * CHUNK, CHUNK), CHUNK)
        out[0, rows] = jnp.concatenate([one[:24], two[:24]], axis=0).astype(BF)
        out[1, rows] = jnp.concatenate([one[24:], two[24:]], axis=0).astype(BF)
        return carry

    lax.fori_loop(0, 16, unpack, 0)


def gather_weights(src):
    return pl.pallas_call(
        gather_kernel,
        out_shape=jax.ShapeDtypeStruct((2, 768, WIDE), BF),
        in_specs=[VM],
        out_specs=VM,
        scratch_shapes=[
            pltpu.VMEM((32, CHUNK, WIDE), BF),
            pltpu.SemaphoreType.DMA((32,)),
            pltpu.SemaphoreType.DMA((32,)),
        ],
        compiler_params=pltpu.CompilerParams(
            collective_id=0, has_side_effects=True, vmem_limit_bytes=48 * 2**20
        ),
        name="gather_weights",
    )(src)


PARTS = (256, 640, 512, 512, 512)


def scatter_kernel(*refs):
    ins, outs = refs[:10], refs[10:15]
    chunks, sib_land, plus_far, minus_far, plus_near, minus_near, one_far, one_near, send_sems, recv_sems = refs[15:]
    y, x, c, z = place()

    def at(j, d):
        yy = (y + j * c + d * (1 - c) + 8) % 4
        xx = (x + j * (1 - c) + d * c + 8) % 4
        return yy, xx

    def who(j, d):
        yy, xx = at(j, d)
        return device(yy, xx, c, z)

    def slot(j, d, core):
        yy, xx = at(j, d)
        return yy * 8 + xx * 2 + core

    sibling = device(y, x, 1 - c, z)
    meet([who(1, 0), who(-1, 0), who(0, 1), who(0, -1), sibling], 5)

    def pack(p, carry):
        rows = pl.ds(pl.multiple_of(p * CHUNK, CHUNK), CHUNK)
        left = 0
        for part, width in enumerate(PARTS):
            one = ins[part][rows].astype(F32)
            two = ins[5 + part][rows].astype(F32)
            cols = slice(left, left + width)
            chunks[2 * p, :, cols] = jnp.concatenate([one[:24], two[:24]], axis=0).astype(BF)
            chunks[2 * p + 1, :, cols] = jnp.concatenate([one[24:], two[24:]], axis=0).astype(BF)
            left += width
        return carry

    lax.fori_loop(0, 16, pack, 0)
    line = Line(send_sems, recv_sems)
    order = [(j, d) for d in (2, 1, -1, 0) for j in (0, -1, 1, 2)]
    swapped = {}
    for n, (j, d) in enumerate(order):
        yy = (y + j * (1 - c) + d * c + 8) % 4
        xx = (x + j * c + d * (1 - c) + 8) % 4
        swapped[j, d] = line.start(chunks.at[yy * 8 + xx * 2 + 1 - c], sib_land.at[n], sibling)

    def join(j, d):
        n = order.index((j, d))
        swapped[j, d].wait_recv()
        mine = slot(j, d, c)
        chunks[mine] = (chunks[mine].astype(F32) + sib_land[n].astype(F32)).astype(BF)
        return chunks.at[mine]

    plus_set, minus_set = (0, -1), (1, 2)
    far = {}
    for j in (0, -1, 1, 2):
        ref = join(j, 2)
        if j in plus_set:
            far[j] = line.start(ref, plus_far.at[plus_set.index(j)], who(0, 1))
        else:
            far[j] = line.start(ref, minus_far.at[minus_set.index(j)], who(0, -1))
    near = {}
    for j in (1, 2):
        near[j, 1] = line.start(join(j, 1), plus_near.at[j], who(0, 1))
    for j in (0, -1):
        near[j, -1] = line.start(join(j, -1), minus_near.at[j % 4], who(0, -1))
    for j in plus_set:
        ref = join(j, 1)
        far[j].wait_recv()
        ref[...] = (ref[...].astype(F32) + plus_far[plus_set.index(j)].astype(F32)).astype(BF)
        near[j, 1] = line.start(ref, plus_near.at[j % 4], who(0, 1))
    for j in minus_set:
        ref = join(j, -1)
        far[j].wait_recv()
        ref[...] = (ref[...].astype(F32) + minus_far[minus_set.index(j)].astype(F32)).astype(BF)
        near[j, -1] = line.start(ref, minus_near.at[j], who(0, -1))
    held = {}
    for j in (2, 1, -1, 0):
        ref = join(j, 0)
        near[j, 1].wait_recv()
        near[j, -1].wait_recv()
        total = ref[...].astype(F32) + plus_near[j % 4].astype(F32) + minus_near[j % 4].astype(F32)
        ref[...] = total.astype(BF)
        held[j] = ref
        if j == 2:
            a = line.start(ref.at[pl.ds(0, 32)], one_far.at[pl.ds(0, 32)], who(1, 0))
            b = line.start(ref.at[pl.ds(32, 16)], one_far.at[pl.ds(32, 16)], who(-1, 0))
    a.wait_recv()
    up = held[1].at[pl.ds(0, 32)]
    up[...] = (up[...].astype(F32) + one_far[:32].astype(F32)).astype(BF)
    last_plus = line.start(held[1], one_near.at[0], who(1, 0))
    b.wait_recv()
    down = held[-1].at[pl.ds(32, 16)]
    down[...] = (down[...].astype(F32) + one_far[32:].astype(F32)).astype(BF)
    last_minus = line.start(held[-1], one_near.at[1], who(-1, 0))
    last_plus.wait_recv()
    last_minus.wait_recv()
    left = 0
    for part, width in enumerate(PARTS):
        cols = slice(left, left + width)
        total = held[0][:, cols].astype(F32) + one_near[0, :, cols].astype(F32) + one_near[1, :, cols].astype(F32)
        outs[part][0] = total[:24]
        outs[part][1] = total[24:]
        left += width
    line.finish()


def scatter_grads(parts):
    chunk = lambda n: pltpu.VMEM((n, CHUNK, WIDE), BF)
    return pl.pallas_call(
        scatter_kernel,
        out_shape=[jax.ShapeDtypeStruct((2, 24, width), F32) for width in PARTS],
        in_specs=[VM] * 10,
        out_specs=[VM] * 5,
        scratch_shapes=[
            chunk(32),
            chunk(16),
            chunk(2),
            chunk(2),
            chunk(4),
            chunk(4),
            pltpu.VMEM((CHUNK, WIDE), BF),
            chunk(2),
            pltpu.SemaphoreType.DMA((32,)),
            pltpu.SemaphoreType.DMA((32,)),
        ],
        compiler_params=pltpu.CompilerParams(
            collective_id=1, has_side_effects=True, vmem_limit_bytes=56 * 2**20
        ),
        name="scatter_grads",
    )(*parts)


def rows_kernel(a0, a1, b0, b1, o0, o1, o2, o3, send_sems, recv_sems):
    y, x, c, z = place()

    def along(dy, dz):
        return device((y + dy + 4) % 4, x, c, (z + dz + 4) % 4)

    meet([along(1, 0), along(-1, 0), along(0, 1), along(0, -1)], 4)
    line = Line(send_sems, recv_sems)

    def quarter(k, first, count):
        return pl.ds(pl.multiple_of(((z + k + 4) % 4) * 64 + first, 32), count)

    work = list(zip((a0, a1, b0, b1), (o0, o1, o2, o3)))
    near, half, full, spread = [], [], [], []
    for src, out in work:
        mine = src.at[0, quarter(0, 0, 64)]
        near.append(
            (
                line.start(mine, out.at[0, 1, quarter(0, 0, 64)], along(1, 0)),
                line.start(mine, out.at[0, 3, quarter(0, 0, 64)], along(-1, 0)),
            )
        )
        full.append(
            (
                line.start(src.at[1], out.at[1, 1], along(1, 0)),
                line.start(src.at[1], out.at[1, 3], along(-1, 0)),
            )
        )
    for (src, out), (plus, minus) in zip(work, near):
        plus.wait_recv()
        p = line.start(out.at[0, 1, quarter(0, 0, 32)], out.at[0, 2, quarter(0, 0, 32)], along(1, 0))
        minus.wait_recv()
        m = line.start(out.at[0, 3, quarter(0, 32, 32)], out.at[0, 2, quarter(0, 32, 32)], along(-1, 0))
        half.append((p, m))
    for (src, out), (plus, minus) in zip(work, half):
        plus.wait_recv()
        minus.wait_recv()
        got = out.at[0, pl.ds(1, 3), quarter(0, 0, 64)]
        spread.append((line.start(got, got, along(0, 1)), line.start(got, got, along(0, -1))))
    last = []
    for (src, out), (plus, minus) in zip(work, full):
        plus.wait_recv()
        p = line.start(out.at[1, 1, pl.ds(0, 128)], out.at[1, 2, pl.ds(0, 128)], along(1, 0))
        minus.wait_recv()
        m = line.start(out.at[1, 3, pl.ds(128, 128)], out.at[1, 2, pl.ds(128, 128)], along(-1, 0))
        last += [p, m]
    for (src, out), (plus, minus) in zip(work, spread):
        plus.wait_recv()
        got = out.at[0, pl.ds(1, 3), quarter(-1, 0, 32)]
        last.append(line.start(got, got, along(0, 1)))
        minus.wait_recv()
        got = out.at[0, pl.ds(1, 3), quarter(1, 32, 32)]
        last.append(line.start(got, got, along(0, -1)))
        out[:, 0] = src[...]
    for copy in last:
        copy.wait_recv()
    line.finish()


def gather_rows(arrays):
    shape = jax.ShapeDtypeStruct((2, 4, 256, 768), BF)
    return pl.pallas_call(
        rows_kernel,
        out_shape=[shape] * 4,
        in_specs=[VM] * 4,
        out_specs=[VM] * 4,
        scratch_shapes=[pltpu.SemaphoreType.DMA((48,)), pltpu.SemaphoreType.DMA((48,))],
        compiler_params=pltpu.CompilerParams(
            collective_id=2, has_side_effects=True, vmem_limit_bytes=48 * 2**20
        ),
        name="gather_rows",
    )(*arrays)


epsilon = 1e-06


def normalize(values, gain):
    return values * lax.rsqrt(jnp.mean(values * values, axis=-1, keepdims=True) + epsilon) * gain


def rotate(values, positions, turn_sign):
    half_dim = values.shape[-1] // 2
    frequency = jnp.exp(-jnp.log(10000.0) * jnp.arange(half_dim).astype(jnp.float32) / half_dim)
    angles = positions[:, None] * frequency[None, :]
    cosine = jnp.cos(angles)[:, None, :]
    sine_part = turn_sign * jnp.sin(angles)[:, None, :]
    front_half = values[..., :half_dim]
    back_half = values[..., half_dim:]
    return jnp.concatenate(
        [front_half * cosine - back_half * sine_part, back_half * cosine + front_half * sine_part],
        axis=-1,
    )


def swish_product(gate_pre, up_pre):
    return jax.nn.silu(gate_pre) * up_pre


def padded_rows(slots):
    flat_rows = slots.reshape(slots.shape[0] * slots.shape[1], slots.shape[2])
    return jnp.concatenate([flat_rows, jnp.zeros((1, slots.shape[2]), slots.dtype)], axis=0)


def shards(
    inputs,
    lengths,
    expert_ids,
    slot_ids,
    attn_gain,
    query_weight,
    key_weight,
    value_weight,
    out_weight,
    ffn_gain,
    router_weight,
    dense_gate,
    dense_up,
    dense_down,
    expert_gate,
    expert_up,
    expert_down,
    cotangent,
):
    seq_count, span, width = inputs.shape
    rows = seq_count * span
    depth_count = attn_gain.shape[0]
    ep_count = lax.axis_size("ep")
    experts_all = expert_gate.shape[1] * ep_count
    capacity = 2 * rows // experts_all
    full_len = span * ep_count
    query_places = lax.axis_index("ep") * span + jnp.arange(span)
    query_pos = query_places.astype(jnp.float32)
    key_places = jnp.arange(full_len)
    allowed = (key_places[None, None, :] <= query_places[None, :, None]) & (
        key_places[None, None, :] < lengths[:, None, None]
    )
    scale = HD ** (-0.5)
    expert_range = jnp.arange(experts_all)
    slot_range = jnp.arange(capacity)

    def masked_scores(queries, key_heads):
        scores = (
            jnp.einsum("sqhd,skhd->shqk", queries, key_heads, preferred_element_type=jnp.float32)
            * scale
        )
        return jnp.where(allowed[:, None], scores, -1e30)

    filler = jnp.zeros((depth_count, 24, 64), BF)
    small = jnp.concatenate(
        [router_weight, attn_gain[:, :, None], ffn_gain[:, :, None], filler[:, :, : 64 - 18]], axis=2
    )
    packed = jnp.concatenate(
        [out_weight, small, query_weight, key_weight, value_weight, filler, dense_gate, dense_up, dense_down],
        axis=2,
    )
    everything = gather_weights(packed.reshape(CHUNK, WIDE))
    gathered = (
        everything[:, :, 208],
        everything[:, :, 256:448],
        everything[:, :, 448:640],
        everything[:, :, 640:832],
        everything[:, :, 0:192],
        everything[:, :, 209],
        everything[:, :, 192:208],
        everything[:, :, 896:1408],
        everything[:, :, 1408:1920],
        everything[:, :, 1920:2432],
    )
    stream = inputs.astype(jnp.float32).reshape(rows, width)
    saved = []
    for depth in range(depth_count):
        norm_one, w_query, w_key, w_value, w_out, norm_two, w_router, w_dgate, w_dup, w_ddown = [
            weight[depth] for weight in gathered
        ]
        normed = normalize(stream, norm_one.astype(jnp.float32)).astype(jnp.bfloat16)
        query_lin = jnp.dot(normed, w_query, preferred_element_type=jnp.float32)
        key_lin = jnp.dot(normed, w_key, preferred_element_type=jnp.float32)
        value_lin = jnp.dot(normed, w_value, preferred_element_type=jnp.float32)
        heads_here = query_lin.shape[1] // HD
        queries = rotate(query_lin.reshape(seq_count, span, heads_here, HD), query_pos, 1.0).astype(
            jnp.bfloat16
        )
        keys_rot = rotate(key_lin.reshape(seq_count, span, heads_here, HD), query_pos, 1.0).astype(
            jnp.bfloat16
        )
        values_low = value_lin.reshape(seq_count, span, heads_here * HD).astype(jnp.bfloat16)
        keys_all, values_all = (
            lax.all_gather(
                keys_rot.reshape(seq_count, span, heads_here * HD), "ep", axis=1, tiled=True
            ),
            lax.all_gather(values_low, "ep", axis=1, tiled=True),
        )
        key_heads = keys_all.reshape(seq_count, full_len, heads_here, HD)
        value_heads = values_all.reshape(seq_count, full_len, heads_here, HD)
        scores = masked_scores(queries, key_heads)
        row_max = jnp.max(scores, axis=-1, keepdims=True)
        expd = jnp.exp(scores - row_max)
        total = jnp.sum(expd, axis=-1, keepdims=True)
        probs = expd / total
        log_total = row_max + jnp.log(total)
        attended = jnp.einsum(
            "shqk,skhd->sqhd",
            probs.astype(jnp.bfloat16),
            value_heads,
            preferred_element_type=jnp.float32,
        )
        attended_low = attended.reshape(rows, heads_here * HD).astype(jnp.bfloat16)
        attn_part = jnp.einsum("rh,dh->rd", attended_low, w_out, preferred_element_type=jnp.float32)
        middle = stream + lax.psum(attn_part.astype(jnp.bfloat16), "tp").astype(jnp.float32)
        ffn_in = normalize(middle, norm_two.astype(jnp.float32)).astype(jnp.bfloat16)
        logits = jnp.dot(ffn_in, w_router, preferred_element_type=jnp.float32)
        gate_dense = jnp.dot(ffn_in, w_dgate, preferred_element_type=jnp.float32)
        up_dense = jnp.dot(ffn_in, w_dup, preferred_element_type=jnp.float32)
        hidden_dense = swish_product(gate_dense, up_dense).astype(jnp.bfloat16)
        dense_part = jnp.einsum(
            "rf,df->rd", hidden_dense, w_ddown, preferred_element_type=jnp.float32
        )
        route_now = expert_ids[depth].reshape(rows, 2)
        slot_now = slot_ids[depth].reshape(rows, 2)
        pair_index = jnp.where(
            slot_now < capacity, route_now * capacity + slot_now, experts_all * capacity
        )
        pick_expert = (route_now[:, :, None] == expert_range).astype(jnp.float32)
        pick_slot = (slot_now[:, :, None] == slot_range).astype(jnp.bfloat16)
        placed = jnp.sum(
            pick_expert.astype(jnp.bfloat16)[:, :, :, None] * pick_slot[:, :, None, :], axis=1
        )
        chosen = jnp.sum(pick_expert * logits[:, None, :], axis=-1)
        shares = jax.nn.softmax(chosen, axis=-1)
        sent = jnp.einsum("rec,rd->ecd", placed, ffn_in, preferred_element_type=jnp.float32).astype(
            jnp.bfloat16
        )
        arrived = lax.all_to_all(sent, "ep", split_axis=0, concat_axis=1, tiled=True)
        gate_exp = jnp.einsum(
            "ecd,edf->ecf", arrived, expert_gate[depth], preferred_element_type=jnp.float32
        )
        up_exp = jnp.einsum(
            "ecd,edf->ecf", arrived, expert_up[depth], preferred_element_type=jnp.float32
        )
        hidden_exp = swish_product(gate_exp, up_exp).astype(jnp.bfloat16)
        out_exp = jnp.einsum(
            "ecf,efd->ecd", hidden_exp, expert_down[depth], preferred_element_type=jnp.float32
        )
        returned = lax.all_to_all(
            out_exp.astype(jnp.bfloat16), "ep", split_axis=1, concat_axis=0, tiled=True
        ).astype(out_exp.dtype)
        picked_rows = padded_rows(returned)[pair_index]
        moe_part = jnp.sum(shares[:, :, None] * picked_rows, axis=1)
        ffn_sum = lax.psum((dense_part + moe_part).astype(jnp.bfloat16), "tp").astype(jnp.float32)
        saved.append(
            (
                stream,
                normed,
                queries,
                key_heads,
                value_heads,
                log_total,
                attended_low,
                middle,
                ffn_in,
                gate_dense,
                up_dense,
                hidden_dense,
                pick_expert,
                pair_index,
                shares,
                arrived,
                gate_exp,
                up_exp,
                hidden_exp,
                picked_rows,
            )
        )
        stream = middle + ffn_sum
    outputs = stream
    shared_parts = [[None] * depth_count for column in range(10)]
    kept_rows = [None] * depth_count
    grad_stream = cotangent.astype(jnp.float32).reshape(rows, width)
    for depth in reversed(range(depth_count)):
        norm_one, w_query, w_key, w_value, w_out, norm_two, w_router, w_dgate, w_dup, w_ddown = [
            weight[depth] for weight in gathered
        ]
        (
            stream_in,
            normed,
            queries,
            key_heads,
            value_heads,
            log_total,
            attended_low,
            middle,
            ffn_in,
            gate_dense,
            up_dense,
            hidden_dense,
            pick_expert,
            pair_index,
            shares,
            arrived,
            gate_exp,
            up_exp,
            hidden_exp,
            picked_rows,
        ) = saved[depth]
        heads_here = queries.shape[2]
        ffn_grad = grad_stream.astype(jnp.bfloat16)
        ffn_grad_wide = ffn_grad.astype(jnp.float32)
        hidden_dense_grad = jnp.einsum(
            "rd,df->rf", ffn_grad, w_ddown, preferred_element_type=jnp.float32
        )
        gate_dense_grad, up_dense_grad = jax.vjp(swish_product, gate_dense, up_dense)[1](
            hidden_dense_grad
        )
        gate_dense_grad = gate_dense_grad.astype(jnp.bfloat16)
        up_dense_grad = up_dense_grad.astype(jnp.bfloat16)
        shared_parts[9][depth] = jnp.einsum(
            "rd,rf->df", ffn_grad, hidden_dense, preferred_element_type=jnp.float32
        )
        shared_parts[7][depth] = jnp.einsum(
            "rd,rf->df", ffn_in, gate_dense_grad, preferred_element_type=jnp.float32
        )
        shared_parts[8][depth] = jnp.einsum(
            "rd,rf->df", ffn_in, up_dense_grad, preferred_element_type=jnp.float32
        )
        dense_input = jnp.einsum(
            "rf,df->rd", gate_dense_grad, w_dgate, preferred_element_type=jnp.float32
        )
        dense_input = dense_input + jnp.einsum(
            "rf,df->rd", up_dense_grad, w_dup, preferred_element_type=jnp.float32
        )
        weighted = shares[:, :, None] * ffn_grad_wide[:, None, :]
        slot_flat = (
            jnp.zeros((experts_all * capacity + 1, width), jnp.float32)
            .at[pair_index.reshape(rows * 2)]
            .add(weighted.reshape(rows * 2, width))
        )
        slot_grad = (
            slot_flat[: experts_all * capacity]
            .reshape(experts_all, capacity, width)
            .astype(jnp.bfloat16)
        )
        share_part = jnp.sum(ffn_grad_wide[:, None, :] * picked_rows, axis=-1)
        back_arrived = lax.all_to_all(slot_grad, "ep", split_axis=0, concat_axis=1, tiled=True)
        hidden_exp_grad = jnp.einsum(
            "ecd,efd->ecf", back_arrived, expert_down[depth], preferred_element_type=jnp.float32
        )
        gate_exp_grad, up_exp_grad = jax.vjp(swish_product, gate_exp, up_exp)[1](hidden_exp_grad)
        gate_exp_grad = gate_exp_grad.astype(jnp.bfloat16)
        up_exp_grad = up_exp_grad.astype(jnp.bfloat16)
        kept_rows[depth] = (arrived, back_arrived)
        arrived_grad = jnp.einsum(
            "ecf,edf->ecd", gate_exp_grad, expert_gate[depth], preferred_element_type=jnp.float32
        )
        arrived_grad = arrived_grad + jnp.einsum(
            "ecf,edf->ecd", up_exp_grad, expert_up[depth], preferred_element_type=jnp.float32
        )
        sent_grad = lax.all_to_all(
            arrived_grad.astype(jnp.bfloat16), "ep", split_axis=1, concat_axis=0, tiled=True
        ).astype(arrived_grad.dtype)
        moe_input = jnp.sum(padded_rows(sent_grad)[pair_index], axis=1)
        input_sum, share_grad = (
            lax.psum((dense_input + moe_input).astype(jnp.bfloat16), "tp").astype(jnp.float32),
            lax.psum(share_part.astype(jnp.bfloat16), "tp").astype(jnp.float32),
        )
        chosen_grad = shares * (share_grad - jnp.sum(shares * share_grad, axis=-1, keepdims=True))
        logit_grad = jnp.sum(chosen_grad[:, :, None] * pick_expert, axis=1).astype(jnp.bfloat16)
        shared_parts[6][depth] = jnp.einsum(
            "rd,re->de", ffn_in, logit_grad, preferred_element_type=jnp.float32
        )
        ffn_in_grad = input_sum + jnp.einsum(
            "re,de->rd", logit_grad, w_router, preferred_element_type=jnp.float32
        )
        middle_norm_grad, gain_two_grad = jax.vjp(normalize, middle, norm_two.astype(jnp.float32))[
            1
        ](ffn_in_grad)
        shared_parts[5][depth] = gain_two_grad
        middle_grad = grad_stream + middle_norm_grad
        attn_grad = middle_grad.astype(jnp.bfloat16)
        shared_parts[4][depth] = jnp.einsum(
            "rd,rh->dh", attn_grad, attended_low, preferred_element_type=jnp.float32
        )
        attended_grad = jnp.einsum(
            "rd,dh->rh", attn_grad, w_out, preferred_element_type=jnp.float32
        ).astype(jnp.bfloat16)
        attended_grad = attended_grad.reshape(seq_count, span, heads_here, HD)
        probs = jnp.exp(masked_scores(queries, key_heads) - log_total)
        probs_grad = jnp.einsum(
            "sqhd,skhd->shqk", attended_grad, value_heads, preferred_element_type=jnp.float32
        )
        score_grad = (
            probs * (probs_grad - jnp.sum(probs * probs_grad, axis=-1, keepdims=True))
        ).astype(jnp.bfloat16)
        queries_grad = (
            jnp.einsum("shqk,skhd->sqhd", score_grad, key_heads, preferred_element_type=jnp.float32)
            * scale
        )
        keys_grad_all = (
            jnp.einsum("shqk,sqhd->skhd", score_grad, queries, preferred_element_type=jnp.float32)
            * scale
        )
        values_grad_all = jnp.einsum(
            "shqk,sqhd->skhd",
            probs.astype(jnp.bfloat16),
            attended_grad,
            preferred_element_type=jnp.float32,
        )
        keys_grad, values_grad = (
            lax.psum_scatter(
                keys_grad_all.reshape(seq_count, full_len, heads_here * HD).astype(jnp.bfloat16),
                "ep",
                scatter_dimension=1,
                tiled=True,
            ).astype(jnp.float32),
            lax.psum_scatter(
                values_grad_all.reshape(seq_count, full_len, heads_here * HD).astype(jnp.bfloat16),
                "ep",
                scatter_dimension=1,
                tiled=True,
            ).astype(jnp.float32),
        )
        query_lin_grad = (
            rotate(queries_grad, query_pos, -1.0)
            .reshape(rows, heads_here * HD)
            .astype(jnp.bfloat16)
        )
        key_lin_grad = (
            rotate(keys_grad.reshape(seq_count, span, heads_here, HD), query_pos, -1.0)
            .reshape(rows, heads_here * HD)
            .astype(jnp.bfloat16)
        )
        value_lin_grad = values_grad.reshape(rows, heads_here * HD).astype(jnp.bfloat16)
        shared_parts[1][depth] = jnp.einsum(
            "rd,rh->dh", normed, query_lin_grad, preferred_element_type=jnp.float32
        )
        shared_parts[2][depth] = jnp.einsum(
            "rd,rh->dh", normed, key_lin_grad, preferred_element_type=jnp.float32
        )
        shared_parts[3][depth] = jnp.einsum(
            "rd,rh->dh", normed, value_lin_grad, preferred_element_type=jnp.float32
        )
        normed_part = jnp.einsum(
            "rh,dh->rd", query_lin_grad, w_query, preferred_element_type=jnp.float32
        )
        normed_part = normed_part + jnp.einsum(
            "rh,dh->rd", key_lin_grad, w_key, preferred_element_type=jnp.float32
        )
        normed_part = normed_part + jnp.einsum(
            "rh,dh->rd", value_lin_grad, w_value, preferred_element_type=jnp.float32
        )
        normed_grad = lax.psum(normed_part.astype(jnp.bfloat16), "tp").astype(jnp.float32)
        stream_norm_grad, gain_one_grad = jax.vjp(
            normalize, stream_in, norm_one.astype(jnp.float32)
        )[1](normed_grad)
        shared_parts[0][depth] = gain_one_grad
        grad_stream = middle_grad + stream_norm_grad
    parts = []
    for depth in range(depth_count):
        col = [column[depth] for column in shared_parts]
        pad = jnp.zeros((width, 64), F32)
        parts += [
            jnp.concatenate([col[4], col[6], col[0][:, None], col[5][:, None], pad[:, : 64 - 18]], axis=1).astype(BF),
            jnp.concatenate([col[1], col[2], col[3], pad], axis=1).astype(BF),
            col[7].astype(BF),
            col[8].astype(BF),
            col[9].astype(BF),
        ]
    first, second, g_gate, g_up, g_down = scatter_grads(parts)
    summed = (
        first[:, :, 208],
        second[:, :, 0:192],
        second[:, :, 192:384],
        second[:, :, 384:576],
        first[:, :, 0:192],
        first[:, :, 209],
        first[:, :, 192:208],
        g_gate,
        g_up,
        g_down,
    )
    rows0, rows1, back0, back1 = gather_rows(
        [kept_rows[0][0], kept_rows[1][0], kept_rows[0][1], kept_rows[1][1]]
    )
    expert_columns = ([], [], [])
    for depth, (all_rows, all_back) in enumerate(((rows0, back0), (rows1, back1))):
        all_rows = all_rows.reshape(2, 1024, width)
        all_back = all_back.reshape(2, 1024, width)
        gate_all = jnp.einsum("ecd,edf->ecf", all_rows, expert_gate[depth], preferred_element_type=F32)
        up_all = jnp.einsum("ecd,edf->ecf", all_rows, expert_up[depth], preferred_element_type=F32)
        hidden_all = swish_product(gate_all, up_all).astype(BF)
        hidden_all_grad = jnp.einsum("ecd,efd->ecf", all_back, expert_down[depth], preferred_element_type=F32)
        gate_all_grad, up_all_grad = jax.vjp(swish_product, gate_all, up_all)[1](hidden_all_grad)
        gate_all_grad, up_all_grad = gate_all_grad.astype(BF), up_all_grad.astype(BF)
        expert_columns[0].append(jnp.einsum("ecd,ecf->edf", all_rows, gate_all_grad, preferred_element_type=F32))
        expert_columns[1].append(jnp.einsum("ecd,ecf->edf", all_rows, up_all_grad, preferred_element_type=F32))
        expert_columns[2].append(jnp.einsum("ecf,ecd->efd", hidden_all, all_back, preferred_element_type=F32))
    expert_sums = [jnp.stack(column) for column in expert_columns]
    outputs = outputs.reshape(seq_count, span, width)
    input_grad = grad_stream.reshape(seq_count, span, width)
    return (
        outputs,
        input_grad,
        summed[0],
        summed[1],
        summed[2],
        summed[3],
        summed[4],
        summed[5],
        summed[6],
        summed[7],
        summed[8],
        summed[9],
        expert_sums[0],
        expert_sums[1],
        expert_sums[2],
    )


def solution(mesh):
    return jax.shard_map(
        shards,
        mesh=mesh,
        in_specs=(
            P("dp", "ep", None),
            P("dp"),
            P(None, "dp", "ep", None),
            P(None, "dp", "ep", None),
            P(None, ("dp", "ep")),
            P(None, ("dp", "ep"), "tp"),
            P(None, ("dp", "ep"), "tp"),
            P(None, ("dp", "ep"), "tp"),
            P(None, ("dp", "ep"), "tp"),
            P(None, ("dp", "ep")),
            P(None, ("dp", "ep"), None),
            P(None, ("dp", "ep"), "tp"),
            P(None, ("dp", "ep"), "tp"),
            P(None, ("dp", "ep"), "tp"),
            P(None, "ep", None, "tp"),
            P(None, "ep", None, "tp"),
            P(None, "ep", "tp", None),
            P("dp", "ep", None),
        ),
        out_specs=(
            P("dp", "ep", None),
            P("dp", "ep", None),
            P(None, ("dp", "ep")),
            P(None, ("dp", "ep"), "tp"),
            P(None, ("dp", "ep"), "tp"),
            P(None, ("dp", "ep"), "tp"),
            P(None, ("dp", "ep"), "tp"),
            P(None, ("dp", "ep")),
            P(None, ("dp", "ep"), None),
            P(None, ("dp", "ep"), "tp"),
            P(None, ("dp", "ep"), "tp"),
            P(None, ("dp", "ep"), "tp"),
            P(None, "ep", None, "tp"),
            P(None, "ep", None, "tp"),
            P(None, "ep", "tp", None),
        ),
        check_vma=False,
    )
```

```python
import functools

import jax
import jax.numpy as jnp
from jax import lax
from jax.experimental import pallas as pl
from jax.experimental.pallas import tpu as pltpu
from jax.sharding import PartitionSpec as P

HD = 64
MESH = pl.DeviceIdType.MESH
BF = jnp.bfloat16
F32 = jnp.float32
WIDE = 2432
CHUNK = 48
VM = pl.BlockSpec(memory_space=pltpu.VMEM)


def place():
    y = lax.axis_index("dp")
    e = lax.axis_index("ep")
    z = lax.axis_index("tp")
    return y, e // 2, e % 2, z


def device(y, x, c, z):
    return (y, x * 2 + c, z)


def meet(givers, takers):
    barrier = pltpu.get_barrier_semaphore()
    for who in givers:
        pl.semaphore_signal(barrier, inc=1, device_id=who, device_id_type=MESH)
    pl.semaphore_wait(barrier, takers)


class Line:
    def __init__(self, send_sems, recv_sems):
        self.send_sems, self.recv_sems, self.used, self.open = send_sems, recv_sems, 0, []

    def start(self, src, dst, who):
        at = self.used
        self.used += 1
        copy = pltpu.make_async_remote_copy(
            src_ref=src,
            dst_ref=dst,
            send_sem=self.send_sems.at[at],
            recv_sem=self.recv_sems.at[at],
            device_id=who,
            device_id_type=MESH,
        )
        copy.start()
        self.open.append(copy)
        return copy

    def finish(self):
        for copy in self.open:
            copy.wait_send()


def gather_kernel(src, out, land, send_sems, recv_sems):
    y, x, c, z = place()

    def at(j, d, core=None):
        yy = (y + j * c + d * (1 - c) + 8) % 4
        xx = (x + j * (1 - c) + d * c + 8) % 4
        return yy, xx

    def who(j, d):
        yy, xx = at(j, d)
        return device(yy, xx, c, z)

    def slot(j, d):
        yy, xx = at(j, d)
        return yy * 8 + xx * 2 + c

    sibling = device(y, x, 1 - c, z)
    near = [who(1, 0), who(-1, 0), who(0, 1), who(0, -1), sibling]
    meet(near, 5)
    line = Line(send_sems, recv_sems)
    sib = []

    def spread(ref, j):
        plus = line.start(ref, land.at[slot(j, 0)], who(0, 1))
        minus = line.start(ref, land.at[slot(j, 0)], who(0, -1))
        sib.append(line.start(ref, land.at[slot(j, 0)], sibling))
        return plus, minus

    first_plus = line.start(src, land.at[slot(0, 0)], who(1, 0))
    first_minus = line.start(src, land.at[slot(0, 0)], who(-1, 0))
    second = {0: spread(src, 0)}
    land[slot(0, 0)] = src[...]
    first_plus.wait_recv()
    below = land.at[slot(-1, 0)]
    on_plus = line.start(below.at[pl.ds(0, 32)], below.at[pl.ds(0, 32)], who(1, 0))
    second[-1] = spread(below, -1)
    first_minus.wait_recv()
    above = land.at[slot(1, 0)]
    on_minus = line.start(above.at[pl.ds(32, 16)], above.at[pl.ds(32, 16)], who(-1, 0))
    second[1] = spread(above, 1)
    on_plus.wait_recv()
    on_minus.wait_recv()
    second[2] = spread(land.at[slot(2, 0)], 2)
    far = []
    for j in (0, -1, 1, 2):
        plus, minus = second[j]
        plus.wait_recv()
        got = land.at[slot(j, -1)]
        sib.append(line.start(got, got, sibling))
        if j in (0, -1):
            far.append((j, line.start(got, got, who(0, 1))))
        minus.wait_recv()
        got = land.at[slot(j, 1)]
        sib.append(line.start(got, got, sibling))
        if j in (1, 2):
            far.append((j, line.start(got, got, who(0, -1))))
    for j, copy in far:
        copy.wait_recv()
        got = land.at[slot(j, 2)]
        sib.append(line.start(got, got, sibling))
    for copy in sib:
        copy.wait_recv()
    line.finish()

    def unpack(p, carry):
        one = land[2 * p].astype(F32)
        two = land[2 * p + 1].astype(F32)
        rows = pl.ds(pl.multiple_of(p * CHUNK, CHUNK), CHUNK)
        out[0, rows] = jnp.concatenate([one[:24], two[:24]], axis=0).astype(BF)
        out[1, rows] = jnp.concatenate([one[24:], two[24:]], axis=0).astype(BF)
        return carry

    lax.fori_loop(0, 16, unpack, 0)


def gather_weights(src):
    return pl.pallas_call(
        gather_kernel,
        out_shape=jax.ShapeDtypeStruct((2, 768, WIDE), BF),
        in_specs=[VM],
        out_specs=VM,
        scratch_shapes=[
            pltpu.VMEM((32, CHUNK, WIDE), BF),
            pltpu.SemaphoreType.DMA((32,)),
            pltpu.SemaphoreType.DMA((32,)),
        ],
        compiler_params=pltpu.CompilerParams(
            collective_id=0, has_side_effects=True, vmem_limit_bytes=48 * 2**20
        ),
        name="gather_weights",
    )(src)


EPS = 1e-06
WIDTHS = (256, 640, 1024, 512)
SMALL = slice(128, 256)
ROUTER = 64
GAIN = 80
OUT = slice(0, 192)
QKV = slice(256, 896)
GATEUP = slice(896, 1920)
GATE = slice(896, 1408)
UP = slice(1408, 1920)
DOWN = slice(1920, 2432)


def mm(a, b):
    return lax.dot_general(a, b, (((1,), (0,)), ((), ())), preferred_element_type=F32)


def mm_t(a, b):
    return lax.dot_general(a, b, (((1,), (1,)), ((), ())), preferred_element_type=F32)


def t_mm(a, b):
    return lax.dot_general(a, b, (((0,), (0,)), ((), ())), preferred_element_type=F32)


def lanes(shape):
    return lax.broadcasted_iota(jnp.int32, shape, 1)


def gain_rows(weights):
    pick = (lanes((8, 128)) == lax.broadcasted_iota(jnp.int32, (8, 128), 0) + GAIN).astype(BF)
    return mm_t(pick, weights[:, SMALL])


def rms(values, gain):
    turn = lax.rsqrt(jnp.mean(values * values, axis=-1, keepdims=True) + EPS)
    return values * turn * gain


def rms_back(values, gain, grad):
    turn = lax.rsqrt(jnp.mean(values * values, axis=-1, keepdims=True) + EPS)
    scaled = grad * gain
    back = turn * scaled - values * (turn * turn * turn) * jnp.mean(values * scaled, axis=-1, keepdims=True)
    return back, jnp.sum(grad * values * turn, axis=0, keepdims=True)


def turned(values, cosine, sine):
    width = values.shape[1]
    front = lanes(values.shape) % HD < HD // 2
    other = jnp.where(front, pltpu.roll(values, width - HD // 2, 1), pltpu.roll(values, HD // 2, 1))
    return values * cosine + other * sine


def sigmoid(v):
    return 1.0 / (1.0 + jnp.exp(-v))


def swish_back(gate, up, grad):
    s = sigmoid(gate)
    return (grad * up * s * (1.0 + gate * (1.0 - s))).astype(BF), (grad * gate * s).astype(BF)


def two(values):
    return jnp.concatenate([values, values], axis=0)


def scatter_kernel(*refs):
    ins, gains, outs = refs[:8], refs[8:10], refs[10:14]
    chunks, sib_land, plus_far, minus_far, plus_near, minus_near, one_far, one_near, columns, send_sems, recv_sems = refs[14:]
    y, x, c, z = place()

    def at(j, d):
        yy = (y + j * c + d * (1 - c) + 8) % 4
        xx = (x + j * (1 - c) + d * c + 8) % 4
        return yy, xx

    def who(j, d):
        yy, xx = at(j, d)
        return device(yy, xx, c, z)

    def slot(j, d, core):
        yy, xx = at(j, d)
        return yy * 8 + xx * 2 + core

    sibling = device(y, x, 1 - c, z)
    meet([who(1, 0), who(-1, 0), who(0, 1), who(0, -1), sibling], 5)

    spot = lanes((8, 256)) == lax.broadcasted_iota(jnp.int32, (8, 256), 0) + 128 + GAIN

    def pack(p, carry):
        rows = pl.ds(pl.multiple_of(p * CHUNK, CHUNK), CHUNK)
        left = 0
        for part, width in enumerate(WIDTHS):
            one = ins[part][rows].astype(F32)
            two = ins[4 + part][rows].astype(F32)
            if part == 0:
                one += columns[0, rows]
                two += columns[1, rows]
            cols = slice(left, left + width)
            chunks[2 * p, :, cols] = jnp.concatenate([one[:24], two[:24]], axis=0).astype(BF)
            chunks[2 * p + 1, :, cols] = jnp.concatenate([one[24:], two[24:]], axis=0).astype(BF)
            left += width
        return carry

    for layer in range(2):
        columns[layer] = t_mm(gains[layer][...].astype(BF), spot.astype(BF))
    lax.fori_loop(0, 16, pack, 0)
    line = Line(send_sems, recv_sems)
    order = [(j, d) for d in (2, 1, -1, 0) for j in (0, -1, 1, 2)]
    swapped = {}
    for n, (j, d) in enumerate(order):
        yy = (y + j * (1 - c) + d * c + 8) % 4
        xx = (x + j * c + d * (1 - c) + 8) % 4
        swapped[j, d] = line.start(chunks.at[yy * 8 + xx * 2 + 1 - c], sib_land.at[n], sibling)

    def join(j, d):
        n = order.index((j, d))
        swapped[j, d].wait_recv()
        mine = slot(j, d, c)
        chunks[mine] = (chunks[mine].astype(F32) + sib_land[n].astype(F32)).astype(BF)
        return chunks.at[mine]

    plus_set, minus_set = (0, -1), (1, 2)
    far = {}
    for j in (0, -1, 1, 2):
        ref = join(j, 2)
        if j in plus_set:
            far[j] = line.start(ref, plus_far.at[plus_set.index(j)], who(0, 1))
        else:
            far[j] = line.start(ref, minus_far.at[minus_set.index(j)], who(0, -1))
    near = {}
    for j in (1, 2):
        near[j, 1] = line.start(join(j, 1), plus_near.at[j], who(0, 1))
    for j in (0, -1):
        near[j, -1] = line.start(join(j, -1), minus_near.at[j % 4], who(0, -1))
    for j in plus_set:
        ref = join(j, 1)
        far[j].wait_recv()
        ref[...] = (ref[...].astype(F32) + plus_far[plus_set.index(j)].astype(F32)).astype(BF)
        near[j, 1] = line.start(ref, plus_near.at[j % 4], who(0, 1))
    for j in minus_set:
        ref = join(j, -1)
        far[j].wait_recv()
        ref[...] = (ref[...].astype(F32) + minus_far[minus_set.index(j)].astype(F32)).astype(BF)
        near[j, -1] = line.start(ref, minus_near.at[j], who(0, -1))
    held = {}
    for j in (2, 1, -1, 0):
        ref = join(j, 0)
        near[j, 1].wait_recv()
        near[j, -1].wait_recv()
        total = ref[...].astype(F32) + plus_near[j % 4].astype(F32) + minus_near[j % 4].astype(F32)
        ref[...] = total.astype(BF)
        held[j] = ref
        if j == 2:
            a = line.start(ref.at[pl.ds(0, 32)], one_far.at[pl.ds(0, 32)], who(1, 0))
            b = line.start(ref.at[pl.ds(32, 16)], one_far.at[pl.ds(32, 16)], who(-1, 0))
    a.wait_recv()
    up = held[1].at[pl.ds(0, 32)]
    up[...] = (up[...].astype(F32) + one_far[:32].astype(F32)).astype(BF)
    last_plus = line.start(held[1], one_near.at[0], who(1, 0))
    b.wait_recv()
    down = held[-1].at[pl.ds(32, 16)]
    down[...] = (down[...].astype(F32) + one_far[32:].astype(F32)).astype(BF)
    last_minus = line.start(held[-1], one_near.at[1], who(-1, 0))
    last_plus.wait_recv()
    last_minus.wait_recv()
    left = 0
    for part, width in enumerate(WIDTHS):
        cols = slice(left, left + width)
        total = held[0][:, cols].astype(F32) + one_near[0, :, cols].astype(F32) + one_near[1, :, cols].astype(F32)
        outs[part][0] = total[:24]
        outs[part][1] = total[24:]
        left += width
    line.finish()


def scatter_grads(parts):
    chunk = lambda n: pltpu.VMEM((n, CHUNK, WIDE), BF)
    return pl.pallas_call(
        scatter_kernel,
        out_shape=[jax.ShapeDtypeStruct((2, 24, width), F32) for width in WIDTHS],
        in_specs=[VM] * 10,
        out_specs=[VM] * 4,
        scratch_shapes=[
            chunk(32),
            chunk(16),
            chunk(2),
            chunk(2),
            chunk(4),
            chunk(4),
            pltpu.VMEM((CHUNK, WIDE), BF),
            chunk(2),
            pltpu.VMEM((2, 768, 256), F32),
            pltpu.SemaphoreType.DMA((32,)),
            pltpu.SemaphoreType.DMA((32,)),
        ],
        compiler_params=pltpu.CompilerParams(
            collective_id=1, has_side_effects=True, vmem_limit_bytes=56 * 2**20
        ),
        name="scatter_grads",
    )(*parts)


def rows_kernel(a0, a1, b0, b1, o0, o1, o2, o3, send_sems, recv_sems):
    y, x, c, z = place()

    def along(dy, dz):
        return device((y + dy + 4) % 4, x, c, (z + dz + 4) % 4)

    meet([along(1, 0), along(-1, 0), along(0, 1), along(0, -1)], 4)
    line = Line(send_sems, recv_sems)

    def quarter(k, first, count):
        return pl.ds(pl.multiple_of(((z + k + 4) % 4) * 64 + first, 32), count)

    work = list(zip((a0, a1, b0, b1), (o0, o1, o2, o3)))
    near, half, full, spread = [], [], [], []
    for src, out in work:
        mine = src.at[0, quarter(0, 0, 64)]
        near.append(
            (
                line.start(mine, out.at[0, 1, quarter(0, 0, 64)], along(1, 0)),
                line.start(mine, out.at[0, 3, quarter(0, 0, 64)], along(-1, 0)),
            )
        )
        full.append(
            (
                line.start(src.at[1], out.at[1, 1], along(1, 0)),
                line.start(src.at[1], out.at[1, 3], along(-1, 0)),
            )
        )
    for (src, out), (plus, minus) in zip(work, near):
        plus.wait_recv()
        p = line.start(out.at[0, 1, quarter(0, 0, 32)], out.at[0, 2, quarter(0, 0, 32)], along(1, 0))
        minus.wait_recv()
        m = line.start(out.at[0, 3, quarter(0, 32, 32)], out.at[0, 2, quarter(0, 32, 32)], along(-1, 0))
        half.append((p, m))
    for (src, out), (plus, minus) in zip(work, half):
        plus.wait_recv()
        minus.wait_recv()
        got = out.at[0, pl.ds(1, 3), quarter(0, 0, 64)]
        spread.append((line.start(got, got, along(0, 1)), line.start(got, got, along(0, -1))))
    last = []
    for (src, out), (plus, minus) in zip(work, full):
        plus.wait_recv()
        p = line.start(out.at[1, 1, pl.ds(0, 128)], out.at[1, 2, pl.ds(0, 128)], along(1, 0))
        minus.wait_recv()
        m = line.start(out.at[1, 3, pl.ds(128, 128)], out.at[1, 2, pl.ds(128, 128)], along(-1, 0))
        last += [p, m]
    for (src, out), (plus, minus) in zip(work, spread):
        plus.wait_recv()
        got = out.at[0, pl.ds(1, 3), quarter(-1, 0, 32)]
        last.append(line.start(got, got, along(0, 1)))
        minus.wait_recv()
        got = out.at[0, pl.ds(1, 3), quarter(1, 32, 32)]
        last.append(line.start(got, got, along(0, -1)))
        out[:, 0] = src[...]
    for copy in last:
        copy.wait_recv()
    line.finish()


def gather_rows(arrays):
    shape = jax.ShapeDtypeStruct((2, 4, 256, 768), BF)
    return pl.pallas_call(
        rows_kernel,
        out_shape=[shape] * 4,
        in_specs=[VM] * 4,
        out_specs=[VM] * 4,
        scratch_shapes=[pltpu.SemaphoreType.DMA((48,)), pltpu.SemaphoreType.DMA((48,))],
        compiler_params=pltpu.CompilerParams(
            collective_id=2, has_side_effects=True, vmem_limit_bytes=48 * 2**20
        ),
        name="gather_rows",
    )(*arrays)


class Wires:
    def __init__(self, sends, recvs):
        self.sends, self.recvs, self.used, self.open = sends, recvs, 0, []

    def plan(self, src, dst, who, when=None):
        at = self.used
        self.used += 1
        copy = pltpu.make_async_remote_copy(
            src_ref=src,
            dst_ref=dst,
            send_sem=self.sends.at[at],
            recv_sem=self.recvs.at[at],
            device_id=who,
            device_id_type=MESH,
        )
        self.open.append((copy, when))
        return copy

    def go(self, src, dst, who):
        copy = self.plan(src, dst, who)
        copy.start()
        return copy

    def finish(self):
        for copy, when in self.open:
            if when is None:
                copy.wait_send()
            else:
                pl.when(when)(copy.wait_send)


def peers(y, e, z):
    row = [(y, (e + k) % 8, z) for k in range(1, 8)]
    return row, [(y, e, (z + k) % 4) for k in range(1, 4)]


def spread_rows(wires, held, y, e, z):
    sent = [wires.go(held.at[z], held.at[z], (y, e, (z + k) % 4)) for k in (2, 1, 3)]
    return lambda: [copy.wait_recv() for copy in sent]


def sum_rows(wires, parts, land, y, e, z):
    sent = []
    for k in (2, 1, 3):
        who = (z + k) % 4
        sent.append(wires.go(parts.at[who], land.at[k - 1], (y, e, who)))

    def total():
        for copy in sent:
            copy.wait_recv()
        return (
            parts[z].astype(F32) + land[0].astype(F32) + land[1].astype(F32) + land[2].astype(F32)
        )

    return total


def scatter_experts(wires, src, dst, y, e, z, i):
    rows = pl.ds(pl.multiple_of(e * 32, 32), 32)
    sent = []
    for k in (4, 3, 5, 2, 6, 1, 7):
        who = (e + k) % 8
        sent.append(wires.go(src.at[2 * who + i], dst.at[i, rows], (y, who, z)))
    dst[i, rows] = src[2 * e + i]
    return lambda: [copy.wait_recv() for copy in sent]


def return_experts(wires, src, dst, y, e, z, i):
    sent = []
    for k in (4, 3, 5, 2, 6, 1, 7):
        who = (e + k) % 8
        rows = pl.ds(pl.multiple_of(who * 32, 32), 32)
        sent.append(wires.go(src.at[i, rows], dst.at[2 * e + i], (y, who, z)))
    dst[2 * e + i] = src[i, pl.ds(pl.multiple_of(e * 32, 32), 32)]
    return lambda: [copy.wait_recv() for copy in sent]


def picks(route):
    slots = lanes((256, 512))
    return slots == route[:, 0:1], slots == route[:, 1:2]


def forward_kernel(
    layer, stream, own, lengths, route, cos, sin, w_all, eg_all, eu_all, ed_all,
    normed, queries, kv, probs, attended, middle, ffn_in, gud, gue, ret, shares, arrived, own_out, stream_out,
    w, eg, eu, ed, part, land, sent, made, local, sends, recvs,
):
    y, x, c, z = place()
    e = 2 * x + c
    row, column = peers(y, e, z)
    fetch = [
        pltpu.make_async_copy(src.at[layer], dst, local.at[n])
        for n, (src, dst) in enumerate(((w_all, w), (eg_all, eg), (eu_all, eu), (ed_all, ed)))
    ]
    for copy in fetch:
        copy.start()
    meet(row + column, 10)
    wires = Wires(sends, recvs)
    fetch[0].wait()
    gains = gain_rows(w)
    values = stream[...].reshape(256, 768).astype(F32)
    normed[...] = rms(values, gains[0:1]).astype(BF)
    lin = turned(mm(normed[...], w[:, QKV]), two(cos[...]), two(sin[...])).astype(BF)
    kv[e] = lin[:, :384]
    queries[...] = lin[:, 384:576]
    sibling = (y, e + 1 - 2 * c, z)
    first, second = [], []
    for k in (2, 3, 1):
        ahead, behind = x + k <= 3, x - k >= 0
        copy = wires.plan(kv.at[e], kv.at[e], (y, (e + 2 * k) % 8, z), ahead)
        pl.when(ahead)(copy.start)
        first.append((k, behind, copy))
    to_core = wires.plan(kv.at[e], kv.at[e], sibling, c == 0)
    pl.when(c == 0)(to_core.start)
    for j in range(8):

        @pl.when(j > e)
        def _():
            kv[j] = jnp.zeros((256, 384), BF)

    for k, behind, copy in reversed(first):
        slot = (e + 8 - 2 * k) % 8
        on = wires.plan(kv.at[slot], kv.at[slot], sibling, behind)

        @pl.when(behind)
        def _():
            copy.wait_recv()
            on.start()

        second.append((behind, on))
    pl.when(c == 1)(to_core.wait_recv)
    for behind, on in second:
        pl.when(behind)(on.wait_recv)
    at_key = lanes((128, 1024))
    at_query = lax.broadcasted_iota(jnp.int32, (128, 1024), 0) + e * 128
    for s in range(2):
        rows = slice(s * 128, s * 128 + 128)
        allowed = (at_key <= at_query) & (at_key < lengths[s : s + 1, 0:1])
        for h in range(3):
            keys = kv[:, rows, 64 * h : 64 * h + 64].reshape(1024, 64)
            vals = kv[:, rows, 192 + 64 * h : 256 + 64 * h].reshape(1024, 64)
            scores = jnp.where(allowed, mm_t(queries[rows, 64 * h : 64 * h + 64], keys) * HD**-0.5, -1e30)
            expd = jnp.exp(scores - jnp.max(scores, axis=-1, keepdims=True))
            low = (expd / jnp.sum(expd, axis=-1, keepdims=True)).astype(BF)
            probs[3 * s + h] = low
            attended[rows, 64 * h : 64 * h + 64] = mm(low, vals).astype(BF)
    part[0] = mm_t(attended[...], w[:, OUT]).astype(BF).reshape(4, 64, 768)
    total = sum_rows(wires, part.at[0], land.at[0], y, e, z)()
    middle[...] = own[...] + total
    ffn_in[z] = rms(middle[...], gains[1:2]).astype(BF)
    spread_rows(wires, ffn_in, y, e, z)()
    rows_in = ffn_in[...].reshape(256, 768)
    ids = route[...]
    pick0, pick1 = picks(ids)
    sent[...] = t_mm((pick0 | pick1).astype(BF), rows_in).astype(BF).reshape(16, 32, 768)
    coming = [scatter_experts(wires, sent, arrived, y, e, z, i) for i in range(2)]
    logits = mm(rows_in, w[:, SMALL])
    lane = lanes((256, 128))
    chosen = [
        jnp.sum(jnp.where(lane == ids[:, 2 + j : 3 + j] + ROUTER, logits, 0.0), axis=-1, keepdims=True)
        for j in range(2)
    ]
    top = jnp.maximum(chosen[0], chosen[1])
    expd = [jnp.exp(v - top) for v in chosen]
    share = [v / (expd[0] + expd[1]) for v in expd]
    shares[...] = jnp.where(lane == 0, share[0], jnp.where(lane == 1, share[1], 0.0))
    gud[...] = mm(rows_in, w[:, GATEUP])
    gate, up = gud[:, :512], gud[:, 512:]
    hidden = (gate * sigmoid(gate) * up).astype(BF)
    dense = mm_t(hidden, w[:, DOWN])
    for copy in fetch[1:]:
        copy.wait()
    back = []
    for i in range(2):
        coming[i]()
        gue[i, :, :512] = mm(arrived[i], eg[i])
        gue[i, :, 512:] = mm(arrived[i], eu[i])
        gate, up = gue[i, :, :512], gue[i, :, 512:]
        hidden = (gate * sigmoid(gate) * up).astype(BF)
        made[i] = mm(hidden, ed[i]).astype(BF)
        back.append(return_experts(wires, made, ret, y, e, z, i))
    for wait in back:
        wait()
    mix = (jnp.where(pick0, share[0], 0.0) + jnp.where(pick1, share[1], 0.0)).astype(BF)
    moe = mm(mix, ret[...].reshape(512, 768))
    part[1] = (dense + moe).astype(BF).reshape(4, 64, 768)
    total = sum_rows(wires, part.at[1], land.at[1], y, e, z)()
    result = middle[...] + total
    own_out[...] = result
    stream_out[z] = result.astype(BF)
    spread_rows(wires, stream_out, y, e, z)()
    wires.finish()


def backward_kernel(
    layer, incoming, grad_own, own, middle, normed, queries, kv, probs, attended, ffn_in, gud, gue, ret, shares, route, cos, sin,
    w_all, eg_all, eu_all, ed_all,
    grad_os, grad_qkv, grad_gu, grad_d, grad_gain, arrived, down_own, down_stream,
    w, eg, eu, ed, part_ffn, land_ffn, part, land, sent, made, sret, gathered, tail, dkv, sib_land, owner_land, lin,
    local, sends, recvs,
):
    y, x, c, z = place()
    e = 2 * x + c
    row, column = peers(y, e, z)
    fetch = [
        pltpu.make_async_copy(src.at[layer], dst, local.at[n])
        for n, (src, dst) in enumerate(((w_all, w), (eg_all, eg), (eu_all, eu), (ed_all, ed)))
    ]
    for copy in fetch:
        copy.start()
    meet(row + column, 10)
    wires = Wires(sends, recvs)
    mine = pl.ds(pl.multiple_of(z * 64, 64), 64)
    ffn_grad = incoming[...].reshape(256, 768)
    rows_in = ffn_in[...].reshape(256, 768)
    pick0, pick1 = picks(route[...])
    mix = (jnp.where(pick0, shares[:, 0:1], 0.0) + jnp.where(pick1, shares[:, 1:2], 0.0)).astype(BF)
    sent[...] = t_mm(mix, ffn_grad).astype(BF).reshape(16, 32, 768)
    coming = [scatter_experts(wires, sent, arrived, y, e, z, i) for i in range(2)]
    fetch[0].wait()
    gains = gain_rows(w)
    gate, up = gud[:, :512], gud[:, 512:]
    hidden_dense = (gate * sigmoid(gate) * up).astype(BF)
    gate_grad, up_grad = swish_back(gate, up, mm(ffn_grad, w[:, DOWN]))
    gu_grad = jnp.concatenate([gate_grad, up_grad], axis=1)
    dense = mm_t(gu_grad, w[:, GATEUP])
    match = mm_t(ffn_grad, ret[...].reshape(512, 768))
    share_grad = [
        jnp.sum(jnp.where(pick, match, 0.0), axis=-1, keepdims=True) for pick in (pick0, pick1)
    ]
    lane = lanes((256, 128))
    extra = jnp.where(lane == 0, share_grad[0], jnp.where(lane == 1, share_grad[1], 0.0))
    part_ffn[:, :, 768:] = extra.astype(BF).reshape(4, 64, 128)
    for copy in fetch[1:]:
        copy.wait()
    back = []
    for i in range(2):
        coming[i]()
        hidden_grad = mm_t(arrived[i], ed[i])
        gate_e, up_e = swish_back(gue[i, :, :512], gue[i, :, 512:], hidden_grad)
        made[i] = (mm_t(gate_e, eg[i]) + mm_t(up_e, eu[i])).astype(BF)
        back.append(return_experts(wires, made, sret, y, e, z, i))
    grad_gu[...] = t_mm(rows_in, gu_grad).astype(BF)
    grad_d[...] = t_mm(ffn_grad, hidden_dense).astype(BF)
    for wait in back:
        wait()
    dense += mm((pick0 | pick1).astype(BF), sret[...].reshape(512, 768))
    part_ffn[:, :, :768] = dense.astype(BF).reshape(4, 64, 768)
    total = sum_rows(wires, part_ffn, land_ffn, y, e, z)()
    input_sum = total[:, :768]
    share = shares[mine]
    ids = route[mine]
    weigh = share[:, 0:1] * total[:, 768:769] + share[:, 1:2] * total[:, 769:770]
    lane = lanes((64, 128))
    logit_grad = jnp.zeros((64, 128), F32)
    for j in range(2):
        chosen_grad = share[:, j : j + 1] * (total[:, 768 + j : 769 + j] - weigh)
        logit_grad += jnp.where(lane == ids[:, 2 + j : 3 + j] + ROUTER, chosen_grad, 0.0)
    logit_grad = logit_grad.astype(BF)
    back_norm, gain_two = rms_back(middle[...], gains[1:2], input_sum + mm_t(logit_grad, w[:, SMALL]))
    middle_grad = grad_own[...] + back_norm
    down_own[...] = middle_grad
    top = lax.broadcasted_iota(jnp.int32, (16, 768), 0) == 0
    gathered[z, :64, :768] = middle_grad.astype(BF)
    gathered[z, :64, 768:] = logit_grad
    gathered[z, 64:, :768] = jnp.where(top, gain_two, 0.0).astype(BF)
    gathered[z, 64:, 768:] = jnp.zeros((16, 128), BF)
    spread_rows(wires, gathered, y, e, z)()
    attn_grad = gathered[:, :64, :768].reshape(256, 768)
    attended_grad = mm(attn_grad, w[:, OUT]).astype(BF)
    for s in range(2):
        rows = slice(s * 128, s * 128 + 128)
        for h in range(3):
            cols = slice(64 * h, 64 * h + 64)
            late = slice(192 + 64 * h, 256 + 64 * h)
            keys = kv[:, rows, cols].reshape(1024, 64)
            vals = kv[:, rows, late].reshape(1024, 64)
            low = probs[3 * s + h]
            wide = low.astype(F32)
            grad_here = attended_grad[rows, cols]
            probs_grad = mm_t(grad_here, vals)
            kept = jnp.sum(wide * probs_grad, axis=-1, keepdims=True)
            score_grad = (wide * (probs_grad - kept)).astype(BF)
            lin[rows, 384 + 64 * h : 448 + 64 * h] = mm(score_grad, keys) * HD**-0.5
            keys_grad = t_mm(score_grad, queries[rows, cols]) * HD**-0.5
            dkv[:, rows, cols] = keys_grad.astype(BF).reshape(8, 128, 64)
            dkv[:, rows, late] = t_mm(low, grad_here).astype(BF).reshape(8, 128, 64)
    sibling = (y, e + 1 - 2 * c, z)
    swaps = []
    for k in range(4):
        gives = (x - k >= 0) & ((c == 1) if k == 0 else True)
        takes = (x - k >= 0) & ((c == 0) if k == 0 else True)
        copy = wires.plan(dkv.at[(2 * (x - k) + 1 - c + 8) % 8], sib_land.at[k], sibling, gives)
        pl.when(gives)(copy.start)
        swaps.append((takes, copy))
    far = []
    for k in (2, 3, 1):
        gives, takes = x - k >= 0, x + k <= 3
        block = (e - 2 * k + 8) % 8
        send = wires.plan(dkv.at[block], owner_land.at[k - 1], (y, block, z), gives)

        @pl.when(gives)
        def _():
            swaps[k][1].wait_recv()
            dkv[block] = (dkv[block].astype(F32) + sib_land[k].astype(F32)).astype(BF)
            send.start()

        far.append((k, takes, send))
    grad_os[:, :192] = t_mm(attn_grad, attended[...]).astype(BF)
    grad_os[:, 192:] = t_mm(rows_in, gathered[:, :64, 768:].reshape(256, 128)).astype(BF)[:, 64:]
    lin[:, :384] = dkv[e].astype(F32)
    lin[:, 576:] = jnp.zeros((256, 64), F32)

    @pl.when(swaps[0][0])
    def _():
        swaps[0][1].wait_recv()
        lin[:, :384] += sib_land[0].astype(F32)

    for k, takes, copy in reversed(far):

        @pl.when(takes)
        def _():
            copy.wait_recv()
            lin[:, :384] += owner_land[k - 1].astype(F32)

    lin_grad = turned(lin[...], two(cos[...]), -two(sin[...])).astype(BF)
    part[...] = mm_t(lin_grad, w[:, QKV]).astype(BF).reshape(4, 64, 768)
    summed = sum_rows(wires, part, land, y, e, z)
    grad_qkv[...] = t_mm(normed[...], lin_grad).astype(BF)
    back_norm, gain_one = rms_back(own[...], gains[0:1], summed())
    result = down_own[...] + back_norm
    down_own[...] = result
    tail[z, :64] = result.astype(BF)
    tail[z, 64:] = jnp.where(top, gain_one, 0.0).astype(BF)
    spread_rows(wires, tail, y, e, z)()
    down_stream[...] = tail[:, :64]
    one = jnp.sum(tail[:, 64:].astype(F32).reshape(64, 768), axis=0, keepdims=True)
    both = jnp.sum(gathered[:, 64:, :768].astype(F32).reshape(64, 768), axis=0, keepdims=True)
    at_row = lax.broadcasted_iota(jnp.int32, (8, 768), 0)
    grad_gain[...] = jnp.where(at_row == 0, one, jnp.where(at_row == 1, both, 0.0))
    wires.finish()


ANY = pl.BlockSpec(memory_space=pl.ANY)
WEIGHTS = [
    pltpu.VMEM((768, WIDE), BF),
    pltpu.VMEM((2, 768, 512), BF),
    pltpu.VMEM((2, 768, 512), BF),
    pltpu.VMEM((2, 512, 768), BF),
]
ROWS4 = (4, 64, 768)
SAVED = [
    ((256, 768), BF),
    ((256, 192), BF),
    ((8, 256, 384), BF),
    ((6, 128, 1024), BF),
    ((256, 192), BF),
    ((64, 768), F32),
    (ROWS4, BF),
    ((256, 1024), F32),
    ((2, 256, 1024), F32),
    ((16, 32, 768), BF),
    ((256, 128), F32),
]


def forward(layer, stream, own, lengths, route, cos, sin, w, eg, eu, ed):
    out = SAVED + [((2, 256, 768), BF), ((64, 768), F32), (ROWS4, BF)]
    return pl.pallas_call(
        functools.partial(forward_kernel, layer),
        out_shape=[jax.ShapeDtypeStruct(*one) for one in out],
        in_specs=[VM] * 6 + [ANY] * 4,
        out_specs=[VM] * len(out),
        scratch_shapes=WEIGHTS
        + [
            pltpu.VMEM((2, 4, 64, 768), BF),
            pltpu.VMEM((2, 3, 64, 768), BF),
            pltpu.VMEM((16, 32, 768), BF),
            pltpu.VMEM((2, 256, 768), BF),
            pltpu.SemaphoreType.DMA((4,)),
            pltpu.SemaphoreType.DMA((48,)),
            pltpu.SemaphoreType.DMA((48,)),
        ],
        compiler_params=pltpu.CompilerParams(
            collective_id=3 + layer, has_side_effects=True, vmem_limit_bytes=52 * 2**20
        ),
        name=f"block_forward_{layer}",
    )(stream, own, lengths, route, cos, sin, w, eg, eu, ed)


def backward(layer, incoming, grad_own, own, saved, route, cos, sin, w, eg, eu, ed):
    normed, queries, kv, probs, attended, middle, ffn_in, gud, gue, ret, shares = saved
    out = [((768, width), BF) for width in WIDTHS] + [
        ((8, 768), F32),
        ((2, 256, 768), BF),
        ((64, 768), F32),
        (ROWS4, BF),
    ]
    return pl.pallas_call(
        functools.partial(backward_kernel, layer),
        out_shape=[jax.ShapeDtypeStruct(*one) for one in out],
        in_specs=[VM] * 17 + [ANY] * 4,
        out_specs=[VM] * len(out),
        scratch_shapes=WEIGHTS
        + [
            pltpu.VMEM((4, 64, 896), BF),
            pltpu.VMEM((3, 64, 896), BF),
            pltpu.VMEM(ROWS4, BF),
            pltpu.VMEM((3, 64, 768), BF),
            pltpu.VMEM((16, 32, 768), BF),
            pltpu.VMEM((2, 256, 768), BF),
            pltpu.VMEM((16, 32, 768), BF),
            pltpu.VMEM((4, 80, 896), BF),
            pltpu.VMEM((4, 80, 768), BF),
            pltpu.VMEM((8, 256, 384), BF),
            pltpu.VMEM((4, 256, 384), BF),
            pltpu.VMEM((3, 256, 384), BF),
            pltpu.VMEM((256, 640), F32),
            pltpu.SemaphoreType.DMA((4,)),
            pltpu.SemaphoreType.DMA((56,)),
            pltpu.SemaphoreType.DMA((56,)),
        ],
        compiler_params=pltpu.CompilerParams(
            collective_id=5 + layer, has_side_effects=True, vmem_limit_bytes=56 * 2**20
        ),
        name=f"block_backward_{layer}",
    )(incoming, grad_own, own, middle, normed, queries, kv, probs, attended, ffn_in, gud, gue, ret, shares, route, cos, sin, w, eg, eu, ed)


def swish_product(gate, up):
    return jax.nn.silu(gate) * up


def rotation(span):
    half = HD // 2
    frequency = jnp.exp(-jnp.log(10000.0) * jnp.arange(half).astype(F32) / half)
    positions = (lax.axis_index("ep") * span + jnp.arange(span)).astype(F32)
    angles = positions[:, None] * frequency[None, :]
    cosine, sine = jnp.cos(angles), jnp.sin(angles)
    cosine = jnp.tile(jnp.concatenate([cosine, cosine], axis=1), (1, 3))
    sine = jnp.tile(jnp.concatenate([-sine, sine], axis=1), (1, 3))
    ones, none = jnp.ones((span, 192), F32), jnp.zeros((span, 192), F32)
    return (
        jnp.concatenate([cosine, ones, cosine, ones[:, :64]], axis=1),
        jnp.concatenate([sine, none, sine, none[:, :64]], axis=1),
    )


def shards(
    inputs, lengths, expert_ids, slot_ids, attn_gain, query_weight, key_weight, value_weight, out_weight, ffn_gain, router_weight,
    dense_gate, dense_up, dense_down, expert_gate, expert_up, expert_down, cotangent,
):
    filler = jnp.zeros((2, 24, 64), BF)
    small = jnp.concatenate(
        [router_weight, attn_gain[:, :, None], ffn_gain[:, :, None], filler[:, :, : 64 - 18]], axis=2
    )
    packed = jnp.concatenate(
        [out_weight, small, key_weight, value_weight, query_weight, filler, dense_gate, dense_up, dense_down],
        axis=2,
    )
    w = gather_weights(packed.reshape(CHUNK, WIDE))
    z = lax.axis_index("tp")
    cos, sin = rotation(128)
    used = jnp.broadcast_to(lengths[:, None], (2, 128))
    ids = expert_ids.reshape(2, 256, 2)
    slots = slot_ids.reshape(2, 256, 2)
    pairs = jnp.where(slots < 32, ids * 32 + slots, 512)
    routes = jnp.concatenate([pairs, ids], axis=2)

    def mine(rows):
        return lax.dynamic_slice_in_dim(rows.reshape(256, 768), z * 64, 64, 0).astype(F32)

    experts = (expert_gate, expert_up, expert_down)
    stream = inputs.reshape(ROWS4)
    own = mine(inputs)
    saved, owns, rows_at = [], [], []
    for layer in range(2):
        *kept, rows, after, stream = forward(layer, stream, own, used, routes[layer], cos, sin, w, *experts)
        saved.append(kept)
        owns.append(own)
        rows_at.append(rows)
        own = after
    outputs = stream
    grad = cotangent.reshape(ROWS4)
    grad_own = mine(cotangent)
    parts, gains, backs = [None, None], [None, None], [None, None]
    for layer in (1, 0):
        *parts[layer], gains[layer], backs[layer], grad_own, grad = backward(
            layer, grad, grad_own, owns[layer], saved[layer], routes[layer], cos, sin, w, *experts
        )
    first, second, third, g_down = scatter_grads(parts[0] + parts[1] + gains)
    rows0, rows1, back0, back1 = gather_rows(rows_at + backs)
    columns = ([], [], [])
    for layer, (all_rows, all_back) in enumerate(((rows0, back0), (rows1, back1))):
        all_rows = all_rows.reshape(2, 1024, 768)
        all_back = all_back.reshape(2, 1024, 768)
        gate = jnp.einsum("ecd,edf->ecf", all_rows, expert_gate[layer], preferred_element_type=F32)
        up = jnp.einsum("ecd,edf->ecf", all_rows, expert_up[layer], preferred_element_type=F32)
        hidden = swish_product(gate, up).astype(BF)
        hidden_grad = jnp.einsum("ecd,efd->ecf", all_back, expert_down[layer], preferred_element_type=F32)
        gate_grad, up_grad = jax.vjp(swish_product, gate, up)[1](hidden_grad)
        gate_grad, up_grad = gate_grad.astype(BF), up_grad.astype(BF)
        columns[0].append(jnp.einsum("ecd,ecf->edf", all_rows, gate_grad, preferred_element_type=F32))
        columns[1].append(jnp.einsum("ecd,ecf->edf", all_rows, up_grad, preferred_element_type=F32))
        columns[2].append(jnp.einsum("ecf,ecd->efd", hidden, all_back, preferred_element_type=F32))
    return (
        outputs.reshape(2, 128, 768).astype(F32),
        grad.reshape(2, 128, 768).astype(F32),
        first[:, :, 208],
        second[:, :, 384:576],
        second[:, :, 0:192],
        second[:, :, 192:384],
        first[:, :, 0:192],
        first[:, :, 209],
        first[:, :, 192:208],
        third[:, :, :512],
        third[:, :, 512:],
        g_down,
        *[jnp.stack(column) for column in columns],
    )


def solution(mesh):
    return jax.shard_map(
        shards,
        mesh=mesh,
        in_specs=(
            P("dp", "ep", None),
            P("dp"),
            P(None, "dp", "ep", None),
            P(None, "dp", "ep", None),
            P(None, ("dp", "ep")),
            P(None, ("dp", "ep"), "tp"),
            P(None, ("dp", "ep"), "tp"),
            P(None, ("dp", "ep"), "tp"),
            P(None, ("dp", "ep"), "tp"),
            P(None, ("dp", "ep")),
            P(None, ("dp", "ep"), None),
            P(None, ("dp", "ep"), "tp"),
            P(None, ("dp", "ep"), "tp"),
            P(None, ("dp", "ep"), "tp"),
            P(None, "ep", None, "tp"),
            P(None, "ep", None, "tp"),
            P(None, "ep", "tp", None),
            P("dp", "ep", None),
        ),
        out_specs=(
            P("dp", "ep", None),
            P("dp", "ep", None),
            P(None, ("dp", "ep")),
            P(None, ("dp", "ep"), "tp"),
            P(None, ("dp", "ep"), "tp"),
            P(None, ("dp", "ep"), "tp"),
            P(None, ("dp", "ep"), "tp"),
            P(None, ("dp", "ep")),
            P(None, ("dp", "ep"), None),
            P(None, ("dp", "ep"), "tp"),
            P(None, ("dp", "ep"), "tp"),
            P(None, ("dp", "ep"), "tp"),
            P(None, "ep", None, "tp"),
            P(None, "ep", None, "tp"),
            P(None, "ep", "tp", None),
        ),
        check_vma=False,
    )
```

```python
import functools

import jax
import jax.numpy as jnp
from jax import lax
from jax.experimental import pallas as pl
from jax.experimental.pallas import tpu as pltpu
from jax.sharding import PartitionSpec as P

HD = 64
MESH = pl.DeviceIdType.MESH
BF = jnp.bfloat16
F32 = jnp.float32
WIDE = 2432
CHUNK = 48
VM = pl.BlockSpec(memory_space=pltpu.VMEM)


def place():
    y = lax.axis_index("dp")
    e = lax.axis_index("ep")
    z = lax.axis_index("tp")
    return y, e // 2, e % 2, z


def device(y, x, c, z):
    return (y, x * 2 + c, z)


def meet(givers, takers):
    barrier = pltpu.get_barrier_semaphore()
    for who in givers:
        pl.semaphore_signal(barrier, inc=1, device_id=who, device_id_type=MESH)
    pl.semaphore_wait(barrier, takers)


class Line:
    def __init__(self, send_sems, recv_sems):
        self.send_sems, self.recv_sems, self.used, self.open = send_sems, recv_sems, 0, []

    def start(self, src, dst, who):
        at = self.used
        self.used += 1
        copy = pltpu.make_async_remote_copy(
            src_ref=src,
            dst_ref=dst,
            send_sem=self.send_sems.at[at],
            recv_sem=self.recv_sems.at[at],
            device_id=who,
            device_id_type=MESH,
        )
        copy.start()
        self.open.append(copy)
        return copy

    def finish(self):
        for copy in self.open:
            copy.wait_send()


def gather_kernel(src, out, land, send_sems, recv_sems):
    y, x, c, z = place()

    def at(j, d, core=None):
        yy = (y + j * c + d * (1 - c) + 8) % 4
        xx = (x + j * (1 - c) + d * c + 8) % 4
        return yy, xx

    def who(j, d):
        yy, xx = at(j, d)
        return device(yy, xx, c, z)

    def slot(j, d):
        yy, xx = at(j, d)
        return yy * 8 + xx * 2 + c

    sibling = device(y, x, 1 - c, z)
    near = [who(1, 0), who(-1, 0), who(0, 1), who(0, -1), sibling]
    meet(near, 5)
    line = Line(send_sems, recv_sems)
    sib = []

    def spread(ref, j):
        plus = line.start(ref, land.at[slot(j, 0)], who(0, 1))
        minus = line.start(ref, land.at[slot(j, 0)], who(0, -1))
        sib.append(line.start(ref, land.at[slot(j, 0)], sibling))
        return plus, minus

    first_plus = line.start(src, land.at[slot(0, 0)], who(1, 0))
    first_minus = line.start(src, land.at[slot(0, 0)], who(-1, 0))
    second = {0: spread(src, 0)}
    land[slot(0, 0)] = src[...]
    first_plus.wait_recv()
    below = land.at[slot(-1, 0)]
    on_plus = line.start(below.at[pl.ds(0, 32)], below.at[pl.ds(0, 32)], who(1, 0))
    second[-1] = spread(below, -1)
    first_minus.wait_recv()
    above = land.at[slot(1, 0)]
    on_minus = line.start(above.at[pl.ds(32, 16)], above.at[pl.ds(32, 16)], who(-1, 0))
    second[1] = spread(above, 1)
    on_plus.wait_recv()
    on_minus.wait_recv()
    second[2] = spread(land.at[slot(2, 0)], 2)
    far = []
    for j in (0, -1, 1, 2):
        plus, minus = second[j]
        plus.wait_recv()
        got = land.at[slot(j, -1)]
        sib.append(line.start(got, got, sibling))
        if j in (0, -1):
            far.append((j, line.start(got, got, who(0, 1))))
        minus.wait_recv()
        got = land.at[slot(j, 1)]
        sib.append(line.start(got, got, sibling))
        if j in (1, 2):
            far.append((j, line.start(got, got, who(0, -1))))
    for j, copy in far:
        copy.wait_recv()
        got = land.at[slot(j, 2)]
        sib.append(line.start(got, got, sibling))
    for copy in sib:
        copy.wait_recv()
    line.finish()

    def unpack(p, carry):
        one = land[2 * p].astype(F32)
        two = land[2 * p + 1].astype(F32)
        rows = pl.ds(pl.multiple_of(p * CHUNK, CHUNK), CHUNK)
        out[0, rows] = jnp.concatenate([one[:24], two[:24]], axis=0).astype(BF)
        out[1, rows] = jnp.concatenate([one[24:], two[24:]], axis=0).astype(BF)
        return carry

    lax.fori_loop(0, 16, unpack, 0)


def gather_weights(src):
    return pl.pallas_call(
        gather_kernel,
        out_shape=jax.ShapeDtypeStruct((2, 768, WIDE), BF),
        in_specs=[VM],
        out_specs=VM,
        scratch_shapes=[
            pltpu.VMEM((32, CHUNK, WIDE), BF),
            pltpu.SemaphoreType.DMA((32,)),
            pltpu.SemaphoreType.DMA((32,)),
        ],
        compiler_params=pltpu.CompilerParams(
            collective_id=0, has_side_effects=True, vmem_limit_bytes=48 * 2**20
        ),
        name="gather_weights",
    )(src)


EPS = 1e-06
SMALL = slice(128, 256)
ROUTER = 64
GAIN = 80
OUT = slice(0, 192)
QKV = slice(256, 896)
GATEUP = slice(896, 1920)
GATE = slice(896, 1408)
UP = slice(1408, 1920)
DOWN = slice(1920, 2432)


def mm(a, b):
    return lax.dot_general(a, b, (((1,), (0,)), ((), ())), preferred_element_type=F32)


def mm_t(a, b):
    return lax.dot_general(a, b, (((1,), (1,)), ((), ())), preferred_element_type=F32)


def t_mm(a, b):
    return lax.dot_general(a, b, (((0,), (0,)), ((), ())), preferred_element_type=F32)


def lanes(shape):
    return lax.broadcasted_iota(jnp.int32, shape, 1)


def gain_rows(weights):
    pick = (lanes((8, 128)) == lax.broadcasted_iota(jnp.int32, (8, 128), 0) + GAIN).astype(BF)
    return mm_t(pick, weights[:, SMALL])


def rms(values, gain):
    turn = lax.rsqrt(jnp.mean(values * values, axis=-1, keepdims=True) + EPS)
    return values * turn * gain


def rms_back(values, gain, grad):
    turn = lax.rsqrt(jnp.mean(values * values, axis=-1, keepdims=True) + EPS)
    scaled = grad * gain
    back = turn * scaled - values * (turn * turn * turn) * jnp.mean(values * scaled, axis=-1, keepdims=True)
    return back, jnp.sum(grad * values * turn, axis=0, keepdims=True)


def turned(values, cosine, sine):
    width = values.shape[1]
    front = lanes(values.shape) % HD < HD // 2
    other = jnp.where(front, pltpu.roll(values, width - HD // 2, 1), pltpu.roll(values, HD // 2, 1))
    return values * cosine + other * sine


def sigmoid(v):
    return 1.0 / (1.0 + jnp.exp(-v))


def swish_back(gate, up, grad):
    s = sigmoid(gate)
    return (grad * up * s * (1.0 + gate * (1.0 - s))).astype(BF), (grad * gate * s).astype(BF)


def two(values):
    return jnp.concatenate([values, values], axis=0)


class Wires:
    def __init__(self, sends, recvs):
        self.sends, self.recvs, self.used, self.open = sends, recvs, 0, []

    def plan(self, src, dst, who, when=None, at=None):
        if at is None:
            at = self.used
            self.used += 1
        copy = pltpu.make_async_remote_copy(
            src_ref=src,
            dst_ref=dst,
            send_sem=self.sends.at[at],
            recv_sem=self.recvs.at[at],
            device_id=who,
            device_id_type=MESH,
        )
        self.open.append((copy, when))
        return copy

    def go(self, src, dst, who):
        copy = self.plan(src, dst, who)
        copy.start()
        return copy

    def finish(self):
        assert self.used <= self.sends.shape[0]
        for copy, when in self.open:
            if when is None:
                copy.wait_send()
            else:
                pl.when(when)(copy.wait_send)


def peers(y, e, z):
    row = [(y, (e + k) % 8, z) for k in range(1, 8)]
    return row + [(y, e, (z + k) % 4) for k in range(1, 4)] + [((y + 1) % 4, e, z), ((y + 3) % 4, e, z)]


def spread_rows(wires, held, y, e, z):
    sent = [wires.go(held.at[z], held.at[z], (y, e, (z + k) % 4)) for k in (2, 1, 3)]
    return lambda: [copy.wait_recv() for copy in sent]


def sum_rows(wires, parts, land, y, e, z):
    sent = []
    for k in (2, 1, 3):
        who = (z + k) % 4
        sent.append(wires.go(parts.at[who], land.at[k - 1], (y, e, who)))

    def total():
        for copy in sent:
            copy.wait_recv()
        return (
            parts[z].astype(F32) + land[0].astype(F32) + land[1].astype(F32) + land[2].astype(F32)
        )

    return total


def scatter_experts(wires, src, dst, y, e, z, i):
    rows = pl.ds(pl.multiple_of(e * 32, 32), 32)
    sent = []
    for k in (4, 3, 5, 2, 6, 1, 7):
        who = (e + k) % 8
        sent.append(wires.go(src.at[2 * who + i], dst.at[i, 0, rows], (y, who, z)))
    dst[i, 0, rows] = src[2 * e + i]
    return lambda: [copy.wait_recv() for copy in sent]


def return_experts(wires, src, dst, y, e, z, i):
    sent = []
    for k in (4, 3, 5, 2, 6, 1, 7):
        who = (e + k) % 8
        rows = pl.ds(pl.multiple_of(who * 32, 32), 32)
        sent.append(wires.go(src.at[i, rows], dst.at[2 * e + i], (y, who, z)))
    dst[2 * e + i] = src[i, pl.ds(pl.multiple_of(e * 32, 32), 32)]
    return lambda: [copy.wait_recv() for copy in sent]


class RowWalk:
    def __init__(self, wires, rows, y, e, z):
        self.wires, self.rows = wires, rows
        self.up, self.down = ((y + 1) % 4, e, z), ((y + 3) % 4, e, z)
        self.near, self.far = [], []

    def start(self, i):
        rows = self.rows
        self.near.append(
            (
                self.wires.go(rows.at[i, 0], rows.at[i, 1], self.up),
                self.wires.go(rows.at[i, 0], rows.at[i, 3], self.down),
            )
        )

    def pass_on(self, i):
        self.near[i][i].wait_recv()
        slot, who = ((1, self.up), (3, self.down))[i]
        self.far.append(self.wires.go(self.rows.at[i, slot], self.rows.at[i, 2], who))

    def finish(self):
        self.near[0][1].wait_recv()
        self.near[1][0].wait_recv()
        for copy in self.far:
            copy.wait_recv()


def picks(route):
    slots = lanes((256, 512))
    return slots == route[:, 0:1], slots == route[:, 1:2]


def forward_kernel(
    layer, stream, own, lengths, route, cos, sin, w_all, eg_all, eu_all, ed_all,
    normed, queries, kv, probs, attended, middle, ffn_in, gud, gue, ret, shares, arrived, own_out, stream_out,
    w, eg, eu, ed, part, land, sent, made, local, sends, recvs,
):
    y, x, c, z = place()
    e = 2 * x + c
    fetch = [
        pltpu.make_async_copy(src.at[layer], dst, local.at[n])
        for n, (src, dst) in enumerate(((w_all, w), (eg_all, eg), (eu_all, eu), (ed_all, ed)))
    ]
    for copy in fetch:
        copy.start()
    meet(peers(y, e, z), 12)
    wires = Wires(sends, recvs)
    fetch[0].wait()
    gains = gain_rows(w)
    values = stream[...].reshape(256, 768).astype(F32)
    normed[...] = rms(values, gains[0:1]).astype(BF)
    lin = turned(mm(normed[...], w[:, QKV]), two(cos[...]), two(sin[...])).astype(BF)
    kv[e] = lin[:, :384]
    queries[...] = lin[:, 384:576]
    sibling = (y, e + 1 - 2 * c, z)
    first, second = [], []
    for k in (2, 3, 1):
        ahead, behind = x + k <= 3, x - k >= 0
        copy = wires.plan(kv.at[e], kv.at[e], (y, (e + 2 * k) % 8, z), ahead)
        pl.when(ahead)(copy.start)
        first.append((k, behind, copy))
    to_core = wires.plan(kv.at[e], kv.at[e], sibling, c == 0)
    pl.when(c == 0)(to_core.start)
    for j in range(8):

        @pl.when(j > e)
        def _():
            kv[j] = jnp.zeros((256, 384), BF)

    for k, behind, copy in reversed(first):
        slot = (e + 8 - 2 * k) % 8
        on = wires.plan(kv.at[slot], kv.at[slot], sibling, behind)

        @pl.when(behind)
        def _():
            copy.wait_recv()
            on.start()

        second.append((behind, on))
    pl.when(c == 1)(to_core.wait_recv)
    for behind, on in second:
        pl.when(behind)(on.wait_recv)
    at_key = lanes((128, 1024))
    at_query = lax.broadcasted_iota(jnp.int32, (128, 1024), 0) + e * 128
    for s in range(2):
        rows = slice(s * 128, s * 128 + 128)
        allowed = (at_key <= at_query) & (at_key < lengths[s : s + 1, 0:1])
        for h in range(3):
            keys = kv[:, rows, 64 * h : 64 * h + 64].reshape(1024, 64)
            vals = kv[:, rows, 192 + 64 * h : 256 + 64 * h].reshape(1024, 64)
            scores = jnp.where(allowed, mm_t(queries[rows, 64 * h : 64 * h + 64], keys) * HD**-0.5, -1e30)
            expd = jnp.exp(scores - jnp.max(scores, axis=-1, keepdims=True))
            low = (expd / jnp.sum(expd, axis=-1, keepdims=True)).astype(BF)
            probs[3 * s + h] = low
            attended[rows, 64 * h : 64 * h + 64] = mm(low, vals).astype(BF)
    part[0] = mm_t(attended[...], w[:, OUT]).astype(BF).reshape(4, 64, 768)
    total = sum_rows(wires, part.at[0], land.at[0], y, e, z)()
    middle[...] = own[...] + total
    ffn_in[z] = rms(middle[...], gains[1:2]).astype(BF)
    spread_rows(wires, ffn_in, y, e, z)()
    rows_in = ffn_in[...].reshape(256, 768)
    ids = route[...]
    pick0, pick1 = picks(ids)
    sent[...] = t_mm((pick0 | pick1).astype(BF), rows_in).astype(BF).reshape(16, 32, 768)
    coming = [scatter_experts(wires, sent, arrived, y, e, z, i) for i in range(2)]
    logits = mm(rows_in, w[:, SMALL])
    lane = lanes((256, 128))
    chosen = [
        jnp.sum(jnp.where(lane == ids[:, 2 + j : 3 + j] + ROUTER, logits, 0.0), axis=-1, keepdims=True)
        for j in range(2)
    ]
    top = jnp.maximum(chosen[0], chosen[1])
    expd = [jnp.exp(v - top) for v in chosen]
    share = [v / (expd[0] + expd[1]) for v in expd]
    shares[...] = jnp.where(lane == 0, share[0], jnp.where(lane == 1, share[1], 0.0))
    gud[...] = mm(rows_in, w[:, GATEUP])
    gate, up = gud[:, :512], gud[:, 512:]
    hidden = (gate * sigmoid(gate) * up).astype(BF)
    dense = mm_t(hidden, w[:, DOWN])
    for copy in fetch[1:]:
        copy.wait()
    walk = RowWalk(wires, arrived, y, e, z)
    back = []
    for i in range(2):
        coming[i]()
        walk.start(i)
        gue[i, :, :512] = mm(arrived[i, 0], eg[i])
        gue[i, :, 512:] = mm(arrived[i, 0], eu[i])
        gate, up = gue[i, :, :512], gue[i, :, 512:]
        hidden = (gate * sigmoid(gate) * up).astype(BF)
        made[i] = mm(hidden, ed[i]).astype(BF)
        back.append(return_experts(wires, made, ret, y, e, z, i))
    for wait in back:
        wait()
    walk.pass_on(0)
    mix = (jnp.where(pick0, share[0], 0.0) + jnp.where(pick1, share[1], 0.0)).astype(BF)
    moe = mm(mix, ret[...].reshape(512, 768))
    part[1] = (dense + moe).astype(BF).reshape(4, 64, 768)
    total = sum_rows(wires, part.at[1], land.at[1], y, e, z)()
    walk.pass_on(1)
    result = middle[...] + total
    own_out[...] = result
    stream_out[z] = result.astype(BF)
    wait = spread_rows(wires, stream_out, y, e, z)
    wait()
    walk.finish()
    wires.finish()


def backward_kernel(
    layer, incoming, grad_own, own, middle, normed, queries, kv, probs, attended, ffn_in, gud, gue, ret, shares, route, cos, sin,
    w_all, eg_all, eu_all, ed_all,
    grads, arrived, down_own, down_stream,
    w, eg, eu, ed, part_ffn, land_ffn, part, land, sent, made, sret, gathered, tail, dkv, sib_land, owner_land, lin,
    local, sends, recvs,
):
    y, x, c, z = place()
    e = 2 * x + c
    fetch = [
        pltpu.make_async_copy(src.at[layer], dst, local.at[n])
        for n, (src, dst) in enumerate(((w_all, w), (eg_all, eg), (eu_all, eu), (ed_all, ed)))
    ]
    for copy in fetch:
        copy.start()
    meet(peers(y, e, z), 12)
    wires = Wires(sends, recvs)
    mine = pl.ds(pl.multiple_of(z * 64, 64), 64)

    def keep(columns, values):
        grads[:, :, columns] = values.astype(BF).reshape(16, CHUNK, values.shape[1])

    ffn_grad = incoming[...].reshape(256, 768)
    rows_in = ffn_in[...].reshape(256, 768)
    pick0, pick1 = picks(route[...])
    mix = (jnp.where(pick0, shares[:, 0:1], 0.0) + jnp.where(pick1, shares[:, 1:2], 0.0)).astype(BF)
    sent[...] = t_mm(mix, ffn_grad).astype(BF).reshape(16, 32, 768)
    coming = [scatter_experts(wires, sent, arrived, y, e, z, i) for i in range(2)]
    fetch[0].wait()
    gains = gain_rows(w)
    gate, up = gud[:, :512], gud[:, 512:]
    hidden_dense = (gate * sigmoid(gate) * up).astype(BF)
    gate_grad, up_grad = swish_back(gate, up, mm(ffn_grad, w[:, DOWN]))
    gu_grad = jnp.concatenate([gate_grad, up_grad], axis=1)
    dense = mm_t(gu_grad, w[:, GATEUP])
    match = mm_t(ffn_grad, ret[...].reshape(512, 768))
    share_grad = [
        jnp.sum(jnp.where(pick, match, 0.0), axis=-1, keepdims=True) for pick in (pick0, pick1)
    ]
    lane = lanes((256, 128))
    extra = jnp.where(lane == 0, share_grad[0], jnp.where(lane == 1, share_grad[1], 0.0))
    part_ffn[:, :, 768:] = extra.astype(BF).reshape(4, 64, 128)
    for copy in fetch[1:]:
        copy.wait()
    walk = RowWalk(wires, arrived, y, e, z)
    back = []
    for i in range(2):
        coming[i]()
        walk.start(i)
        hidden_grad = mm_t(arrived[i, 0], ed[i])
        gate_e, up_e = swish_back(gue[i, :, :512], gue[i, :, 512:], hidden_grad)
        made[i] = (mm_t(gate_e, eg[i]) + mm_t(up_e, eu[i])).astype(BF)
        back.append(return_experts(wires, made, sret, y, e, z, i))
    keep(GATEUP, t_mm(rows_in, gu_grad))
    keep(DOWN, t_mm(ffn_grad, hidden_dense))
    for wait in back:
        wait()
    dense += mm((pick0 | pick1).astype(BF), sret[...].reshape(512, 768))
    part_ffn[:, :, :768] = dense.astype(BF).reshape(4, 64, 768)
    total = sum_rows(wires, part_ffn, land_ffn, y, e, z)()
    input_sum = total[:, :768]
    share = shares[mine]
    ids = route[mine]
    weigh = share[:, 0:1] * total[:, 768:769] + share[:, 1:2] * total[:, 769:770]
    lane = lanes((64, 128))
    logit_grad = jnp.zeros((64, 128), F32)
    for j in range(2):
        chosen_grad = share[:, j : j + 1] * (total[:, 768 + j : 769 + j] - weigh)
        logit_grad += jnp.where(lane == ids[:, 2 + j : 3 + j] + ROUTER, chosen_grad, 0.0)
    logit_grad = logit_grad.astype(BF)
    back_norm, gain_two = rms_back(middle[...], gains[1:2], input_sum + mm_t(logit_grad, w[:, SMALL]))
    middle_grad = grad_own[...] + back_norm
    down_own[...] = middle_grad
    top = lax.broadcasted_iota(jnp.int32, (16, 768), 0) == 0
    gathered[z, :64, :768] = middle_grad.astype(BF)
    gathered[z, :64, 768:] = logit_grad
    gathered[z, 64:, :768] = jnp.where(top, gain_two, 0.0).astype(BF)
    gathered[z, 64:, 768:] = jnp.zeros((16, 128), BF)
    spread_rows(wires, gathered, y, e, z)()
    walk.pass_on(0)
    walk.pass_on(1)
    attn_grad = gathered[:, :64, :768].reshape(256, 768)
    attended_grad = mm(attn_grad, w[:, OUT]).astype(BF)
    for s in range(2):
        rows = slice(s * 128, s * 128 + 128)
        for h in range(3):
            cols = slice(64 * h, 64 * h + 64)
            late = slice(192 + 64 * h, 256 + 64 * h)
            keys = kv[:, rows, cols].reshape(1024, 64)
            vals = kv[:, rows, late].reshape(1024, 64)
            low = probs[3 * s + h]
            wide = low.astype(F32)
            grad_here = attended_grad[rows, cols]
            probs_grad = mm_t(grad_here, vals)
            kept = jnp.sum(wide * probs_grad, axis=-1, keepdims=True)
            score_grad = (wide * (probs_grad - kept)).astype(BF)
            lin[rows, 384 + 64 * h : 448 + 64 * h] = mm(score_grad, keys) * HD**-0.5
            keys_grad = t_mm(score_grad, queries[rows, cols]) * HD**-0.5
            dkv[:, rows, cols] = keys_grad.astype(BF).reshape(8, 128, 64)
            dkv[:, rows, late] = t_mm(low, grad_here).astype(BF).reshape(8, 128, 64)
    sibling = (y, e + 1 - 2 * c, z)
    swaps = []
    for k in range(4):
        gives = (x - k >= 0) & ((c == 1) if k == 0 else True)
        takes = (x - k >= 0) & ((c == 0) if k == 0 else True)
        copy = wires.plan(dkv.at[(2 * (x - k) + 1 - c + 8) % 8], sib_land.at[k], sibling, gives)
        pl.when(gives)(copy.start)
        swaps.append((takes, copy))
    far = []
    for k in (2, 3, 1):
        gives, takes = x - k >= 0, x + k <= 3
        block = (e - 2 * k + 8) % 8
        send = wires.plan(dkv.at[block], owner_land.at[k - 1], (y, block, z), gives)

        @pl.when(gives)
        def _():
            swaps[k][1].wait_recv()
            dkv[block] = (dkv[block].astype(F32) + sib_land[k].astype(F32)).astype(BF)
            send.start()

        far.append((k, takes, send))
    keep(OUT, t_mm(attn_grad, attended[...]))
    router_grad = t_mm(rows_in, gathered[:, :64, 768:].reshape(256, 128))
    lin[:, :384] = dkv[e].astype(F32)
    lin[:, 576:] = jnp.zeros((256, 64), F32)

    @pl.when(swaps[0][0])
    def _():
        swaps[0][1].wait_recv()
        lin[:, :384] += sib_land[0].astype(F32)

    for k, takes, copy in reversed(far):

        @pl.when(takes)
        def _():
            copy.wait_recv()
            lin[:, :384] += owner_land[k - 1].astype(F32)

    lin_grad = turned(lin[...], two(cos[...]), -two(sin[...])).astype(BF)
    part[...] = mm_t(lin_grad, w[:, QKV]).astype(BF).reshape(4, 64, 768)
    summed = sum_rows(wires, part, land, y, e, z)
    keep(QKV, t_mm(normed[...], lin_grad))
    back_norm, gain_one = rms_back(own[...], gains[0:1], summed())
    result = down_own[...] + back_norm
    down_own[...] = result
    tail[z, :64] = result.astype(BF)
    tail[z, 64:] = jnp.where(top, gain_one, 0.0).astype(BF)
    spread_rows(wires, tail, y, e, z)()
    down_stream[...] = tail[:, :64]
    one = jnp.sum(tail[:, 64:].astype(F32).reshape(64, 768), axis=0, keepdims=True)
    both = jnp.sum(gathered[:, 64:, :768].astype(F32).reshape(64, 768), axis=0, keepdims=True)
    at_row = lax.broadcasted_iota(jnp.int32, (16, 768), 0)
    gain_grads = jnp.where(at_row == 0, one, jnp.where(at_row == 1, both, 0.0)).astype(BF)
    spot = (lanes((16, 128)) == lax.broadcasted_iota(jnp.int32, (16, 128), 0) + GAIN).astype(BF)
    keep(slice(192, 256), (router_grad + t_mm(gain_grads, spot))[:, 64:])
    walk.finish()
    wires.finish()


ANY = pl.BlockSpec(memory_space=pl.ANY)
WEIGHTS = [
    pltpu.VMEM((768, WIDE), BF),
    pltpu.VMEM((2, 768, 512), BF),
    pltpu.VMEM((2, 768, 512), BF),
    pltpu.VMEM((2, 512, 768), BF),
]
ROWS4 = (4, 64, 768)
SAVED = [
    ((256, 768), BF),
    ((256, 192), BF),
    ((8, 256, 384), BF),
    ((6, 128, 1024), BF),
    ((256, 192), BF),
    ((64, 768), F32),
    (ROWS4, BF),
    ((256, 1024), F32),
    ((2, 256, 1024), F32),
    ((16, 32, 768), BF),
    ((256, 128), F32),
]


def scatter_kernel(
    grads0, grads1, o_q, o_k, o_v, o_o, o_small, o_gate, o_up, o_down,
    acc, sib_land, plus_far, minus_far, plus_near, minus_near, one_far, one_near, total, other, local, sends, recvs,
):
    y, x, c, z = place()

    def at(j, d, core):
        yy = (y + j * core + d * (1 - core) + 8) % 4
        xx = (x + j * (1 - core) + d * core + 8) % 4
        return yy, xx

    def who(j, d):
        yy, xx = at(j, d, c)
        return device(yy, xx, c, z)

    def chip(j, d, core):
        yy, xx = at(j, d, core)
        return yy * 4 + xx

    sibling = device(y, x, 1 - c, z)
    mine = [pltpu.make_async_copy(grads, acc, local) for grads in (grads0, grads1)]
    for core in range(2):
        pl.when(c == core)(mine[core].start)
    meet([who(1, 0), who(-1, 0), who(0, 1), who(0, -1), sibling], 5)
    wires = Wires(sends, recvs)
    order = [(j, d) for d in (2, 1, -1, 0) for j in (0, -1, 1, 2)]
    swapped = {}
    for n, (j, d) in enumerate(order):
        block = chip(j, d, 1 - c)
        at_sem = wires.used
        wires.used += 1
        for core, grads in enumerate((grads1, grads0)):
            copy = wires.plan(grads.at[block], sib_land.at[n], sibling, c == core, at_sem)
            pl.when(c == core)(copy.start)
        swapped[j, d] = copy
    for core in range(2):
        pl.when(c == core)(mine[core].wait)

    def join(j, d):
        n = order.index((j, d))
        swapped[j, d].wait_recv()
        block = chip(j, d, c)
        acc[block] = (acc[block].astype(F32) + sib_land[n].astype(F32)).astype(BF)
        return acc.at[block]

    plus_set, minus_set = (0, -1), (1, 2)
    far, near, held = {}, {}, {}
    for j in (0, 1, -1, 2):
        ref = join(j, 2)
        if j in plus_set:
            far[j] = wires.go(ref, plus_far.at[plus_set.index(j)], who(0, 1))
        else:
            far[j] = wires.go(ref, minus_far.at[minus_set.index(j)], who(0, -1))
    for j, k in ((1, 0), (2, -1)):
        near[j, 1] = wires.go(join(j, 1), plus_near.at[j], who(0, 1))
        near[k, -1] = wires.go(join(k, -1), minus_near.at[k % 4], who(0, -1))
    for j, k in zip(plus_set, minus_set):
        ref = join(j, 1)
        far[j].wait_recv()
        ref[...] = (ref[...].astype(F32) + plus_far[plus_set.index(j)].astype(F32)).astype(BF)
        near[j, 1] = wires.go(ref, plus_near.at[j % 4], who(0, 1))
        ref = join(k, -1)
        far[k].wait_recv()
        ref[...] = (ref[...].astype(F32) + minus_far[minus_set.index(k)].astype(F32)).astype(BF)
        near[k, -1] = wires.go(ref, minus_near.at[k], who(0, -1))
    for j in (2, 1, -1, 0):
        held[j] = join(j, 0)
    for j in (2, 1, -1, 0):
        ref = held[j]
        near[j, 1].wait_recv()
        near[j, -1].wait_recv()
        ref[...] = (ref[...].astype(F32) + plus_near[j % 4].astype(F32) + minus_near[j % 4].astype(F32)).astype(BF)
        if j == 2:
            a = wires.go(ref.at[pl.ds(0, 32)], one_far.at[pl.ds(0, 32)], who(1, 0))
            b = wires.go(ref.at[pl.ds(32, 16)], one_far.at[pl.ds(32, 16)], who(-1, 0))
    a.wait_recv()
    up = held[1].at[pl.ds(0, 32)]
    up[...] = (up[...].astype(F32) + one_far[:32].astype(F32)).astype(BF)
    last_plus = wires.go(held[1], one_near.at[0], who(1, 0))
    b.wait_recv()
    down = held[-1].at[pl.ds(32, 16)]
    down[...] = (down[...].astype(F32) + one_far[32:].astype(F32)).astype(BF)
    last_minus = wires.go(held[-1], one_near.at[1], who(-1, 0))
    last_plus.wait_recv()
    last_minus.wait_recv()
    total[...] = held[0][...].astype(F32) + one_near[0].astype(F32) + one_near[1].astype(F32)
    trade = wires.go(total.at[pl.ds(pl.multiple_of(24 - 24 * c, 8), 24)], other, sibling)
    spots = (
        (o_o, OUT), (o_small, slice(128, 256)), (o_k, slice(256, 448)), (o_v, slice(448, 640)), (o_q, slice(640, 832)),
        (o_gate, GATE), (o_up, UP), (o_down, DOWN),
    )
    own = total[pl.ds(pl.multiple_of(24 * c, 8), 24)]
    for ref, columns in spots:
        ref[c] = own[:, columns]
    trade.wait_recv()
    for ref, columns in spots:
        ref[1 - c] = other[:, columns]
    wires.finish()


def scatter_grads(grads):
    chunk = lambda n: pltpu.VMEM((n, CHUNK, WIDE), BF)
    widths = (192, 192, 192, 192, 128, 512, 512, 512)
    return pl.pallas_call(
        scatter_kernel,
        out_shape=[jax.ShapeDtypeStruct((2, 24, width), F32) for width in widths],
        in_specs=[ANY] * 2,
        out_specs=[VM] * 8,
        scratch_shapes=[
            chunk(16),
            chunk(16),
            chunk(2),
            chunk(2),
            chunk(4),
            chunk(4),
            pltpu.VMEM((CHUNK, WIDE), BF),
            chunk(2),
            pltpu.VMEM((CHUNK, WIDE), F32),
            pltpu.VMEM((24, WIDE), F32),
            pltpu.SemaphoreType.DMA,
            pltpu.SemaphoreType.DMA((40,)),
            pltpu.SemaphoreType.DMA((40,)),
        ],
        compiler_params=pltpu.CompilerParams(
            collective_id=1, has_side_effects=True, vmem_limit_bytes=48 * 2**20
        ),
        name="scatter_grads",
    )(*grads)


def expert_kernel(rows, grads, eg, eu, ed, *rest):
    g_gate, g_up, g_down, hidden, gu = rest[-5:]
    weights = jnp.concatenate([eg[...], eu[...]], axis=1)

    def piece(n, carry):
        some = pl.ds(pl.multiple_of(n * 256, 256), 256)
        both = mm(rows[n], weights)
        gate, up = both[:, :256], both[:, 256:]
        hidden_grad = mm_t(grads[n], ed[...])
        s = sigmoid(gate)
        silu = gate * s
        hidden[some] = (silu * up).astype(BF)
        gu[some, :256] = (hidden_grad * up * (s * (1.0 + gate * (1.0 - s)))).astype(BF)
        gu[some, 256:] = (hidden_grad * silu).astype(BF)
        return carry

    lax.fori_loop(0, 4, piece, 0)
    both = t_mm(rows[...].reshape(1024, 768), gu[...])
    g_gate[...] = both[:, :256]
    g_up[...] = both[:, 256:]
    g_down[...] = t_mm(hidden[...], grads[...].reshape(1024, 768))


def expert_grads(layer, rows, grads, eg, eu, ed, before=None):
    whole = pl.BlockSpec((None, 4, 256, 768), lambda i, f: (i, 0, 0, 0))
    wide = pl.BlockSpec((None, None, 768, 256), lambda i, f: (layer, i, 0, f))
    tall = pl.BlockSpec((None, None, 256, 768), lambda i, f: (layer, i, f, 0))
    before = [] if before is None else list(before)
    return pl.pallas_call(
        expert_kernel,
        grid=(2, 2),
        out_shape=[
            jax.ShapeDtypeStruct((2, 2, 768, 512), F32),
            jax.ShapeDtypeStruct((2, 2, 768, 512), F32),
            jax.ShapeDtypeStruct((2, 2, 512, 768), F32),
        ],
        in_specs=[whole, whole, wide, wide, tall] + [ANY] * len(before),
        out_specs=[wide, wide, tall],
        scratch_shapes=[pltpu.VMEM((1024, 256), BF), pltpu.VMEM((1024, 512), BF)],
        input_output_aliases={5 + n: n for n in range(len(before))},
        compiler_params=pltpu.CompilerParams(vmem_limit_bytes=40 * 2**20),
        cost_estimate=pl.CostEstimate(flops=9_700_000_000, bytes_accessed=20_000_000, transcendentals=2_000_000),
        name=f"expert_grads_{layer}",
    )(rows, grads, eg, eu, ed, *before)


def forward(layer, stream, own, lengths, route, cos, sin, w, eg, eu, ed):
    out = SAVED + [((2, 4, 256, 768), BF), ((64, 768), F32), (ROWS4, BF)]
    return pl.pallas_call(
        functools.partial(forward_kernel, layer),
        out_shape=[jax.ShapeDtypeStruct(*one) for one in out],
        in_specs=[VM] * 6 + [ANY] * 4,
        out_specs=[VM] * len(out),
        scratch_shapes=WEIGHTS
        + [
            pltpu.VMEM((2, 4, 64, 768), BF),
            pltpu.VMEM((2, 3, 64, 768), BF),
            pltpu.VMEM((16, 32, 768), BF),
            pltpu.VMEM((2, 256, 768), BF),
            pltpu.SemaphoreType.DMA((4,)),
            pltpu.SemaphoreType.DMA((64,)),
            pltpu.SemaphoreType.DMA((64,)),
        ],
        compiler_params=pltpu.CompilerParams(
            collective_id=3 + layer, has_side_effects=True, vmem_limit_bytes=52 * 2**20
        ),
        name=f"block_forward_{layer}",
    )(stream, own, lengths, route, cos, sin, w, eg, eu, ed)


def backward(layer, incoming, grad_own, own, saved, route, cos, sin, w, eg, eu, ed):
    normed, queries, kv, probs, attended, middle, ffn_in, gud, gue, ret, shares = saved
    out = [
        ((16, CHUNK, WIDE), BF),
        ((2, 4, 256, 768), BF),
        ((64, 768), F32),
        (ROWS4, BF),
    ]
    return pl.pallas_call(
        functools.partial(backward_kernel, layer),
        out_shape=[jax.ShapeDtypeStruct(*one) for one in out],
        in_specs=[VM] * 17 + [ANY] * 4,
        out_specs=[VM] * len(out),
        scratch_shapes=WEIGHTS
        + [
            pltpu.VMEM((4, 64, 896), BF),
            pltpu.VMEM((3, 64, 896), BF),
            pltpu.VMEM(ROWS4, BF),
            pltpu.VMEM((3, 64, 768), BF),
            pltpu.VMEM((16, 32, 768), BF),
            pltpu.VMEM((2, 256, 768), BF),
            pltpu.VMEM((16, 32, 768), BF),
            pltpu.VMEM((4, 80, 896), BF),
            pltpu.VMEM((4, 80, 768), BF),
            pltpu.VMEM((8, 256, 384), BF),
            pltpu.VMEM((4, 256, 384), BF),
            pltpu.VMEM((3, 256, 384), BF),
            pltpu.VMEM((256, 640), F32),
            pltpu.SemaphoreType.DMA((4,)),
            pltpu.SemaphoreType.DMA((64,)),
            pltpu.SemaphoreType.DMA((64,)),
        ],
        compiler_params=pltpu.CompilerParams(
            collective_id=5 + layer, has_side_effects=True, vmem_limit_bytes=56 * 2**20
        ),
        name=f"block_backward_{layer}",
    )(incoming, grad_own, own, middle, normed, queries, kv, probs, attended, ffn_in, gud, gue, ret, shares, route, cos, sin, w, eg, eu, ed)


def rotation(span):
    half = HD // 2
    frequency = jnp.exp(-jnp.log(10000.0) * jnp.arange(half).astype(F32) / half)
    positions = (lax.axis_index("ep") * span + jnp.arange(span)).astype(F32)
    angles = positions[:, None] * frequency[None, :]
    cosine, sine = jnp.cos(angles), jnp.sin(angles)
    cosine = jnp.tile(jnp.concatenate([cosine, cosine], axis=1), (1, 3))
    sine = jnp.tile(jnp.concatenate([-sine, sine], axis=1), (1, 3))
    ones, none = jnp.ones((span, 192), F32), jnp.zeros((span, 192), F32)
    return (
        jnp.concatenate([cosine, ones, cosine, ones[:, :64]], axis=1),
        jnp.concatenate([sine, none, sine, none[:, :64]], axis=1),
    )


def shards(
    inputs, lengths, expert_ids, slot_ids, attn_gain, query_weight, key_weight, value_weight, out_weight, ffn_gain, router_weight,
    dense_gate, dense_up, dense_down, expert_gate, expert_up, expert_down, cotangent,
):
    filler = jnp.zeros((2, 24, 64), BF)
    small = jnp.concatenate(
        [router_weight, attn_gain[:, :, None], ffn_gain[:, :, None], filler[:, :, : 64 - 18]], axis=2
    )
    packed = jnp.concatenate(
        [out_weight, small, key_weight, value_weight, query_weight, filler, dense_gate, dense_up, dense_down],
        axis=2,
    )
    w = gather_weights(packed.reshape(CHUNK, WIDE))
    z = lax.axis_index("tp")
    cos, sin = rotation(128)
    used = jnp.broadcast_to(lengths[:, None], (2, 128))
    ids = expert_ids.reshape(2, 256, 2)
    slots = slot_ids.reshape(2, 256, 2)
    pairs = jnp.where(slots < 32, ids * 32 + slots, 512)
    routes = jnp.concatenate([pairs, ids], axis=2)

    def mine(rows):
        return lax.dynamic_slice_in_dim(rows.reshape(256, 768), z * 64, 64, 0).astype(F32)

    experts = (expert_gate, expert_up, expert_down)
    stream = inputs.reshape(ROWS4)
    own = mine(inputs)
    saved, owns, rows_at = [], [], []
    for layer in range(2):
        *kept, rows, after, stream = forward(layer, stream, own, used, routes[layer], cos, sin, w, *experts)
        saved.append(kept)
        owns.append(own)
        rows_at.append(rows)
        own = after
    outputs = stream
    grad = cotangent.reshape(ROWS4)
    grad_own = mine(cotangent)
    parts, results = [None, None], None
    for layer in (1, 0):
        parts[layer], back, grad_own, grad = backward(
            layer, grad, grad_own, owns[layer], saved[layer], routes[layer], cos, sin, w, *experts
        )
        results = expert_grads(layer, rows_at[layer], back, *experts, before=results)
    g_q, g_k, g_v, g_o, g_small, g_gate, g_up, g_down = scatter_grads(parts)
    return (
        outputs.reshape(2, 128, 768).astype(F32),
        grad.reshape(2, 128, 768).astype(F32),
        g_small[:, :, GAIN],
        g_q,
        g_k,
        g_v,
        g_o,
        g_small[:, :, GAIN + 1],
        g_small[:, :, ROUTER : ROUTER + 16],
        g_gate,
        g_up,
        g_down,
        *results,
    )


def solution(mesh):
    return jax.shard_map(
        shards,
        mesh=mesh,
        in_specs=(
            P("dp", "ep", None),
            P("dp"),
            P(None, "dp", "ep", None),
            P(None, "dp", "ep", None),
            P(None, ("dp", "ep")),
            P(None, ("dp", "ep"), "tp"),
            P(None, ("dp", "ep"), "tp"),
            P(None, ("dp", "ep"), "tp"),
            P(None, ("dp", "ep"), "tp"),
            P(None, ("dp", "ep")),
            P(None, ("dp", "ep"), None),
            P(None, ("dp", "ep"), "tp"),
            P(None, ("dp", "ep"), "tp"),
            P(None, ("dp", "ep"), "tp"),
            P(None, "ep", None, "tp"),
            P(None, "ep", None, "tp"),
            P(None, "ep", "tp", None),
            P("dp", "ep", None),
        ),
        out_specs=(
            P("dp", "ep", None),
            P("dp", "ep", None),
            P(None, ("dp", "ep")),
            P(None, ("dp", "ep"), "tp"),
            P(None, ("dp", "ep"), "tp"),
            P(None, ("dp", "ep"), "tp"),
            P(None, ("dp", "ep"), "tp"),
            P(None, ("dp", "ep")),
            P(None, ("dp", "ep"), None),
            P(None, ("dp", "ep"), "tp"),
            P(None, ("dp", "ep"), "tp"),
            P(None, ("dp", "ep"), "tp"),
            P(None, "ep", None, "tp"),
            P(None, "ep", None, "tp"),
            P(None, "ep", "tp", None),
        ),
        check_vma=False,
    )
```

```python
import jax
import jax.numpy as jnp
import numpy as np
from jax import lax
from jax.experimental import pallas as pl
from jax.experimental.pallas import tpu as pltpu
from jax.sharding import PartitionSpec as P

HD = 64
EPS = 1e-06
MESH = pl.DeviceIdType.MESH
BF = jnp.bfloat16
F32 = jnp.float32
VM = pl.BlockSpec(memory_space=pltpu.VMEM)
ANY = pl.BlockSpec(memory_space=pl.ANY)
SMEM = pl.BlockSpec(memory_space=pltpu.SMEM)
WIDE = 2560
CHUNK = 48
ATTN = slice(0, 512)
FEED = slice(512, 1280)
SMALL = slice(128, 256)
ROUTER = 64
GAIN = 80
OUT = slice(0, 192)
QKV = slice(256, 896)
GATE = slice(1024, 1536)
UP = slice(1536, 2048)
GATEUP = slice(1024, 2048)
DOWN = slice(2048, 2560)
ROWS = (2, 4, 32, 768)


class Box:
    def __init__(self, names, refs):
        self.__dict__.update(zip(names, refs, strict=True))


def place():
    y = lax.axis_index("dp")
    e = lax.axis_index("ep")
    z = lax.axis_index("tp")
    return y, e // 2, e % 2, z


def device(y, x, c, z):
    return (y, x * 2 + c, z)


def greet(others):
    for who in others:
        pl.semaphore_signal(pltpu.get_barrier_semaphore(), inc=1, device_id=who, device_id_type=MESH)


def met(others):
    pl.semaphore_wait(pltpu.get_barrier_semaphore(), len(others))


def mm(a, b):
    return lax.dot_general(a, b, (((1,), (0,)), ((), ())), preferred_element_type=F32)


def mm_t(a, b):
    return lax.dot_general(a, b, (((1,), (1,)), ((), ())), preferred_element_type=F32)


def t_mm(a, b):
    return lax.dot_general(a, b, (((0,), (0,)), ((), ())), preferred_element_type=F32)


def lanes(shape):
    return lax.broadcasted_iota(jnp.int32, shape, 1)


def gain_rows(weights):
    pick = (lanes((8, 128)) == lax.broadcasted_iota(jnp.int32, (8, 128), 0) + GAIN).astype(BF)
    return mm_t(pick, weights[:, SMALL])


def rms(values, gain):
    turn = lax.rsqrt(jnp.mean(values * values, axis=-1, keepdims=True) + EPS)
    return values * turn * gain


def rms_back(values, gain, grad):
    turn = lax.rsqrt(jnp.mean(values * values, axis=-1, keepdims=True) + EPS)
    scaled = grad * gain
    back = turn * scaled - values * (turn * turn * turn) * jnp.mean(values * scaled, axis=-1, keepdims=True)
    return back, jnp.sum(grad * values * turn, axis=0, keepdims=True)


def turned(values, cosine, sine):
    width = values.shape[1]
    front = lanes(values.shape) % HD < HD // 2
    other = jnp.where(front, pltpu.roll(values, width - HD // 2, 1), pltpu.roll(values, HD // 2, 1))
    return values * cosine + other * sine


def sigmoid(v):
    return 1.0 / (1.0 + jnp.exp(-v))


def swish_back(gate, up, grad):
    s = sigmoid(gate)
    return (grad * up * s * (1.0 + gate * (1.0 - s))).astype(BF), (grad * gate * s).astype(BF)


def turns(t, sign):
    cosine, sine = t.turn[:, :128], sign * t.turn[:, 128:]
    first = lanes((128, 128)) < HD
    one, none = jnp.ones((128, 128), F32), jnp.zeros((128, 128), F32)
    mixed, mixed_sine = jnp.where(first, cosine, 1.0), jnp.where(first, sine, 0.0)
    cosine = jnp.concatenate([cosine, mixed, one, cosine, mixed], axis=1)
    sine = jnp.concatenate([sine, mixed_sine, none, sine, mixed_sine], axis=1)
    return cosine, sine


def set_route(t, layer):
    row = lax.broadcasted_iota(jnp.int32, (16, 128), 0)
    unit = (row == lanes((16, 128))).astype(BF)
    for s in range(2):
        stacked = jnp.zeros((16, 128), jnp.int32)
        for n, ref in enumerate((t.ids, t.slots)):
            for j in range(2):
                stacked = jnp.where(row == 2 * n + j, ref[layer, s, j : j + 1], stacked)
        columns = t_mm(stacked.astype(F32).astype(BF), unit).astype(jnp.int32)
        rows = slice(s * 128, s * 128 + 128)
        for j in range(2):
            expert, slot = columns[:, j : j + 1], columns[:, 2 + j : 3 + j]
            t.route[rows, j : j + 1] = jnp.where(slot < 32, expert * 32 + slot, 512)
            t.route[rows, 2 + j : 3 + j] = expert


class Wires:
    def __init__(self, sends, recvs):
        self.sends, self.recvs, self.used, self.open = sends, recvs, 0, []

    def plan(self, src, dst, who, when=None, at=None):
        if at is None:
            at = self.used
            self.used += 1
        copy = pltpu.make_async_remote_copy(
            src_ref=src,
            dst_ref=dst,
            send_sem=self.sends.at[at],
            recv_sem=self.recvs.at[at],
            device_id=who,
            device_id_type=MESH,
        )
        self.open.append((copy, when))
        return copy

    def go(self, src, dst, who):
        copy = self.plan(src, dst, who)
        copy.start()
        return copy

    def finish(self):
        assert self.used <= self.sends.shape[0]
        for copy, when in self.open:
            if when is None:
                copy.wait_send()
            else:
                pl.when(when)(copy.wait_send)


class Moves:
    def __init__(self, sems):
        self.sems, self.used, self.open = sems, 0, []

    def go(self, src, dst):
        copy = pltpu.make_async_copy(src, dst, self.sems.at[self.used])
        self.used += 1
        copy.start()
        self.open.append(copy)
        return copy

    def need(self, copy):
        self.open = [other for other in self.open if other is not copy]
        copy.wait()

    def finish(self):
        assert self.used <= self.sems.shape[0]
        for copy in self.open:
            copy.wait()


def peers(y, e, z):
    row = [(y, (e + k) % 8, z) for k in range(1, 8)]
    return row + [(y, e, (z + k) % 4) for k in range(1, 4)] + [((y + k) % 4, e, z) for k in range(1, 4)]


class TpSum:
    def __init__(self, wires, parts, land, held):
        self.wires, self.parts, self.land, self.held = wires, parts, land, held
        self.y, self.e, self.z = (lax.axis_index(name) for name in ("dp", "ep", "tp"))
        self.sums, self.spread = [None, None], [None, None]

    def send(self, h):
        self.sums[h] = []
        for k in (1, 3, 2):
            who = (self.z + k) % 4
            copy = self.wires.go(self.parts.at[h, who], self.land.at[h, k - 1], (self.y, self.e, who))
            self.sums[h].append(copy)

    def half(self, h, finish):
        for copy in self.sums[h]:
            copy.wait_recv()
        total = self.parts[h, self.z].astype(F32)
        for k in range(3):
            total += self.land[h, k].astype(F32)
        finish(h, slice(32 * h, 32 * h + 32), total)
        self.spread[h] = self.everywhere(self.held.at[h, self.z])

    def everywhere(self, spot):
        return [self.wires.go(spot, spot, (self.y, self.e, (self.z + k) % 4)) for k in (1, 3, 2)]

    def wait(self, h):
        for copy in self.spread[h]:
            copy.wait_recv()


def scatter_experts(wires, src, dst, y, e, z, i):
    rows = pl.ds(pl.multiple_of(e * 32, 32), 32)
    sent = []
    for k in (1, 7, 2, 6, 3, 5, 4):
        who = (e + k) % 8
        sent.append(wires.go(src.at[2 * who + i], dst.at[i, rows], (y, who, z)))
    dst[i, rows] = src[2 * e + i]
    return lambda: [copy.wait_recv() for copy in sent]


def return_experts(wires, src, dst, y, e, z, i):
    sent = []
    for k in (1, 7, 2, 6, 3, 5, 4):
        who = (e + k) % 8
        rows = pl.ds(pl.multiple_of(who * 32, 32), 32)
        sent.append(wires.go(src.at[i, rows], dst.at[2 * e + i], (y, who, z)))
    dst[2 * e + i] = src[i, pl.ds(pl.multiple_of(e * 32, 32), 32)]
    return lambda: [copy.wait_recv() for copy in sent]


class RowWalk:
    def __init__(self, wires, moves, own, rows, y, e, z):
        self.wires, self.moves, self.own, self.rows = wires, moves, own, rows
        self.up, self.down = ((y + 1) % 4, e, z), ((y + 3) % 4, e, z)
        self.near, self.far = [], []

    def start(self, i):
        own, rows = self.own.at[i], self.rows
        self.near.append(
            (self.wires.go(own, rows.at[i, 1], self.up), self.wires.go(own, rows.at[i, 3], self.down))
        )
        self.moves.go(own, rows.at[i, 0])

    def pass_on(self, i):
        self.near[i][i].wait_recv()
        slot, who = ((1, self.up), (3, self.down))[i]
        self.far.append(self.wires.go(self.rows.at[i, slot], self.rows.at[i, 2], who))

    def finish(self):
        self.near[0][1].wait_recv()
        self.near[1][0].wait_recv()
        for copy in self.far:
            copy.wait_recv()


class Gather:
    def __init__(self, wires, land, columns):
        self.wires, self.land, self.columns = wires, land, columns
        self.y, self.x, self.c, self.z = place()
        self.sib, self.second, self.far = [], {}, []

    def who(self, j, d):
        yy = (self.y + j * self.c + d * (1 - self.c) + 8) % 4
        xx = (self.x + j * (1 - self.c) + d * self.c + 8) % 4
        return device(yy, xx, self.c, self.z)

    def spot(self, j, d, rows=slice(None)):
        yy, ee, zz = self.who(j, d)
        return self.land.at[yy * 8 + ee, rows, self.columns]

    def pair(self, spot):
        self.sib.append(self.wires.go(spot, spot, device(self.y, self.x, 1 - self.c, self.z)))

    def spread(self, j):
        spot = self.spot(j, 0)
        self.second[j] = self.wires.go(spot, spot, self.who(0, 1)), self.wires.go(spot, spot, self.who(0, -1))
        self.pair(spot)

    def step0(self):
        spot = self.spot(0, 0)
        self.first = self.wires.go(spot, spot, self.who(1, 0)), self.wires.go(spot, spot, self.who(-1, 0))
        self.spread(0)

    def step1(self):
        self.first[0].wait_recv()
        spot = self.spot(-1, 0, pl.ds(0, 32))
        self.on = [self.wires.go(spot, spot, self.who(1, 0))]
        self.spread(-1)
        self.first[1].wait_recv()
        spot = self.spot(1, 0, pl.ds(32, 16))
        self.on.append(self.wires.go(spot, spot, self.who(-1, 0)))
        self.spread(1)

    def step2(self):
        for copy in self.on:
            copy.wait_recv()
        self.spread(2)

    def step3(self):
        for j in (0, -1, 1, 2):
            for n, d in enumerate((-1, 1)):
                self.second[j][n].wait_recv()
                spot = self.spot(j, d)
                if (j in (0, -1)) == (n == 0):
                    self.far.append((j, self.wires.go(spot, spot, self.who(0, -d))))
                self.pair(spot)

    def step4(self):
        for j, copy in self.far:
            copy.wait_recv()
            self.pair(self.spot(j, 2))

    def step5(self):
        for copy in self.sib:
            copy.wait_recv()


class ShortGather(Gather):
    def reach(self, spot, whos):
        return [self.wires.go(spot, spot, who) for who in whos]

    def spread(self, j):
        spot = self.spot(j, 0)
        self.second[j] = self.reach(spot, [self.who(0, d) for d in (2, 1, -1)])
        self.pair(spot)

    def step0(self):
        self.first = self.reach(self.spot(0, 0), [self.who(j, 0) for j in (2, 1, -1)])
        self.spread(0)

    def step1(self):
        for n, j in ((1, -1), (2, 1), (0, 2)):
            self.first[n].wait_recv()
            self.spread(j)

    def step2(self):
        for j in (0, -1, 1, 2):
            for n, d in ((1, -1), (2, 1), (0, 2)):
                self.second[j][n].wait_recv()
                self.pair(self.spot(j, d))


def unpack(land, columns, w, left):
    half = columns.stop - columns.start

    def some(p, carry):
        one = land[2 * p, :, columns].astype(F32)
        two = land[2 * p + 1, :, columns].astype(F32)
        rows = pl.ds(pl.multiple_of(p * CHUNK, CHUNK), CHUNK)
        w[rows, left : left + half] = jnp.concatenate([one[:24], two[:24]], axis=0).astype(BF)
        w[rows, left + half : left + 2 * half] = jnp.concatenate([one[24:], two[24:]], axis=0).astype(BF)
        return carry

    lax.fori_loop(0, 16, some, 0)


def picks(route):
    slots = lanes((256, 512))
    return slots == route[:, 0:1], slots == route[:, 1:2]


def scatter_grads(wires, acc, t, outs):
    y, x, c, z = place()

    def at(j, d, core):
        yy = (y + j * core + d * (1 - core) + 8) % 4
        xx = (x + j * (1 - core) + d * core + 8) % 4
        return yy, xx

    def who(j, d):
        yy, xx = at(j, d, c)
        return device(yy, xx, c, z)

    def chip(j, d, core):
        yy, xx = at(j, d, core)
        return yy * 4 + xx

    sibling = device(y, x, 1 - c, z)
    order = [(j, d) for d in (2, 1, -1, 0) for j in (0, -1, 1, 2)]
    swapped = {}
    for n, (j, d) in enumerate(order):
        block = chip(j, d, 1 - c)
        swapped[j, d] = wires.go(acc.at[1 - c, block], t.sib_grads.at[n], sibling)

    def join(j, d):
        n = order.index((j, d))
        swapped[j, d].wait_recv()
        block = chip(j, d, c)
        acc[c, block] = (acc[c, block].astype(F32) + t.sib_grads[n].astype(F32)).astype(BF)
        return acc.at[c, block]

    plus_set, minus_set = (0, -1), (1, 2)
    far, near, held = {}, {}, {}
    for j in (0, 1, -1, 2):
        ref = join(j, 2)
        if j in plus_set:
            far[j] = wires.go(ref, t.plus_far.at[plus_set.index(j)], who(0, 1))
        else:
            far[j] = wires.go(ref, t.minus_far.at[minus_set.index(j)], who(0, -1))
    for j, k in ((1, 0), (2, -1)):
        near[j, 1] = wires.go(join(j, 1), t.plus_near.at[j], who(0, 1))
        near[k, -1] = wires.go(join(k, -1), t.minus_near.at[k % 4], who(0, -1))
    for j, k in zip(plus_set, minus_set):
        ref = join(j, 1)
        far[j].wait_recv()
        ref[...] = (ref[...].astype(F32) + t.plus_far[plus_set.index(j)].astype(F32)).astype(BF)
        near[j, 1] = wires.go(ref, t.plus_near.at[j % 4], who(0, 1))
        ref = join(k, -1)
        far[k].wait_recv()
        ref[...] = (ref[...].astype(F32) + t.minus_far[minus_set.index(k)].astype(F32)).astype(BF)
        near[k, -1] = wires.go(ref, t.minus_near.at[k], who(0, -1))
    for j in (2, 1, -1, 0):
        held[j] = join(j, 0)
    for j in (2, 1, -1, 0):
        ref = held[j]
        near[j, 1].wait_recv()
        near[j, -1].wait_recv()
        ref[...] = (ref[...].astype(F32) + t.plus_near[j % 4].astype(F32) + t.minus_near[j % 4].astype(F32)).astype(BF)
        if j == 2:
            a = wires.go(ref.at[pl.ds(0, 32)], t.one_far.at[pl.ds(0, 32)], who(1, 0))
            b = wires.go(ref.at[pl.ds(32, 16)], t.one_far.at[pl.ds(32, 16)], who(-1, 0))
    a.wait_recv()
    up = held[1].at[pl.ds(0, 32)]
    up[...] = (up[...].astype(F32) + t.one_far[:32].astype(F32)).astype(BF)
    last_plus = wires.go(held[1], t.one_near.at[0], who(1, 0))
    b.wait_recv()
    down = held[-1].at[pl.ds(32, 16)]
    down[...] = (down[...].astype(F32) + t.one_far[32:].astype(F32)).astype(BF)
    last_minus = wires.go(held[-1], t.one_near.at[1], who(-1, 0))
    last_plus.wait_recv()
    last_minus.wait_recv()
    t.total[...] = held[0][...].astype(F32) + t.one_near[0].astype(F32) + t.one_near[1].astype(F32)
    trade = wires.go(t.total.at[pl.ds(pl.multiple_of(24 - 24 * c, 8), 24)], t.other, sibling)
    outs[c] = t.total[pl.ds(pl.multiple_of(24 * c, 8), 24)]
    trade.wait_recv()
    outs[1 - c] = t.other[...]


def forward_block(wires, moves, t, w, need, stream, own, lengths, pump, done, dp_rows=None):
    y, x, c, z = place()
    e = 2 * x + c
    gains = gain_rows(w)
    values = stream[...].reshape(256, 768).astype(F32)
    t.normed[...] = rms(values, gains[0:1]).astype(BF)
    done("normed")
    sibling = (y, e + 1 - 2 * c, z)
    cosine, sine = turns(t, 1.0)
    spans = (slice(0, 128), slice(128, 256))
    first, to_core = [], []
    for s, rows in enumerate(spans):
        lin = turned(mm(t.normed[rows], w[:, QKV]), cosine, sine).astype(BF)
        t.kv[e, rows] = lin[:, :384]
        t.queries[rows] = lin[:, 384:576]
        here = t.kv.at[e, pl.ds(s * 128, 128)]
        first.append([])
        for k in (1, 3, 2):
            ahead = x + k <= 3
            copy = wires.plan(here, here, (y, (e + 2 * k) % 8, z), ahead)
            pl.when(ahead)(copy.start)
            first[s].append((k, copy))
        to_core.append(wires.plan(here, here, sibling, c == 0))
        pl.when(c == 0)(to_core[s].start)
    done("queries")
    for j in range(8):

        @pl.when(j > e)
        def _():
            t.kv[j] = jnp.zeros((256, 384), BF)

    pump()
    tp = TpSum(wires, t.part.at[0], t.land.at[0], t.ffn_in)
    at_key = lanes((128, 1024))
    at_query = lax.broadcasted_iota(jnp.int32, (128, 1024), 0) + e * 128
    for s, rows in enumerate(spans):
        second = []
        for k, copy in first[s]:
            behind = x - k >= 0
            there = t.kv.at[(e + 8 - 2 * k) % 8, pl.ds(s * 128, 128)]
            on = wires.plan(there, there, sibling, behind)

            @pl.when(behind)
            def _():
                copy.wait_recv()
                on.start()

            second.append((behind, on))
        pl.when(c == 1)(to_core[s].wait_recv)
        for behind, on in second:
            pl.when(behind)(on.wait_recv)
        allowed = (at_key <= at_query) & (at_key < lengths[s])
        for h in range(3):
            keys = t.kv[:, rows, 64 * h : 64 * h + 64].reshape(1024, 64)
            vals = t.kv[:, rows, 192 + 64 * h : 256 + 64 * h].reshape(1024, 64)
            scores = jnp.where(allowed, mm_t(t.queries[rows, 64 * h : 64 * h + 64], keys) * HD**-0.5, -1e30)
            expd = jnp.exp(scores - jnp.max(scores, axis=-1, keepdims=True))
            low = (expd / jnp.sum(expd, axis=-1, keepdims=True)).astype(BF)
            t.probs[3 * s + h] = low
            t.attended[rows, 64 * h : 64 * h + 64] = mm(low, vals).astype(BF)
        t.part[0, s] = mm_t(t.attended[rows], w[:, OUT]).astype(BF).reshape(4, 32, 768)
        tp.send(s)
    done("kv", "probs", "attended")
    pump()

    def finish(h, rows, total):
        t.middle[rows] = own[rows] + total
        t.ffn_in[h, z] = rms(t.middle[rows], gains[1:2]).astype(BF)

    tp.half(0, finish)
    tp.half(1, finish)
    done("middle")
    pump()
    tp.wait(0)
    tp.wait(1)
    done("ffn_in")
    rows_in = t.ffn_in[...].reshape(256, 768)
    ids = t.route[...]
    pick0, pick1 = picks(ids)
    t.sent[...] = t_mm((pick0 | pick1).astype(BF), rows_in).astype(BF).reshape(16, 32, 768)
    coming = [scatter_experts(wires, t.sent, t.arrived, y, e, z, i) for i in range(2)]
    pump()
    logits = mm(rows_in, w[:, SMALL])
    lane = lanes((256, 128))
    chosen = [
        jnp.sum(jnp.where(lane == ids[:, 2 + j : 3 + j] + ROUTER, logits, 0.0), axis=-1, keepdims=True)
        for j in range(2)
    ]
    top = jnp.maximum(chosen[0], chosen[1])
    expd = [jnp.exp(v - top) for v in chosen]
    share = [v / (expd[0] + expd[1]) for v in expd]
    t.shares[...] = jnp.where(lane == 0, share[0], jnp.where(lane == 1, share[1], 0.0))
    t.gud[...] = mm(rows_in, w[:, GATEUP])
    gate, up = t.gud[:, :512], t.gud[:, 512:]
    hidden = (gate * sigmoid(gate) * up).astype(BF)
    dense = mm_t(hidden, w[:, DOWN])
    done("gud", "shares")
    pump()
    need("eg", "eu", "ed")
    walk = None if dp_rows is None else RowWalk(wires, moves, t.arrived, dp_rows, y, e, z)
    back = []
    for i in range(2):
        coming[i]()
        if walk is not None:
            walk.start(i)
        t.gue[i, :, :512] = mm(t.arrived[i], t.eg[i])
        t.gue[i, :, 512:] = mm(t.arrived[i], t.eu[i])
        gate, up = t.gue[i, :, :512], t.gue[i, :, 512:]
        hidden = (gate * sigmoid(gate) * up).astype(BF)
        t.made[i] = mm(hidden, t.ed[i]).astype(BF)
        back.append(return_experts(wires, t.made, t.ret, y, e, z, i))
    done("arrived", "gue")
    pump()
    for wait in back:
        wait()
    done("ret")
    mix = (jnp.where(pick0, share[0], 0.0) + jnp.where(pick1, share[1], 0.0)).astype(BF)
    tp = TpSum(wires, t.part.at[1], t.land.at[1], t.stream_out)
    for h, rows in enumerate(spans):
        moe = mm(mix[rows], t.ret[...].reshape(512, 768))
        t.part[1, h] = (dense[rows] + moe).astype(BF).reshape(4, 32, 768)
        tp.send(h)
    pump()

    def finish(h, rows, total):
        result = t.middle[rows] + total
        t.own_out[rows] = result
        t.stream_out[h, z] = result.astype(BF)

    tp.half(0, finish)
    tp.half(1, finish)
    done("own_out")
    pump()
    tp.wait(0)
    tp.wait(1)
    done("stream_out")
    return walk


def backward_block(wires, moves, t, w, need, incoming, grad_own, own, pump, dp_rows, grads):
    y, x, c, z = place()
    e = 2 * x + c

    def keep(columns, values):
        grads[:, :, columns] = values.astype(BF).reshape(16, CHUNK, values.shape[1])

    need("shares")
    ffn_grad = incoming[...].reshape(256, 768)
    pick0, pick1 = picks(t.route[...])
    mix = (jnp.where(pick0, t.shares[:, 0:1], 0.0) + jnp.where(pick1, t.shares[:, 1:2], 0.0)).astype(BF)
    t.bsent[...] = t_mm(mix, ffn_grad).astype(BF).reshape(16, 32, 768)
    coming = [scatter_experts(wires, t.bsent, t.back, y, e, z, i) for i in range(2)]
    pump()
    need("w", "gud", "ret", "ffn_in")
    rows_in = t.ffn_in[...].reshape(256, 768)
    gains = gain_rows(w)
    gate, up = t.gud[:, :512], t.gud[:, 512:]
    hidden_dense = (gate * sigmoid(gate) * up).astype(BF)
    gate_grad, up_grad = swish_back(gate, up, mm(ffn_grad, w[:, DOWN]))
    gu_grad = jnp.concatenate([gate_grad, up_grad], axis=1)
    dense = mm_t(gu_grad, w[:, GATEUP])
    match = mm_t(ffn_grad, t.ret[...].reshape(512, 768))
    share_grad = [
        jnp.sum(jnp.where(pick, match, 0.0), axis=-1, keepdims=True) for pick in (pick0, pick1)
    ]
    lane = lanes((256, 128))
    extra = jnp.where(lane == 0, share_grad[0], jnp.where(lane == 1, share_grad[1], 0.0))
    t.part_ffn[:, :, :, 768:] = extra.astype(BF).reshape(2, 4, 32, 128)
    pump()
    need("ed", "gue", "eg", "eu")
    walk = RowWalk(wires, moves, t.back, dp_rows, y, e, z)
    back = []
    for i in range(2):
        coming[i]()
        walk.start(i)
        hidden_grad = mm_t(t.back[i], t.ed[i])
        gate_e, up_e = swish_back(t.gue[i, :, :512], t.gue[i, :, 512:], hidden_grad)
        t.bmade[i] = (mm_t(gate_e, t.eg[i]) + mm_t(up_e, t.eu[i])).astype(BF)
        back.append(return_experts(wires, t.bmade, t.sret, y, e, z, i))
    pump()
    keep(GATEUP, t_mm(rows_in, gu_grad))
    keep(DOWN, t_mm(ffn_grad, hidden_dense))
    for wait in back:
        wait()
    tp = TpSum(wires, t.part_ffn, t.land_ffn, t.gathered)
    spans = (slice(0, 128), slice(128, 256))
    placed = (pick0 | pick1).astype(BF)
    for h, rows in enumerate(spans):
        total = dense[rows] + mm(placed[rows], t.sret[...].reshape(512, 768))
        t.part_ffn[h, :, :, :768] = total.astype(BF).reshape(4, 32, 768)
        tp.send(h)
    need("middle")
    top = lax.broadcasted_iota(jnp.int32, (16, 768), 0) == 0
    lane32 = lanes((32, 128))
    gain_parts = []

    def finish(h, rows, total):
        mine = pl.ds(pl.multiple_of(128 * h + 32 * z, 32), 32)
        share, ids = t.shares[mine], t.route[mine]
        weigh = share[:, 0:1] * total[:, 768:769] + share[:, 1:2] * total[:, 769:770]
        logit_grad = jnp.zeros((32, 128), F32)
        for j in range(2):
            chosen_grad = share[:, j : j + 1] * (total[:, 768 + j : 769 + j] - weigh)
            logit_grad += jnp.where(lane32 == ids[:, 2 + j : 3 + j] + ROUTER, chosen_grad, 0.0)
        logit_grad = logit_grad.astype(BF)
        grad_in = total[:, :768] + mm_t(logit_grad, w[:, SMALL])
        back_norm, gain_two = rms_back(t.middle[rows], gains[1:2], grad_in)
        gain_parts.append(gain_two)
        middle_grad = grad_own[rows] + back_norm
        t.down_own[rows] = middle_grad
        t.gathered[h, z, :, :768] = middle_grad.astype(BF)
        t.gathered[h, z, :, 768:] = logit_grad

    tp.half(0, finish)
    tp.half(1, finish)
    t.gains[1, z] = jnp.where(top, gain_parts[0] + gain_parts[1], 0.0).astype(BF)
    gain_copies = tp.everywhere(t.gains.at[1, z])
    grads_tp = tp
    need("probs", "kv", "queries", "attended", "normed")
    sibling = (y, e + 1 - 2 * c, z)

    def attend_back(s, between):
        rows = spans[s]
        grad = t.gathered[s, :, :, :768].reshape(128, 768)
        attended_grad = mm(grad, w[:, OUT]).astype(BF)
        for h in range(3):
            cols = slice(64 * h, 64 * h + 64)
            late = slice(192 + 64 * h, 256 + 64 * h)
            keys = t.kv[:, rows, cols].reshape(1024, 64)
            vals = t.kv[:, rows, late].reshape(1024, 64)
            low = t.probs[3 * s + h]
            wide = low.astype(F32)
            grad_here = attended_grad[:, cols]
            probs_grad = mm_t(grad_here, vals)
            kept = jnp.sum(wide * probs_grad, axis=-1, keepdims=True)
            score_grad = (wide * (probs_grad - kept)).astype(BF)
            t.lin[rows, 384 + 64 * h : 448 + 64 * h] = mm(score_grad, keys) * HD**-0.5
            keys_grad = t_mm(score_grad, t.queries[rows, cols]) * HD**-0.5
            t.dkv[:, rows, cols] = keys_grad.astype(BF).reshape(8, 128, 64)
            t.dkv[:, rows, late] = t_mm(low, grad_here).astype(BF).reshape(8, 128, 64)
            if h == 0:
                between()

    def swap(s):
        rows = pl.ds(s * 128, 128)
        swaps = []
        for k in range(4):
            gives = (x - k >= 0) & ((c == 1) if k == 0 else True)
            takes = (x - k >= 0) & ((c == 0) if k == 0 else True)
            block = (2 * (x - k) + 1 - c + 8) % 8
            copy = wires.plan(t.dkv.at[block, rows], t.sib_land.at[k, rows], sibling, gives)
            pl.when(gives)(copy.start)
            swaps.append((takes, copy))
        return swaps

    def send_far(s, swaps):
        rows = pl.ds(s * 128, 128)
        far = []
        for k in (1, 3, 2):
            gives, takes = x - k >= 0, x + k <= 3
            block = (e - 2 * k + 8) % 8
            send = wires.plan(t.dkv.at[block, rows], t.owner_land.at[k - 1, rows], (y, block, z), gives)

            @pl.when(gives)
            def _():
                swaps[k][1].wait_recv()
                both = t.dkv[block, rows].astype(F32) + t.sib_land[k, rows].astype(F32)
                t.dkv[block, rows] = both.astype(BF)
                send.start()

            far.append((k, takes, send))
        return far

    cosine, sine = turns(t, -1.0)
    tp = TpSum(wires, t.bpart, t.bland, t.tail)

    def collect(s, swaps, far):
        rows = spans[s]
        t.lin[rows, :384] = t.dkv[e, rows].astype(F32)
        t.lin[rows, 576:] = jnp.zeros((128, 64), F32)

        @pl.when(swaps[0][0])
        def _():
            swaps[0][1].wait_recv()
            t.lin[rows, :384] += t.sib_land[0, rows].astype(F32)

        for k, takes, copy in far:

            @pl.when(takes)
            def _():
                copy.wait_recv()
                t.lin[rows, :384] += t.owner_land[k - 1, rows].astype(F32)

        t.lin_low[rows] = turned(t.lin[rows], cosine, sine).astype(BF)
        t.bpart[s] = mm_t(t.lin_low[rows], w[:, QKV]).astype(BF).reshape(4, 32, 768)
        tp.send(s)

    grads_tp.wait(0)
    attend_back(0, lambda: None)
    swaps0 = swap(0)
    walk.pass_on(0)
    walk.pass_on(1)
    grads_tp.wait(1)
    far0 = []
    attend_back(1, lambda: far0.extend(send_far(0, swaps0)))
    swaps1 = swap(1)
    keep(OUT, t_mm(t.gathered[:, :, :, :768].reshape(256, 768), t.attended[...]))
    far1 = send_far(1, swaps1)
    router_grad = t_mm(rows_in, t.gathered[:, :, :, 768:].reshape(256, 128))
    collect(0, swaps0, far0)
    collect(1, swaps1, far1)
    tail_parts = []

    def finish(h, rows, total):
        back_norm, gain_one = rms_back(own[rows], gains[0:1], total)
        tail_parts.append(gain_one)
        result = t.down_own[rows] + back_norm
        t.down_own[rows] = result
        t.tail[h, z] = result.astype(BF)

    keep(QKV, t_mm(t.normed[...], t.lin_low[...]))
    tp.half(0, finish)
    tp.half(1, finish)
    t.gains[0, z] = jnp.where(top, tail_parts[0] + tail_parts[1], 0.0).astype(BF)
    gain_copies += tp.everywhere(t.gains.at[0, z])
    tp.wait(0)
    tp.wait(1)
    t.down_stream[...] = t.tail[...]
    for copy in gain_copies:
        copy.wait_recv()
    at_row = lax.broadcasted_iota(jnp.int32, (16, 768), 0)
    gain_grads = jnp.zeros((16, 768), F32)
    for n in range(2):
        total = jnp.sum(t.gains[n].astype(F32).reshape(64, 768), axis=0, keepdims=True)
        gain_grads = jnp.where(at_row == n, total, gain_grads)
    spot = (lanes((16, 128)) == lax.broadcasted_iota(jnp.int32, (16, 128), 0) + GAIN).astype(BF)
    keep(slice(192, 256), (router_grad + t_mm(gain_grads.astype(BF), spot))[:, 64:])
    return walk


MOVE_SEMS, WIRE_SEMS = 48, 192
SAVED = {
    "normed": ((256, 768), BF),
    "queries": ((256, 192), BF),
    "kv": ((8, 256, 384), BF),
    "probs": ((6, 128, 1024), BF),
    "attended": ((256, 192), BF),
    "middle": ((64, 768), F32),
    "ffn_in": (ROWS, BF),
    "gud": ((256, 1024), F32),
    "gue": ((2, 256, 1024), F32),
    "ret": ((16, 32, 768), BF),
    "shares": ((256, 128), F32),
}
WEIGHTS = {"w": ((768, WIDE), BF), "eg": ((2, 768, 512), BF), "eu": ((2, 768, 512), BF), "ed": ((2, 512, 768), BF)}
FORWARD = {
    "arrived": ((2, 256, 768), BF),
    "own_out": ((64, 768), F32),
    "stream_out": (ROWS, BF),
    "part": ((2, *ROWS), BF),
    "land": ((2, 2, 3, 32, 768), BF),
    "sent": ((16, 32, 768), BF),
    "made": ((2, 256, 768), BF),
}
BACKWARD = {
    "back": ((2, 256, 768), BF),
    "bsent": ((16, 32, 768), BF),
    "bmade": ((2, 256, 768), BF),
    "sret": ((16, 32, 768), BF),
    "part_ffn": ((2, 4, 32, 896), BF),
    "land_ffn": ((2, 3, 32, 896), BF),
    "bpart": (ROWS, BF),
    "bland": ((2, 3, 32, 768), BF),
    "gathered": ((2, 4, 32, 896), BF),
    "tail": (ROWS, BF),
    "gains": ((2, 4, 16, 768), BF),
    "dkv": ((8, 256, 384), BF),
    "sib_land": ((4, 256, 384), BF),
    "owner_land": ((3, 256, 384), BF),
    "lin": ((256, 640), F32),
    "lin_low": ((256, 640), BF),
    "down_own": ((64, 768), F32),
    "down_stream": (ROWS, BF),
}
SCATTER = {
    "acc": ((2, 16, CHUNK, WIDE), BF),
    "sib_grads": ((16, CHUNK, WIDE), BF),
    "plus_far": ((2, CHUNK, WIDE), BF),
    "minus_far": ((2, CHUNK, WIDE), BF),
    "plus_near": ((4, CHUNK, WIDE), BF),
    "minus_near": ((4, CHUNK, WIDE), BF),
    "one_far": ((CHUNK, WIDE), BF),
    "one_near": ((2, CHUNK, WIDE), BF),
    "total": ((CHUNK, WIDE), F32),
    "other": ((24, WIDE), F32),
}
DP_ROWS = ((2, 4, 256, 768), BF)
GRADS = ((16, CHUNK, WIDE), BF)


def launch(body, number, name, ins, outs, scratch, args):
    def kernel(*refs):
        names = list(ins) + list(outs) + list(scratch)
        t = Box(names, refs[: len(names)])
        moves, sends, recvs = refs[len(names) :]
        body(t, Moves(moves), Wires(sends, recvs))

    return pl.pallas_call(
        kernel,
        out_shape=[jax.ShapeDtypeStruct(*shape) for shape, space in outs.values()],
        in_specs=list(ins.values()),
        out_specs=[space for shape, space in outs.values()],
        scratch_shapes=[pltpu.VMEM(*shape) for shape in scratch.values()]
        + [
            pltpu.SemaphoreType.DMA((MOVE_SEMS,)),
            pltpu.SemaphoreType.DMA((WIRE_SEMS,)),
            pltpu.SemaphoreType.DMA((WIRE_SEMS,)),
        ],
        compiler_params=pltpu.CompilerParams(
            collective_id=number, has_side_effects=True, vmem_limit_bytes=60 * 2**20
        ),
        name=name,
    )(*args)


def fetcher(moves, pairs):
    coming = {name: moves.go(src, dst) for name, src, dst in pairs}

    def need(*names):
        for name in names:
            if name in coming:
                moves.need(coming.pop(name))

    return need


def pumper(steps):
    steps = iter(steps)

    def pump():
        for step in next(steps, ()):
            step()

    return pump


def prepare(t, moves, wires, layer):
    y, x, c, z = place()
    others = peers(y, 2 * x + c, z)
    greet(others)
    turn = moves.go(t.table.at[pl.ds(pl.multiple_of((2 * x + c) * 128, 128), 128)], t.turn)
    set_route(t, layer)
    return y, 2 * x + c, z, others, turn


def pack(t, land, layer, me, columns):
    names = (("o", 0), ("k", 256), ("v", 448), ("q", 640)) if columns is ATTN else (("g", 1024), ("u", 1536), ("d", 2048))
    if columns is ATTN:
        row = lax.broadcasted_iota(jnp.int32, (32, 24), 0)
        one, other = t.again[layer : layer + 1].astype(F32), t.fgain[layer : layer + 1].astype(F32)
        gains = jnp.where(row == 16, one, jnp.where(row == 17, other, 0.0))
        router = jnp.concatenate([t.router[layer].astype(F32), jnp.zeros((16, 24), F32)], axis=0)
        spot = (lanes((32, 128)) == lax.broadcasted_iota(jnp.int32, (32, 128), 0) + ROUTER).astype(BF)
        t.stage[:, 192:256] = t_mm((gains + router).astype(BF), spot)[:, 64:]
        t.stage[:, 832:1024] = jnp.zeros((24, 192), F32)
    for name, left in names:
        ref = getattr(t, name)
        t.stage[:, left : left + ref.shape[2]] = ref[layer].astype(F32)
    left, middle, right = (0, 512, 1024) if columns is ATTN else (1024, 1792, 2560)
    halves = [t.stage[:, left:middle], t.stage[:, middle:right]]
    land[me, :, columns] = jnp.concatenate(halves, axis=0).astype(BF)


def first_body(t, moves, wires):
    y, e, z, others, turn = prepare(t, moves, wires, 0)
    need = fetcher(moves, [(n, getattr(t, n + "_all").at[0], getattr(t, n)) for n in ("eg", "eu", "ed")])
    me = y * 8 + e
    pack(t, t.land0, 0, me, ATTN)
    met(others)
    attn, feed = ShortGather(wires, t.land0, ATTN), Gather(wires, t.land0, FEED)
    late = Gather(wires, t.land1, slice(0, 1280))
    attn.step0()
    pack(t, t.land0, 0, me, FEED)
    attn.step1()
    pack(t, t.land1, 1, me, ATTN)
    pack(t, t.land1, 1, me, FEED)
    t.own0[...] = t.stream[:, z].astype(F32).reshape(64, 768)
    attn.step2()
    feed.step0()
    attn.step5()
    feed.step1()
    unpack(t.land0, ATTN, t.w, 0)
    feed.step2()
    moves.need(turn)

    def feed_ready():
        unpack(t.land0, FEED, t.w, 1024)
        moves.go(t.w, t.w_out.at[0])

    def late_ready():
        unpack(t.land1, ATTN, t.w1, 0)
        unpack(t.land1, FEED, t.w1, 1024)
        moves.go(t.w1, t.w_out.at[1])

    pump = pumper(
        [
            (feed.step3,),
            (feed.step4, late.step0),
            (feed.step5, feed_ready, late.step1),
            (late.step2,),
            (late.step3,),
            (late.step4,),
            (late.step5,),
            (late_ready,),
        ]
    )

    def done(*names):
        for name in names:
            moves.go(getattr(t, name), getattr(t, name + "_out"))

    forward_block(wires, moves, t, t.w, need, t.stream, t.own0, t.lengths, pump, done)
    wires.finish()
    moves.finish()


def second_body(t, moves, wires):
    y, e, z, others, turn = prepare(t, moves, wires, 1)
    need = fetcher(
        moves, [(n, getattr(t, n + "_all").at[1], getattr(t, n)) for n in ("w", "eg", "eu", "ed")]
    )
    t.cot_own[...] = t.cotangent[:, z].astype(F32).reshape(64, 768)
    met(others)
    early = RowWalk(wires, moves, t.arrived0, t.rows0, y, e, z)
    early.start(0)
    early.start(1)
    need("w")
    moves.need(turn)
    none = lambda *names: None
    pump = pumper([(), (), (lambda: early.pass_on(0), lambda: early.pass_on(1)), (), (), (early.finish,)])
    walk = forward_block(
        wires, moves, t, t.w, need, t.stream, t.own, t.lengths, pump, none, t.rows1
    )
    t.outputs[...] = t.stream_out[...]
    t.outputs_own[...] = t.own_out[...]
    pump = pumper([(lambda: walk.pass_on(0), lambda: walk.pass_on(1)), (), (walk.finish,)])
    walk = backward_block(
        wires, moves, t, t.w, need, t.cotangent, t.cot_own, t.own, pump, t.back1, t.grads
    )
    moves.go(t.grads, t.grads1)
    t.grad_own[...] = t.down_own[...]
    t.grad_stream[...] = t.down_stream[...]
    walk.finish()
    wires.finish()
    moves.finish()


def third_body(t, moves, wires):
    y, e, z, others, turn = prepare(t, moves, wires, 0)
    order = ("shares", "w", "gud", "ret", "ffn_in", "ed", "gue", "eg", "eu", "middle", "probs", "kv", "queries", "attended", "normed")
    source = lambda n: getattr(t, n + "_all").at[0] if n in WEIGHTS else getattr(t, n + "_in")
    need = fetcher(moves, [(n, source(n), getattr(t, n)) for n in order] + [("grads1", t.grads1, t.acc.at[1])])
    t.own0[...] = t.inputs[:, z].astype(F32).reshape(64, 768)
    moves.need(turn)
    met(others)
    walk = backward_block(
        wires, moves, t, t.w, need, t.incoming, t.grad_own, t.own0, pumper([]), t.back0, t.acc.at[0]
    )
    need("grads1")
    t.input_grad[...] = t.down_stream[...]
    t.input_own[...] = t.down_own[...]
    scatter_grads(wires, t.acc, t, t.sums)
    walk.finish()
    wires.finish()
    moves.finish()


def expert_kernel(rows, grads, eg, eu, ed, *rest):
    hidden, gu = rest[-2:]
    g_gate, g_up, g_down = rest[:3]
    for n in range(4):
        some = slice(n * 256, n * 256 + 256)
        gate, up, hidden_grad = mm(rows[n], eg[...]), mm(rows[n], eu[...]), mm_t(grads[n], ed[...])
        s = sigmoid(gate)
        silu = gate * s
        hidden[some] = (silu * up).astype(BF)
        gu[some, :256] = (hidden_grad * up * (s * (1.0 + gate * (1.0 - s)))).astype(BF)
        gu[some, 256:] = (hidden_grad * silu).astype(BF)
    both = t_mm(rows[...].reshape(1024, 768), gu[...])
    g_gate[...] = both[:, :256]
    g_up[...] = both[:, 256:]
    g_down[...] = t_mm(hidden[...], grads[...].reshape(1024, 768))


def last_kernel(rows, grads, eg, eu, ed, keep0, keep1, keep2, sums, outputs, own, input_grad, own_grad, *rest):
    expert_kernel(rows, grads, eg, eu, ed, *rest[:3], *rest[-2:])
    o_out, o_in, o_router, o_again, o_fgain, *o_parts = rest[3:-2]

    @pl.when((pl.program_id(0) == 0) & (pl.program_id(1) == 0))
    def _():
        z = lax.axis_index("tp")
        o_out[...] = outputs[...].astype(F32)
        o_out[:, z] = own[...].reshape(2, 32, 768)
        o_in[...] = input_grad[...].astype(F32)
        o_in[:, z] = own_grad[...].reshape(2, 32, 768)
        columns = (OUT, slice(256, 448), slice(448, 640), slice(640, 832), GATE, UP, DOWN)
        pick = (lanes((24, 128)) == lax.broadcasted_iota(jnp.int32, (24, 128), 0) + ROUTER).astype(F32)
        for layer in range(2):
            for ref, some in zip(o_parts, columns):
                ref[layer] = sums[layer, :, some]
            small = lax.dot_general(
                pick,
                sums[layer, :, SMALL],
                (((1,), (1,)), ((), ())),
                precision=lax.Precision.HIGHEST,
                preferred_element_type=F32,
            )
            o_router[layer] = small[:16]
            o_again[layer : layer + 1] = small[16:17]
            o_fgain[layer : layer + 1] = small[17:18]


def expert_grads(layer, rows, grads, eg, eu, ed, before=(), others=()):
    whole = pl.BlockSpec((None, 4, 256, 768), lambda i, f: (i, 0, 0, 0))
    wide = pl.BlockSpec((None, None, 768, 256), lambda i, f: (layer, i, 0, f))
    tall = pl.BlockSpec((None, None, 256, 768), lambda i, f: (layer, i, f, 0))
    fixed = lambda shape: pl.BlockSpec(shape, lambda i, f: (0,) * len(shape))
    more = []
    if others:
        more = [ROWS, ROWS, (2, 16, 24), (2, 24), (2, 24)] + [(2, 24, n) for n in (192, 192, 192, 192, 512, 512, 512)]
    return pl.pallas_call(
        last_kernel if others else expert_kernel,
        grid=(2, 2),
        out_shape=[
            jax.ShapeDtypeStruct((2, 2, 768, 512), F32),
            jax.ShapeDtypeStruct((2, 2, 768, 512), F32),
            jax.ShapeDtypeStruct((2, 2, 512, 768), F32),
        ]
        + [jax.ShapeDtypeStruct(shape, F32) for shape in more],
        in_specs=[whole, whole, wide, wide, tall] + [ANY] * len(before) + [fixed(other.shape) for other in others],
        out_specs=[wide, wide, tall] + [fixed(shape) for shape in more],
        scratch_shapes=[pltpu.VMEM((1024, 256), BF), pltpu.VMEM((1024, 512), BF)],
        input_output_aliases={5 + n: n for n in range(len(before))},
        compiler_params=pltpu.CompilerParams(vmem_limit_bytes=60 * 2**20),
        cost_estimate=pl.CostEstimate(flops=9_700_000_000, bytes_accessed=20_000_000, transcendentals=2_000_000),
        name=f"expert_grads_{layer}",
    )(rows, grads, eg, eu, ed, *before, *others)


def rotation_table():
    half = HD // 2
    frequency = np.exp(-np.log(10000.0) * np.arange(half) / half)
    angles = np.arange(1024)[:, None] * frequency[None, :]
    cosine, sine = np.cos(angles), np.sin(angles)
    return np.concatenate([cosine, cosine, cosine, cosine, -sine, sine, -sine, sine], axis=1).astype(np.float32)


def shards(
    inputs, lengths, expert_ids, slot_ids, attn_gain, query_weight, key_weight, value_weight, out_weight, ffn_gain, router_weight,
    dense_gate, dense_up, dense_down, expert_gate, expert_up, expert_down, cotangent,
):
    ids, slots = jnp.swapaxes(expert_ids, 2, 3), jnp.swapaxes(slot_ids, 2, 3)
    stream = inputs.reshape(ROWS)
    experts = (expert_gate, expert_up, expert_down)
    common = {"ids": VM, "slots": VM, "table": ANY, "eg_all": ANY, "eu_all": ANY, "ed_all": ANY}
    given = (ids, slots, rotation_table(), *experts)
    always = {"route": ((256, 4), jnp.int32), "turn": ((128, 256), F32)}
    leaving = dict(SAVED, arrived=FORWARD["arrived"], own_out=FORWARD["own_out"], stream_out=FORWARD["stream_out"])
    ins = ("stream", "again", "q", "k", "v", "o", "fgain", "router", "g", "u", "d")
    *saved, arrived, own, after, w = launch(
        first_body,
        0,
        "gather_forward_0",
        dict(common, lengths=SMEM, **{n: VM for n in ins}),
        dict({n + "_out": (shape, ANY) for n, shape in leaving.items()}, w_out=(((2, 768, WIDE), BF), ANY)),
        dict(
            SAVED, **WEIGHTS, **FORWARD, **always, land0=((32, CHUNK, 1280), BF), land1=((32, CHUNK, 1280), BF),
            w1=WEIGHTS["w"], own0=((64, 768), F32), stage=((24, WIDE), F32),
        ),
        (
            *given, lengths, stream, attn_gain, query_weight, key_weight, value_weight, out_weight, ffn_gain,
            jnp.swapaxes(router_weight, 1, 2), dense_gate, dense_up, dense_down,
        ),
    )
    last, last_own, grads1, rows0, rows1, back1, grad_own, grad_stream = launch(
        second_body,
        1,
        "forward_backward_1",
        dict(common, lengths=SMEM, stream=VM, own=VM, cotangent=VM, arrived0=ANY, w_all=ANY),
        dict(
            outputs=((ROWS, BF), VM), outputs_own=(((64, 768), F32), VM), grads1=(GRADS, ANY), rows0=(DP_ROWS, ANY),
            rows1=(DP_ROWS, ANY), back1=(DP_ROWS, ANY), grad_own=(((64, 768), F32), VM), grad_stream=((ROWS, BF), VM),
        ),
        dict(SAVED, **WEIGHTS, **FORWARD, **BACKWARD, **always, cot_own=((64, 768), F32), grads=GRADS),
        (*given, lengths, after, own, cotangent.reshape(ROWS), arrived, w),
    )
    results = expert_grads(1, rows1, back1, *experts)
    sums, first, first_own, back0 = launch(
        third_body,
        2,
        "backward_0_scatter",
        dict(common, incoming=VM, grad_own=VM, inputs=VM, **{n + "_in": ANY for n in SAVED}, w_all=ANY, grads1=ANY),
        dict(
            sums=(((2, 24, WIDE), F32), VM), input_grad=((ROWS, BF), VM), input_own=(((64, 768), F32), VM), back0=(DP_ROWS, ANY)
        ),
        dict(SAVED, **WEIGHTS, **BACKWARD, **SCATTER, **always, own0=((64, 768), F32)),
        (*given, grad_stream, grad_own, stream, *saved, w, grads1),
    )
    g_eg, g_eu, g_ed, o_out, o_in, g_router, g_again, g_fgain, g_o, g_k, g_v, g_q, g_gate, g_up, g_down = expert_grads(
        0, rows0, back0, *experts, before=results, others=(sums, last, last_own, first, first_own)
    )
    return (
        o_out.reshape(2, 128, 768),
        o_in.reshape(2, 128, 768),
        g_again,
        g_q,
        g_k,
        g_v,
        g_o,
        g_fgain,
        jnp.swapaxes(g_router, 1, 2),
        g_gate,
        g_up,
        g_down,
        g_eg,
        g_eu,
        g_ed,
    )


def solution(mesh):
    return jax.shard_map(
        shards,
        mesh=mesh,
        in_specs=(
            P("dp", "ep", None),
            P("dp"),
            P(None, "dp", "ep", None),
            P(None, "dp", "ep", None),
            P(None, ("dp", "ep")),
            P(None, ("dp", "ep"), "tp"),
            P(None, ("dp", "ep"), "tp"),
            P(None, ("dp", "ep"), "tp"),
            P(None, ("dp", "ep"), "tp"),
            P(None, ("dp", "ep")),
            P(None, ("dp", "ep"), None),
            P(None, ("dp", "ep"), "tp"),
            P(None, ("dp", "ep"), "tp"),
            P(None, ("dp", "ep"), "tp"),
            P(None, "ep", None, "tp"),
            P(None, "ep", None, "tp"),
            P(None, "ep", "tp", None),
            P("dp", "ep", None),
        ),
        out_specs=(
            P("dp", "ep", None),
            P("dp", "ep", None),
            P(None, ("dp", "ep")),
            P(None, ("dp", "ep"), "tp"),
            P(None, ("dp", "ep"), "tp"),
            P(None, ("dp", "ep"), "tp"),
            P(None, ("dp", "ep"), "tp"),
            P(None, ("dp", "ep")),
            P(None, ("dp", "ep"), None),
            P(None, ("dp", "ep"), "tp"),
            P(None, ("dp", "ep"), "tp"),
            P(None, ("dp", "ep"), "tp"),
            P(None, "ep", None, "tp"),
            P(None, "ep", None, "tp"),
            P(None, "ep", "tp", None),
        ),
        check_vma=False,
    )
```

```python
import jax
import jax.numpy as jnp
import numpy as np
from jax import lax
from jax.experimental import pallas as pl
from jax.experimental.pallas import tpu as pltpu
from jax.sharding import PartitionSpec as P

HD = 64
EPS = 1e-06
MESH = pl.DeviceIdType.MESH
BF = jnp.bfloat16
F32 = jnp.float32
VM = pl.BlockSpec(memory_space=pltpu.VMEM)
ANY = pl.BlockSpec(memory_space=pl.ANY)
SMEM = pl.BlockSpec(memory_space=pltpu.SMEM)
WIDE = 2560
HALF = 1280
CHUNK = 48
ATTN = slice(0, 512)
FEED = slice(512, 1280)
SMALL = slice(128, 256)
ROUTER = 64
GAIN = 80
OUT = slice(0, 192)
QKV = slice(256, 896)
GATE = slice(1024, 1536)
UP = slice(1536, 2048)
GATEUP = slice(1024, 2048)
DOWN = slice(2048, 2560)
ROWS = (2, 4, 32, 768)


class Box:
    def __init__(self, names, refs):
        self.__dict__.update(zip(names, refs, strict=True))


def place():
    y = lax.axis_index("dp")
    e = lax.axis_index("ep")
    z = lax.axis_index("tp")
    return y, e // 2, e % 2, z


def device(y, x, c, z):
    return (y, x * 2 + c, z)


def greet(others):
    for who in others:
        pl.semaphore_signal(pltpu.get_barrier_semaphore(), inc=1, device_id=who, device_id_type=MESH)


def met(others):
    pl.semaphore_wait(pltpu.get_barrier_semaphore(), len(others))


def mm(a, b):
    return lax.dot_general(a, b, (((1,), (0,)), ((), ())), preferred_element_type=F32)


def mm_t(a, b):
    return lax.dot_general(a, b, (((1,), (1,)), ((), ())), preferred_element_type=F32)


def t_mm(a, b):
    return lax.dot_general(a, b, (((0,), (0,)), ((), ())), preferred_element_type=F32)


def lanes(shape):
    return lax.broadcasted_iota(jnp.int32, shape, 1)


def gain_rows(weights):
    pick = (lanes((8, 128)) == lax.broadcasted_iota(jnp.int32, (8, 128), 0) + GAIN).astype(BF)
    return mm_t(pick, weights[:, SMALL])


def rms(values, gain):
    turn = lax.rsqrt(jnp.mean(values * values, axis=-1, keepdims=True) + EPS)
    return values * turn * gain


def rms_back(values, gain, grad):
    turn = lax.rsqrt(jnp.mean(values * values, axis=-1, keepdims=True) + EPS)
    scaled = grad * gain
    back = turn * scaled - values * (turn * turn * turn) * jnp.mean(values * scaled, axis=-1, keepdims=True)
    return back, jnp.sum(grad * values * turn, axis=0, keepdims=True)


def turned(values, cosine, sine):
    width = values.shape[1]
    front = lanes(values.shape) % HD < HD // 2
    other = jnp.where(front, pltpu.roll(values, width - HD // 2, 1), pltpu.roll(values, HD // 2, 1))
    return values * cosine + other * sine


def sigmoid(v):
    return 1.0 / (1.0 + jnp.exp(-v))


def swish_back(gate, up, grad):
    s = sigmoid(gate)
    return (grad * up * s * (1.0 + gate * (1.0 - s))).astype(BF), (grad * gate * s).astype(BF)


def turns(t, sign):
    cosine, sine = t.turn[:, :128], sign * t.turn[:, 128:]
    first = lanes((128, 128)) < HD
    one, none = jnp.ones((128, 128), F32), jnp.zeros((128, 128), F32)
    mixed, mixed_sine = jnp.where(first, cosine, 1.0), jnp.where(first, sine, 0.0)
    cosine = jnp.concatenate([cosine, mixed, one, cosine, mixed], axis=1)
    sine = jnp.concatenate([sine, mixed_sine, none, sine, mixed_sine], axis=1)
    return cosine, sine


def set_route(t, layer):
    row = lax.broadcasted_iota(jnp.int32, (16, 128), 0)
    unit = (row == lanes((16, 128))).astype(BF)
    for s in range(2):
        stacked = jnp.zeros((16, 128), jnp.int32)
        for n, ref in enumerate((t.ids, t.slots)):
            for j in range(2):
                stacked = jnp.where(row == 2 * n + j, ref[layer, s, j : j + 1], stacked)
        columns = t_mm(stacked.astype(F32).astype(BF), unit).astype(jnp.int32)
        rows = slice(s * 128, s * 128 + 128)
        for j in range(2):
            expert, slot = columns[:, j : j + 1], columns[:, 2 + j : 3 + j]
            t.route[rows, j : j + 1] = jnp.where(slot < 32, expert * 32 + slot, 512)
            t.route[rows, 2 + j : 3 + j] = expert


class Wires:
    def __init__(self, sends, recvs):
        self.sends, self.recvs, self.used, self.open = sends, recvs, 0, []

    def plan(self, src, dst, who, when=None, at=None):
        if at is None:
            at = self.used
            self.used += 1
        copy = pltpu.make_async_remote_copy(
            src_ref=src,
            dst_ref=dst,
            send_sem=self.sends.at[at],
            recv_sem=self.recvs.at[at],
            device_id=who,
            device_id_type=MESH,
        )
        self.open.append((copy, when))
        return copy

    def go(self, src, dst, who):
        copy = self.plan(src, dst, who)
        copy.start()
        return copy

    def finish(self):
        assert self.used <= self.sends.shape[0]
        for copy, when in self.open:
            if when is None:
                copy.wait_send()
            else:
                pl.when(when)(copy.wait_send)


class Moves:
    def __init__(self, sems):
        self.sems, self.used, self.open = sems, 0, []

    def go(self, src, dst):
        copy = pltpu.make_async_copy(src, dst, self.sems.at[self.used])
        self.used += 1
        copy.start()
        self.open.append(copy)
        return copy

    def need(self, copy):
        self.open = [other for other in self.open if other is not copy]
        copy.wait()

    def finish(self):
        assert self.used <= self.sems.shape[0]
        for copy in self.open:
            copy.wait()


def peers(y, e, z):
    row = [(y, (e + k) % 8, z) for k in range(1, 8)]
    return row + [(y, e, (z + k) % 4) for k in range(1, 4)] + [((y + k) % 4, e, z) for k in range(1, 4)]


class TpSum:
    def __init__(self, wires, parts, land, held):
        self.wires, self.parts, self.land, self.held = wires, parts, land, held
        self.y, self.e, self.z = (lax.axis_index(name) for name in ("dp", "ep", "tp"))
        self.sums, self.spread = [None, None], [None, None]

    def send(self, h):
        self.sums[h] = []
        for k in (1, 3, 2):
            who = (self.z + k) % 4
            copy = self.wires.go(self.parts.at[h, who], self.land.at[h, k - 1], (self.y, self.e, who))
            self.sums[h].append(copy)

    def half(self, h, finish):
        for copy in self.sums[h]:
            copy.wait_recv()
        total = self.parts[h, self.z].astype(F32)
        for k in range(3):
            total += self.land[h, k].astype(F32)
        finish(h, slice(32 * h, 32 * h + 32), total)
        self.spread[h] = self.everywhere(self.held.at[h, self.z])

    def everywhere(self, spot):
        return [self.wires.go(spot, spot, (self.y, self.e, (self.z + k) % 4)) for k in (1, 3, 2)]

    def wait(self, h):
        for copy in self.spread[h]:
            copy.wait_recv()


def scatter_experts(wires, src, dst, y, e, z, i):
    rows = pl.ds(pl.multiple_of(e * 32, 32), 32)
    sent = []
    for k in (1, 7, 2, 6, 3, 5, 4):
        who = (e + k) % 8
        sent.append(wires.go(src.at[2 * who + i], dst.at[i, rows], (y, who, z)))
    dst[i, rows] = src[2 * e + i]
    return lambda: [copy.wait_recv() for copy in sent]


def return_experts(wires, src, dst, y, e, z, i):
    sent = []
    for k in (1, 7, 2, 6, 3, 5, 4):
        who = (e + k) % 8
        rows = pl.ds(pl.multiple_of(who * 32, 32), 32)
        sent.append(wires.go(src.at[i, rows], dst.at[2 * e + i], (y, who, z)))
    dst[2 * e + i] = src[i, pl.ds(pl.multiple_of(e * 32, 32), 32)]
    return lambda: [copy.wait_recv() for copy in sent]


class RowWalk:
    def __init__(self, wires, moves, own, rows, y, e, z):
        self.wires, self.moves, self.own, self.rows = wires, moves, own, rows
        self.up, self.down = ((y + 1) % 4, e, z), ((y + 3) % 4, e, z)
        self.near, self.far = [], []

    def start(self, i):
        own, rows = self.own.at[i], self.rows
        self.near.append(
            (self.wires.go(own, rows.at[i, 1], self.up), self.wires.go(own, rows.at[i, 3], self.down))
        )
        self.moves.go(own, rows.at[i, 0])

    def pass_on(self, i):
        self.near[i][i].wait_recv()
        slot, who = ((1, self.up), (3, self.down))[i]
        self.far.append(self.wires.go(self.rows.at[i, slot], self.rows.at[i, 2], who))

    def finish(self):
        self.near[0][1].wait_recv()
        self.near[1][0].wait_recv()
        for copy in self.far:
            copy.wait_recv()


class Gather:
    def __init__(self, wires, land, columns):
        self.wires, self.land, self.columns = wires, land, columns
        self.y, self.x, self.c, self.z = place()
        self.sib, self.second, self.far = [], {}, []

    def who(self, j, d):
        yy = (self.y + j * self.c + d * (1 - self.c) + 8) % 4
        xx = (self.x + j * (1 - self.c) + d * self.c + 8) % 4
        return device(yy, xx, self.c, self.z)

    def spot(self, j, d, rows=slice(None)):
        yy, ee, zz = self.who(j, d)
        return self.land.at[yy * 8 + ee, rows, self.columns]

    def pair(self, spot):
        self.sib.append(self.wires.go(spot, spot, device(self.y, self.x, 1 - self.c, self.z)))

    def spread(self, j):
        spot = self.spot(j, 0)
        self.second[j] = self.wires.go(spot, spot, self.who(0, 1)), self.wires.go(spot, spot, self.who(0, -1))
        self.pair(spot)

    def step0(self):
        spot = self.spot(0, 0)
        self.first = self.wires.go(spot, spot, self.who(1, 0)), self.wires.go(spot, spot, self.who(-1, 0))
        self.spread(0)

    def step1(self):
        self.first[0].wait_recv()
        spot = self.spot(-1, 0, pl.ds(0, 32))
        self.on = [self.wires.go(spot, spot, self.who(1, 0))]
        self.spread(-1)
        self.first[1].wait_recv()
        spot = self.spot(1, 0, pl.ds(32, 16))
        self.on.append(self.wires.go(spot, spot, self.who(-1, 0)))
        self.spread(1)

    def step2(self):
        for copy in self.on:
            copy.wait_recv()
        self.spread(2)

    def step3(self):
        for j in (0, -1, 1, 2):
            for n, d in enumerate((-1, 1)):
                self.second[j][n].wait_recv()
                spot = self.spot(j, d)
                if (j in (0, -1)) == (n == 0):
                    self.far.append((j, self.wires.go(spot, spot, self.who(0, -d))))
                self.pair(spot)

    def step4(self):
        for j, copy in self.far:
            copy.wait_recv()
            self.pair(self.spot(j, 2))

    def step5(self):
        for copy in self.sib:
            copy.wait_recv()


class ShortGather(Gather):
    def reach(self, spot, whos):
        return [self.wires.go(spot, spot, who) for who in whos]

    def spread(self, j):
        spot = self.spot(j, 0)
        self.second[j] = self.reach(spot, [self.who(0, d) for d in (2, 1, -1)])
        self.pair(spot)

    def step0(self):
        self.first = self.reach(self.spot(0, 0), [self.who(j, 0) for j in (2, 1, -1)])
        self.spread(0)

    def step1(self):
        for n, j in ((1, -1), (2, 1), (0, 2)):
            self.first[n].wait_recv()
            self.spread(j)

    def step2(self):
        for j in (0, -1, 1, 2):
            for n, d in ((1, -1), (2, 1), (0, 2)):
                self.second[j][n].wait_recv()
                self.pair(self.spot(j, d))


def unpack(land, columns, w, left):
    half = columns.stop - columns.start

    def some(p, carry):
        one = land[2 * p, :, columns].astype(F32)
        two = land[2 * p + 1, :, columns].astype(F32)
        rows = pl.ds(pl.multiple_of(p * CHUNK, CHUNK), CHUNK)
        w[rows, left : left + half] = jnp.concatenate([one[:24], two[:24]], axis=0).astype(BF)
        w[rows, left + half : left + 2 * half] = jnp.concatenate([one[24:], two[24:]], axis=0).astype(BF)
        return carry

    lax.fori_loop(0, 16, some, 0)


def picks(route):
    slots = lanes((256, 512))
    return slots == route[:, 0:1], slots == route[:, 1:2]


class Scatter:
    PLUS, MINUS = (0, -1), (1, 2)

    def __init__(self, wires, acc, pool, total, other, out):
        self.wires, self.acc, self.pool, self.total, self.other, self.out = wires, acc, pool, total, other, out
        self.y, self.x, self.c, self.z = place()
        self.sibling = device(self.y, self.x, 1 - self.c, self.z)
        self.order = [(j, d) for d in (2, 1, -1, 0) for j in (0, -1, 1, 2)]
        self.swapped, self.far, self.near = {}, {}, {}

    def at(self, j, d, core):
        yy = (self.y + j * core + d * (1 - core) + 8) % 4
        xx = (self.x + j * (1 - core) + d * core + 8) % 4
        return yy, xx

    def who(self, j, d):
        yy, xx = self.at(j, d, self.c)
        return device(yy, xx, self.c, self.z)

    def mine(self, j, d, core):
        yy, xx = self.at(j, d, core)
        return yy * 4 + xx

    def add(self, ref, *others):
        total = ref[...].astype(F32)
        for other in others:
            total += other[...].astype(F32)
        ref[...] = total.astype(BF)

    def join(self, j, d):
        self.swapped[j, d].wait_recv()
        ref = self.acc.at[self.c, self.mine(j, d, self.c)]
        self.add(ref, self.pool.at[self.order.index((j, d))])
        return ref

    def step0(self):
        for n, (j, d) in enumerate(self.order):
            block = self.acc.at[1 - self.c, self.mine(j, d, 1 - self.c)]
            self.swapped[j, d] = self.wires.go(block, self.pool.at[n], self.sibling)

    def step1(self):
        for j in (0, 1, -1, 2):
            ref = self.join(j, 2)
            n, d = (16 + self.PLUS.index(j), 1) if j in self.PLUS else (18 + self.MINUS.index(j), -1)
            self.far[j] = self.wires.go(ref, self.pool.at[n], self.who(0, d))
        for j, k in zip(self.MINUS, self.PLUS):
            self.near[j, 1] = self.wires.go(self.join(j, 1), self.pool.at[20 + j], self.who(0, 1))
            self.near[k, -1] = self.wires.go(self.join(k, -1), self.pool.at[24 + k % 4], self.who(0, -1))
        self.up = {j: self.join(j, 1) for j in self.PLUS}
        self.down = {j: self.join(j, -1) for j in self.MINUS}

    def step2(self):
        for n, (j, k) in enumerate(zip(self.PLUS, self.MINUS)):
            self.far[j].wait_recv()
            self.add(self.up[j], self.pool.at[16 + n])
            self.near[j, 1] = self.wires.go(self.up[j], self.pool.at[20 + j % 4], self.who(0, 1))
            self.far[k].wait_recv()
            self.add(self.down[k], self.pool.at[18 + n])
            self.near[k, -1] = self.wires.go(self.down[k], self.pool.at[24 + k], self.who(0, -1))
        self.held = {j: self.join(j, 0) for j in (2, 1, -1, 0)}

    def step3(self):
        for j in (2, 1, -1, 0):
            self.near[j, 1].wait_recv()
            self.near[j, -1].wait_recv()
            ref = self.held[j]
            self.add(ref, self.pool.at[20 + j % 4], self.pool.at[24 + j % 4])
            if j == 2:
                spot = self.pool.at[28]
                self.one = [
                    self.wires.go(ref.at[rows], spot.at[rows], self.who(d, 0))
                    for rows, d in ((pl.ds(0, 32), 1), (pl.ds(32, 16), -1))
                ]

    def step4(self):
        self.last = []
        for n, (rows, d) in enumerate(((pl.ds(0, 32), 1), (pl.ds(32, 16), -1))):
            self.one[n].wait_recv()
            self.add(self.held[d].at[rows], self.pool.at[28].at[rows])
            self.last.append(self.wires.go(self.held[d], self.pool.at[29 + n], self.who(d, 0)))

    def step5(self):
        for copy in self.last:
            copy.wait_recv()
        self.total[...] = self.held[0][...].astype(F32) + self.pool[29].astype(F32) + self.pool[30].astype(F32)
        away = pl.ds(pl.multiple_of(24 - 24 * self.c, 8), 24)
        self.trade = self.wires.go(self.total.at[away], self.other, self.sibling)
        self.out[self.c] = self.total[pl.ds(pl.multiple_of(24 * self.c, 8), 24)]

    def step6(self):
        self.trade.wait_recv()
        self.out[1 - self.c] = self.other[...]


def forward_block(wires, moves, t, w, need, stream, own, lengths, pump, done, dp_rows=None):
    y, x, c, z = place()
    e = 2 * x + c
    gains = gain_rows(w)
    values = stream[...].reshape(256, 768).astype(F32)
    t.normed[...] = rms(values, gains[0:1]).astype(BF)
    done("normed")
    sibling = (y, e + 1 - 2 * c, z)
    cosine, sine = turns(t, 1.0)
    spans = (slice(0, 128), slice(128, 256))
    first, to_core = [], []
    for s, rows in enumerate(spans):
        lin = turned(mm(t.normed[rows], w[:, QKV]), cosine, sine).astype(BF)
        t.kv[e, rows] = lin[:, :384]
        t.queries[rows] = lin[:, 384:576]
        here = t.kv.at[e, pl.ds(s * 128, 128)]
        first.append([])
        for k in (1, 3, 2):
            ahead = x + k <= 3
            copy = wires.plan(here, here, (y, (e + 2 * k) % 8, z), ahead)
            pl.when(ahead)(copy.start)
            first[s].append((k, copy))
        to_core.append(wires.plan(here, here, sibling, c == 0))
        pl.when(c == 0)(to_core[s].start)
    done("queries")
    for j in range(8):

        @pl.when(j > e)
        def _():
            t.kv[j] = jnp.zeros((256, 384), BF)

    pump()
    tp = TpSum(wires, t.part.at[0], t.land.at[0], t.ffn_in)
    at_key = lanes((128, 1024))
    at_query = lax.broadcasted_iota(jnp.int32, (128, 1024), 0) + e * 128
    for s, rows in enumerate(spans):
        second = []
        for k, copy in first[s]:
            behind = x - k >= 0
            there = t.kv.at[(e + 8 - 2 * k) % 8, pl.ds(s * 128, 128)]
            on = wires.plan(there, there, sibling, behind)

            @pl.when(behind)
            def _():
                copy.wait_recv()
                on.start()

            second.append((behind, on))
        pl.when(c == 1)(to_core[s].wait_recv)
        for behind, on in second:
            pl.when(behind)(on.wait_recv)
        allowed = (at_key <= at_query) & (at_key < lengths[s])
        for h in range(3):
            keys = t.kv[:, rows, 64 * h : 64 * h + 64].reshape(1024, 64)
            vals = t.kv[:, rows, 192 + 64 * h : 256 + 64 * h].reshape(1024, 64)
            scores = jnp.where(allowed, mm_t(t.queries[rows, 64 * h : 64 * h + 64], keys) * HD**-0.5, -1e30)
            expd = jnp.exp(scores - jnp.max(scores, axis=-1, keepdims=True))
            low = (expd / jnp.sum(expd, axis=-1, keepdims=True)).astype(BF)
            t.probs[3 * s + h] = low
            t.attended[rows, 64 * h : 64 * h + 64] = mm(low, vals).astype(BF)
        t.part[0, s] = mm_t(t.attended[rows], w[:, OUT]).astype(BF).reshape(4, 32, 768)
        tp.send(s)
    done("kv", "probs", "attended")
    pump()

    def finish(h, rows, total):
        t.middle[rows] = own[rows] + total
        t.ffn_in[h, z] = rms(t.middle[rows], gains[1:2]).astype(BF)

    tp.half(0, finish)
    tp.half(1, finish)
    done("middle")
    pump()
    tp.wait(0)
    tp.wait(1)
    done("ffn_in")
    rows_in = t.ffn_in[...].reshape(256, 768)
    ids = t.route[...]
    pick0, pick1 = picks(ids)
    t.sent[...] = t_mm((pick0 | pick1).astype(BF), rows_in).astype(BF).reshape(16, 32, 768)
    coming = [scatter_experts(wires, t.sent, t.arrived, y, e, z, i) for i in range(2)]
    pump()
    logits = mm(rows_in, w[:, SMALL])
    lane = lanes((256, 128))
    chosen = [
        jnp.sum(jnp.where(lane == ids[:, 2 + j : 3 + j] + ROUTER, logits, 0.0), axis=-1, keepdims=True)
        for j in range(2)
    ]
    top = jnp.maximum(chosen[0], chosen[1])
    expd = [jnp.exp(v - top) for v in chosen]
    share = [v / (expd[0] + expd[1]) for v in expd]
    t.shares[...] = jnp.where(lane == 0, share[0], jnp.where(lane == 1, share[1], 0.0))
    t.gud[...] = mm(rows_in, w[:, GATEUP])
    gate, up = t.gud[:, :512], t.gud[:, 512:]
    hidden = (gate * sigmoid(gate) * up).astype(BF)
    dense = mm_t(hidden, w[:, DOWN])
    done("gud", "shares")
    pump()
    need("eg", "eu", "ed")
    walk = None if dp_rows is None else RowWalk(wires, moves, t.arrived, dp_rows, y, e, z)
    back = []
    for i in range(2):
        coming[i]()
        if walk is not None:
            walk.start(i)
        t.gue[i, :, :512] = mm(t.arrived[i], t.eg[i])
        t.gue[i, :, 512:] = mm(t.arrived[i], t.eu[i])
        gate, up = t.gue[i, :, :512], t.gue[i, :, 512:]
        hidden = (gate * sigmoid(gate) * up).astype(BF)
        t.made[i] = mm(hidden, t.ed[i]).astype(BF)
        back.append(return_experts(wires, t.made, t.ret, y, e, z, i))
    done("arrived", "gue")
    pump()
    for wait in back:
        wait()
    done("ret")
    mix = (jnp.where(pick0, share[0], 0.0) + jnp.where(pick1, share[1], 0.0)).astype(BF)
    tp = TpSum(wires, t.part.at[1], t.land.at[1], t.stream_out)
    for h, rows in enumerate(spans):
        moe = mm(mix[rows], t.ret[...].reshape(512, 768))
        t.part[1, h] = (dense[rows] + moe).astype(BF).reshape(4, 32, 768)
        tp.send(h)
    pump()

    def finish(h, rows, total):
        result = t.middle[rows] + total
        t.own_out[rows] = result
        t.stream_out[h, z] = result.astype(BF)

    def halves():
        tp.half(0, finish)
        tp.half(1, finish)
        done("own_out")
        pump()

    def wait():
        tp.wait(0)
        tp.wait(1)
        done("stream_out")

    return walk, halves, wait


def backward_start(wires, t, w, need, incoming):
    y, x, c, z = place()
    e = 2 * x + c
    need("shares")
    ffn_grad = incoming[...].reshape(256, 768)
    pick0, pick1 = picks(t.route[...])
    mix = (jnp.where(pick0, t.shares[:, 0:1], 0.0) + jnp.where(pick1, t.shares[:, 1:2], 0.0)).astype(BF)
    t.bsent[...] = t_mm(mix, ffn_grad).astype(BF).reshape(16, 32, 768)
    coming = [scatter_experts(wires, t.bsent, t.back, y, e, z, i) for i in range(2)]
    need("w", "gud", "ffn_in")
    gate, up = t.gud[:, :512], t.gud[:, 512:]
    hidden_dense = (gate * sigmoid(gate) * up).astype(BF)
    gate_grad, up_grad = swish_back(gate, up, mm(ffn_grad, w[:, DOWN]))
    gu_grad = jnp.concatenate([gate_grad, up_grad], axis=1)
    t.dense[...] = mm_t(gu_grad, w[:, GATEUP])
    t.gu_grad[...] = gu_grad
    t.hidden_dense[...] = hidden_dense
    return coming


def backward_block(wires, moves, t, w, need, incoming, grad_own, own, coming, pump, dp_rows, grads):
    y, x, c, z = place()
    e = 2 * x + c

    def keep(columns, values):
        for half, start in enumerate((0, HALF)):
            left, right = max(columns.start, start), min(columns.stop, start + HALF)
            if left < right:
                some = values[:, left - columns.start : right - columns.start].astype(BF)
                grads[half, :, :, left - start : right - start] = some.reshape(16, CHUNK, right - left)

    need("ret")
    ffn_grad = incoming[...].reshape(256, 768)
    rows_in = t.ffn_in[...].reshape(256, 768)
    gains = gain_rows(w)
    pick0, pick1 = picks(t.route[...])
    match = mm_t(ffn_grad, t.ret[...].reshape(512, 768))
    share_grad = [
        jnp.sum(jnp.where(pick, match, 0.0), axis=-1, keepdims=True) for pick in (pick0, pick1)
    ]
    lane = lanes((256, 128))
    extra = jnp.where(lane == 0, share_grad[0], jnp.where(lane == 1, share_grad[1], 0.0))
    t.part_ffn[:, :, :, 768:] = extra.astype(BF).reshape(2, 4, 32, 128)
    pump()
    need("ed", "gue", "eg", "eu")
    walk = RowWalk(wires, moves, t.back, dp_rows, y, e, z)
    back = []
    for i in range(2):
        coming[i]()
        walk.start(i)
        hidden_grad = mm_t(t.back[i], t.ed[i])
        gate_e, up_e = swish_back(t.gue[i, :, :512], t.gue[i, :, 512:], hidden_grad)
        t.bmade[i] = (mm_t(gate_e, t.eg[i]) + mm_t(up_e, t.eu[i])).astype(BF)
        back.append(return_experts(wires, t.bmade, t.sret, y, e, z, i))
    pump()
    keep(GATEUP, t_mm(rows_in, t.gu_grad[...]))
    keep(DOWN, t_mm(ffn_grad, t.hidden_dense[...]))
    for wait in back:
        wait()
    tp = TpSum(wires, t.part_ffn, t.land_ffn, t.gathered)
    spans = (slice(0, 128), slice(128, 256))
    placed = (pick0 | pick1).astype(BF)
    for h, rows in enumerate(spans):
        total = t.dense[rows] + mm(placed[rows], t.sret[...].reshape(512, 768))
        t.part_ffn[h, :, :, :768] = total.astype(BF).reshape(4, 32, 768)
        tp.send(h)
    pump()
    need("middle")
    top = lax.broadcasted_iota(jnp.int32, (16, 768), 0) == 0
    lane32 = lanes((32, 128))
    gain_parts = []

    def finish(h, rows, total):
        mine = pl.ds(pl.multiple_of(128 * h + 32 * z, 32), 32)
        share, ids = t.shares[mine], t.route[mine]
        weigh = share[:, 0:1] * total[:, 768:769] + share[:, 1:2] * total[:, 769:770]
        logit_grad = jnp.zeros((32, 128), F32)
        for j in range(2):
            chosen_grad = share[:, j : j + 1] * (total[:, 768 + j : 769 + j] - weigh)
            logit_grad += jnp.where(lane32 == ids[:, 2 + j : 3 + j] + ROUTER, chosen_grad, 0.0)
        logit_grad = logit_grad.astype(BF)
        grad_in = total[:, :768] + mm_t(logit_grad, w[:, SMALL])
        back_norm, gain_two = rms_back(t.middle[rows], gains[1:2], grad_in)
        gain_parts.append(gain_two)
        middle_grad = grad_own[rows] + back_norm
        t.down_own[rows] = middle_grad
        t.gathered[h, z, :, :768] = middle_grad.astype(BF)
        t.gathered[h, z, :, 768:] = logit_grad

    tp.half(0, finish)
    tp.half(1, finish)
    t.gains[1, z] = jnp.where(top, gain_parts[0] + gain_parts[1], 0.0).astype(BF)
    gain_copies = tp.everywhere(t.gains.at[1, z])
    grads_tp = tp
    pump()
    need("probs", "kv", "queries", "attended", "normed")
    sibling = (y, e + 1 - 2 * c, z)

    def attend_back(s, between):
        rows = spans[s]
        grad = t.gathered[s, :, :, :768].reshape(128, 768)
        attended_grad = mm(grad, w[:, OUT]).astype(BF)
        for h in range(3):
            cols = slice(64 * h, 64 * h + 64)
            late = slice(192 + 64 * h, 256 + 64 * h)
            keys = t.kv[:, rows, cols].reshape(1024, 64)
            vals = t.kv[:, rows, late].reshape(1024, 64)
            low = t.probs[3 * s + h]
            wide = low.astype(F32)
            grad_here = attended_grad[:, cols]
            probs_grad = mm_t(grad_here, vals)
            kept = jnp.sum(wide * probs_grad, axis=-1, keepdims=True)
            score_grad = (wide * (probs_grad - kept)).astype(BF)
            t.lin[rows, 384 + 64 * h : 448 + 64 * h] = mm(score_grad, keys) * HD**-0.5
            keys_grad = t_mm(score_grad, t.queries[rows, cols]) * HD**-0.5
            t.dkv[:, rows, cols] = keys_grad.astype(BF).reshape(8, 128, 64)
            t.dkv[:, rows, late] = t_mm(low, grad_here).astype(BF).reshape(8, 128, 64)
            if h == 0:
                between()

    def swap(s):
        rows = pl.ds(s * 128, 128)
        swaps = []
        for k in range(4):
            gives = (x - k >= 0) & ((c == 1) if k == 0 else True)
            takes = (x - k >= 0) & ((c == 0) if k == 0 else True)
            block = (2 * (x - k) + 1 - c + 8) % 8
            copy = wires.plan(t.dkv.at[block, rows], t.sib_land.at[k, rows], sibling, gives)
            pl.when(gives)(copy.start)
            swaps.append((takes, copy))
        return swaps

    def send_far(s, swaps):
        rows = pl.ds(s * 128, 128)
        far = []
        for k in (1, 3, 2):
            gives, takes = x - k >= 0, x + k <= 3
            block = (e - 2 * k + 8) % 8
            send = wires.plan(t.dkv.at[block, rows], t.owner_land.at[k - 1, rows], (y, block, z), gives)

            @pl.when(gives)
            def _():
                swaps[k][1].wait_recv()
                both = t.dkv[block, rows].astype(F32) + t.sib_land[k, rows].astype(F32)
                t.dkv[block, rows] = both.astype(BF)
                send.start()

            far.append((k, takes, send))
        return far

    cosine, sine = turns(t, -1.0)
    tp = TpSum(wires, t.bpart, t.bland, t.tail)

    def collect(s, swaps, far):
        rows = spans[s]
        t.lin[rows, :384] = t.dkv[e, rows].astype(F32)
        t.lin[rows, 576:] = jnp.zeros((128, 64), F32)

        @pl.when(swaps[0][0])
        def _():
            swaps[0][1].wait_recv()
            t.lin[rows, :384] += t.sib_land[0, rows].astype(F32)

        for k, takes, copy in far:

            @pl.when(takes)
            def _():
                copy.wait_recv()
                t.lin[rows, :384] += t.owner_land[k - 1, rows].astype(F32)

        t.lin_low[rows] = turned(t.lin[rows], cosine, sine).astype(BF)
        t.bpart[s] = mm_t(t.lin_low[rows], w[:, QKV]).astype(BF).reshape(4, 32, 768)
        tp.send(s)

    grads_tp.wait(0)
    attend_back(0, lambda: None)
    swaps0 = swap(0)
    walk.pass_on(0)
    walk.pass_on(1)
    grads_tp.wait(1)
    far0 = []
    attend_back(1, lambda: far0.extend(send_far(0, swaps0)))
    swaps1 = swap(1)
    keep(OUT, t_mm(t.gathered[:, :, :, :768].reshape(256, 768), t.attended[...]))
    far1 = send_far(1, swaps1)
    router_grad = t_mm(rows_in, t.gathered[:, :, :, 768:].reshape(256, 128))
    pump()
    collect(0, swaps0, far0)
    collect(1, swaps1, far1)
    tail_parts = []

    def finish(h, rows, total):
        back_norm, gain_one = rms_back(own[rows], gains[0:1], total)
        tail_parts.append(gain_one)
        result = t.down_own[rows] + back_norm
        t.down_own[rows] = result
        t.tail[h, z] = result.astype(BF)

    keep(QKV, t_mm(t.normed[...], t.lin_low[...]))
    pump()
    tp.half(0, finish)
    tp.half(1, finish)
    t.gains[0, z] = jnp.where(top, tail_parts[0] + tail_parts[1], 0.0).astype(BF)
    gain_copies += tp.everywhere(t.gains.at[0, z])
    pump()
    tp.wait(0)
    tp.wait(1)
    t.down_stream[...] = t.tail[...]
    for copy in gain_copies:
        copy.wait_recv()
    at_row = lax.broadcasted_iota(jnp.int32, (16, 768), 0)
    gain_grads = jnp.zeros((16, 768), F32)
    for n in range(2):
        total = jnp.sum(t.gains[n].astype(F32).reshape(64, 768), axis=0, keepdims=True)
        gain_grads = jnp.where(at_row == n, total, gain_grads)
    spot = (lanes((16, 128)) == lax.broadcasted_iota(jnp.int32, (16, 128), 0) + GAIN).astype(BF)
    keep(slice(192, 256), (router_grad + t_mm(gain_grads.astype(BF), spot))[:, 64:])
    return walk


MOVE_SEMS, WIRE_SEMS = 48, 192
SAVED = {
    "normed": ((256, 768), BF),
    "queries": ((256, 192), BF),
    "kv": ((8, 256, 384), BF),
    "probs": ((6, 128, 1024), BF),
    "attended": ((256, 192), BF),
    "middle": ((64, 768), F32),
    "ffn_in": (ROWS, BF),
    "gud": ((256, 1024), F32),
    "gue": ((2, 256, 1024), F32),
    "ret": ((16, 32, 768), BF),
    "shares": ((256, 128), F32),
}
WEIGHTS = {"w": ((768, WIDE), BF), "eg": ((2, 768, 512), BF), "eu": ((2, 768, 512), BF), "ed": ((2, 512, 768), BF)}
FORWARD = {
    "arrived": ((2, 256, 768), BF),
    "own_out": ((64, 768), F32),
    "stream_out": (ROWS, BF),
    "part": ((2, *ROWS), BF),
    "land": ((2, 2, 3, 32, 768), BF),
    "sent": ((16, 32, 768), BF),
    "made": ((2, 256, 768), BF),
}
BACKWARD = {
    "back": ((2, 256, 768), BF),
    "bsent": ((16, 32, 768), BF),
    "bmade": ((2, 256, 768), BF),
    "sret": ((16, 32, 768), BF),
    "part_ffn": ((2, 4, 32, 896), BF),
    "land_ffn": ((2, 3, 32, 896), BF),
    "bpart": (ROWS, BF),
    "bland": ((2, 3, 32, 768), BF),
    "gathered": ((2, 4, 32, 896), BF),
    "tail": (ROWS, BF),
    "gains": ((2, 4, 16, 768), BF),
    "dkv": ((8, 256, 384), BF),
    "sib_land": ((4, 256, 384), BF),
    "owner_land": ((3, 256, 384), BF),
    "dense": ((256, 768), F32),
    "gu_grad": ((256, 1024), BF),
    "hidden_dense": ((256, 512), BF),
    "lin": ((256, 640), F32),
    "lin_low": ((256, 640), BF),
    "down_own": ((64, 768), F32),
    "down_stream": (ROWS, BF),
}
SCATTER = {
    "acc": ((2, 2, 16, CHUNK, HALF), BF),
    "pool": ((2, 31, CHUNK, HALF), BF),
    "total": ((2, CHUNK, HALF), F32),
    "other": ((2, 24, HALF), F32),
}
DP_ROWS = ((2, 4, 256, 768), BF)
GRADS = ((2, 16, CHUNK, HALF), BF)


def launch(body, number, name, ins, outs, scratch, args):
    def kernel(*refs):
        names = list(ins) + list(outs) + list(scratch)
        t = Box(names, refs[: len(names)])
        moves, sends, recvs = refs[len(names) :]
        body(t, Moves(moves), Wires(sends, recvs))

    return pl.pallas_call(
        kernel,
        out_shape=[jax.ShapeDtypeStruct(*shape) for shape, space in outs.values()],
        in_specs=list(ins.values()),
        out_specs=[space for shape, space in outs.values()],
        scratch_shapes=[pltpu.VMEM(*shape) for shape in scratch.values()]
        + [
            pltpu.SemaphoreType.DMA((MOVE_SEMS,)),
            pltpu.SemaphoreType.DMA((WIRE_SEMS,)),
            pltpu.SemaphoreType.DMA((WIRE_SEMS,)),
        ],
        compiler_params=pltpu.CompilerParams(
            collective_id=number, has_side_effects=True, vmem_limit_bytes=60 * 2**20
        ),
        name=name,
    )(*args)


def fetcher(moves, pairs):
    coming = {name: moves.go(src, dst) for name, src, dst in pairs}

    def need(*names):
        for name in names:
            if name in coming:
                moves.need(coming.pop(name))

    return need


def pumper(steps):
    steps = iter(steps)

    def pump():
        for step in next(steps, ()):
            step()

    return pump


def prepare(t, moves, wires, layer):
    y, x, c, z = place()
    others = peers(y, 2 * x + c, z)
    greet(others)
    turn = moves.go(t.table.at[pl.ds(pl.multiple_of((2 * x + c) * 128, 128), 128)], t.turn)
    set_route(t, layer)
    return y, 2 * x + c, z, others, turn


def pack(t, land, layer, me, columns):
    names = (("o", 0), ("k", 256), ("v", 448), ("q", 640)) if columns is ATTN else (("g", 1024), ("u", 1536), ("d", 2048))
    if columns is ATTN:
        row = lax.broadcasted_iota(jnp.int32, (32, 24), 0)
        one, other = t.again[layer : layer + 1].astype(F32), t.fgain[layer : layer + 1].astype(F32)
        gains = jnp.where(row == 16, one, jnp.where(row == 17, other, 0.0))
        router = jnp.concatenate([t.router[layer].astype(F32), jnp.zeros((16, 24), F32)], axis=0)
        spot = (lanes((32, 128)) == lax.broadcasted_iota(jnp.int32, (32, 128), 0) + ROUTER).astype(BF)
        t.stage[:, 192:256] = t_mm((gains + router).astype(BF), spot)[:, 64:]
        t.stage[:, 832:1024] = jnp.zeros((24, 192), F32)
    for name, left in names:
        ref = getattr(t, name)
        t.stage[:, left : left + ref.shape[2]] = ref[layer].astype(F32)
    left, middle, right = (0, 512, 1024) if columns is ATTN else (1024, 1792, 2560)
    halves = [t.stage[:, left:middle], t.stage[:, middle:right]]
    land[me, :, columns] = jnp.concatenate(halves, axis=0).astype(BF)


def first_body(t, moves, wires):
    y, e, z, others, turn = prepare(t, moves, wires, 0)
    need = fetcher(moves, [(n, getattr(t, n + "_all").at[0], getattr(t, n)) for n in ("eg", "eu", "ed")])
    me = y * 8 + e
    pack(t, t.land0, 0, me, ATTN)
    met(others)
    attn, feed = ShortGather(wires, t.land0, ATTN), Gather(wires, t.land0, FEED)
    late = Gather(wires, t.land1, slice(0, 1280))
    attn.step0()
    pack(t, t.land0, 0, me, FEED)
    attn.step1()
    t.own0[...] = t.stream[:, z].astype(F32).reshape(64, 768)
    attn.step2()
    feed.step0()
    attn.step5()
    unpack(t.land0, ATTN, t.w, 0)
    moves.need(turn)

    def feed_ready():
        unpack(t.land0, FEED, t.w, 1024)
        moves.go(t.w, t.w_out.at[0])

    def late_ready():
        unpack(t.land1, ATTN, t.w1, 0)
        unpack(t.land1, FEED, t.w1, 1024)
        moves.go(t.w1, t.w_out.at[1])

    def late_start():
        pack(t, t.land1, 1, me, ATTN)
        pack(t, t.land1, 1, me, FEED)
        late.step0()

    pump = pumper(
        [
            (feed.step1,),
            (feed.step2, late_start),
            (feed.step3, late.step1),
            (feed.step4, feed.step5, feed_ready, late.step2),
            (late.step3,),
            (late.step4,),
            (late.step5,),
            (late_ready,),
        ]
    )

    def done(*names):
        for name in names:
            moves.go(getattr(t, name), getattr(t, name + "_out"))

    walk, halves, wait = forward_block(wires, moves, t, t.w, need, t.stream, t.own0, t.lengths, pump, done)
    halves()
    wait()
    wires.finish()
    moves.finish()


def second_body(t, moves, wires):
    y, e, z, others, turn = prepare(t, moves, wires, 1)
    need = fetcher(
        moves, [(n, getattr(t, n + "_all").at[1], getattr(t, n)) for n in ("w", "eg", "eu", "ed")]
    )
    t.cot_own[...] = t.cotangent[:, z].astype(F32).reshape(64, 768)
    met(others)
    early = RowWalk(wires, moves, t.arrived0, t.rows0, y, e, z)
    early.start(0)
    early.start(1)
    need("w")
    moves.need(turn)
    none = lambda *names: None
    coming = []
    start = lambda: coming.extend(backward_start(wires, t, t.w, need, t.cotangent))
    pump = pumper([(), (), (lambda: early.pass_on(0), lambda: early.pass_on(1)), (), (), (early.finish, start)])
    walk, halves, wait = forward_block(
        wires, moves, t, t.w, need, t.stream, t.own, t.lengths, pump, none, t.rows1
    )
    pump = pumper([(lambda: walk.pass_on(0), lambda: walk.pass_on(1)), (halves, walk.finish)])
    walk = backward_block(
        wires, moves, t, t.w, need, t.cotangent, t.cot_own, t.own, coming, pump, t.back1, t.grads
    )
    wait()
    t.outputs[...] = t.stream_out[...]
    t.outputs_own[...] = t.own_out[...]
    moves.go(t.grads, t.grads1)
    t.grad_own[...] = t.down_own[...]
    t.grad_stream[...] = t.down_stream[...]
    walk.finish()
    wires.finish()
    moves.finish()


def third_body(t, moves, wires):
    y, e, z, others, turn = prepare(t, moves, wires, 0)
    order = ("shares", "w", "gud", "ret", "ffn_in", "ed", "gue", "eg", "eu", "middle", "probs", "kv", "queries", "attended", "normed")
    source = lambda n: getattr(t, n + "_all").at[0] if n in WEIGHTS else getattr(t, n + "_in")
    need = fetcher(moves, [(n, source(n), getattr(t, n)) for n in order] + [("grads1", t.grads1, t.acc.at[1])])
    one, zero = [
        Scatter(wires, t.acc.at[n], t.pool.at[n], t.total.at[n], t.other.at[n], t.sums.at[n]) for n in (1, 0)
    ]
    t.own0[...] = t.inputs[:, z].astype(F32).reshape(64, 768)
    moves.need(turn)
    met(others)
    coming = backward_start(wires, t, t.w, need, t.incoming)
    pump = pumper(
        [(lambda: need("grads1"), one.step0), (), (one.step1,), (one.step2,), (one.step3,), (one.step4,), (one.step5,)]
    )
    walk = backward_block(
        wires, moves, t, t.w, need, t.incoming, t.grad_own, t.own0, coming, pump, t.back0, t.acc.at[0]
    )
    zero.step0()
    t.input_grad[...] = t.down_stream[...]
    t.input_own[...] = t.down_own[...]
    one.step6()
    for step in (zero.step1, zero.step2, zero.step3, zero.step4, zero.step5, zero.step6):
        step()
    walk.finish()
    wires.finish()
    moves.finish()


def last_kernel(rows0, rows1, back0, back1, eg, eu, ed, sums, outputs, own, input_grad, own_grad, *rest):
    rows, grads, hidden, gu, sems = rest[-5:]
    g_gate, g_up, g_down, o_out, o_in, o_router, o_again, o_fgain, *o_parts = rest[:-5]
    at = pl.program_id(0) * 2 + pl.program_id(1)
    begins = pl.program_id(2) == 0
    sources = [(src, back, i) for src, back in ((rows1, back1), (rows0, back0)) for i in range(2)]

    def copies(n):
        src, back, i = sources[n]
        return (
            pltpu.make_async_copy(src.at[i], rows.at[n % 2], sems.at[n % 2, 0]),
            pltpu.make_async_copy(back.at[i], grads.at[n % 2], sems.at[n % 2, 1]),
        )

    for n in range(4):

        @pl.when(begins & (at == n))
        def _():
            if n == 0:
                for copy in copies(0):
                    copy.start()
            if n < 3:
                for copy in copies(n + 1):
                    copy.start()
            for copy in copies(n):
                copy.wait()

    slot = at % 2
    for n in range(4):
        some = slice(n * 256, n * 256 + 256)
        mine = rows[slot, n]
        gate, up, hidden_grad = mm(mine, eg[...]), mm(mine, eu[...]), mm_t(grads[slot, n], ed[...])
        s = sigmoid(gate)
        silu = gate * s
        hidden[some] = (silu * up).astype(BF)
        gu[some, :256] = (hidden_grad * up * (s * (1.0 + gate * (1.0 - s)))).astype(BF)
        gu[some, 256:] = (hidden_grad * silu).astype(BF)
    both = t_mm(rows[slot].reshape(1024, 768), gu[...])
    g_gate[...] = both[:, :256]
    g_up[...] = both[:, 256:]
    g_down[...] = t_mm(hidden[...], grads[slot].reshape(1024, 768))

    @pl.when(begins & (at == 0))
    def _():
        z = lax.axis_index("tp")
        o_out[...] = outputs[...].astype(F32)
        o_out[:, z] = own[...].reshape(2, 32, 768)
        o_in[...] = input_grad[...].astype(F32)
        o_in[:, z] = own_grad[...].reshape(2, 32, 768)
        pick = (lanes((24, 128)) == lax.broadcasted_iota(jnp.int32, (24, 128), 0) + ROUTER).astype(F32)
        for layer in range(2):
            left, right = sums[layer, 0], sums[layer, 1]
            o_o, o_k, o_v, o_q, o_gate, o_up, o_down = [ref.at[layer] for ref in o_parts]
            o_o[...] = left[:, OUT]
            o_k[...] = left[:, 256:448]
            o_v[...] = left[:, 448:640]
            o_q[...] = left[:, 640:832]
            o_gate[:, :256] = left[:, 1024:]
            o_gate[:, 256:] = right[:, :256]
            o_up[...] = right[:, 256:768]
            o_down[...] = right[:, 768:]
            small = lax.dot_general(
                pick,
                left[:, SMALL],
                (((1,), (1,)), ((), ())),
                precision=lax.Precision.HIGHEST,
                preferred_element_type=F32,
            )
            o_router[layer] = small[:16]
            o_again[layer : layer + 1] = small[16:17]
            o_fgain[layer : layer + 1] = small[17:18]


def last_results(rows, experts, others):
    wide = pl.BlockSpec((None, None, 768, 256), lambda n, i, f: (1 - n, i, 0, f))
    tall = pl.BlockSpec((None, None, 256, 768), lambda n, i, f: (1 - n, i, f, 0))
    fixed = lambda shape: pl.BlockSpec(shape, lambda n, i, f: (0,) * len(shape))
    more = [ROWS, ROWS, (2, 16, 24), (2, 24), (2, 24)] + [(2, 24, n) for n in (192, 192, 192, 192, 512, 512, 512)]
    shapes = [(2, 2, 768, 512), (2, 2, 768, 512), (2, 2, 512, 768), *more]
    return pl.pallas_call(
        last_kernel,
        grid=(2, 2, 2),
        out_shape=[jax.ShapeDtypeStruct(shape, F32) for shape in shapes],
        in_specs=[ANY] * 4 + [wide, wide, tall] + [fixed(other.shape) for other in others],
        out_specs=[wide, wide, tall] + [fixed(shape) for shape in more],
        scratch_shapes=[
            pltpu.VMEM((2, 4, 256, 768), BF),
            pltpu.VMEM((2, 4, 256, 768), BF),
            pltpu.VMEM((1024, 256), BF),
            pltpu.VMEM((1024, 512), BF),
            pltpu.SemaphoreType.DMA((2, 2)),
        ],
        compiler_params=pltpu.CompilerParams(vmem_limit_bytes=60 * 2**20),
        cost_estimate=pl.CostEstimate(flops=19_400_000_000, bytes_accessed=40_000_000, transcendentals=4_000_000),
        name="expert_grads",
    )(*rows, *experts, *others)


def rotation_table():
    half = HD // 2
    frequency = np.exp(-np.log(10000.0) * np.arange(half) / half)
    angles = np.arange(1024)[:, None] * frequency[None, :]
    cosine, sine = np.cos(angles), np.sin(angles)
    return np.concatenate([cosine, cosine, cosine, cosine, -sine, sine, -sine, sine], axis=1).astype(np.float32)


def shards(
    inputs, lengths, expert_ids, slot_ids, attn_gain, query_weight, key_weight, value_weight, out_weight, ffn_gain, router_weight,
    dense_gate, dense_up, dense_down, expert_gate, expert_up, expert_down, cotangent,
):
    ids, slots = jnp.swapaxes(expert_ids, 2, 3), jnp.swapaxes(slot_ids, 2, 3)
    stream = inputs.reshape(ROWS)
    experts = (expert_gate, expert_up, expert_down)
    common = {"ids": VM, "slots": VM, "table": ANY, "eg_all": ANY, "eu_all": ANY, "ed_all": ANY}
    given = (ids, slots, rotation_table(), *experts)
    always = {"route": ((256, 4), jnp.int32), "turn": ((128, 256), F32)}
    leaving = dict(SAVED, arrived=FORWARD["arrived"], own_out=FORWARD["own_out"], stream_out=FORWARD["stream_out"])
    ins = ("stream", "again", "q", "k", "v", "o", "fgain", "router", "g", "u", "d")
    *saved, arrived, own, after, w = launch(
        first_body,
        0,
        "gather_forward_0",
        dict(common, lengths=SMEM, **{n: VM for n in ins}),
        dict({n + "_out": (shape, ANY) for n, shape in leaving.items()}, w_out=(((2, 768, WIDE), BF), ANY)),
        dict(
            SAVED, **WEIGHTS, **FORWARD, **always, land0=((32, CHUNK, 1280), BF), land1=((32, CHUNK, 1280), BF),
            w1=WEIGHTS["w"], own0=((64, 768), F32), stage=((24, WIDE), F32),
        ),
        (
            *given, lengths, stream, attn_gain, query_weight, key_weight, value_weight, out_weight, ffn_gain,
            jnp.swapaxes(router_weight, 1, 2), dense_gate, dense_up, dense_down,
        ),
    )
    last, last_own, grads1, rows0, rows1, back1, grad_own, grad_stream = launch(
        second_body,
        1,
        "forward_backward_1",
        dict(common, lengths=SMEM, stream=VM, own=VM, cotangent=VM, arrived0=ANY, w_all=ANY),
        dict(
            outputs=((ROWS, BF), VM), outputs_own=(((64, 768), F32), VM), grads1=(GRADS, ANY), rows0=(DP_ROWS, ANY),
            rows1=(DP_ROWS, ANY), back1=(DP_ROWS, ANY), grad_own=(((64, 768), F32), VM), grad_stream=((ROWS, BF), VM),
        ),
        dict(SAVED, **WEIGHTS, **FORWARD, **BACKWARD, **always, cot_own=((64, 768), F32), grads=GRADS),
        (*given, lengths, after, own, cotangent.reshape(ROWS), arrived, w),
    )
    sums, first, first_own, back0 = launch(
        third_body,
        2,
        "backward_0_scatter",
        dict(common, incoming=VM, grad_own=VM, inputs=VM, **{n + "_in": ANY for n in SAVED}, w_all=ANY, grads1=ANY),
        dict(
            sums=(((2, 2, 24, HALF), F32), VM), input_grad=((ROWS, BF), VM), input_own=(((64, 768), F32), VM), back0=(DP_ROWS, ANY)
        ),
        dict(SAVED, **WEIGHTS, **BACKWARD, **SCATTER, **always, own0=((64, 768), F32)),
        (*given, grad_stream, grad_own, stream, *saved, w, grads1),
    )
    g_eg, g_eu, g_ed, o_out, o_in, g_router, g_again, g_fgain, g_o, g_k, g_v, g_q, g_gate, g_up, g_down = last_results(
        (rows0, rows1, back0, back1), experts, (sums, last, last_own, first, first_own)
    )
    return (
        o_out.reshape(2, 128, 768),
        o_in.reshape(2, 128, 768),
        g_again,
        g_q,
        g_k,
        g_v,
        g_o,
        g_fgain,
        jnp.swapaxes(g_router, 1, 2),
        g_gate,
        g_up,
        g_down,
        g_eg,
        g_eu,
        g_ed,
    )


def solution(mesh):
    return jax.shard_map(
        shards,
        mesh=mesh,
        in_specs=(
            P("dp", "ep", None),
            P("dp"),
            P(None, "dp", "ep", None),
            P(None, "dp", "ep", None),
            P(None, ("dp", "ep")),
            P(None, ("dp", "ep"), "tp"),
            P(None, ("dp", "ep"), "tp"),
            P(None, ("dp", "ep"), "tp"),
            P(None, ("dp", "ep"), "tp"),
            P(None, ("dp", "ep")),
            P(None, ("dp", "ep"), None),
            P(None, ("dp", "ep"), "tp"),
            P(None, ("dp", "ep"), "tp"),
            P(None, ("dp", "ep"), "tp"),
            P(None, "ep", None, "tp"),
            P(None, "ep", None, "tp"),
            P(None, "ep", "tp", None),
            P("dp", "ep", None),
        ),
        out_specs=(
            P("dp", "ep", None),
            P("dp", "ep", None),
            P(None, ("dp", "ep")),
            P(None, ("dp", "ep"), "tp"),
            P(None, ("dp", "ep"), "tp"),
            P(None, ("dp", "ep"), "tp"),
            P(None, ("dp", "ep"), "tp"),
            P(None, ("dp", "ep")),
            P(None, ("dp", "ep"), None),
            P(None, ("dp", "ep"), "tp"),
            P(None, ("dp", "ep"), "tp"),
            P(None, ("dp", "ep"), "tp"),
            P(None, "ep", None, "tp"),
            P(None, "ep", None, "tp"),
            P(None, "ep", "tp", None),
        ),
        check_vma=False,
    )
```

```python
import jax
import jax.numpy as jnp
import numpy as np
from jax import lax
from jax.experimental import pallas as pl
from jax.experimental.pallas import tpu as pltpu
from jax.sharding import PartitionSpec as P

HD = 64
EPS = 1e-06
MESH = pl.DeviceIdType.MESH
BF = jnp.bfloat16
F32 = jnp.float32
VM = pl.BlockSpec(memory_space=pltpu.VMEM)
ANY = pl.BlockSpec(memory_space=pl.ANY)
SMEM = pl.BlockSpec(memory_space=pltpu.SMEM)
WIDE = 2560
HALF = 1280
CHUNK = 48
ATTN = slice(0, 512)
FEED = slice(512, 1280)
SMALL = slice(128, 256)
SPOTS = ((0, 512, 0, 0), (512, 1024, 1, 0), (1024, 1792, 0, 512), (1792, 2560, 1, 512))
ROUTER = 64
GAIN = 80
OUT = slice(0, 192)
QKV = slice(256, 896)
GATE = slice(1024, 1536)
UP = slice(1536, 2048)
GATEUP = slice(1024, 2048)
DOWN = slice(2048, 2560)
ROWS = (2, 4, 32, 768)


class Box:
    def __init__(self, names, refs):
        self.__dict__.update(zip(names, refs, strict=True))


def place():
    y = lax.axis_index("dp")
    e = lax.axis_index("ep")
    z = lax.axis_index("tp")
    return y, e // 2, e % 2, z


def device(y, x, c, z):
    return (y, x * 2 + c, z)


def greet(others):
    for who in others:
        pl.semaphore_signal(pltpu.get_barrier_semaphore(), inc=1, device_id=who, device_id_type=MESH)


def met(others):
    pl.semaphore_wait(pltpu.get_barrier_semaphore(), len(others))


def mm(a, b):
    return lax.dot_general(a, b, (((1,), (0,)), ((), ())), preferred_element_type=F32)


def mm_t(a, b):
    return lax.dot_general(a, b, (((1,), (1,)), ((), ())), preferred_element_type=F32)


def t_mm(a, b):
    return lax.dot_general(a, b, (((0,), (0,)), ((), ())), preferred_element_type=F32)


def lanes(shape):
    return lax.broadcasted_iota(jnp.int32, shape, 1)


def gain_rows(weights):
    pick = (lanes((8, 128)) == lax.broadcasted_iota(jnp.int32, (8, 128), 0) + GAIN).astype(BF)
    return mm_t(pick, weights[:, SMALL])


def rms(values, gain):
    turn = lax.rsqrt(jnp.mean(values * values, axis=-1, keepdims=True) + EPS)
    return values * turn * gain


def rms_back(values, gain, grad):
    turn = lax.rsqrt(jnp.mean(values * values, axis=-1, keepdims=True) + EPS)
    scaled = grad * gain
    back = turn * scaled - values * (turn * turn * turn) * jnp.mean(values * scaled, axis=-1, keepdims=True)
    return back, jnp.sum(grad * values * turn, axis=0, keepdims=True)


def turned(values, cosine, sine):
    width = values.shape[1]
    front = lanes(values.shape) % HD < HD // 2
    other = jnp.where(front, pltpu.roll(values, width - HD // 2, 1), pltpu.roll(values, HD // 2, 1))
    return values * cosine + other * sine


def sigmoid(v):
    return 1.0 / (1.0 + jnp.exp(-v))


def swish_back(gate, up, grad):
    s = sigmoid(gate)
    return (grad * up * s * (1.0 + gate * (1.0 - s))).astype(BF), (grad * gate * s).astype(BF)


def turns(t, sign):
    cosine, sine = t.turn[:, :128], sign * t.turn[:, 128:]
    first = lanes((128, 128)) < HD
    one, none = jnp.ones((128, 128), F32), jnp.zeros((128, 128), F32)
    mixed, mixed_sine = jnp.where(first, cosine, 1.0), jnp.where(first, sine, 0.0)
    cosine = jnp.concatenate([cosine, mixed, one, cosine, mixed], axis=1)
    sine = jnp.concatenate([sine, mixed_sine, none, sine, mixed_sine], axis=1)
    return cosine, sine


def set_route(t, layer):
    row = lax.broadcasted_iota(jnp.int32, (16, 128), 0)
    unit = (row == lanes((16, 128))).astype(BF)
    for s in range(2):
        stacked = jnp.zeros((16, 128), jnp.int32)
        for n, ref in enumerate((t.ids, t.slots)):
            for j in range(2):
                stacked = jnp.where(row == 2 * n + j, ref[layer, s, j : j + 1], stacked)
        columns = t_mm(stacked.astype(F32).astype(BF), unit).astype(jnp.int32)
        rows = slice(s * 128, s * 128 + 128)
        for j in range(2):
            expert, slot = columns[:, j : j + 1], columns[:, 2 + j : 3 + j]
            t.route[rows, j : j + 1] = jnp.where(slot < 32, expert * 32 + slot, 512)
            t.route[rows, 2 + j : 3 + j] = expert


class Wires:
    def __init__(self, sends, recvs):
        self.sends, self.recvs, self.used, self.open = sends, recvs, 0, []

    def plan(self, src, dst, who, when=None, at=None):
        if at is None:
            at = self.used
            self.used += 1
        copy = pltpu.make_async_remote_copy(
            src_ref=src,
            dst_ref=dst,
            send_sem=self.sends.at[at],
            recv_sem=self.recvs.at[at],
            device_id=who,
            device_id_type=MESH,
        )
        self.open.append((copy, when))
        return copy

    def go(self, src, dst, who):
        copy = self.plan(src, dst, who)
        copy.start()
        return copy

    def finish(self):
        assert self.used <= self.sends.shape[0]
        for copy, when in self.open:
            if when is None:
                copy.wait_send()
            else:
                pl.when(when)(copy.wait_send)


class Moves:
    def __init__(self, sems):
        self.sems, self.used, self.open = sems, 0, []

    def go(self, src, dst):
        copy = pltpu.make_async_copy(src, dst, self.sems.at[self.used])
        self.used += 1
        copy.start()
        self.open.append(copy)
        return copy

    def need(self, copy):
        self.open = [other for other in self.open if other is not copy]
        copy.wait()

    def finish(self):
        assert self.used <= self.sems.shape[0]
        for copy in self.open:
            copy.wait()


def peers(y, e, z):
    row = [(y, (e + k) % 8, z) for k in range(1, 8)]
    return row + [(y, e, (z + k) % 4) for k in range(1, 4)] + [((y + k) % 4, e, z) for k in range(1, 4)]


class TpSum:
    def __init__(self, wires, parts, land, held):
        self.wires, self.parts, self.land, self.held = wires, parts, land, held
        self.y, self.e, self.z = (lax.axis_index(name) for name in ("dp", "ep", "tp"))
        self.sums, self.spread = [None, None], [None, None]

    def send(self, h):
        self.sums[h] = []
        for k in (1, 3, 2):
            who = (self.z + k) % 4
            copy = self.wires.go(self.parts.at[h, who], self.land.at[h, k - 1], (self.y, self.e, who))
            self.sums[h].append(copy)

    def half(self, h, finish):
        for copy in self.sums[h]:
            copy.wait_recv()
        total = self.parts[h, self.z].astype(F32)
        for k in range(3):
            total += self.land[h, k].astype(F32)
        finish(h, slice(32 * h, 32 * h + 32), total)
        self.spread[h] = self.everywhere(self.held.at[h, self.z])

    def everywhere(self, spot):
        return [self.wires.go(spot, spot, (self.y, self.e, (self.z + k) % 4)) for k in (1, 3, 2)]

    def wait(self, h):
        for copy in self.spread[h]:
            copy.wait_recv()


def scatter_experts(wires, src, dst, y, e, z, i):
    rows = pl.ds(pl.multiple_of(e * 32, 32), 32)
    sent = []
    for k in (1, 7, 2, 6, 3, 5, 4):
        who = (e + k) % 8
        sent.append(wires.go(src.at[2 * who + i], dst.at[i, rows], (y, who, z)))
    dst[i, rows] = src[2 * e + i]
    return lambda: [copy.wait_recv() for copy in sent]


def return_experts(wires, src, dst, y, e, z, i):
    sent = []
    for k in (1, 7, 2, 6, 3, 5, 4):
        who = (e + k) % 8
        rows = pl.ds(pl.multiple_of(who * 32, 32), 32)
        sent.append(wires.go(src.at[i, rows], dst.at[2 * e + i], (y, who, z)))
    dst[2 * e + i] = src[i, pl.ds(pl.multiple_of(e * 32, 32), 32)]
    return lambda: [copy.wait_recv() for copy in sent]


class RowWalk:
    def __init__(self, wires, moves, own, rows, y, e, z):
        self.wires, self.moves, self.own, self.rows = wires, moves, own, rows
        self.up, self.down = ((y + 1) % 4, e, z), ((y + 3) % 4, e, z)
        self.near, self.far = [], []

    def start(self, i):
        own, rows = self.own.at[i], self.rows
        self.near.append(
            (self.wires.go(own, rows.at[i, 1], self.up), self.wires.go(own, rows.at[i, 3], self.down))
        )
        self.moves.go(own, rows.at[i, 0])

    def pass_on(self, i):
        self.near[i][i].wait_recv()
        slot, who = ((1, self.up), (3, self.down))[i]
        self.far.append(self.wires.go(self.rows.at[i, slot], self.rows.at[i, 2], who))

    def finish(self):
        self.near[0][1].wait_recv()
        self.near[1][0].wait_recv()
        for copy in self.far:
            copy.wait_recv()


class Gather:
    def __init__(self, wires, land, columns):
        self.wires, self.land, self.columns = wires, land, columns
        self.y, self.x, self.c, self.z = place()
        self.second, self.far = {}, []

    def who(self, j, d):
        yy = (self.y + j * self.c + d * (1 - self.c) + 8) % 4
        xx = (self.x + j * (1 - self.c) + d * self.c + 8) % 4
        return device(yy, xx, self.c, self.z)

    def spot(self, j, d, rows=slice(None)):
        yy, ee, zz = self.who(j, d)
        return self.land.at[self.c * 16 + yy * 4 + ee // 2, rows, self.columns]

    def reach(self, spot, whos):
        return [self.wires.go(spot, spot, who) for who in whos]

    def spread(self, j):
        self.second[j] = self.reach(self.spot(j, 0), [self.who(0, 1), self.who(0, -1)])

    def step0(self):
        self.first = self.reach(self.spot(0, 0), [self.who(1, 0), self.who(-1, 0)])
        self.spread(0)

    def step1(self):
        self.first[0].wait_recv()
        spot = self.spot(-1, 0, pl.ds(0, 32))
        self.on = [self.wires.go(spot, spot, self.who(1, 0))]
        self.spread(-1)
        self.first[1].wait_recv()
        spot = self.spot(1, 0, pl.ds(32, 16))
        self.on.append(self.wires.go(spot, spot, self.who(-1, 0)))
        self.spread(1)

    def step2(self):
        for copy in self.on:
            copy.wait_recv()
        self.spread(2)

    def step3(self):
        for j in (0, -1, 1, 2):
            for n, d in enumerate((-1, 1)):
                self.second[j][n].wait_recv()
                if (j in (0, -1)) == (n == 0):
                    spot = self.spot(j, d)
                    self.far.append(self.wires.go(spot, spot, self.who(0, -d)))

    def step4(self):
        for copy in self.far:
            copy.wait_recv()
        self.pair()

    def pair(self):
        spot = self.land.at[pl.ds(pl.multiple_of(self.c * 16, 16), 16), :, self.columns]
        self.swap = self.wires.go(spot, spot, device(self.y, self.x, 1 - self.c, self.z))

    def step5(self):
        self.swap.wait_recv()


class ShortGather(Gather):
    def spread(self, j):
        self.second[j] = self.reach(self.spot(j, 0), [self.who(0, d) for d in (1, -1, 2)])

    def step0(self):
        self.first = self.reach(self.spot(0, 0), [self.who(j, 0) for j in (1, -1, 2)])
        self.spread(0)

    def step1(self):
        for n, j in ((0, -1), (1, 1), (2, 2)):
            self.first[n].wait_recv()
            self.spread(j)

    def step2(self):
        for j in (0, -1, 1, 2):
            for copy in self.second[j]:
                copy.wait_recv()
        self.pair()


def unpack(land, columns, w, left):
    half = columns.stop - columns.start

    def some(p, carry):
        one = land[p, :, columns].astype(F32)
        two = land[16 + p, :, columns].astype(F32)
        rows = pl.ds(pl.multiple_of(p * CHUNK, CHUNK), CHUNK)
        w[rows, left : left + half] = jnp.concatenate([one[:24], two[:24]], axis=0).astype(BF)
        w[rows, left + half : left + 2 * half] = jnp.concatenate([one[24:], two[24:]], axis=0).astype(BF)
        return carry

    lax.fori_loop(0, 16, some, 0)


def picks(route):
    slots = lanes((256, 512))
    return slots == route[:, 0:1], slots == route[:, 1:2]


class Scatter:
    PLUS, MINUS = (0, -1), (1, 2)

    def __init__(self, wires, columns, *refs):
        self.wires, self.columns = wires, columns
        self.acc, self.pool, self.total, self.other, self.out = refs
        self.y, self.x, self.c, self.z = place()
        self.sibling = device(self.y, self.x, 1 - self.c, self.z)
        self.far, self.near = {}, {}

    def at(self, j, d, core):
        yy = (self.y + j * core + d * (1 - core) + 8) % 4
        xx = (self.x + j * (1 - core) + d * core + 8) % 4
        return yy, xx

    def who(self, j, d):
        yy, xx = self.at(j, d, self.c)
        return device(yy, xx, self.c, self.z)

    def mine(self, j, d, core):
        yy, xx = self.at(j, d, core)
        return yy * 4 + xx

    def chunk(self, core, block):
        return self.acc.at[core, block, :, self.columns]

    def slot(self, n):
        return self.pool.at[n, :, self.columns]

    def add(self, ref, *others):
        total = ref[...].astype(F32)
        for other in others:
            total += other[...].astype(F32)
        ref[...] = total.astype(BF)

    def join(self, j, d):
        block = self.mine(j, d, self.c)
        ref = self.chunk(self.c, block)
        self.add(ref, self.slot(block))
        return ref

    def step0(self):
        half = self.acc.at[1 - self.c, :, :, self.columns]
        self.swap = self.wires.go(half, self.pool.at[pl.ds(0, 16), :, self.columns], self.sibling)

    def step1(self):
        self.swap.wait_recv()
        for j in (0, 1, -1, 2):
            ref = self.join(j, 2)
            n, d = (16 + self.PLUS.index(j), 1) if j in self.PLUS else (18 + self.MINUS.index(j), -1)
            self.far[j] = self.wires.go(ref, self.slot(n), self.who(0, d))
        for j, k in zip(self.MINUS, self.PLUS):
            self.near[j, 1] = self.wires.go(self.join(j, 1), self.slot(20 + j), self.who(0, 1))
            self.near[k, -1] = self.wires.go(self.join(k, -1), self.slot(24 + k % 4), self.who(0, -1))
        self.up = {j: self.join(j, 1) for j in self.PLUS}
        self.down = {j: self.join(j, -1) for j in self.MINUS}

    def step2(self):
        for n, (j, k) in enumerate(zip(self.PLUS, self.MINUS)):
            self.far[j].wait_recv()
            self.add(self.up[j], self.slot(16 + n))
            self.near[j, 1] = self.wires.go(self.up[j], self.slot(20 + j % 4), self.who(0, 1))
            self.far[k].wait_recv()
            self.add(self.down[k], self.slot(18 + n))
            self.near[k, -1] = self.wires.go(self.down[k], self.slot(24 + k), self.who(0, -1))
        self.held = {j: self.join(j, 0) for j in (2, 1, -1, 0)}

    def step3(self):
        for j in (2, 1, -1, 0):
            self.near[j, 1].wait_recv()
            self.near[j, -1].wait_recv()
            ref = self.held[j]
            self.add(ref, self.slot(20 + j % 4), self.slot(24 + j % 4))
            if j == 2:
                spot = self.slot(28)
                self.one = [
                    self.wires.go(ref.at[rows], spot.at[rows], self.who(d, 0))
                    for rows, d in ((pl.ds(0, 32), 1), (pl.ds(32, 16), -1))
                ]

    def step4(self):
        self.last = []
        for n, (rows, d) in enumerate(((pl.ds(0, 32), 1), (pl.ds(32, 16), -1))):
            self.one[n].wait_recv()
            self.add(self.held[d].at[rows], self.slot(28).at[rows])
            self.last.append(self.wires.go(self.held[d], self.slot(29 + n), self.who(d, 0)))

    def step5(self):
        for copy in self.last:
            copy.wait_recv()
        columns = self.columns
        near = self.pool[29, :, columns].astype(F32) + self.pool[30, :, columns].astype(F32)
        self.total[:, columns] = self.held[0][...].astype(F32) + near
        away = pl.ds(pl.multiple_of(24 - 24 * self.c, 8), 24)
        self.trade = self.wires.go(self.total.at[away, columns], self.other.at[:, columns], self.sibling)
        self.out[self.c, :, columns] = self.total[pl.ds(pl.multiple_of(24 * self.c, 8), 24), columns]

    def step6(self):
        self.trade.wait_recv()
        self.out[1 - self.c, :, self.columns] = self.other[:, self.columns]


def forward_block(wires, moves, t, w, need, stream, own, lengths, pump, done, dp_rows=None):
    y, x, c, z = place()
    e = 2 * x + c
    gains = gain_rows(w)
    values = stream[...].reshape(256, 768).astype(F32)
    t.normed[...] = rms(values, gains[0:1]).astype(BF)
    done("normed")
    sibling = (y, e + 1 - 2 * c, z)
    cosine, sine = turns(t, 1.0)
    spans = (slice(0, 128), slice(128, 256))
    first, to_core = [], []
    for s, rows in enumerate(spans):
        lin = turned(mm(t.normed[rows], w[:, QKV]), cosine, sine).astype(BF)
        t.kv[e, rows] = lin[:, :384]
        t.queries[rows] = lin[:, 384:576]
        here = t.kv.at[e, pl.ds(s * 128, 128)]
        first.append([])
        for k in (1, 3, 2):
            ahead = x + k <= 3
            copy = wires.plan(here, here, (y, (e + 2 * k) % 8, z), ahead)
            pl.when(ahead)(copy.start)
            first[s].append((k, copy))
        to_core.append(wires.plan(here, here, sibling, c == 0))
        pl.when(c == 0)(to_core[s].start)
    done("queries")
    for j in range(8):

        @pl.when(j > e)
        def _():
            t.kv[j] = jnp.zeros((256, 384), BF)

    pump()
    tp = TpSum(wires, t.part.at[0], t.land.at[0], t.ffn_in)
    at_key = lanes((128, 1024))
    at_query = lax.broadcasted_iota(jnp.int32, (128, 1024), 0) + e * 128
    for s, rows in enumerate(spans):
        second = []
        for k, copy in first[s]:
            behind = x - k >= 0
            there = t.kv.at[(e + 8 - 2 * k) % 8, pl.ds(s * 128, 128)]
            on = wires.plan(there, there, sibling, behind)

            @pl.when(behind)
            def _():
                copy.wait_recv()
                on.start()

            second.append((behind, on))
        pl.when(c == 1)(to_core[s].wait_recv)
        for behind, on in second:
            pl.when(behind)(on.wait_recv)
        allowed = (at_key <= at_query) & (at_key < lengths[s])
        for h in range(3):
            keys = t.kv[:, rows, 64 * h : 64 * h + 64].reshape(1024, 64)
            vals = t.kv[:, rows, 192 + 64 * h : 256 + 64 * h].reshape(1024, 64)
            scores = jnp.where(allowed, mm_t(t.queries[rows, 64 * h : 64 * h + 64], keys) * HD**-0.5, -1e30)
            expd = jnp.exp(scores - jnp.max(scores, axis=-1, keepdims=True))
            low = (expd / jnp.sum(expd, axis=-1, keepdims=True)).astype(BF)
            t.probs[3 * s + h] = low
            t.attended[rows, 64 * h : 64 * h + 64] = mm(low, vals).astype(BF)
        t.part[0, s] = mm_t(t.attended[rows], w[:, OUT]).astype(BF).reshape(4, 32, 768)
        tp.send(s)
    done("kv", "probs", "attended")
    pump()

    def finish(h, rows, total):
        t.middle[rows] = own[rows] + total
        t.ffn_in[h, z] = rms(t.middle[rows], gains[1:2]).astype(BF)

    tp.half(0, finish)
    tp.half(1, finish)
    done("middle")
    pump()
    tp.wait(0)
    tp.wait(1)
    done("ffn_in")
    rows_in = t.ffn_in[...].reshape(256, 768)
    ids = t.route[...]
    pick0, pick1 = picks(ids)
    t.sent[...] = t_mm((pick0 | pick1).astype(BF), rows_in).astype(BF).reshape(16, 32, 768)
    coming = [scatter_experts(wires, t.sent, t.arrived, y, e, z, i) for i in range(2)]
    pump()
    logits = mm(rows_in, w[:, SMALL])
    lane = lanes((256, 128))
    chosen = [
        jnp.sum(jnp.where(lane == ids[:, 2 + j : 3 + j] + ROUTER, logits, 0.0), axis=-1, keepdims=True)
        for j in range(2)
    ]
    top = jnp.maximum(chosen[0], chosen[1])
    expd = [jnp.exp(v - top) for v in chosen]
    share = [v / (expd[0] + expd[1]) for v in expd]
    t.shares[...] = jnp.where(lane == 0, share[0], jnp.where(lane == 1, share[1], 0.0))
    t.gud[...] = mm(rows_in, w[:, GATEUP])
    gate, up = t.gud[:, :512], t.gud[:, 512:]
    hidden = (gate * sigmoid(gate) * up).astype(BF)
    dense = mm_t(hidden, w[:, DOWN])
    done("gud", "shares")
    pump()
    need("eg", "eu", "ed")
    walk = None if dp_rows is None else RowWalk(wires, moves, t.arrived, dp_rows, y, e, z)
    back = []
    for i in range(2):
        coming[i]()
        if walk is not None:
            walk.start(i)
        t.gue[i, :, :512] = mm(t.arrived[i], t.eg[i])
        t.gue[i, :, 512:] = mm(t.arrived[i], t.eu[i])
        gate, up = t.gue[i, :, :512], t.gue[i, :, 512:]
        hidden = (gate * sigmoid(gate) * up).astype(BF)
        t.made[i] = mm(hidden, t.ed[i]).astype(BF)
        back.append(return_experts(wires, t.made, t.ret, y, e, z, i))
    done("arrived", "gue")
    pump()
    for wait in back:
        wait()
    done("ret")
    mix = (jnp.where(pick0, share[0], 0.0) + jnp.where(pick1, share[1], 0.0)).astype(BF)
    tp = TpSum(wires, t.part.at[1], t.land.at[1], t.stream_out)
    for h, rows in enumerate(spans):
        moe = mm(mix[rows], t.ret[...].reshape(512, 768))
        t.part[1, h] = (dense[rows] + moe).astype(BF).reshape(4, 32, 768)
        tp.send(h)
    pump()

    def finish(h, rows, total):
        result = t.middle[rows] + total
        t.own_out[rows] = result
        t.stream_out[h, z] = result.astype(BF)

    def halves():
        tp.half(0, finish)
        tp.half(1, finish)
        done("own_out")
        pump()

    def wait():
        tp.wait(0)
        tp.wait(1)
        done("stream_out")

    return walk, halves, wait


def backward_start(wires, t, w, need, incoming):
    y, x, c, z = place()
    e = 2 * x + c
    need("shares")
    ffn_grad = incoming[...].reshape(256, 768)
    pick0, pick1 = picks(t.route[...])
    mix = (jnp.where(pick0, t.shares[:, 0:1], 0.0) + jnp.where(pick1, t.shares[:, 1:2], 0.0)).astype(BF)
    t.bsent[...] = t_mm(mix, ffn_grad).astype(BF).reshape(16, 32, 768)
    coming = [scatter_experts(wires, t.bsent, t.back, y, e, z, i) for i in range(2)]
    need("w", "gud", "ffn_in")
    gate, up = t.gud[:, :512], t.gud[:, 512:]
    hidden_dense = (gate * sigmoid(gate) * up).astype(BF)
    gate_grad, up_grad = swish_back(gate, up, mm(ffn_grad, w[:, DOWN]))
    gu_grad = jnp.concatenate([gate_grad, up_grad], axis=1)
    t.dense[...] = mm_t(gu_grad, w[:, GATEUP])
    t.gu_grad[...] = gu_grad
    t.hidden_dense[...] = hidden_dense
    return coming


def backward_block(wires, moves, t, w, need, incoming, grad_own, own, coming, pump, dp_rows, grads):
    y, x, c, z = place()
    e = 2 * x + c

    def keep(columns, values):
        for start, stop, half, lane in SPOTS:
            left, right = max(columns.start, start), min(columns.stop, stop)
            if left < right:
                some = values[:, left - columns.start : right - columns.start].astype(BF)
                lane += left - start
                grads[half, :, :, lane : lane + right - left] = some.reshape(16, CHUNK, right - left)

    need("ret")
    ffn_grad = incoming[...].reshape(256, 768)
    rows_in = t.ffn_in[...].reshape(256, 768)
    gains = gain_rows(w)
    pick0, pick1 = picks(t.route[...])
    match = mm_t(ffn_grad, t.ret[...].reshape(512, 768))
    share_grad = [
        jnp.sum(jnp.where(pick, match, 0.0), axis=-1, keepdims=True) for pick in (pick0, pick1)
    ]
    lane = lanes((256, 128))
    extra = jnp.where(lane == 0, share_grad[0], jnp.where(lane == 1, share_grad[1], 0.0))
    t.part_ffn[:, :, :, 768:] = extra.astype(BF).reshape(2, 4, 32, 128)
    pump()
    need("ed", "gue", "eg", "eu")
    walk = RowWalk(wires, moves, t.back, dp_rows, y, e, z)
    back = []
    for i in range(2):
        coming[i]()
        walk.start(i)
        hidden_grad = mm_t(t.back[i], t.ed[i])
        gate_e, up_e = swish_back(t.gue[i, :, :512], t.gue[i, :, 512:], hidden_grad)
        t.bmade[i] = (mm_t(gate_e, t.eg[i]) + mm_t(up_e, t.eu[i])).astype(BF)
        back.append(return_experts(wires, t.bmade, t.sret, y, e, z, i))
    pump()
    keep(GATEUP, t_mm(rows_in, t.gu_grad[...]))
    keep(DOWN, t_mm(ffn_grad, t.hidden_dense[...]))
    for wait in back:
        wait()
    tp = TpSum(wires, t.part_ffn, t.land_ffn, t.gathered)
    spans = (slice(0, 128), slice(128, 256))
    placed = (pick0 | pick1).astype(BF)
    for h, rows in enumerate(spans):
        total = t.dense[rows] + mm(placed[rows], t.sret[...].reshape(512, 768))
        t.part_ffn[h, :, :, :768] = total.astype(BF).reshape(4, 32, 768)
        tp.send(h)
    pump()
    need("middle")
    top = lax.broadcasted_iota(jnp.int32, (16, 768), 0) == 0
    lane32 = lanes((32, 128))
    gain_parts = []

    def finish(h, rows, total):
        mine = pl.ds(pl.multiple_of(128 * h + 32 * z, 32), 32)
        share, ids = t.shares[mine], t.route[mine]
        weigh = share[:, 0:1] * total[:, 768:769] + share[:, 1:2] * total[:, 769:770]
        logit_grad = jnp.zeros((32, 128), F32)
        for j in range(2):
            chosen_grad = share[:, j : j + 1] * (total[:, 768 + j : 769 + j] - weigh)
            logit_grad += jnp.where(lane32 == ids[:, 2 + j : 3 + j] + ROUTER, chosen_grad, 0.0)
        logit_grad = logit_grad.astype(BF)
        grad_in = total[:, :768] + mm_t(logit_grad, w[:, SMALL])
        back_norm, gain_two = rms_back(t.middle[rows], gains[1:2], grad_in)
        gain_parts.append(gain_two)
        middle_grad = grad_own[rows] + back_norm
        t.down_own[rows] = middle_grad
        t.gathered[h, z, :, :768] = middle_grad.astype(BF)
        t.gathered[h, z, :, 768:] = logit_grad

    tp.half(0, finish)
    tp.half(1, finish)
    t.gains[1, z] = jnp.where(top, gain_parts[0] + gain_parts[1], 0.0).astype(BF)
    gain_copies = tp.everywhere(t.gains.at[1, z])
    grads_tp = tp
    pump()
    need("probs", "kv", "queries", "attended", "normed")
    sibling = (y, e + 1 - 2 * c, z)

    def attend_back(s, between):
        rows = spans[s]
        grad = t.gathered[s, :, :, :768].reshape(128, 768)
        attended_grad = mm(grad, w[:, OUT]).astype(BF)
        for h in range(3):
            cols = slice(64 * h, 64 * h + 64)
            late = slice(192 + 64 * h, 256 + 64 * h)
            keys = t.kv[:, rows, cols].reshape(1024, 64)
            vals = t.kv[:, rows, late].reshape(1024, 64)
            low = t.probs[3 * s + h]
            wide = low.astype(F32)
            grad_here = attended_grad[:, cols]
            probs_grad = mm_t(grad_here, vals)
            kept = jnp.sum(wide * probs_grad, axis=-1, keepdims=True)
            score_grad = (wide * (probs_grad - kept)).astype(BF)
            t.lin[rows, 384 + 64 * h : 448 + 64 * h] = mm(score_grad, keys) * HD**-0.5
            keys_grad = t_mm(score_grad, t.queries[rows, cols]) * HD**-0.5
            t.dkv[:, rows, cols] = keys_grad.astype(BF).reshape(8, 128, 64)
            t.dkv[:, rows, late] = t_mm(low, grad_here).astype(BF).reshape(8, 128, 64)
            if h == 0:
                between()

    def swap(s):
        rows = pl.ds(s * 128, 128)
        swaps = []
        for k in range(4):
            gives = (x - k >= 0) & ((c == 1) if k == 0 else True)
            takes = (x - k >= 0) & ((c == 0) if k == 0 else True)
            block = (2 * (x - k) + 1 - c + 8) % 8
            copy = wires.plan(t.dkv.at[block, rows], t.sib_land.at[k, rows], sibling, gives)
            pl.when(gives)(copy.start)
            swaps.append((takes, copy))
        return swaps

    def send_far(s, swaps):
        rows = pl.ds(s * 128, 128)
        far = []
        for k in (1, 3, 2):
            gives, takes = x - k >= 0, x + k <= 3
            block = (e - 2 * k + 8) % 8
            send = wires.plan(t.dkv.at[block, rows], t.owner_land.at[k - 1, rows], (y, block, z), gives)

            @pl.when(gives)
            def _():
                swaps[k][1].wait_recv()
                both = t.dkv[block, rows].astype(F32) + t.sib_land[k, rows].astype(F32)
                t.dkv[block, rows] = both.astype(BF)
                send.start()

            far.append((k, takes, send))
        return far

    cosine, sine = turns(t, -1.0)
    tp = TpSum(wires, t.bpart, t.bland, t.tail)

    def collect(s, swaps, far):
        rows = spans[s]
        t.lin[rows, :384] = t.dkv[e, rows].astype(F32)
        t.lin[rows, 576:] = jnp.zeros((128, 64), F32)

        @pl.when(swaps[0][0])
        def _():
            swaps[0][1].wait_recv()
            t.lin[rows, :384] += t.sib_land[0, rows].astype(F32)

        for k, takes, copy in far:

            @pl.when(takes)
            def _():
                copy.wait_recv()
                t.lin[rows, :384] += t.owner_land[k - 1, rows].astype(F32)

        t.lin_low[rows] = turned(t.lin[rows], cosine, sine).astype(BF)
        t.bpart[s] = mm_t(t.lin_low[rows], w[:, QKV]).astype(BF).reshape(4, 32, 768)
        tp.send(s)

    grads_tp.wait(0)
    attend_back(0, lambda: None)
    swaps0 = swap(0)
    walk.pass_on(0)
    walk.pass_on(1)
    grads_tp.wait(1)
    far0 = []
    attend_back(1, lambda: far0.extend(send_far(0, swaps0)))
    swaps1 = swap(1)
    keep(OUT, t_mm(t.gathered[:, :, :, :768].reshape(256, 768), t.attended[...]))
    far1 = send_far(1, swaps1)
    router_grad = t_mm(rows_in, t.gathered[:, :, :, 768:].reshape(256, 128))
    pump()
    collect(0, swaps0, far0)
    collect(1, swaps1, far1)
    tail_parts = []

    def finish(h, rows, total):
        back_norm, gain_one = rms_back(own[rows], gains[0:1], total)
        tail_parts.append(gain_one)
        result = t.down_own[rows] + back_norm
        t.down_own[rows] = result
        t.tail[h, z] = result.astype(BF)

    keep(QKV, t_mm(t.normed[...], t.lin_low[...]))
    pump()
    tp.half(0, finish)
    tp.half(1, finish)
    t.gains[0, z] = jnp.where(top, tail_parts[0] + tail_parts[1], 0.0).astype(BF)
    gain_copies += tp.everywhere(t.gains.at[0, z])
    pump()
    tp.wait(0)
    tp.wait(1)
    t.down_stream[...] = t.tail[...]
    for copy in gain_copies:
        copy.wait_recv()
    at_row = lax.broadcasted_iota(jnp.int32, (16, 768), 0)
    gain_grads = jnp.zeros((16, 768), F32)
    for n in range(2):
        total = jnp.sum(t.gains[n].astype(F32).reshape(64, 768), axis=0, keepdims=True)
        gain_grads = jnp.where(at_row == n, total, gain_grads)
    spot = (lanes((16, 128)) == lax.broadcasted_iota(jnp.int32, (16, 128), 0) + GAIN).astype(BF)
    keep(slice(192, 256), (router_grad + t_mm(gain_grads.astype(BF), spot))[:, 64:])
    return walk


MOVE_SEMS, WIRE_SEMS = 48, 192
SAVED = {
    "normed": ((256, 768), BF),
    "queries": ((256, 192), BF),
    "kv": ((8, 256, 384), BF),
    "probs": ((6, 128, 1024), BF),
    "attended": ((256, 192), BF),
    "middle": ((64, 768), F32),
    "ffn_in": (ROWS, BF),
    "gud": ((256, 1024), F32),
    "gue": ((2, 256, 1024), F32),
    "ret": ((16, 32, 768), BF),
    "shares": ((256, 128), F32),
}
WEIGHTS = {"w": ((768, WIDE), BF), "eg": ((2, 768, 512), BF), "eu": ((2, 768, 512), BF), "ed": ((2, 512, 768), BF)}
FORWARD = {
    "arrived": ((2, 256, 768), BF),
    "own_out": ((64, 768), F32),
    "stream_out": (ROWS, BF),
    "part": ((2, *ROWS), BF),
    "land": ((2, 2, 3, 32, 768), BF),
    "sent": ((16, 32, 768), BF),
    "made": ((2, 256, 768), BF),
}
BACKWARD = {
    "back": ((2, 256, 768), BF),
    "bsent": ((16, 32, 768), BF),
    "bmade": ((2, 256, 768), BF),
    "sret": ((16, 32, 768), BF),
    "part_ffn": ((2, 4, 32, 896), BF),
    "land_ffn": ((2, 3, 32, 896), BF),
    "bpart": (ROWS, BF),
    "bland": ((2, 3, 32, 768), BF),
    "gathered": ((2, 4, 32, 896), BF),
    "tail": (ROWS, BF),
    "gains": ((2, 4, 16, 768), BF),
    "dkv": ((8, 256, 384), BF),
    "sib_land": ((4, 256, 384), BF),
    "owner_land": ((3, 256, 384), BF),
    "dense": ((256, 768), F32),
    "gu_grad": ((256, 1024), BF),
    "hidden_dense": ((256, 512), BF),
    "lin": ((256, 640), F32),
    "lin_low": ((256, 640), BF),
    "down_own": ((64, 768), F32),
    "down_stream": (ROWS, BF),
}
SCATTER = {
    "acc": ((2, 2, 16, CHUNK, HALF), BF),
    "pool": ((2, 31, CHUNK, HALF), BF),
    "total": ((2, CHUNK, HALF), F32),
    "other": ((2, 24, HALF), F32),
}
DP_ROWS = ((2, 4, 256, 768), BF)
GRADS = ((2, 16, CHUNK, HALF), BF)


def launch(body, number, name, ins, outs, scratch, args):
    def kernel(*refs):
        names = list(ins) + list(outs) + list(scratch)
        t = Box(names, refs[: len(names)])
        moves, sends, recvs = refs[len(names) :]
        body(t, Moves(moves), Wires(sends, recvs))

    return pl.pallas_call(
        kernel,
        out_shape=[jax.ShapeDtypeStruct(*shape) for shape, space in outs.values()],
        in_specs=list(ins.values()),
        out_specs=[space for shape, space in outs.values()],
        scratch_shapes=[pltpu.VMEM(*shape) for shape in scratch.values()]
        + [
            pltpu.SemaphoreType.DMA((MOVE_SEMS,)),
            pltpu.SemaphoreType.DMA((WIRE_SEMS,)),
            pltpu.SemaphoreType.DMA((WIRE_SEMS,)),
        ],
        compiler_params=pltpu.CompilerParams(
            collective_id=number, has_side_effects=True, vmem_limit_bytes=60 * 2**20
        ),
        name=name,
    )(*args)


def fetcher(moves, pairs):
    coming = {name: moves.go(src, dst) for name, src, dst in pairs}

    def need(*names):
        for name in names:
            if name in coming:
                moves.need(coming.pop(name))

    return need


def pumper(steps):
    steps = iter(steps)

    def pump():
        for step in next(steps, ()):
            step()

    return pump


def prepare(t, moves, wires, layer):
    y, x, c, z = place()
    others = peers(y, 2 * x + c, z)
    greet(others)
    turn = moves.go(t.table.at[pl.ds(pl.multiple_of((2 * x + c) * 128, 128), 128)], t.turn)
    set_route(t, layer)
    return y, 2 * x + c, z, others, turn


def pack(t, land, layer, me, columns):
    names = (("o", 0), ("k", 256), ("v", 448), ("q", 640)) if columns is ATTN else (("g", 1024), ("u", 1536), ("d", 2048))
    if columns is ATTN:
        row = lax.broadcasted_iota(jnp.int32, (32, 24), 0)
        one, other = t.again[layer : layer + 1].astype(F32), t.fgain[layer : layer + 1].astype(F32)
        gains = jnp.where(row == 16, one, jnp.where(row == 17, other, 0.0))
        router = jnp.concatenate([t.router[layer].astype(F32), jnp.zeros((16, 24), F32)], axis=0)
        spot = (lanes((32, 128)) == lax.broadcasted_iota(jnp.int32, (32, 128), 0) + ROUTER).astype(BF)
        t.stage[:, 192:256] = t_mm((gains + router).astype(BF), spot)[:, 64:]
        t.stage[:, 832:1024] = jnp.zeros((24, 192), F32)
    for name, left in names:
        ref = getattr(t, name)
        t.stage[:, left : left + ref.shape[2]] = ref[layer].astype(F32)
    left, middle, right = (0, 512, 1024) if columns is ATTN else (1024, 1792, 2560)
    halves = [t.stage[:, left:middle], t.stage[:, middle:right]]
    land[me, :, columns] = jnp.concatenate(halves, axis=0).astype(BF)


def first_body(t, moves, wires):
    y, e, z, others, turn = prepare(t, moves, wires, 0)
    need = fetcher(moves, [(n, getattr(t, n + "_all").at[0], getattr(t, n)) for n in ("eg", "eu", "ed")])
    me = e % 2 * 16 + y * 4 + e // 2
    pack(t, t.land0, 0, me, ATTN)
    met(others)
    attn, feed = ShortGather(wires, t.land0, ATTN), Gather(wires, t.land0, FEED)
    late = Gather(wires, t.land1, slice(0, 1280))
    attn.step0()
    pack(t, t.land0, 0, me, FEED)
    attn.step1()
    t.own0[...] = t.stream[:, z].astype(F32).reshape(64, 768)
    attn.step2()
    feed.step0()
    attn.step5()
    unpack(t.land0, ATTN, t.w, 0)
    moves.need(turn)

    def feed_ready():
        unpack(t.land0, FEED, t.w, 1024)
        moves.go(t.w, t.w_out.at[0])

    def late_ready():
        unpack(t.land1, ATTN, t.w1, 0)
        unpack(t.land1, FEED, t.w1, 1024)
        moves.go(t.w1, t.w_out.at[1])

    def late_start():
        pack(t, t.land1, 1, me, ATTN)
        pack(t, t.land1, 1, me, FEED)
        late.step0()

    pump = pumper(
        [
            (feed.step1,),
            (feed.step2, late_start),
            (feed.step3, late.step1),
            (feed.step4, feed.step5, feed_ready, late.step2),
            (late.step3,),
            (late.step4,),
            (late.step5,),
            (late_ready,),
        ]
    )

    def done(*names):
        for name in names:
            moves.go(getattr(t, name), getattr(t, name + "_out"))

    walk, halves, wait = forward_block(wires, moves, t, t.w, need, t.stream, t.own0, t.lengths, pump, done)
    halves()
    wait()
    wires.finish()
    moves.finish()


def second_body(t, moves, wires):
    y, e, z, others, turn = prepare(t, moves, wires, 1)
    need = fetcher(
        moves, [(n, getattr(t, n + "_all").at[1], getattr(t, n)) for n in ("w", "eg", "eu", "ed")]
    )
    t.cot_own[...] = t.cotangent[:, z].astype(F32).reshape(64, 768)
    met(others)
    early = RowWalk(wires, moves, t.arrived0, t.rows0, y, e, z)
    early.start(0)
    early.start(1)
    need("w")
    moves.need(turn)
    none = lambda *names: None
    coming = []
    start = lambda: coming.extend(backward_start(wires, t, t.w, need, t.cotangent))
    pump = pumper([(), (), (lambda: early.pass_on(0), lambda: early.pass_on(1)), (), (), (early.finish, start)])
    walk, halves, wait = forward_block(
        wires, moves, t, t.w, need, t.stream, t.own, t.lengths, pump, none, t.rows1
    )
    pump = pumper([(lambda: walk.pass_on(0), lambda: walk.pass_on(1)), (halves, walk.finish)])
    walk = backward_block(
        wires, moves, t, t.w, need, t.cotangent, t.cot_own, t.own, coming, pump, t.back1, t.grads
    )
    wait()
    t.outputs[...] = t.stream_out[...]
    t.outputs_own[...] = t.own_out[...]
    moves.go(t.grads, t.grads1)
    t.grad_own[...] = t.down_own[...]
    t.grad_stream[...] = t.down_stream[...]
    walk.finish()
    wires.finish()
    moves.finish()


def third_body(t, moves, wires):
    y, e, z, others, turn = prepare(t, moves, wires, 0)
    order = ("shares", "w", "gud", "ret", "ffn_in", "ed", "gue", "eg", "eu", "middle", "probs", "kv", "queries", "attended", "normed")
    source = lambda n: getattr(t, n + "_all").at[0] if n in WEIGHTS else getattr(t, n + "_in")
    need = fetcher(moves, [(n, source(n), getattr(t, n)) for n in order] + [("grads1", t.grads1, t.acc.at[1])])
    one, feed, attn = [
        Scatter(wires, columns, t.acc.at[n], t.pool.at[n], t.total.at[n], t.other.at[n], t.sums.at[n])
        for n, columns in ((1, slice(0, HALF)), (0, FEED), (0, ATTN))
    ]
    t.own0[...] = t.inputs[:, z].astype(F32).reshape(64, 768)
    moves.need(turn)
    met(others)
    coming = backward_start(wires, t, t.w, need, t.incoming)
    pump = pumper(
        [
            (lambda: need("grads1"), one.step0),
            (),
            (one.step1, feed.step0),
            (one.step2, feed.step1),
            (one.step3, feed.step2),
            (one.step4, feed.step3),
            (one.step5, feed.step4),
        ]
    )
    walk = backward_block(
        wires, moves, t, t.w, need, t.incoming, t.grad_own, t.own0, coming, pump, t.back0, t.acc.at[0]
    )
    attn.step0()
    t.input_grad[...] = t.down_stream[...]
    t.input_own[...] = t.down_own[...]
    attn.step1()
    feed.step5()
    one.step6()
    attn.step2()
    attn.step3()
    feed.step6()
    attn.step4()
    attn.step5()
    attn.step6()
    walk.finish()
    wires.finish()
    moves.finish()


def last_kernel(rows0, rows1, back0, back1, eg, eu, ed, sums, outputs, own, input_grad, own_grad, *rest):
    rows, grads, hidden, gu, sems = rest[-5:]
    g_gate, g_up, g_down, o_out, o_in, o_router, o_again, o_fgain, *o_parts = rest[:-5]
    at = pl.program_id(0) * 2 + pl.program_id(1)
    sources = [(src, back, i) for src, back in ((rows1, back1), (rows0, back0)) for i in range(2)]

    def copies(n):
        src, back, i = sources[n]
        return (
            pltpu.make_async_copy(src.at[i], rows.at[n % 2], sems.at[n % 2, 0]),
            pltpu.make_async_copy(back.at[i], grads.at[n % 2], sems.at[n % 2, 1]),
        )

    for n in range(4):

        @pl.when(at == n)
        def _():
            if n == 0:
                for copy in copies(0):
                    copy.start()
            if n < 3:
                for copy in copies(n + 1):
                    copy.start()
            for copy in copies(n):
                copy.wait()

    slot = at % 2
    for n in range(4):
        some = slice(n * 256, n * 256 + 256)
        mine = rows[slot, n]
        gate, up, hidden_grad = mm(mine, eg[...]), mm(mine, eu[...]), mm_t(grads[slot, n], ed[...])
        s = sigmoid(gate)
        silu = gate * s
        hidden[some] = (silu * up).astype(BF)
        gu[some, :512] = (hidden_grad * up * (s * (1.0 + gate * (1.0 - s)))).astype(BF)
        gu[some, 512:] = (hidden_grad * silu).astype(BF)
    both = t_mm(rows[slot].reshape(1024, 768), gu[...])
    g_gate[...] = both[:, :512]
    g_up[...] = both[:, 512:]
    g_down[...] = t_mm(hidden[...], grads[slot].reshape(1024, 768))

    @pl.when(at == 0)
    def _():
        z = lax.axis_index("tp")
        o_out[...] = outputs[...].astype(F32)
        o_out[:, z] = own[...].reshape(2, 32, 768)
        o_in[...] = input_grad[...].astype(F32)
        o_in[:, z] = own_grad[...].reshape(2, 32, 768)
        pick = (lanes((24, 128)) == lax.broadcasted_iota(jnp.int32, (24, 128), 0) + ROUTER).astype(F32)
        for layer in range(2):
            left, right = sums[layer, 0], sums[layer, 1]
            o_o, o_k, o_v, o_q, o_gate, o_up, o_down = [ref.at[layer] for ref in o_parts]
            o_o[...] = left[:, OUT]
            o_k[...] = left[:, 256:448]
            o_v[:, :64] = left[:, 448:512]
            o_v[:, 64:] = right[:, :128]
            o_q[...] = right[:, 128:320]
            o_gate[...] = left[:, 512:1024]
            o_up[:, :256] = left[:, 1024:]
            o_up[:, 256:] = right[:, 512:768]
            o_down[...] = right[:, 768:]
            small = lax.dot_general(
                pick,
                left[:, SMALL],
                (((1,), (1,)), ((), ())),
                precision=lax.Precision.HIGHEST,
                preferred_element_type=F32,
            )
            o_router[layer] = small[:16]
            o_again[layer : layer + 1] = small[16:17]
            o_fgain[layer : layer + 1] = small[17:18]


def last_results(rows, experts, others):
    wide = pl.BlockSpec((None, None, 768, 512), lambda n, i: (1 - n, i, 0, 0))
    tall = pl.BlockSpec((None, None, 512, 768), lambda n, i: (1 - n, i, 0, 0))
    fixed = lambda shape: pl.BlockSpec(shape, lambda n, i: (0,) * len(shape))
    more = [ROWS, ROWS, (2, 16, 24), (2, 24), (2, 24)] + [(2, 24, n) for n in (192, 192, 192, 192, 512, 512, 512)]
    shapes = [(2, 2, 768, 512), (2, 2, 768, 512), (2, 2, 512, 768), *more]
    return pl.pallas_call(
        last_kernel,
        grid=(2, 2),
        out_shape=[jax.ShapeDtypeStruct(shape, F32) for shape in shapes],
        in_specs=[ANY] * 4 + [wide, wide, tall] + [fixed(other.shape) for other in others],
        out_specs=[wide, wide, tall] + [fixed(shape) for shape in more],
        scratch_shapes=[
            pltpu.VMEM((2, 4, 256, 768), BF),
            pltpu.VMEM((2, 4, 256, 768), BF),
            pltpu.VMEM((1024, 512), BF),
            pltpu.VMEM((1024, 1024), BF),
            pltpu.SemaphoreType.DMA((2, 2)),
        ],
        compiler_params=pltpu.CompilerParams(vmem_limit_bytes=60 * 2**20),
        cost_estimate=pl.CostEstimate(flops=19_400_000_000, bytes_accessed=40_000_000, transcendentals=4_000_000),
        name="expert_grads",
    )(*rows, *experts, *others)


def rotation_table():
    half = HD // 2
    frequency = np.exp(-np.log(10000.0) * np.arange(half) / half)
    angles = np.arange(1024)[:, None] * frequency[None, :]
    cosine, sine = np.cos(angles), np.sin(angles)
    return np.concatenate([cosine, cosine, cosine, cosine, -sine, sine, -sine, sine], axis=1).astype(np.float32)


def shards(
    inputs, lengths, expert_ids, slot_ids, attn_gain, query_weight, key_weight, value_weight, out_weight, ffn_gain, router_weight,
    dense_gate, dense_up, dense_down, expert_gate, expert_up, expert_down, cotangent,
):
    ids, slots = jnp.swapaxes(expert_ids, 2, 3), jnp.swapaxes(slot_ids, 2, 3)
    stream = inputs.reshape(ROWS)
    experts = (expert_gate, expert_up, expert_down)
    common = {"ids": VM, "slots": VM, "table": ANY, "eg_all": ANY, "eu_all": ANY, "ed_all": ANY}
    given = (ids, slots, rotation_table(), *experts)
    always = {"route": ((256, 4), jnp.int32), "turn": ((128, 256), F32)}
    leaving = dict(SAVED, arrived=FORWARD["arrived"], own_out=FORWARD["own_out"], stream_out=FORWARD["stream_out"])
    ins = ("stream", "again", "q", "k", "v", "o", "fgain", "router", "g", "u", "d")
    *saved, arrived, own, after, w = launch(
        first_body,
        0,
        "gather_forward_0",
        dict(common, lengths=SMEM, **{n: VM for n in ins}),
        dict({n + "_out": (shape, ANY) for n, shape in leaving.items()}, w_out=(((2, 768, WIDE), BF), ANY)),
        dict(
            SAVED, **WEIGHTS, **FORWARD, **always, land0=((32, CHUNK, 1280), BF), land1=((32, CHUNK, 1280), BF),
            w1=WEIGHTS["w"], own0=((64, 768), F32), stage=((24, WIDE), F32),
        ),
        (
            *given, lengths, stream, attn_gain, query_weight, key_weight, value_weight, out_weight, ffn_gain,
            jnp.swapaxes(router_weight, 1, 2), dense_gate, dense_up, dense_down,
        ),
    )
    last, last_own, grads1, rows0, rows1, back1, grad_own, grad_stream = launch(
        second_body,
        1,
        "forward_backward_1",
        dict(common, lengths=SMEM, stream=VM, own=VM, cotangent=VM, arrived0=ANY, w_all=ANY),
        dict(
            outputs=((ROWS, BF), VM), outputs_own=(((64, 768), F32), VM), grads1=(GRADS, ANY), rows0=(DP_ROWS, ANY),
            rows1=(DP_ROWS, ANY), back1=(DP_ROWS, ANY), grad_own=(((64, 768), F32), VM), grad_stream=((ROWS, BF), VM),
        ),
        dict(SAVED, **WEIGHTS, **FORWARD, **BACKWARD, **always, cot_own=((64, 768), F32), grads=GRADS),
        (*given, lengths, after, own, cotangent.reshape(ROWS), arrived, w),
    )
    sums, first, first_own, back0 = launch(
        third_body,
        2,
        "backward_0_scatter",
        dict(common, incoming=VM, grad_own=VM, inputs=VM, **{n + "_in": ANY for n in SAVED}, w_all=ANY, grads1=ANY),
        dict(
            sums=(((2, 2, 24, HALF), F32), VM), input_grad=((ROWS, BF), VM), input_own=(((64, 768), F32), VM), back0=(DP_ROWS, ANY)
        ),
        dict(SAVED, **WEIGHTS, **BACKWARD, **SCATTER, **always, own0=((64, 768), F32)),
        (*given, grad_stream, grad_own, stream, *saved, w, grads1),
    )
    g_eg, g_eu, g_ed, o_out, o_in, g_router, g_again, g_fgain, g_o, g_k, g_v, g_q, g_gate, g_up, g_down = last_results(
        (rows0, rows1, back0, back1), experts, (sums, last, last_own, first, first_own)
    )
    return (
        o_out.reshape(2, 128, 768),
        o_in.reshape(2, 128, 768),
        g_again,
        g_q,
        g_k,
        g_v,
        g_o,
        g_fgain,
        jnp.swapaxes(g_router, 1, 2),
        g_gate,
        g_up,
        g_down,
        g_eg,
        g_eu,
        g_ed,
    )


def solution(mesh):
    return jax.shard_map(
        shards,
        mesh=mesh,
        in_specs=(
            P("dp", "ep", None),
            P("dp"),
            P(None, "dp", "ep", None),
            P(None, "dp", "ep", None),
            P(None, ("dp", "ep")),
            P(None, ("dp", "ep"), "tp"),
            P(None, ("dp", "ep"), "tp"),
            P(None, ("dp", "ep"), "tp"),
            P(None, ("dp", "ep"), "tp"),
            P(None, ("dp", "ep")),
            P(None, ("dp", "ep"), None),
            P(None, ("dp", "ep"), "tp"),
            P(None, ("dp", "ep"), "tp"),
            P(None, ("dp", "ep"), "tp"),
            P(None, "ep", None, "tp"),
            P(None, "ep", None, "tp"),
            P(None, "ep", "tp", None),
            P("dp", "ep", None),
        ),
        out_specs=(
            P("dp", "ep", None),
            P("dp", "ep", None),
            P(None, ("dp", "ep")),
            P(None, ("dp", "ep"), "tp"),
            P(None, ("dp", "ep"), "tp"),
            P(None, ("dp", "ep"), "tp"),
            P(None, ("dp", "ep"), "tp"),
            P(None, ("dp", "ep")),
            P(None, ("dp", "ep"), None),
            P(None, ("dp", "ep"), "tp"),
            P(None, ("dp", "ep"), "tp"),
            P(None, ("dp", "ep"), "tp"),
            P(None, "ep", None, "tp"),
            P(None, "ep", None, "tp"),
            P(None, "ep", "tp", None),
        ),
        check_vma=False,
    )
```

```python
import jax
import jax.numpy as jnp
import numpy as np
from jax import lax
from jax.experimental import pallas as pl
from jax.experimental.pallas import tpu as pltpu
from jax.sharding import PartitionSpec as P

HD = 64
EPS = 1e-06
MESH = pl.DeviceIdType.MESH
BF = jnp.bfloat16
F32 = jnp.float32
VM = pl.BlockSpec(memory_space=pltpu.VMEM)
ANY = pl.BlockSpec(memory_space=pl.ANY)
SMEM = pl.BlockSpec(memory_space=pltpu.SMEM)
WIDE = 2560
HALF = 1280
CHUNK = 48
ATTN = slice(0, 512)
FEED = slice(512, 1280)
SMALL = slice(128, 256)
SPOTS = ((0, 512, 0, 0), (512, 1024, 1, 0), (1024, 1792, 0, 512), (1792, 2560, 1, 512))
ROUTER = 64
GAIN = 80
OUT = slice(0, 192)
QKV = slice(256, 896)
GATE = slice(1024, 1536)
UP = slice(1536, 2048)
GATEUP = slice(1024, 2048)
DOWN = slice(2048, 2560)
ROWS = (2, 4, 32, 768)


class Box:
    def __init__(self, names, refs):
        self.__dict__.update(zip(names, refs, strict=True))

    def but(self, **others):
        return Box([*self.__dict__, *others], [*self.__dict__.values(), *others.values()])


def place():
    y = lax.axis_index("dp")
    e = lax.axis_index("ep")
    z = lax.axis_index("tp")
    return y, e // 2, e % 2, z


def device(y, x, c, z):
    return (y, x * 2 + c, z)


def greet(others):
    for who in others:
        pl.semaphore_signal(pltpu.get_barrier_semaphore(), inc=1, device_id=who, device_id_type=MESH)


def met(others):
    pl.semaphore_wait(pltpu.get_barrier_semaphore(), len(others))


def mm(a, b):
    return lax.dot_general(a, b, (((1,), (0,)), ((), ())), preferred_element_type=F32)


def mm_t(a, b):
    return lax.dot_general(a, b, (((1,), (1,)), ((), ())), preferred_element_type=F32)


def t_mm(a, b):
    return lax.dot_general(a, b, (((0,), (0,)), ((), ())), preferred_element_type=F32)


def lanes(shape):
    return lax.broadcasted_iota(jnp.int32, shape, 1)


def gain_rows(weights):
    pick = (lanes((8, 128)) == lax.broadcasted_iota(jnp.int32, (8, 128), 0) + GAIN).astype(BF)
    return mm_t(pick, weights[:, SMALL])


def rms(values, gain):
    turn = lax.rsqrt(jnp.mean(values * values, axis=-1, keepdims=True) + EPS)
    return values * turn * gain


def rms_back(values, gain, grad):
    turn = lax.rsqrt(jnp.mean(values * values, axis=-1, keepdims=True) + EPS)
    scaled = grad * gain
    back = turn * scaled - values * (turn * turn * turn) * jnp.mean(values * scaled, axis=-1, keepdims=True)
    return back, jnp.sum(grad * values * turn, axis=0, keepdims=True)


def turned(values, cosine, sine):
    width = values.shape[1]
    front = lanes(values.shape) % HD < HD // 2
    other = jnp.where(front, pltpu.roll(values, width - HD // 2, 1), pltpu.roll(values, HD // 2, 1))
    return values * cosine + other * sine


def sigmoid(v):
    return 1.0 / (1.0 + jnp.exp(-v))


def swish_back(gate, up, grad):
    s = sigmoid(gate)
    return (grad * up * s * (1.0 + gate * (1.0 - s))).astype(BF), (grad * gate * s).astype(BF)


def turns(t, sign):
    cosine, sine = t.turn[:, :128], sign * t.turn[:, 128:]
    first = lanes((128, 128)) < HD
    one, none = jnp.ones((128, 128), F32), jnp.zeros((128, 128), F32)
    mixed, mixed_sine = jnp.where(first, cosine, 1.0), jnp.where(first, sine, 0.0)
    cosine = jnp.concatenate([cosine, mixed, one, cosine, mixed], axis=1)
    sine = jnp.concatenate([sine, mixed_sine, none, sine, mixed_sine], axis=1)
    return cosine, sine


def set_route(t, layer, route):
    row = lax.broadcasted_iota(jnp.int32, (16, 128), 0)
    unit = (row == lanes((16, 128))).astype(BF)
    for s in range(2):
        stacked = jnp.zeros((16, 128), jnp.int32)
        for n, ref in enumerate((t.ids, t.slots)):
            for j in range(2):
                stacked = jnp.where(row == 2 * n + j, ref[layer, s, j : j + 1], stacked)
        columns = t_mm(stacked.astype(F32).astype(BF), unit).astype(jnp.int32)
        rows = slice(s * 128, s * 128 + 128)
        for j in range(2):
            expert, slot = columns[:, j : j + 1], columns[:, 2 + j : 3 + j]
            route[rows, j : j + 1] = jnp.where(slot < 32, expert * 32 + slot, 512)
            route[rows, 2 + j : 3 + j] = expert


class Wires:
    def __init__(self, sends, recvs):
        self.sends, self.recvs, self.used, self.open = sends, recvs, 0, []

    def plan(self, src, dst, who, when=None, at=None):
        if at is None:
            at = self.used
            self.used += 1
        copy = pltpu.make_async_remote_copy(
            src_ref=src,
            dst_ref=dst,
            send_sem=self.sends.at[at],
            recv_sem=self.recvs.at[at],
            device_id=who,
            device_id_type=MESH,
        )
        self.open.append((copy, when))
        return copy

    def go(self, src, dst, who):
        copy = self.plan(src, dst, who)
        copy.start()
        return copy

    def settle(self, copies):
        for copy, when in copies:
            if when is None:
                copy.wait_send()
            else:
                pl.when(when)(copy.wait_send)

    def finish(self):
        assert self.used <= self.sends.shape[0]
        self.settle(self.open)


class Moves:
    def __init__(self, sems):
        self.sems, self.used, self.open = sems, 0, []

    def go(self, src, dst):
        copy = pltpu.make_async_copy(src, dst, self.sems.at[self.used])
        self.used += 1
        copy.start()
        self.open.append(copy)
        return copy

    def need(self, copy):
        self.open = [other for other in self.open if other is not copy]
        copy.wait()

    def finish(self):
        assert self.used <= self.sems.shape[0]
        for copy in self.open:
            copy.wait()
        self.open = []


def peers(y, e, z):
    row = [(y, (e + k) % 8, z) for k in range(1, 8)]
    return row + [(y, e, (z + k) % 4) for k in range(1, 4)] + [((y + k) % 4, e, z) for k in range(1, 4)]


class TpSum:
    def __init__(self, wires, parts, land, held):
        self.wires, self.parts, self.land, self.held = wires, parts, land, held
        self.y, self.e, self.z = (lax.axis_index(name) for name in ("dp", "ep", "tp"))
        self.sums, self.spread = [None, None], [None, None]

    def send(self, h):
        self.sums[h] = []
        for k in (1, 3, 2):
            who = (self.z + k) % 4
            copy = self.wires.go(self.parts.at[h, who], self.land.at[h, k - 1], (self.y, self.e, who))
            self.sums[h].append(copy)

    def half(self, h, finish):
        for copy in self.sums[h]:
            copy.wait_recv()
        total = self.parts[h, self.z].astype(F32)
        for k in range(3):
            total += self.land[h, k].astype(F32)
        finish(h, slice(32 * h, 32 * h + 32), total)
        self.spread[h] = self.everywhere(self.held.at[h, self.z])

    def everywhere(self, spot):
        return [self.wires.go(spot, spot, (self.y, self.e, (self.z + k) % 4)) for k in (1, 3, 2)]

    def wait(self, h):
        for copy in self.spread[h]:
            copy.wait_recv()


def scatter_experts(wires, src, dst, y, e, z, i):
    rows = pl.ds(pl.multiple_of(e * 32, 32), 32)
    sent = []
    for k in (1, 7, 2, 6, 3, 5, 4):
        who = (e + k) % 8
        sent.append(wires.go(src.at[2 * who + i], dst.at[i, rows], (y, who, z)))
    dst[i, rows] = src[2 * e + i]
    return lambda: [copy.wait_recv() for copy in sent]


def return_experts(wires, src, dst, y, e, z, i):
    sent = []
    for k in (1, 7, 2, 6, 3, 5, 4):
        who = (e + k) % 8
        rows = pl.ds(pl.multiple_of(who * 32, 32), 32)
        sent.append(wires.go(src.at[i, rows], dst.at[2 * e + i], (y, who, z)))
    dst[2 * e + i] = src[i, pl.ds(pl.multiple_of(e * 32, 32), 32)]
    return lambda: [copy.wait_recv() for copy in sent]


class RowWalk:
    def __init__(self, wires, moves, own, rows, y, e, z):
        self.wires, self.moves, self.own, self.rows = wires, moves, own, rows
        self.up, self.down = ((y + 1) % 4, e, z), ((y + 3) % 4, e, z)
        self.near, self.far = [], []

    def start(self, i):
        own, rows = self.own.at[i], self.rows
        self.near.append(
            (self.wires.go(own, rows.at[i, 1], self.up), self.wires.go(own, rows.at[i, 3], self.down))
        )
        self.moves.go(own, rows.at[i, 0])

    def pass_on(self, i):
        self.near[i][i].wait_recv()
        slot, who = ((1, self.up), (3, self.down))[i]
        self.far.append(self.wires.go(self.rows.at[i, slot], self.rows.at[i, 2], who))

    def finish(self):
        self.near[0][1].wait_recv()
        self.near[1][0].wait_recv()
        for copy in self.far:
            copy.wait_recv()


class Gather:
    def __init__(self, wires, land, columns):
        self.wires, self.land, self.columns = wires, land, columns
        self.y, self.x, self.c, self.z = place()
        self.second, self.far = {}, []

    def who(self, j, d):
        yy = (self.y + j * self.c + d * (1 - self.c) + 8) % 4
        xx = (self.x + j * (1 - self.c) + d * self.c + 8) % 4
        return device(yy, xx, self.c, self.z)

    def spot(self, j, d, rows=slice(None)):
        yy, ee, zz = self.who(j, d)
        return self.land.at[self.c, yy * 4 + ee // 2, rows, self.columns]

    def reach(self, spot, whos):
        return [self.wires.go(spot, spot, who) for who in whos]

    def spread(self, j):
        self.second[j] = self.reach(self.spot(j, 0), [self.who(0, 1), self.who(0, -1)])

    def step0(self):
        self.first = self.reach(self.spot(0, 0), [self.who(1, 0), self.who(-1, 0)])
        self.spread(0)

    def step1(self):
        self.first[0].wait_recv()
        spot = self.spot(-1, 0, pl.ds(0, 32))
        self.on = [self.wires.go(spot, spot, self.who(1, 0))]
        self.spread(-1)
        self.first[1].wait_recv()
        spot = self.spot(1, 0, pl.ds(32, 16))
        self.on.append(self.wires.go(spot, spot, self.who(-1, 0)))
        self.spread(1)

    def step2(self):
        for copy in self.on:
            copy.wait_recv()
        self.spread(2)

    def step3(self):
        for j in (0, -1, 1, 2):
            for n, d in enumerate((-1, 1)):
                self.second[j][n].wait_recv()
                if (j in (0, -1)) == (n == 0):
                    spot = self.spot(j, d)
                    self.far.append(self.wires.go(spot, spot, self.who(0, -d)))

    def step4(self):
        for copy in self.far:
            copy.wait_recv()
        self.pair()

    def pair(self):
        spot = self.land.at[self.c, :, :, self.columns]
        self.swap = self.wires.go(spot, spot, device(self.y, self.x, 1 - self.c, self.z))

    def step5(self):
        self.swap.wait_recv()


class ShortGather(Gather):
    def spread(self, j):
        self.second[j] = self.reach(self.spot(j, 0), [self.who(0, d) for d in (1, -1, 2)])

    def step0(self):
        self.first = self.reach(self.spot(0, 0), [self.who(j, 0) for j in (1, -1, 2)])
        self.spread(0)

    def step1(self):
        for n, j in ((0, -1), (1, 1), (2, 2)):
            self.first[n].wait_recv()
            self.spread(j)

    def step2(self):
        for j in (0, -1, 1, 2):
            for copy in self.second[j]:
                copy.wait_recv()
        self.pair()


def unpack(land, columns, w, left):
    half = columns.stop - columns.start

    def some(p, carry):
        one = land[0, p, :, columns].astype(F32)
        two = land[1, p, :, columns].astype(F32)
        rows = pl.ds(pl.multiple_of(p * CHUNK, CHUNK), CHUNK)
        w[rows, left : left + half] = jnp.concatenate([one[:24], two[:24]], axis=0).astype(BF)
        w[rows, left + half : left + 2 * half] = jnp.concatenate([one[24:], two[24:]], axis=0).astype(BF)
        return carry

    lax.fori_loop(0, 16, some, 0)


def picks(route):
    slots = lanes((256, 512))
    return slots == route[:, 0:1], slots == route[:, 1:2]


class Scatter:
    PLUS, MINUS = (0, -1), (1, 2)

    def __init__(self, wires, columns, *refs):
        self.wires, self.columns = wires, columns
        self.acc, self.pool, self.total, self.other, self.out = refs
        self.y, self.x, self.c, self.z = place()
        self.sibling = device(self.y, self.x, 1 - self.c, self.z)
        self.far, self.near = {}, {}

    def at(self, j, d, core):
        yy = (self.y + j * core + d * (1 - core) + 8) % 4
        xx = (self.x + j * (1 - core) + d * core + 8) % 4
        return yy, xx

    def who(self, j, d):
        yy, xx = self.at(j, d, self.c)
        return device(yy, xx, self.c, self.z)

    def mine(self, j, d, core):
        yy, xx = self.at(j, d, core)
        return yy * 4 + xx

    def chunk(self, core, block):
        return self.acc.at[core, block, :, self.columns]

    def slot(self, n):
        return self.pool.at[n, :, self.columns]

    def add(self, ref, *others):
        total = ref[...].astype(F32)
        for other in others:
            total += other[...].astype(F32)
        ref[...] = total.astype(BF)

    def join(self, j, d):
        block = self.mine(j, d, self.c)
        ref = self.chunk(self.c, block)
        self.add(ref, self.slot(block))
        return ref

    def step0(self):
        half = self.acc.at[1 - self.c, :, :, self.columns]
        self.swap = self.wires.go(half, self.pool.at[pl.ds(0, 16), :, self.columns], self.sibling)

    def step1(self):
        self.swap.wait_recv()
        for j in (0, 1, -1, 2):
            ref = self.join(j, 2)
            n, d = (16 + self.PLUS.index(j), 1) if j in self.PLUS else (18 + self.MINUS.index(j), -1)
            self.far[j] = self.wires.go(ref, self.slot(n), self.who(0, d))
        for j, k in zip(self.MINUS, self.PLUS):
            self.near[j, 1] = self.wires.go(self.join(j, 1), self.slot(20 + j), self.who(0, 1))
            self.near[k, -1] = self.wires.go(self.join(k, -1), self.slot(24 + k % 4), self.who(0, -1))
        self.up = {j: self.join(j, 1) for j in self.PLUS}
        self.down = {j: self.join(j, -1) for j in self.MINUS}

    def step2(self):
        for n, (j, k) in enumerate(zip(self.PLUS, self.MINUS)):
            self.far[j].wait_recv()
            self.add(self.up[j], self.slot(16 + n))
            self.near[j, 1] = self.wires.go(self.up[j], self.slot(20 + j % 4), self.who(0, 1))
            self.far[k].wait_recv()
            self.add(self.down[k], self.slot(18 + n))
            self.near[k, -1] = self.wires.go(self.down[k], self.slot(24 + k), self.who(0, -1))
        self.held = {j: self.join(j, 0) for j in (2, 1, -1, 0)}

    def step3(self):
        for j in (2, 1, -1, 0):
            self.near[j, 1].wait_recv()
            self.near[j, -1].wait_recv()
            ref = self.held[j]
            self.add(ref, self.slot(20 + j % 4), self.slot(24 + j % 4))
            if j == 2:
                spot = self.slot(28)
                self.one = [
                    self.wires.go(ref.at[rows], spot.at[rows], self.who(d, 0))
                    for rows, d in ((pl.ds(0, 32), 1), (pl.ds(32, 16), -1))
                ]

    def step4(self):
        self.last = []
        for n, (rows, d) in enumerate(((pl.ds(0, 32), 1), (pl.ds(32, 16), -1))):
            self.one[n].wait_recv()
            self.add(self.held[d].at[rows], self.slot(28).at[rows])
            self.last.append(self.wires.go(self.held[d], self.slot(29 + n), self.who(d, 0)))

    def step5(self):
        for copy in self.last:
            copy.wait_recv()
        columns = self.columns
        near = self.pool[29, :, columns].astype(F32) + self.pool[30, :, columns].astype(F32)
        self.total[:, columns] = self.held[0][...].astype(F32) + near
        away = pl.ds(pl.multiple_of(24 - 24 * self.c, 8), 24)
        self.trade = self.wires.go(self.total.at[away, columns], self.other.at[:, columns], self.sibling)
        self.out[self.c, :, columns] = self.total[pl.ds(pl.multiple_of(24 * self.c, 8), 24), columns]

    def step6(self):
        self.trade.wait_recv()
        self.out[1 - self.c, :, self.columns] = self.other[:, self.columns]


def forward_block(wires, moves, t, w, need, stream, own, lengths, ready, pump, done, dp_rows=None):
    y, x, c, z = place()
    e = 2 * x + c
    gains = gain_rows(w)
    sibling = (y, e + 1 - 2 * c, z)
    cosine, sine = turns(t, 1.0)
    spans = (slice(0, 128), slice(128, 256))
    first, to_core = [], []
    for s, rows in enumerate(spans):
        ready(s)
        t.normed[rows] = rms(stream[s].reshape(128, 768).astype(F32), gains[0:1]).astype(BF)
        lin = turned(mm(t.normed[rows], w[:, QKV]), cosine, sine).astype(BF)
        t.kv[e, rows] = lin[:, :384]
        t.queries[rows] = lin[:, 384:576]
        here = t.kv.at[e, pl.ds(s * 128, 128)]
        first.append([])
        for k in (1, 3, 2):
            ahead = x + k <= 3
            copy = wires.plan(here, here, (y, (e + 2 * k) % 8, z), ahead)
            pl.when(ahead)(copy.start)
            first[s].append((k, copy))
        to_core.append(wires.plan(here, here, sibling, c == 0))
        pl.when(c == 0)(to_core[s].start)
    done("normed", "queries")
    for j in range(8):

        @pl.when(j > e)
        def _():
            t.kv[j] = jnp.zeros((256, 384), BF)

    pump()
    tp = TpSum(wires, t.part.at[0], t.land.at[0], t.ffn_in)
    at_key = lanes((128, 1024))
    at_query = lax.broadcasted_iota(jnp.int32, (128, 1024), 0) + e * 128
    for s, rows in enumerate(spans):
        second = []
        for k, copy in first[s]:
            behind = x - k >= 0
            there = t.kv.at[(e + 8 - 2 * k) % 8, pl.ds(s * 128, 128)]
            on = wires.plan(there, there, sibling, behind)

            @pl.when(behind)
            def _():
                copy.wait_recv()
                on.start()

            second.append((behind, on))
        pl.when(c == 1)(to_core[s].wait_recv)
        for behind, on in second:
            pl.when(behind)(on.wait_recv)
        allowed = (at_key <= at_query) & (at_key < lengths[s])
        for h in range(3):
            keys = t.kv[:, rows, 64 * h : 64 * h + 64].reshape(1024, 64)
            vals = t.kv[:, rows, 192 + 64 * h : 256 + 64 * h].reshape(1024, 64)
            scores = jnp.where(allowed, mm_t(t.queries[rows, 64 * h : 64 * h + 64], keys) * HD**-0.5, -1e30)
            expd = jnp.exp(scores - jnp.max(scores, axis=-1, keepdims=True))
            low = (expd / jnp.sum(expd, axis=-1, keepdims=True)).astype(BF)
            t.probs[3 * s + h] = low
            t.attended[rows, 64 * h : 64 * h + 64] = mm(low, vals).astype(BF)
        t.part[0, s] = mm_t(t.attended[rows], w[:, OUT]).astype(BF).reshape(4, 32, 768)
        tp.send(s)
    done("kv", "probs", "attended")
    pump()

    def finish(h, rows, total):
        t.middle[rows] = own[rows] + total
        t.ffn_in[h, z] = rms(t.middle[rows], gains[1:2]).astype(BF)

    tp.half(0, finish)
    tp.half(1, finish)
    done("middle")
    pump()
    tp.wait(0)
    tp.wait(1)
    done("ffn_in")
    rows_in = t.ffn_in[...].reshape(256, 768)
    ids = t.route[...]
    pick0, pick1 = picks(ids)
    t.sent[...] = t_mm((pick0 | pick1).astype(BF), rows_in).astype(BF).reshape(16, 32, 768)
    coming = [scatter_experts(wires, t.sent, t.arrived, y, e, z, i) for i in range(2)]
    pump()
    logits = mm(rows_in, w[:, SMALL])
    lane = lanes((256, 128))
    chosen = [
        jnp.sum(jnp.where(lane == ids[:, 2 + j : 3 + j] + ROUTER, logits, 0.0), axis=-1, keepdims=True)
        for j in range(2)
    ]
    top = jnp.maximum(chosen[0], chosen[1])
    expd = [jnp.exp(v - top) for v in chosen]
    share = [v / (expd[0] + expd[1]) for v in expd]
    t.shares[...] = jnp.where(lane == 0, share[0], jnp.where(lane == 1, share[1], 0.0))
    t.gud[...] = mm(rows_in, w[:, GATEUP])
    gate, up = t.gud[:, :512], t.gud[:, 512:]
    hidden = (gate * sigmoid(gate) * up).astype(BF)
    dense = mm_t(hidden, w[:, DOWN])
    done("gud", "shares")
    pump()
    need("eg", "eu", "ed")
    walk = None if dp_rows is None else RowWalk(wires, moves, t.arrived, dp_rows, y, e, z)
    back = []
    for i in range(2):
        coming[i]()
        if walk is not None:
            walk.start(i)
        t.gue[i, :, :512] = mm(t.arrived[i], t.eg[i])
        t.gue[i, :, 512:] = mm(t.arrived[i], t.eu[i])
        gate, up = t.gue[i, :, :512], t.gue[i, :, 512:]
        hidden = (gate * sigmoid(gate) * up).astype(BF)
        t.made[i] = mm(hidden, t.ed[i]).astype(BF)
        back.append(return_experts(wires, t.made, t.ret, y, e, z, i))
    done("arrived", "gue")
    pump()
    for wait in back:
        wait()
    done("ret")
    mix = (jnp.where(pick0, share[0], 0.0) + jnp.where(pick1, share[1], 0.0)).astype(BF)
    tp = TpSum(wires, t.part.at[1], t.land.at[1], t.stream_out)
    for h, rows in enumerate(spans):
        moe = mm(mix[rows], t.ret[...].reshape(512, 768))
        t.part[1, h] = (dense[rows] + moe).astype(BF).reshape(4, 32, 768)
        tp.send(h)
    pump()

    def finish(h, rows, total):
        result = t.middle[rows] + total
        t.own_out[rows] = result
        t.stream_out[h, z] = result.astype(BF)

    def halves():
        tp.half(0, finish)
        tp.half(1, finish)
        done("own_out")
        pump()

    return walk, halves, tp.wait


def backward_start(wires, t, w, need, incoming):
    y, x, c, z = place()
    e = 2 * x + c
    need("shares")
    ffn_grad = incoming[...].reshape(256, 768)
    pick0, pick1 = picks(t.route[...])
    mix = (jnp.where(pick0, t.shares[:, 0:1], 0.0) + jnp.where(pick1, t.shares[:, 1:2], 0.0)).astype(BF)
    t.bsent[...] = t_mm(mix, ffn_grad).astype(BF).reshape(16, 32, 768)
    coming = [scatter_experts(wires, t.bsent, t.back, y, e, z, i) for i in range(2)]
    need("w", "gud", "ffn_in")
    gate, up = t.gud[:, :512], t.gud[:, 512:]
    hidden_dense = (gate * sigmoid(gate) * up).astype(BF)
    gate_grad, up_grad = swish_back(gate, up, mm(ffn_grad, w[:, DOWN]))
    gu_grad = jnp.concatenate([gate_grad, up_grad], axis=1)
    t.dense[...] = mm_t(gu_grad, w[:, GATEUP])
    t.gu_grad[...] = gu_grad
    t.hidden_dense[...] = hidden_dense
    return coming


def backward_block(wires, moves, t, w, need, incoming, grad_own, own, coming, pump, dp_rows, grads):
    y, x, c, z = place()
    e = 2 * x + c

    def keep(columns, values):
        for start, stop, half, lane in SPOTS:
            left, right = max(columns.start, start), min(columns.stop, stop)
            if left < right:
                some = values[:, left - columns.start : right - columns.start].astype(BF)
                lane += left - start
                grads[half, :, :, lane : lane + right - left] = some.reshape(16, CHUNK, right - left)

    need("ret")
    ffn_grad = incoming[...].reshape(256, 768)
    rows_in = t.ffn_in[...].reshape(256, 768)
    gains = gain_rows(w)
    pick0, pick1 = picks(t.route[...])
    match = mm_t(ffn_grad, t.ret[...].reshape(512, 768))
    share_grad = [
        jnp.sum(jnp.where(pick, match, 0.0), axis=-1, keepdims=True) for pick in (pick0, pick1)
    ]
    lane = lanes((256, 128))
    extra = jnp.where(lane == 0, share_grad[0], jnp.where(lane == 1, share_grad[1], 0.0))
    t.part_ffn[:, :, :, 768:] = extra.astype(BF).reshape(2, 4, 32, 128)
    pump()
    need("ed", "gue", "eg", "eu")
    walk = RowWalk(wires, moves, t.back, dp_rows, y, e, z)
    back = []
    for i in range(2):
        coming[i]()
        walk.start(i)
        hidden_grad = mm_t(t.back[i], t.ed[i])
        gate_e, up_e = swish_back(t.gue[i, :, :512], t.gue[i, :, 512:], hidden_grad)
        t.bmade[i] = (mm_t(gate_e, t.eg[i]) + mm_t(up_e, t.eu[i])).astype(BF)
        back.append(return_experts(wires, t.bmade, t.sret, y, e, z, i))
    pump()
    keep(GATEUP, t_mm(rows_in, t.gu_grad[...]))
    keep(DOWN, t_mm(ffn_grad, t.hidden_dense[...]))
    for wait in back:
        wait()
    tp = TpSum(wires, t.part_ffn, t.land_ffn, t.gathered)
    spans = (slice(0, 128), slice(128, 256))
    placed = (pick0 | pick1).astype(BF)
    for h, rows in enumerate(spans):
        total = t.dense[rows] + mm(placed[rows], t.sret[...].reshape(512, 768))
        t.part_ffn[h, :, :, :768] = total.astype(BF).reshape(4, 32, 768)
        tp.send(h)
    pump()
    need("middle")
    top = lax.broadcasted_iota(jnp.int32, (16, 768), 0) == 0
    lane32 = lanes((32, 128))
    gain_parts = []

    def finish(h, rows, total):
        mine = pl.ds(pl.multiple_of(128 * h + 32 * z, 32), 32)
        share, ids = t.shares[mine], t.route[mine]
        weigh = share[:, 0:1] * total[:, 768:769] + share[:, 1:2] * total[:, 769:770]
        logit_grad = jnp.zeros((32, 128), F32)
        for j in range(2):
            chosen_grad = share[:, j : j + 1] * (total[:, 768 + j : 769 + j] - weigh)
            logit_grad += jnp.where(lane32 == ids[:, 2 + j : 3 + j] + ROUTER, chosen_grad, 0.0)
        logit_grad = logit_grad.astype(BF)
        grad_in = total[:, :768] + mm_t(logit_grad, w[:, SMALL])
        back_norm, gain_two = rms_back(t.middle[rows], gains[1:2], grad_in)
        gain_parts.append(gain_two)
        middle_grad = grad_own[rows] + back_norm
        t.down_own[rows] = middle_grad
        t.gathered[h, z, :, :768] = middle_grad.astype(BF)
        t.gathered[h, z, :, 768:] = logit_grad

    tp.half(0, finish)
    tp.half(1, finish)
    t.gains[1, z] = jnp.where(top, gain_parts[0] + gain_parts[1], 0.0).astype(BF)
    gain_copies = tp.everywhere(t.gains.at[1, z])
    grads_tp = tp
    pump()
    need("probs", "kv", "queries", "attended", "normed")
    sibling = (y, e + 1 - 2 * c, z)

    def attend_back(s, between):
        rows = spans[s]
        grad = t.gathered[s, :, :, :768].reshape(128, 768)
        attended_grad = mm(grad, w[:, OUT]).astype(BF)
        for h in range(3):
            cols = slice(64 * h, 64 * h + 64)
            late = slice(192 + 64 * h, 256 + 64 * h)
            keys = t.kv[:, rows, cols].reshape(1024, 64)
            vals = t.kv[:, rows, late].reshape(1024, 64)
            low = t.probs[3 * s + h]
            wide = low.astype(F32)
            grad_here = attended_grad[:, cols]
            probs_grad = mm_t(grad_here, vals)
            kept = jnp.sum(wide * probs_grad, axis=-1, keepdims=True)
            score_grad = (wide * (probs_grad - kept)).astype(BF)
            t.lin[rows, 384 + 64 * h : 448 + 64 * h] = mm(score_grad, keys) * HD**-0.5
            keys_grad = t_mm(score_grad, t.queries[rows, cols]) * HD**-0.5
            t.dkv[:, rows, cols] = keys_grad.astype(BF).reshape(8, 128, 64)
            t.dkv[:, rows, late] = t_mm(low, grad_here).astype(BF).reshape(8, 128, 64)
            if h == 0:
                between()

    def swap(s):
        rows = pl.ds(s * 128, 128)
        swaps = []
        for k in range(4):
            gives = (x - k >= 0) & ((c == 1) if k == 0 else True)
            takes = (x - k >= 0) & ((c == 0) if k == 0 else True)
            block = (2 * (x - k) + 1 - c + 8) % 8
            copy = wires.plan(t.dkv.at[block, rows], t.sib_land.at[k, rows], sibling, gives)
            pl.when(gives)(copy.start)
            swaps.append((takes, copy))
        return swaps

    def send_far(s, swaps):
        rows = pl.ds(s * 128, 128)
        far = []
        for k in (1, 3, 2):
            gives, takes = x - k >= 0, x + k <= 3
            block = (e - 2 * k + 8) % 8
            send = wires.plan(t.dkv.at[block, rows], t.owner_land.at[k - 1, rows], (y, block, z), gives)

            @pl.when(gives)
            def _():
                swaps[k][1].wait_recv()
                both = t.dkv[block, rows].astype(F32) + t.sib_land[k, rows].astype(F32)
                t.dkv[block, rows] = both.astype(BF)
                send.start()

            far.append((k, takes, send))
        return far

    cosine, sine = turns(t, -1.0)
    tp = TpSum(wires, t.bpart, t.bland, t.tail)

    def collect(s, swaps, far):
        rows = spans[s]
        t.lin[rows, :384] = t.dkv[e, rows].astype(F32)
        t.lin[rows, 576:] = jnp.zeros((128, 64), F32)

        @pl.when(swaps[0][0])
        def _():
            swaps[0][1].wait_recv()
            t.lin[rows, :384] += t.sib_land[0, rows].astype(F32)

        for k, takes, copy in far:

            @pl.when(takes)
            def _():
                copy.wait_recv()
                t.lin[rows, :384] += t.owner_land[k - 1, rows].astype(F32)

        t.lin_low[rows] = turned(t.lin[rows], cosine, sine).astype(BF)
        t.bpart[s] = mm_t(t.lin_low[rows], w[:, QKV]).astype(BF).reshape(4, 32, 768)
        tp.send(s)

    grads_tp.wait(0)
    attend_back(0, lambda: None)
    swaps0 = swap(0)
    walk.pass_on(0)
    walk.pass_on(1)
    grads_tp.wait(1)
    far0 = []
    attend_back(1, lambda: far0.extend(send_far(0, swaps0)))
    swaps1 = swap(1)
    keep(OUT, t_mm(t.gathered[:, :, :, :768].reshape(256, 768), t.attended[...]))
    far1 = send_far(1, swaps1)
    router_grad = t_mm(rows_in, t.gathered[:, :, :, 768:].reshape(256, 128))
    pump()
    collect(0, swaps0, far0)
    collect(1, swaps1, far1)
    tail_parts = []

    def finish(h, rows, total):
        back_norm, gain_one = rms_back(own[rows], gains[0:1], total)
        tail_parts.append(gain_one)
        result = t.down_own[rows] + back_norm
        t.down_own[rows] = result
        t.tail[h, z] = result.astype(BF)

    keep(QKV, t_mm(t.normed[...], t.lin_low[...]))
    pump()
    tp.half(0, finish)
    tp.half(1, finish)
    t.gains[0, z] = jnp.where(top, tail_parts[0] + tail_parts[1], 0.0).astype(BF)
    gain_copies += tp.everywhere(t.gains.at[0, z])
    pump()
    tp.wait(0)
    tp.wait(1)
    t.down_stream[...] = t.tail[...]
    for copy in gain_copies:
        copy.wait_recv()
    at_row = lax.broadcasted_iota(jnp.int32, (16, 768), 0)
    gain_grads = jnp.zeros((16, 768), F32)
    for n in range(2):
        total = jnp.sum(t.gains[n].astype(F32).reshape(64, 768), axis=0, keepdims=True)
        gain_grads = jnp.where(at_row == n, total, gain_grads)
    spot = (lanes((16, 128)) == lax.broadcasted_iota(jnp.int32, (16, 128), 0) + GAIN).astype(BF)
    keep(slice(192, 256), (router_grad + t_mm(gain_grads.astype(BF), spot))[:, 64:])
    return walk


MOVE_SEMS, WIRE_SEMS = 48, 320
SAVED = {
    "normed": ((256, 768), BF),
    "queries": ((256, 192), BF),
    "kv": ((8, 256, 384), BF),
    "probs": ((6, 128, 1024), BF),
    "attended": ((256, 192), BF),
    "middle": ((64, 768), F32),
    "ffn_in": (ROWS, BF),
    "gud": ((256, 1024), F32),
    "gue": ((2, 256, 1024), F32),
    "ret": ((16, 32, 768), BF),
    "shares": ((256, 128), F32),
}
WEIGHTS = {"w": ((768, WIDE), BF), "eg": ((2, 768, 512), BF), "eu": ((2, 768, 512), BF), "ed": ((2, 512, 768), BF)}
FORWARD = {
    "arrived": ((2, 256, 768), BF),
    "own_out": ((64, 768), F32),
    "stream_out": (ROWS, BF),
    "part": ((2, *ROWS), BF),
    "land": ((2, 2, 3, 32, 768), BF),
    "sent": ((16, 32, 768), BF),
    "made": ((2, 256, 768), BF),
}
BACKWARD = {
    "back": ((2, 256, 768), BF),
    "bsent": ((16, 32, 768), BF),
    "bmade": ((2, 256, 768), BF),
    "sret": ((16, 32, 768), BF),
    "part_ffn": ((2, 4, 32, 896), BF),
    "land_ffn": ((2, 3, 32, 896), BF),
    "bpart": (ROWS, BF),
    "bland": ((2, 3, 32, 768), BF),
    "gathered": ((2, 4, 32, 896), BF),
    "tail": (ROWS, BF),
    "gains": ((2, 4, 16, 768), BF),
    "dkv": ((8, 256, 384), BF),
    "sib_land": ((4, 256, 384), BF),
    "owner_land": ((3, 256, 384), BF),
    "dense": ((256, 768), F32),
    "gu_grad": ((256, 1024), BF),
    "hidden_dense": ((256, 512), BF),
    "lin": ((256, 640), F32),
    "lin_low": ((256, 640), BF),
    "down_own": ((64, 768), F32),
    "down_stream": (ROWS, BF),
}
SCATTER = {
    "acc": ((2, 2, 16, CHUNK, HALF), BF),
    "pool": ((2, 31, CHUNK, HALF), BF),
    "total": ((2, CHUNK, HALF), F32),
    "other": ((2, 24, HALF), F32),
}
DP_ROWS = ((2, 4, 256, 768), BF)
GRADS = ((2, 16, CHUNK, HALF), BF)


def launch(body, number, name, ins, outs, scratch, args):
    def kernel(*refs):
        names = list(ins) + list(outs) + list(scratch)
        t = Box(names, refs[: len(names)])
        moves, sends, recvs = refs[len(names) :]
        body(t, Moves(moves), Wires(sends, recvs))

    return pl.pallas_call(
        kernel,
        out_shape=[jax.ShapeDtypeStruct(*shape) for shape, space in outs.values()],
        in_specs=list(ins.values()),
        out_specs=[space for shape, space in outs.values()],
        scratch_shapes=[pltpu.VMEM(*shape) for shape in scratch.values()]
        + [
            pltpu.SemaphoreType.DMA((MOVE_SEMS,)),
            pltpu.SemaphoreType.DMA((WIRE_SEMS,)),
            pltpu.SemaphoreType.DMA((WIRE_SEMS,)),
        ],
        compiler_params=pltpu.CompilerParams(
            collective_id=number, has_side_effects=True, vmem_limit_bytes=60 * 2**20
        ),
        name=name,
    )(*args)


def fetcher(moves, pairs):
    coming = {name: moves.go(src, dst) for name, src, dst in pairs}

    def need(*names):
        for name in names:
            if name in coming:
                moves.need(coming.pop(name))

    return need


def pumper(steps):
    steps = iter(steps)

    def pump():
        for step in next(steps, ()):
            step()

    return pump


def prepare(t, moves, wires, *routes):
    y, x, c, z = place()
    others = peers(y, 2 * x + c, z)
    greet(others)
    turn = moves.go(t.table.at[pl.ds(pl.multiple_of((2 * x + c) * 128, 128), 128)], t.turn)
    for layer, route in routes:
        set_route(t, layer, route)
    return y, 2 * x + c, z, others, turn


def pack(t, land, layer, me, columns):
    names = (("o", 0), ("k", 256), ("v", 448), ("q", 640)) if columns is ATTN else (("g", 1024), ("u", 1536), ("d", 2048))
    if columns is ATTN:
        row = lax.broadcasted_iota(jnp.int32, (32, 24), 0)
        one, other = t.again[layer : layer + 1].astype(F32), t.fgain[layer : layer + 1].astype(F32)
        gains = jnp.where(row == 16, one, jnp.where(row == 17, other, 0.0))
        router = jnp.concatenate([t.router[layer].astype(F32), jnp.zeros((16, 24), F32)], axis=0)
        spot = (lanes((32, 128)) == lax.broadcasted_iota(jnp.int32, (32, 128), 0) + ROUTER).astype(BF)
        t.stage[:, 192:256] = t_mm((gains + router).astype(BF), spot)[:, 64:]
        t.stage[:, 832:1024] = jnp.zeros((24, 192), F32)
    for name, left in names:
        ref = getattr(t, name)
        t.stage[:, left : left + ref.shape[2]] = ref[layer].astype(F32)
    left, middle, right = (0, 512, 1024) if columns is ATTN else (1024, 1792, 2560)
    halves = [t.stage[:, left:middle], t.stage[:, middle:right]]
    land[*me, :, columns] = jnp.concatenate(halves, axis=0).astype(BF)


def first_body(t, moves, wires):
    y, e, z, others, turn = prepare(t, moves, wires, (0, t.route), (1, t.route1))
    need = fetcher(moves, [(n, getattr(t, n + "_all").at[0], getattr(t, n)) for n in ("eg", "eu", "ed")])
    me = (e % 2, y * 4 + e // 2)
    pack(t, t.land0, 0, me, ATTN)
    met(others)
    attn, feed = ShortGather(wires, t.land0, ATTN), Gather(wires, t.land0, FEED)
    late = Gather(wires, t.land1, slice(0, 1280))
    attn.step0()
    pack(t, t.land0, 0, me, FEED)
    attn.step1()
    t.own0[...] = t.stream[:, z].astype(F32).reshape(64, 768)
    attn.step2()
    feed.step0()
    attn.step5()
    unpack(t.land0, ATTN, t.w, 0)
    moves.need(turn)

    def feed_ready():
        unpack(t.land0, FEED, t.w, 1024)
        moves.go(t.w, t.w_out)

    def late_ready():
        unpack(t.land1, ATTN, t.w1, 0)
        unpack(t.land1, FEED, t.w1, 1024)

    def late_start():
        pack(t, t.land1, 1, me, ATTN)
        pack(t, t.land1, 1, me, FEED)
        late.step0()

    def fetch():
        for n in ("eg", "eu", "ed"):
            moves.go(getattr(t, n + "_all").at[1], getattr(t, n))

    pump = pumper(
        [
            (feed.step1,),
            (feed.step2, late_start),
            (feed.step3, late.step1),
            (feed.step4, feed.step5, feed_ready, late.step2),
            (late.step3,),
            (late.step4, fetch),
            (late.step5,),
            (late_ready,),
        ]
    )

    def done(*names):
        for name in names:
            if name in SAVED:
                moves.go(getattr(t, name), getattr(t, name + "_out"))

    none = lambda *names: None
    walk, halves, wait = forward_block(
        wires, moves, t, t.w, need, t.stream, t.own0, t.lengths, none, pump, done
    )
    t.cot_own[...] = t.cotangent[:, z].astype(F32).reshape(64, 768)
    halves()
    earlier, wires.open = wires.open, []
    b = t.but(
        kv=t.kv1, ffn_in=t.ffn_in1, arrived=t.arrived1, ret=t.ret1, land=t.land_f1, part=t.part1, own_out=t.own_out1,
        stream_out=t.stream_out1, route=t.route1, sent=t.sent1, made=t.made1,
    )
    moves.finish()
    early = RowWalk(wires, moves, t.arrived, t.rows0, y, e, z)
    early.start(0)
    early.start(1)
    coming = []
    start = lambda: coming.extend(backward_start(wires, b, t.w1, none, t.cotangent))
    pump = pumper([(), (), (lambda: early.pass_on(0), lambda: early.pass_on(1)), (lambda: wires.settle(earlier),), (), (early.finish, start)])
    walk, halves, last_wait = forward_block(
        wires, moves, b, t.w1, none, t.stream_out, t.own_out, t.lengths, wait, pump, none, t.rows1
    )
    pump = pumper([(lambda: walk.pass_on(0), lambda: walk.pass_on(1)), (halves, walk.finish)])
    walk = backward_block(
        wires, moves, b, t.w1, none, t.cotangent, t.cot_own, t.own_out, coming, pump, t.back1, t.land1
    )
    last_wait(0)
    last_wait(1)
    t.outputs[...] = b.stream_out[...]
    t.outputs_own[...] = b.own_out[...]
    moves.go(t.land1, t.grads1)
    t.grad_own[...] = t.down_own[...]
    t.grad_stream[...] = t.down_stream[...]
    walk.finish()
    wires.finish()
    moves.finish()


def third_body(t, moves, wires):
    y, e, z, others, turn = prepare(t, moves, wires, (0, t.route))
    order = ("shares", "w", "gud", "ret", "ffn_in", "ed", "gue", "eg", "eu", "middle", "probs", "kv", "queries", "attended", "normed")

    def source(n):
        if n in SAVED or n == "w":
            return getattr(t, n + "_in")
        return getattr(t, n + "_all").at[0]

    need = fetcher(moves, [(n, source(n), getattr(t, n)) for n in order] + [("grads1", t.grads1, t.acc.at[1])])
    one, feed, attn = [
        Scatter(wires, columns, t.acc.at[n], t.pool.at[n], t.total.at[n], t.other.at[n], t.sums.at[n])
        for n, columns in ((1, slice(0, HALF)), (0, FEED), (0, ATTN))
    ]
    t.own0[...] = t.inputs[:, z].astype(F32).reshape(64, 768)
    moves.need(turn)
    met(others)
    coming = backward_start(wires, t, t.w, need, t.incoming)
    pump = pumper(
        [
            (lambda: need("grads1"), one.step0),
            (),
            (one.step1, feed.step0),
            (one.step2, feed.step1),
            (one.step3, feed.step2),
            (one.step4, feed.step3),
            (one.step5, feed.step4),
        ]
    )
    walk = backward_block(
        wires, moves, t, t.w, need, t.incoming, t.grad_own, t.own0, coming, pump, t.back0, t.acc.at[0]
    )
    attn.step0()
    t.input_grad[...] = t.down_stream[...]
    t.input_own[...] = t.down_own[...]
    attn.step1()
    feed.step5()
    one.step6()
    attn.step2()
    attn.step3()
    feed.step6()
    attn.step4()
    attn.step5()
    attn.step6()
    walk.finish()
    wires.finish()
    moves.finish()


def last_kernel(rows0, rows1, back0, back1, eg, eu, ed, sums, outputs, own, input_grad, own_grad, *rest):
    rows, grads, hidden, gu, sems = rest[-5:]
    g_gate, g_up, g_down, o_out, o_in, o_router, o_again, o_fgain, *o_parts = rest[:-5]
    at = pl.program_id(0) * 2 + pl.program_id(1)
    sources = [(src, back, i) for src, back in ((rows1, back1), (rows0, back0)) for i in range(2)]

    def copies(n):
        src, back, i = sources[n]
        return (
            pltpu.make_async_copy(src.at[i], rows.at[n % 2], sems.at[n % 2, 0]),
            pltpu.make_async_copy(back.at[i], grads.at[n % 2], sems.at[n % 2, 1]),
        )

    for n in range(4):

        @pl.when(at == n)
        def _():
            if n == 0:
                for copy in copies(0):
                    copy.start()
            if n < 3:
                for copy in copies(n + 1):
                    copy.start()
            for copy in copies(n):
                copy.wait()

    slot = at % 2
    for n in range(4):
        some = slice(n * 256, n * 256 + 256)
        mine = rows[slot, n]
        gate, up, hidden_grad = mm(mine, eg[...]), mm(mine, eu[...]), mm_t(grads[slot, n], ed[...])
        s = sigmoid(gate)
        silu = gate * s
        hidden[some] = (silu * up).astype(BF)
        gu[some, :512] = (hidden_grad * up * (s * (1.0 + gate * (1.0 - s)))).astype(BF)
        gu[some, 512:] = (hidden_grad * silu).astype(BF)
    both = t_mm(rows[slot].reshape(1024, 768), gu[...])
    g_gate[...] = both[:, :512]
    g_up[...] = both[:, 512:]
    g_down[...] = t_mm(hidden[...], grads[slot].reshape(1024, 768))

    @pl.when(at == 0)
    def _():
        z = lax.axis_index("tp")
        o_out[...] = outputs[...].astype(F32)
        o_out[:, z] = own[...].reshape(2, 32, 768)
        o_in[...] = input_grad[...].astype(F32)
        o_in[:, z] = own_grad[...].reshape(2, 32, 768)
        pick = (lanes((24, 128)) == lax.broadcasted_iota(jnp.int32, (24, 128), 0) + ROUTER).astype(F32)
        for layer in range(2):
            left, right = sums[layer, 0], sums[layer, 1]
            o_o, o_k, o_v, o_q, o_gate, o_up, o_down = [ref.at[layer] for ref in o_parts]
            o_o[...] = left[:, OUT]
            o_k[...] = left[:, 256:448]
            o_v[:, :64] = left[:, 448:512]
            o_v[:, 64:] = right[:, :128]
            o_q[...] = right[:, 128:320]
            o_gate[...] = left[:, 512:1024]
            o_up[:, :256] = left[:, 1024:]
            o_up[:, 256:] = right[:, 512:768]
            o_down[...] = right[:, 768:]
            small = lax.dot_general(
                pick,
                left[:, SMALL],
                (((1,), (1,)), ((), ())),
                precision=lax.Precision.HIGHEST,
                preferred_element_type=F32,
            )
            o_router[layer] = small[:16]
            o_again[layer : layer + 1] = small[16:17]
            o_fgain[layer : layer + 1] = small[17:18]


def last_results(rows, experts, others):
    wide = pl.BlockSpec((None, None, 768, 512), lambda n, i: (1 - n, i, 0, 0))
    tall = pl.BlockSpec((None, None, 512, 768), lambda n, i: (1 - n, i, 0, 0))
    fixed = lambda shape: pl.BlockSpec(shape, lambda n, i: (0,) * len(shape))
    more = [ROWS, ROWS, (2, 16, 24), (2, 24), (2, 24)] + [(2, 24, n) for n in (192, 192, 192, 192, 512, 512, 512)]
    shapes = [(2, 2, 768, 512), (2, 2, 768, 512), (2, 2, 512, 768), *more]
    return pl.pallas_call(
        last_kernel,
        grid=(2, 2),
        out_shape=[jax.ShapeDtypeStruct(shape, F32) for shape in shapes],
        in_specs=[ANY] * 4 + [wide, wide, tall] + [fixed(other.shape) for other in others],
        out_specs=[wide, wide, tall] + [fixed(shape) for shape in more],
        scratch_shapes=[
            pltpu.VMEM((2, 4, 256, 768), BF),
            pltpu.VMEM((2, 4, 256, 768), BF),
            pltpu.VMEM((1024, 512), BF),
            pltpu.VMEM((1024, 1024), BF),
            pltpu.SemaphoreType.DMA((2, 2)),
        ],
        compiler_params=pltpu.CompilerParams(vmem_limit_bytes=60 * 2**20),
        cost_estimate=pl.CostEstimate(flops=19_400_000_000, bytes_accessed=40_000_000, transcendentals=4_000_000),
        name="expert_grads",
    )(*rows, *experts, *others)


def rotation_table():
    half = HD // 2
    frequency = np.exp(-np.log(10000.0) * np.arange(half) / half)
    angles = np.arange(1024)[:, None] * frequency[None, :]
    cosine, sine = np.cos(angles), np.sin(angles)
    return np.concatenate([cosine, cosine, cosine, cosine, -sine, sine, -sine, sine], axis=1).astype(np.float32)


def shards(
    inputs, lengths, expert_ids, slot_ids, attn_gain, query_weight, key_weight, value_weight, out_weight, ffn_gain, router_weight,
    dense_gate, dense_up, dense_down, expert_gate, expert_up, expert_down, cotangent,
):
    ids, slots = jnp.swapaxes(expert_ids, 2, 3), jnp.swapaxes(slot_ids, 2, 3)
    stream = inputs.reshape(ROWS)
    experts = (expert_gate, expert_up, expert_down)
    common = {"ids": VM, "slots": VM, "table": ANY, "eg_all": ANY, "eu_all": ANY, "ed_all": ANY}
    given = (ids, slots, rotation_table(), *experts)
    always = {"route": ((256, 4), jnp.int32), "turn": ((128, 256), F32)}
    ins = ("stream", "cotangent", "again", "q", "k", "v", "o", "fgain", "router", "g", "u", "d")
    again = ("kv", "ffn_in", "arrived", "ret", "part", "own_out", "stream_out", "sent", "made")
    both = dict(SAVED, **FORWARD)
    *saved, w, last, last_own, grads1, rows0, rows1, back1, grad_own, grad_stream = launch(
        first_body,
        0,
        "forward_backward",
        dict(common, lengths=SMEM, **{n: VM for n in ins}),
        dict(
            {n + "_out": (shape, ANY) for n, shape in SAVED.items()}, w_out=(WEIGHTS["w"], ANY),
            outputs=((ROWS, BF), VM), outputs_own=(((64, 768), F32), VM), grads1=(GRADS, ANY), rows0=(DP_ROWS, ANY),
            rows1=(DP_ROWS, ANY), back1=(DP_ROWS, ANY), grad_own=(((64, 768), F32), VM), grad_stream=((ROWS, BF), VM),
        ),
        dict(
            both, **WEIGHTS, **BACKWARD, **always, **{n + "1": both[n] for n in again}, land_f1=FORWARD["land"],
            route1=always["route"], w1=WEIGHTS["w"], land0=GRADS, land1=GRADS,
            own0=((64, 768), F32), stage=((24, WIDE), F32), cot_own=((64, 768), F32),
        ),
        (
            *given, lengths, stream, cotangent.reshape(ROWS), attn_gain, query_weight, key_weight, value_weight,
            out_weight, ffn_gain, jnp.swapaxes(router_weight, 1, 2), dense_gate, dense_up, dense_down,
        ),
    )
    sums, first, first_own, back0 = launch(
        third_body,
        2,
        "backward_0_scatter",
        dict(common, incoming=VM, grad_own=VM, inputs=VM, **{n + "_in": ANY for n in SAVED}, w_in=ANY, grads1=ANY),
        dict(
            sums=(((2, 2, 24, HALF), F32), VM), input_grad=((ROWS, BF), VM), input_own=(((64, 768), F32), VM), back0=(DP_ROWS, ANY)
        ),
        dict(SAVED, **WEIGHTS, **BACKWARD, **SCATTER, **always, own0=((64, 768), F32)),
        (*given, grad_stream, grad_own, stream, *saved, w, grads1),
    )
    g_eg, g_eu, g_ed, o_out, o_in, g_router, g_again, g_fgain, g_o, g_k, g_v, g_q, g_gate, g_up, g_down = last_results(
        (rows0, rows1, back0, back1), experts, (sums, last, last_own, first, first_own)
    )
    return (
        o_out.reshape(2, 128, 768),
        o_in.reshape(2, 128, 768),
        g_again,
        g_q,
        g_k,
        g_v,
        g_o,
        g_fgain,
        jnp.swapaxes(g_router, 1, 2),
        g_gate,
        g_up,
        g_down,
        g_eg,
        g_eu,
        g_ed,
    )


def solution(mesh):
    return jax.shard_map(
        shards,
        mesh=mesh,
        in_specs=(
            P("dp", "ep", None),
            P("dp"),
            P(None, "dp", "ep", None),
            P(None, "dp", "ep", None),
            P(None, ("dp", "ep")),
            P(None, ("dp", "ep"), "tp"),
            P(None, ("dp", "ep"), "tp"),
            P(None, ("dp", "ep"), "tp"),
            P(None, ("dp", "ep"), "tp"),
            P(None, ("dp", "ep")),
            P(None, ("dp", "ep"), None),
            P(None, ("dp", "ep"), "tp"),
            P(None, ("dp", "ep"), "tp"),
            P(None, ("dp", "ep"), "tp"),
            P(None, "ep", None, "tp"),
            P(None, "ep", None, "tp"),
            P(None, "ep", "tp", None),
            P("dp", "ep", None),
        ),
        out_specs=(
            P("dp", "ep", None),
            P("dp", "ep", None),
            P(None, ("dp", "ep")),
            P(None, ("dp", "ep"), "tp"),
            P(None, ("dp", "ep"), "tp"),
            P(None, ("dp", "ep"), "tp"),
            P(None, ("dp", "ep"), "tp"),
            P(None, ("dp", "ep")),
            P(None, ("dp", "ep"), None),
            P(None, ("dp", "ep"), "tp"),
            P(None, ("dp", "ep"), "tp"),
            P(None, ("dp", "ep"), "tp"),
            P(None, "ep", None, "tp"),
            P(None, "ep", None, "tp"),
            P(None, "ep", "tp", None),
        ),
        check_vma=False,
    )
```

```python
import jax
import jax.numpy as jnp
import numpy as np
from jax import lax
from jax.experimental import pallas as pl
from jax.experimental.pallas import tpu as pltpu
from jax.sharding import PartitionSpec as P

HD = 64
EPS = 1e-06
MESH = pl.DeviceIdType.MESH
BF = jnp.bfloat16
F32 = jnp.float32
VM = pl.BlockSpec(memory_space=pltpu.VMEM)
ANY = pl.BlockSpec(memory_space=pl.ANY)
SMEM = pl.BlockSpec(memory_space=pltpu.SMEM)
WIDE = 2560
HALF = 1280
CHUNK = 48
ATTN = slice(0, 512)
FEED = slice(512, 1280)
SMALL = slice(128, 256)
SPOTS = ((0, 512, 0, 0), (512, 1024, 1, 0), (1024, 1792, 0, 512), (1792, 2560, 1, 512))
ROUTER = 64
GAIN = 80
OUT = slice(0, 192)
QKV = slice(256, 896)
GATE = slice(1024, 1536)
UP = slice(1536, 2048)
GATEUP = slice(1024, 2048)
DOWN = slice(2048, 2560)
ROWS = (2, 4, 32, 768)


class Box:
    def __init__(self, names, refs):
        self.__dict__.update(zip(names, refs, strict=True))

    def but(self, **others):
        return Box([*self.__dict__, *others], [*self.__dict__.values(), *others.values()])


def place():
    y = lax.axis_index("dp")
    e = lax.axis_index("ep")
    z = lax.axis_index("tp")
    return y, e // 2, e % 2, z


def device(y, x, c, z):
    return (y, x * 2 + c, z)


def greet(others):
    for who in others:
        pl.semaphore_signal(pltpu.get_barrier_semaphore(), inc=1, device_id=who, device_id_type=MESH)


def met(others):
    pl.semaphore_wait(pltpu.get_barrier_semaphore(), len(others))


def mm(a, b):
    return lax.dot_general(a, b, (((1,), (0,)), ((), ())), preferred_element_type=F32)


def mm_t(a, b):
    return lax.dot_general(a, b, (((1,), (1,)), ((), ())), preferred_element_type=F32)


def t_mm(a, b):
    return lax.dot_general(a, b, (((0,), (0,)), ((), ())), preferred_element_type=F32)


def lanes(shape):
    return lax.broadcasted_iota(jnp.int32, shape, 1)


def gain_rows(weights):
    pick = (lanes((8, 128)) == lax.broadcasted_iota(jnp.int32, (8, 128), 0) + GAIN).astype(BF)
    return mm_t(pick, weights[:, SMALL])


def rms(values, gain):
    turn = lax.rsqrt(jnp.mean(values * values, axis=-1, keepdims=True) + EPS)
    return values * turn * gain


def rms_back(values, gain, grad):
    turn = lax.rsqrt(jnp.mean(values * values, axis=-1, keepdims=True) + EPS)
    scaled = grad * gain
    back = turn * scaled - values * (turn * turn * turn) * jnp.mean(values * scaled, axis=-1, keepdims=True)
    return back, jnp.sum(grad * values * turn, axis=0, keepdims=True)


def turned(values, cosine, sine):
    width = values.shape[1]
    front = lanes(values.shape) % HD < HD // 2
    other = jnp.where(front, pltpu.roll(values, width - HD // 2, 1), pltpu.roll(values, HD // 2, 1))
    return values * cosine + other * sine


def sigmoid(v):
    return 1.0 / (1.0 + jnp.exp(-v))


def swish_back(gate, up, grad):
    s = sigmoid(gate)
    return (grad * up * s * (1.0 + gate * (1.0 - s))).astype(BF), (grad * gate * s).astype(BF)


def turns(t, sign):
    cosine, sine = t.turn[:, :128], sign * t.turn[:, 128:]
    first = lanes((128, 128)) < HD
    one, none = jnp.ones((128, 128), F32), jnp.zeros((128, 128), F32)
    mixed, mixed_sine = jnp.where(first, cosine, 1.0), jnp.where(first, sine, 0.0)
    cosine = jnp.concatenate([cosine, mixed, one, cosine, mixed], axis=1)
    sine = jnp.concatenate([sine, mixed_sine, none, sine, mixed_sine], axis=1)
    return cosine, sine


def set_route(t, layer, route):
    row = lax.broadcasted_iota(jnp.int32, (16, 128), 0)
    unit = (row == lanes((16, 128))).astype(BF)
    for s in range(2):
        stacked = jnp.zeros((16, 128), jnp.int32)
        for n, ref in enumerate((t.ids, t.slots)):
            for j in range(2):
                stacked = jnp.where(row == 2 * n + j, ref[layer, s, j : j + 1], stacked)
        columns = t_mm(stacked.astype(F32).astype(BF), unit).astype(jnp.int32)
        rows = slice(s * 128, s * 128 + 128)
        for j in range(2):
            expert, slot = columns[:, j : j + 1], columns[:, 2 + j : 3 + j]
            route[rows, j : j + 1] = jnp.where(slot < 32, expert * 32 + slot, 512)
            route[rows, 2 + j : 3 + j] = expert


class Wires:
    def __init__(self, sends, recvs):
        self.sends, self.recvs, self.used, self.open = sends, recvs, 0, []

    def plan(self, src, dst, who, when=None, at=None):
        if at is None:
            at = self.used
            self.used += 1
        copy = pltpu.make_async_remote_copy(
            src_ref=src,
            dst_ref=dst,
            send_sem=self.sends.at[at],
            recv_sem=self.recvs.at[at],
            device_id=who,
            device_id_type=MESH,
        )
        self.open.append((copy, when))
        return copy

    def go(self, src, dst, who):
        copy = self.plan(src, dst, who)
        copy.start()
        return copy

    def settle(self, copies):
        for copy, when in copies:
            if when is None:
                copy.wait_send()
            else:
                pl.when(when)(copy.wait_send)

    def finish(self):
        assert self.used <= self.sends.shape[0]
        self.settle(self.open)


class Moves:
    def __init__(self, sems):
        self.sems, self.used, self.open = sems, 0, []

    def go(self, src, dst):
        copy = pltpu.make_async_copy(src, dst, self.sems.at[self.used])
        self.used += 1
        copy.start()
        self.open.append(copy)
        return copy

    def need(self, copy):
        self.open = [other for other in self.open if other is not copy]
        copy.wait()

    def finish(self):
        assert self.used <= self.sems.shape[0]
        for copy in self.open:
            copy.wait()
        self.open = []


def peers(y, e, z):
    row = [(y, (e + k) % 8, z) for k in range(1, 8)]
    return row + [(y, e, (z + k) % 4) for k in range(1, 4)] + [((y + k) % 4, e, z) for k in range(1, 4)]


class TpSum:
    def __init__(self, wires, parts, land, held):
        self.wires, self.parts, self.land, self.held = wires, parts, land, held
        self.y, self.e, self.z = (lax.axis_index(name) for name in ("dp", "ep", "tp"))
        self.sums, self.spread = [None, None], [None, None]

    def send(self, h):
        self.sums[h] = []
        for k in (1, 3, 2):
            who = (self.z + k) % 4
            copy = self.wires.go(self.parts.at[h, who], self.land.at[h, k - 1], (self.y, self.e, who))
            self.sums[h].append(copy)

    def half(self, h, finish):
        for copy in self.sums[h]:
            copy.wait_recv()
        total = self.parts[h, self.z].astype(F32)
        for k in range(3):
            total += self.land[h, k].astype(F32)
        finish(h, slice(32 * h, 32 * h + 32), total)
        self.spread[h] = self.everywhere(self.held.at[h, self.z])

    def everywhere(self, spot):
        return [self.wires.go(spot, spot, (self.y, self.e, (self.z + k) % 4)) for k in (1, 3, 2)]

    def wait(self, h):
        for copy in self.spread[h]:
            copy.wait_recv()


def scatter_experts(wires, src, dst, y, e, z, i):
    rows = pl.ds(pl.multiple_of(e * 32, 32), 32)
    sent = []
    for k in (1, 7, 2, 6, 3, 5, 4):
        who = (e + k) % 8
        sent.append(wires.go(src.at[2 * who + i], dst.at[i, rows], (y, who, z)))
    dst[i, rows] = src[2 * e + i]
    return lambda: [copy.wait_recv() for copy in sent]


def return_experts(wires, src, dst, y, e, z, i):
    sent = []
    for k in (1, 7, 2, 6, 3, 5, 4):
        who = (e + k) % 8
        rows = pl.ds(pl.multiple_of(who * 32, 32), 32)
        sent.append(wires.go(src.at[i, rows], dst.at[2 * e + i], (y, who, z)))
    dst[2 * e + i] = src[i, pl.ds(pl.multiple_of(e * 32, 32), 32)]
    return lambda: [copy.wait_recv() for copy in sent]


class RowWalk:
    def __init__(self, wires, moves, own, rows, y, e, z):
        self.wires, self.moves, self.own, self.rows = wires, moves, own, rows
        self.up, self.down = ((y + 1) % 4, e, z), ((y + 3) % 4, e, z)
        self.near, self.far = [], []

    def start(self, i):
        own, rows = self.own.at[i], self.rows
        self.near.append(
            (self.wires.go(own, rows.at[i, 1], self.up), self.wires.go(own, rows.at[i, 3], self.down))
        )
        self.moves.go(own, rows.at[i, 0])

    def pass_on(self, i):
        self.near[i][i].wait_recv()
        slot, who = ((1, self.up), (3, self.down))[i]
        self.far.append(self.wires.go(self.rows.at[i, slot], self.rows.at[i, 2], who))

    def finish(self):
        self.near[0][1].wait_recv()
        self.near[1][0].wait_recv()
        for copy in self.far:
            copy.wait_recv()


class Gather:
    def __init__(self, wires, land, columns):
        self.wires, self.land, self.columns = wires, land, columns
        self.y, self.x, self.c, self.z = place()
        self.second, self.far = {}, []

    def who(self, j, d):
        yy = (self.y + j * self.c + d * (1 - self.c) + 8) % 4
        xx = (self.x + j * (1 - self.c) + d * self.c + 8) % 4
        return device(yy, xx, self.c, self.z)

    def spot(self, j, d, rows=slice(None)):
        yy, ee, zz = self.who(j, d)
        return self.land.at[self.c, yy * 4 + ee // 2, rows, self.columns]

    def reach(self, spot, whos):
        return [self.wires.go(spot, spot, who) for who in whos]

    def spread(self, j):
        self.second[j] = self.reach(self.spot(j, 0), [self.who(0, 1), self.who(0, -1)])

    def step0(self):
        self.first = self.reach(self.spot(0, 0), [self.who(1, 0), self.who(-1, 0)])
        self.spread(0)

    def step1(self):
        self.first[0].wait_recv()
        spot = self.spot(-1, 0, pl.ds(0, 32))
        self.on = [self.wires.go(spot, spot, self.who(1, 0))]
        self.spread(-1)
        self.first[1].wait_recv()
        spot = self.spot(1, 0, pl.ds(32, 16))
        self.on.append(self.wires.go(spot, spot, self.who(-1, 0)))
        self.spread(1)

    def step2(self):
        for copy in self.on:
            copy.wait_recv()
        self.spread(2)

    def step3(self):
        for j in (0, -1, 1, 2):
            for n, d in enumerate((-1, 1)):
                self.second[j][n].wait_recv()
                if (j in (0, -1)) == (n == 0):
                    spot = self.spot(j, d)
                    self.far.append(self.wires.go(spot, spot, self.who(0, -d)))

    def step4(self):
        for copy in self.far:
            copy.wait_recv()
        self.pair()

    def pair(self):
        spot = self.land.at[self.c, :, :, self.columns]
        self.swap = self.wires.go(spot, spot, device(self.y, self.x, 1 - self.c, self.z))

    def step5(self):
        self.swap.wait_recv()


class ShortGather(Gather):
    def spread(self, j):
        self.second[j] = self.reach(self.spot(j, 0), [self.who(0, d) for d in (1, -1, 2)])

    def step0(self):
        self.first = self.reach(self.spot(0, 0), [self.who(j, 0) for j in (1, -1, 2)])
        self.spread(0)

    def step1(self):
        for n, j in ((0, -1), (1, 1), (2, 2)):
            self.first[n].wait_recv()
            self.spread(j)

    def step2(self):
        for j in (0, -1, 1, 2):
            for copy in self.second[j]:
                copy.wait_recv()
        self.pair()


def unpack(land, columns, w, left):
    half = columns.stop - columns.start

    def some(p, carry):
        one = land[0, p, :, columns].astype(F32)
        two = land[1, p, :, columns].astype(F32)
        rows = pl.ds(pl.multiple_of(p * CHUNK, CHUNK), CHUNK)
        w[rows, left : left + half] = jnp.concatenate([one[:24], two[:24]], axis=0).astype(BF)
        w[rows, left + half : left + 2 * half] = jnp.concatenate([one[24:], two[24:]], axis=0).astype(BF)
        return carry

    lax.fori_loop(0, 16, some, 0)


def picks(route):
    slots = lanes((256, 512))
    return slots == route[:, 0:1], slots == route[:, 1:2]


class Scatter:
    PLUS, MINUS = (0, -1), (1, 2)

    def __init__(self, wires, columns, *refs):
        self.wires, self.columns = wires, columns
        self.acc, self.pool, self.total, self.other, self.out = refs
        self.y, self.x, self.c, self.z = place()
        self.sibling = device(self.y, self.x, 1 - self.c, self.z)
        self.far, self.near = {}, {}

    def at(self, j, d, core):
        yy = (self.y + j * core + d * (1 - core) + 8) % 4
        xx = (self.x + j * (1 - core) + d * core + 8) % 4
        return yy, xx

    def who(self, j, d):
        yy, xx = self.at(j, d, self.c)
        return device(yy, xx, self.c, self.z)

    def mine(self, j, d, core):
        yy, xx = self.at(j, d, core)
        return yy * 4 + xx

    def chunk(self, core, block):
        return self.acc.at[core, block, :, self.columns]

    def slot(self, n):
        return self.pool.at[n, :, self.columns]

    def add(self, ref, *others):
        total = ref[...].astype(F32)
        for other in others:
            total += other[...].astype(F32)
        ref[...] = total.astype(BF)

    def join(self, j, d):
        block = self.mine(j, d, self.c)
        ref = self.chunk(self.c, block)
        self.add(ref, self.slot(block))
        return ref

    def step0(self):
        half = self.acc.at[1 - self.c, :, :, self.columns]
        self.swap = self.wires.go(half, self.pool.at[pl.ds(0, 16), :, self.columns], self.sibling)

    def step1(self):
        self.swap.wait_recv()
        for j in (0, 1, -1, 2):
            ref = self.join(j, 2)
            n, d = (16 + self.PLUS.index(j), 1) if j in self.PLUS else (18 + self.MINUS.index(j), -1)
            self.far[j] = self.wires.go(ref, self.slot(n), self.who(0, d))
        for j, k in zip(self.MINUS, self.PLUS):
            self.near[j, 1] = self.wires.go(self.join(j, 1), self.slot(20 + j), self.who(0, 1))
            self.near[k, -1] = self.wires.go(self.join(k, -1), self.slot(24 + k % 4), self.who(0, -1))
        self.up = {j: self.join(j, 1) for j in self.PLUS}
        self.down = {j: self.join(j, -1) for j in self.MINUS}

    def step2(self):
        for n, (j, k) in enumerate(zip(self.PLUS, self.MINUS)):
            self.far[j].wait_recv()
            self.add(self.up[j], self.slot(16 + n))
            self.near[j, 1] = self.wires.go(self.up[j], self.slot(20 + j % 4), self.who(0, 1))
            self.far[k].wait_recv()
            self.add(self.down[k], self.slot(18 + n))
            self.near[k, -1] = self.wires.go(self.down[k], self.slot(24 + k), self.who(0, -1))
        self.held = {j: self.join(j, 0) for j in (2, 1, -1, 0)}

    def step3(self):
        for j in (2, 1, -1, 0):
            self.near[j, 1].wait_recv()
            self.near[j, -1].wait_recv()
            ref = self.held[j]
            self.add(ref, self.slot(20 + j % 4), self.slot(24 + j % 4))
            if j == 2:
                spot = self.slot(28)
                self.one = [
                    self.wires.go(ref.at[rows], spot.at[rows], self.who(d, 0))
                    for rows, d in ((pl.ds(0, 32), 1), (pl.ds(32, 16), -1))
                ]

    def step4(self):
        self.last = []
        for n, (rows, d) in enumerate(((pl.ds(0, 32), 1), (pl.ds(32, 16), -1))):
            self.one[n].wait_recv()
            self.add(self.held[d].at[rows], self.slot(28).at[rows])
            self.last.append(self.wires.go(self.held[d], self.slot(29 + n), self.who(d, 0)))

    def step5(self):
        for copy in self.last:
            copy.wait_recv()
        columns = self.columns
        near = self.pool[29, :, columns].astype(F32) + self.pool[30, :, columns].astype(F32)
        self.total[:, columns] = self.held[0][...].astype(F32) + near
        away = pl.ds(pl.multiple_of(24 - 24 * self.c, 8), 24)
        self.trade = self.wires.go(self.total.at[away, columns], self.other.at[:, columns], self.sibling)
        self.out[self.c, :, columns] = self.total[pl.ds(pl.multiple_of(24 * self.c, 8), 24), columns]

    def step6(self):
        self.trade.wait_recv()
        self.out[1 - self.c, :, self.columns] = self.other[:, self.columns]


def forward_block(wires, moves, t, w, need, stream, own, lengths, ready, pump, done, dp_rows=None):
    y, x, c, z = place()
    e = 2 * x + c
    gains = gain_rows(w)
    sibling = (y, e + 1 - 2 * c, z)
    cosine, sine = turns(t, 1.0)
    spans = (slice(0, 128), slice(128, 256))
    first, to_core = [], []
    for s, rows in enumerate(spans):
        ready(s)
        t.normed[rows] = rms(stream[s].reshape(128, 768).astype(F32), gains[0:1]).astype(BF)
        lin = turned(mm(t.normed[rows], w[:, QKV]), cosine, sine).astype(BF)
        t.kv[e, rows] = lin[:, :384]
        t.queries[rows] = lin[:, 384:576]
        here = t.kv.at[e, pl.ds(s * 128, 128)]
        first.append([])
        for k in (1, 3, 2):
            ahead = x + k <= 3
            copy = wires.plan(here, here, (y, (e + 2 * k) % 8, z), ahead)
            pl.when(ahead)(copy.start)
            first[s].append((k, copy))
        to_core.append(wires.plan(here, here, sibling, c == 0))
        pl.when(c == 0)(to_core[s].start)
    done("normed", "queries")
    for j in range(8):

        @pl.when(j > e)
        def _():
            t.kv[j] = jnp.zeros((256, 384), BF)

    pump()
    tp = TpSum(wires, t.part.at[0], t.land.at[0], t.ffn_in)
    at_key = lanes((128, 1024))
    at_query = lax.broadcasted_iota(jnp.int32, (128, 1024), 0) + e * 128
    for s, rows in enumerate(spans):
        second = []
        for k, copy in first[s]:
            behind = x - k >= 0
            there = t.kv.at[(e + 8 - 2 * k) % 8, pl.ds(s * 128, 128)]
            on = wires.plan(there, there, sibling, behind)

            @pl.when(behind)
            def _():
                copy.wait_recv()
                on.start()

            second.append((behind, on))
        pl.when(c == 1)(to_core[s].wait_recv)
        for behind, on in second:
            pl.when(behind)(on.wait_recv)
        allowed = (at_key <= at_query) & (at_key < lengths[s])
        for h in range(3):
            keys = t.kv[:, rows, 64 * h : 64 * h + 64].reshape(1024, 64)
            vals = t.kv[:, rows, 192 + 64 * h : 256 + 64 * h].reshape(1024, 64)
            scores = jnp.where(allowed, mm_t(t.queries[rows, 64 * h : 64 * h + 64], keys) * HD**-0.5, -1e30)
            expd = jnp.exp(scores - jnp.max(scores, axis=-1, keepdims=True))
            low = (expd / jnp.sum(expd, axis=-1, keepdims=True)).astype(BF)
            t.probs[3 * s + h] = low
            t.attended[rows, 64 * h : 64 * h + 64] = mm(low, vals).astype(BF)
        t.part[0, s] = mm_t(t.attended[rows], w[:, OUT]).astype(BF).reshape(4, 32, 768)
        tp.send(s)
    done("kv", "probs", "attended")
    pump()

    def finish(h, rows, total):
        t.middle[rows] = own[rows] + total
        t.ffn_in[h, z] = rms(t.middle[rows], gains[1:2]).astype(BF)

    ids = t.route[...]
    pick0, pick1 = picks(ids)
    placed = (pick0 | pick1).astype(BF)
    tp.half(0, finish)
    tp.half(1, finish)
    done("middle")
    pump()
    tp.wait(0)
    tp.wait(1)
    done("ffn_in")
    rows_in = t.ffn_in[...].reshape(256, 768)
    t.sent[...] = t_mm(placed, rows_in).astype(BF).reshape(16, 32, 768)
    coming = [scatter_experts(wires, t.sent, t.arrived, y, e, z, i) for i in range(2)]
    pump()
    logits = mm(rows_in, w[:, SMALL])
    lane = lanes((256, 128))
    chosen = [
        jnp.sum(jnp.where(lane == ids[:, 2 + j : 3 + j] + ROUTER, logits, 0.0), axis=-1, keepdims=True)
        for j in range(2)
    ]
    top = jnp.maximum(chosen[0], chosen[1])
    expd = [jnp.exp(v - top) for v in chosen]
    share = [v / (expd[0] + expd[1]) for v in expd]
    t.shares[...] = jnp.where(lane == 0, share[0], jnp.where(lane == 1, share[1], 0.0))
    t.gud[...] = mm(rows_in, w[:, GATEUP])
    gate, up = t.gud[:, :512], t.gud[:, 512:]
    hidden = (gate * sigmoid(gate) * up).astype(BF)
    dense = mm_t(hidden, w[:, DOWN])
    done("gud", "shares")
    pump()
    need("eg", "eu", "ed")
    walk = None if dp_rows is None else RowWalk(wires, moves, t.arrived, dp_rows, y, e, z)
    back = []
    for i in range(2):
        coming[i]()
        t.gue[i, :, :512] = mm(t.arrived[i], t.eg[i])
        t.gue[i, :, 512:] = mm(t.arrived[i], t.eu[i])
        gate, up = t.gue[i, :, :512], t.gue[i, :, 512:]
        hidden = (gate * sigmoid(gate) * up).astype(BF)
        t.made[i] = mm(hidden, t.ed[i]).astype(BF)
        back.append(return_experts(wires, t.made, t.ret, y, e, z, i))
        if walk is not None:
            walk.start(i)
    done("arrived", "gue")
    mix = (jnp.where(pick0, share[0], 0.0) + jnp.where(pick1, share[1], 0.0)).astype(BF)
    pump()
    for wait in back:
        wait()
    done("ret")
    tp = TpSum(wires, t.part.at[1], t.land.at[1], t.stream_out)
    for h, rows in enumerate(spans):
        moe = mm(mix[rows], t.ret[...].reshape(512, 768))
        t.part[1, h] = (dense[rows] + moe).astype(BF).reshape(4, 32, 768)
        tp.send(h)
    pump()

    def finish(h, rows, total):
        result = t.middle[rows] + total
        t.own_out[rows] = result
        t.stream_out[h, z] = result.astype(BF)

    def halves():
        tp.half(0, finish)
        tp.half(1, finish)
        done("own_out")
        pump()

    return walk, halves, tp.wait


def backward_start(wires, t, w, need, incoming):
    y, x, c, z = place()
    e = 2 * x + c
    need("shares")
    ffn_grad = incoming[...].reshape(256, 768)
    pick0, pick1 = picks(t.route[...])
    mix = (jnp.where(pick0, t.shares[:, 0:1], 0.0) + jnp.where(pick1, t.shares[:, 1:2], 0.0)).astype(BF)
    t.bsent[...] = t_mm(mix, ffn_grad).astype(BF).reshape(16, 32, 768)
    coming = [scatter_experts(wires, t.bsent, t.back, y, e, z, i) for i in range(2)]
    need("w", "gud", "ffn_in")
    gate, up = t.gud[:, :512], t.gud[:, 512:]
    hidden_dense = (gate * sigmoid(gate) * up).astype(BF)
    gate_grad, up_grad = swish_back(gate, up, mm(ffn_grad, w[:, DOWN]))
    gu_grad = jnp.concatenate([gate_grad, up_grad], axis=1)
    t.dense[...] = mm_t(gu_grad, w[:, GATEUP])
    t.gu_grad[...] = gu_grad
    t.hidden_dense[...] = hidden_dense
    return coming


def backward_block(wires, moves, t, w, need, incoming, grad_own, own, coming, pump, dp_rows, grads):
    y, x, c, z = place()
    e = 2 * x + c

    def keep(columns, values):
        for start, stop, half, lane in SPOTS:
            left, right = max(columns.start, start), min(columns.stop, stop)
            if left < right:
                some = values[:, left - columns.start : right - columns.start].astype(BF)
                lane += left - start
                grads[half, :, :, lane : lane + right - left] = some.reshape(16, CHUNK, right - left)

    need("ret")
    ffn_grad = incoming[...].reshape(256, 768)
    rows_in = t.ffn_in[...].reshape(256, 768)
    gains = gain_rows(w)
    pick0, pick1 = picks(t.route[...])
    match = mm_t(ffn_grad, t.ret[...].reshape(512, 768))
    share_grad = [
        jnp.sum(jnp.where(pick, match, 0.0), axis=-1, keepdims=True) for pick in (pick0, pick1)
    ]
    lane = lanes((256, 128))
    extra = jnp.where(lane == 0, share_grad[0], jnp.where(lane == 1, share_grad[1], 0.0))
    t.part_ffn[:, :, :, 768:] = extra.astype(BF).reshape(2, 4, 32, 128)
    pump()
    need("ed", "gue", "eg", "eu")
    walk = RowWalk(wires, moves, t.back, dp_rows, y, e, z)
    back = []
    for i in range(2):
        coming[i]()
        hidden_grad = mm_t(t.back[i], t.ed[i])
        gate_e, up_e = swish_back(t.gue[i, :, :512], t.gue[i, :, 512:], hidden_grad)
        t.bmade[i] = (mm_t(gate_e, t.eg[i]) + mm_t(up_e, t.eu[i])).astype(BF)
        back.append(return_experts(wires, t.bmade, t.sret, y, e, z, i))
        walk.start(i)
    pump()
    placed = (pick0 | pick1).astype(BF)
    keep(GATEUP, t_mm(rows_in, t.gu_grad[...]))
    keep(DOWN, t_mm(ffn_grad, t.hidden_dense[...]))
    for wait in back:
        wait()
    tp = TpSum(wires, t.part_ffn, t.land_ffn, t.gathered)
    spans = (slice(0, 128), slice(128, 256))
    for h, rows in enumerate(spans):
        total = t.dense[rows] + mm(placed[rows], t.sret[...].reshape(512, 768))
        t.part_ffn[h, :, :, :768] = total.astype(BF).reshape(4, 32, 768)
        tp.send(h)
    pump()
    need("middle")
    top = lax.broadcasted_iota(jnp.int32, (16, 768), 0) == 0
    lane32 = lanes((32, 128))
    gain_parts = []

    def finish(h, rows, total):
        mine = pl.ds(pl.multiple_of(128 * h + 32 * z, 32), 32)
        share, ids = t.shares[mine], t.route[mine]
        weigh = share[:, 0:1] * total[:, 768:769] + share[:, 1:2] * total[:, 769:770]
        logit_grad = jnp.zeros((32, 128), F32)
        for j in range(2):
            chosen_grad = share[:, j : j + 1] * (total[:, 768 + j : 769 + j] - weigh)
            logit_grad += jnp.where(lane32 == ids[:, 2 + j : 3 + j] + ROUTER, chosen_grad, 0.0)
        logit_grad = logit_grad.astype(BF)
        grad_in = total[:, :768] + mm_t(logit_grad, w[:, SMALL])
        back_norm, gain_two = rms_back(t.middle[rows], gains[1:2], grad_in)
        gain_parts.append(gain_two)
        middle_grad = grad_own[rows] + back_norm
        t.down_own[rows] = middle_grad
        t.gathered[h, z, :, :768] = middle_grad.astype(BF)
        t.gathered[h, z, :, 768:] = logit_grad

    tp.half(0, finish)
    tp.half(1, finish)
    t.gains[1, z] = jnp.where(top, gain_parts[0] + gain_parts[1], 0.0).astype(BF)
    gain_copies = tp.everywhere(t.gains.at[1, z])
    grads_tp = tp
    pump()
    need("probs", "kv", "queries", "attended", "normed")
    sibling = (y, e + 1 - 2 * c, z)

    def attend_back(s, between):
        rows = spans[s]
        grad = t.gathered[s, :, :, :768].reshape(128, 768)
        attended_grad = mm(grad, w[:, OUT]).astype(BF)
        for h in range(3):
            cols = slice(64 * h, 64 * h + 64)
            late = slice(192 + 64 * h, 256 + 64 * h)
            keys = t.kv[:, rows, cols].reshape(1024, 64)
            vals = t.kv[:, rows, late].reshape(1024, 64)
            low = t.probs[3 * s + h]
            wide = low.astype(F32)
            grad_here = attended_grad[:, cols]
            probs_grad = mm_t(grad_here, vals)
            kept = jnp.sum(wide * probs_grad, axis=-1, keepdims=True)
            score_grad = (wide * (probs_grad - kept)).astype(BF)
            t.lin[rows, 384 + 64 * h : 448 + 64 * h] = mm(score_grad, keys) * HD**-0.5
            keys_grad = t_mm(score_grad, t.queries[rows, cols]) * HD**-0.5
            t.dkv[:, rows, cols] = keys_grad.astype(BF).reshape(8, 128, 64)
            t.dkv[:, rows, late] = t_mm(low, grad_here).astype(BF).reshape(8, 128, 64)
            if h == 0:
                between()

    def swap(s):
        rows = pl.ds(s * 128, 128)
        swaps = []
        for k in range(4):
            gives = (x - k >= 0) & ((c == 1) if k == 0 else True)
            takes = (x - k >= 0) & ((c == 0) if k == 0 else True)
            block = (2 * (x - k) + 1 - c + 8) % 8
            copy = wires.plan(t.dkv.at[block, rows], t.sib_land.at[k, rows], sibling, gives)
            pl.when(gives)(copy.start)
            swaps.append((takes, copy))
        return swaps

    def send_far(s, swaps):
        rows = pl.ds(s * 128, 128)
        far = []
        for k in (1, 3, 2):
            gives, takes = x - k >= 0, x + k <= 3
            block = (e - 2 * k + 8) % 8
            send = wires.plan(t.dkv.at[block, rows], t.owner_land.at[k - 1, rows], (y, block, z), gives)

            @pl.when(gives)
            def _():
                swaps[k][1].wait_recv()
                both = t.dkv[block, rows].astype(F32) + t.sib_land[k, rows].astype(F32)
                t.dkv[block, rows] = both.astype(BF)
                send.start()

            far.append((k, takes, send))
        return far

    cosine, sine = turns(t, -1.0)
    tp = TpSum(wires, t.bpart, t.bland, t.tail)

    def collect(s, swaps, far):
        rows = spans[s]
        t.lin[rows, :384] = t.dkv[e, rows].astype(F32)
        t.lin[rows, 576:] = jnp.zeros((128, 64), F32)

        @pl.when(swaps[0][0])
        def _():
            swaps[0][1].wait_recv()
            t.lin[rows, :384] += t.sib_land[0, rows].astype(F32)

        for k, takes, copy in far:

            @pl.when(takes)
            def _():
                copy.wait_recv()
                t.lin[rows, :384] += t.owner_land[k - 1, rows].astype(F32)

        t.lin_low[rows] = turned(t.lin[rows], cosine, sine).astype(BF)
        t.bpart[s] = mm_t(t.lin_low[rows], w[:, QKV]).astype(BF).reshape(4, 32, 768)
        tp.send(s)

    grads_tp.wait(0)
    attend_back(0, lambda: None)
    swaps0 = swap(0)
    walk.pass_on(0)
    walk.pass_on(1)
    grads_tp.wait(1)
    far0 = []
    attend_back(1, lambda: far0.extend(send_far(0, swaps0)))
    swaps1 = swap(1)
    keep(OUT, t_mm(t.gathered[:, :, :, :768].reshape(256, 768), t.attended[...]))
    far1 = send_far(1, swaps1)
    router_grad = t_mm(rows_in, t.gathered[:, :, :, 768:].reshape(256, 128))
    pump()
    collect(0, swaps0, far0)
    collect(1, swaps1, far1)
    tail_parts = []

    def finish(h, rows, total):
        back_norm, gain_one = rms_back(own[rows], gains[0:1], total)
        tail_parts.append(gain_one)
        result = t.down_own[rows] + back_norm
        t.down_own[rows] = result
        t.tail[h, z] = result.astype(BF)

    keep(QKV, t_mm(t.normed[...], t.lin_low[...]))
    pump()
    tp.half(0, finish)
    tp.half(1, finish)
    t.gains[0, z] = jnp.where(top, tail_parts[0] + tail_parts[1], 0.0).astype(BF)
    gain_copies += tp.everywhere(t.gains.at[0, z])
    pump()
    tp.wait(0)
    tp.wait(1)
    t.down_stream[...] = t.tail[...]
    for copy in gain_copies:
        copy.wait_recv()
    at_row = lax.broadcasted_iota(jnp.int32, (16, 768), 0)
    gain_grads = jnp.zeros((16, 768), F32)
    for n in range(2):
        total = jnp.sum(t.gains[n].astype(F32).reshape(64, 768), axis=0, keepdims=True)
        gain_grads = jnp.where(at_row == n, total, gain_grads)
    spot = (lanes((16, 128)) == lax.broadcasted_iota(jnp.int32, (16, 128), 0) + GAIN).astype(BF)
    keep(slice(192, 256), (router_grad + t_mm(gain_grads.astype(BF), spot))[:, 64:])
    return walk


MOVE_SEMS, WIRE_SEMS = 48, 320
SAVED = {
    "normed": ((256, 768), BF),
    "queries": ((256, 192), BF),
    "kv": ((8, 256, 384), BF),
    "probs": ((6, 128, 1024), BF),
    "attended": ((256, 192), BF),
    "middle": ((64, 768), F32),
    "ffn_in": (ROWS, BF),
    "gud": ((256, 1024), F32),
    "gue": ((2, 256, 1024), F32),
    "ret": ((16, 32, 768), BF),
    "shares": ((256, 128), F32),
}
WEIGHTS = {"w": ((768, WIDE), BF), "eg": ((2, 768, 512), BF), "eu": ((2, 768, 512), BF), "ed": ((2, 512, 768), BF)}
FORWARD = {
    "arrived": ((2, 256, 768), BF),
    "own_out": ((64, 768), F32),
    "stream_out": (ROWS, BF),
    "part": ((2, *ROWS), BF),
    "land": ((2, 2, 3, 32, 768), BF),
    "sent": ((16, 32, 768), BF),
    "made": ((2, 256, 768), BF),
}
BACKWARD = {
    "back": ((2, 256, 768), BF),
    "bsent": ((16, 32, 768), BF),
    "bmade": ((2, 256, 768), BF),
    "sret": ((16, 32, 768), BF),
    "part_ffn": ((2, 4, 32, 896), BF),
    "land_ffn": ((2, 3, 32, 896), BF),
    "bpart": (ROWS, BF),
    "bland": ((2, 3, 32, 768), BF),
    "gathered": ((2, 4, 32, 896), BF),
    "tail": (ROWS, BF),
    "gains": ((2, 4, 16, 768), BF),
    "dkv": ((8, 256, 384), BF),
    "sib_land": ((4, 256, 384), BF),
    "owner_land": ((3, 256, 384), BF),
    "dense": ((256, 768), F32),
    "gu_grad": ((256, 1024), BF),
    "hidden_dense": ((256, 512), BF),
    "lin": ((256, 640), F32),
    "lin_low": ((256, 640), BF),
    "down_own": ((64, 768), F32),
    "down_stream": (ROWS, BF),
}
SCATTER = {
    "acc": ((2, 2, 16, CHUNK, HALF), BF),
    "pool": ((2, 31, CHUNK, HALF), BF),
    "total": ((2, CHUNK, HALF), F32),
    "other": ((2, 24, HALF), F32),
}
DP_ROWS = ((2, 4, 256, 768), BF)
GRADS = ((2, 16, CHUNK, HALF), BF)


def launch(body, number, name, ins, outs, scratch, args):
    def kernel(*refs):
        names = list(ins) + list(outs) + list(scratch)
        t = Box(names, refs[: len(names)])
        moves, sends, recvs = refs[len(names) :]
        body(t, Moves(moves), Wires(sends, recvs))

    return pl.pallas_call(
        kernel,
        out_shape=[jax.ShapeDtypeStruct(*shape) for shape, space in outs.values()],
        in_specs=list(ins.values()),
        out_specs=[space for shape, space in outs.values()],
        scratch_shapes=[pltpu.VMEM(*shape) for shape in scratch.values()]
        + [
            pltpu.SemaphoreType.DMA((MOVE_SEMS,)),
            pltpu.SemaphoreType.DMA((WIRE_SEMS,)),
            pltpu.SemaphoreType.DMA((WIRE_SEMS,)),
        ],
        compiler_params=pltpu.CompilerParams(
            collective_id=number, has_side_effects=True, vmem_limit_bytes=60 * 2**20
        ),
        name=name,
    )(*args)


def fetcher(moves, pairs):
    coming = {name: moves.go(src, dst) for name, src, dst in pairs}

    def need(*names):
        for name in names:
            if name in coming:
                moves.need(coming.pop(name))

    return need


def pumper(steps):
    steps = iter(steps)

    def pump():
        for step in next(steps, ()):
            step()

    return pump


def prepare(t, moves, wires, *routes):
    y, x, c, z = place()
    others = peers(y, 2 * x + c, z)
    greet(others)
    turn = moves.go(t.table.at[pl.ds(pl.multiple_of((2 * x + c) * 128, 128), 128)], t.turn)
    for layer, route in routes:
        set_route(t, layer, route)
    return y, 2 * x + c, z, others, turn


def pack(t, land, layer, me, columns):
    names = (("o", 0), ("k", 256), ("v", 448), ("q", 640)) if columns is ATTN else (("g", 1024), ("u", 1536), ("d", 2048))
    if columns is ATTN:
        row = lax.broadcasted_iota(jnp.int32, (32, 24), 0)
        one, other = t.again[layer : layer + 1].astype(F32), t.fgain[layer : layer + 1].astype(F32)
        gains = jnp.where(row == 16, one, jnp.where(row == 17, other, 0.0))
        router = jnp.concatenate([t.router[layer].astype(F32), jnp.zeros((16, 24), F32)], axis=0)
        spot = (lanes((32, 128)) == lax.broadcasted_iota(jnp.int32, (32, 128), 0) + ROUTER).astype(BF)
        t.stage[:, 192:256] = t_mm((gains + router).astype(BF), spot)[:, 64:]
        t.stage[:, 832:1024] = jnp.zeros((24, 192), F32)
    for name, left in names:
        ref = getattr(t, name)
        t.stage[:, left : left + ref.shape[2]] = ref[layer].astype(F32)
    left, middle, right = (0, 512, 1024) if columns is ATTN else (1024, 1792, 2560)
    halves = [t.stage[:, left:middle], t.stage[:, middle:right]]
    land[*me, :, columns] = jnp.concatenate(halves, axis=0).astype(BF)


def first_body(t, moves, wires):
    y, e, z, others, turn = prepare(t, moves, wires, (0, t.route), (1, t.route1))
    need = fetcher(moves, [(n, getattr(t, n + "_all").at[0], getattr(t, n)) for n in ("eg", "eu", "ed")])
    me = (e % 2, y * 4 + e // 2)
    pack(t, t.land0, 0, me, ATTN)
    met(others)
    attn, feed = ShortGather(wires, t.land0, ATTN), Gather(wires, t.land0, FEED)
    late = Gather(wires, t.land1, slice(0, 1280))
    attn.step0()
    pack(t, t.land0, 0, me, FEED)
    attn.step1()
    t.own0[...] = t.stream[:, z].astype(F32).reshape(64, 768)
    attn.step2()
    feed.step0()
    attn.step5()
    unpack(t.land0, ATTN, t.w, 0)
    moves.need(turn)

    def feed_ready():
        unpack(t.land0, FEED, t.w, 1024)
        moves.go(t.w, t.w_out)

    def late_ready():
        unpack(t.land1, ATTN, t.w1, 0)
        unpack(t.land1, FEED, t.w1, 1024)

    def late_start():
        pack(t, t.land1, 1, me, ATTN)
        pack(t, t.land1, 1, me, FEED)
        late.step0()

    def fetch():
        for n in ("eg", "eu", "ed"):
            moves.go(getattr(t, n + "_all").at[1], getattr(t, n))

    pump = pumper(
        [
            (feed.step1,),
            (feed.step2, late_start),
            (feed.step3, late.step1),
            (feed.step4, feed.step5, feed_ready, late.step2),
            (late.step3,),
            (late.step4, fetch),
            (late.step5,),
            (late_ready,),
        ]
    )

    def done(*names):
        for name in names:
            if name in SAVED:
                moves.go(getattr(t, name), getattr(t, name + "_out"))

    none = lambda *names: None
    walk, halves, wait = forward_block(
        wires, moves, t, t.w, need, t.stream, t.own0, t.lengths, none, pump, done
    )
    t.cot_own[...] = t.cotangent[:, z].astype(F32).reshape(64, 768)
    halves()
    earlier, wires.open = wires.open, []
    b = t.but(
        kv=t.kv1, ffn_in=t.ffn_in1, arrived=t.arrived1, ret=t.ret1, land=t.land_f1, part=t.part1, own_out=t.own_out1,
        stream_out=t.stream_out1, route=t.route1, sent=t.sent1, made=t.made1,
    )
    moves.finish()
    early = RowWalk(wires, moves, t.arrived, t.rows0, y, e, z)
    early.start(0)
    early.start(1)
    coming = []
    start = lambda: coming.extend(backward_start(wires, b, t.w1, none, t.cotangent))
    pump = pumper([(), (), (lambda: early.pass_on(0), lambda: early.pass_on(1)), (lambda: wires.settle(earlier),), (), (early.finish, start)])
    walk, halves, last_wait = forward_block(
        wires, moves, b, t.w1, none, t.stream_out, t.own_out, t.lengths, wait, pump, none, t.rows1
    )
    pump = pumper([(lambda: walk.pass_on(0), lambda: walk.pass_on(1)), (halves, walk.finish)])
    walk = backward_block(
        wires, moves, b, t.w1, none, t.cotangent, t.cot_own, t.own_out, coming, pump, t.back1, t.land1
    )
    last_wait(0)
    last_wait(1)
    t.outputs[...] = b.stream_out[...]
    t.outputs_own[...] = b.own_out[...]
    moves.go(t.land1, t.grads1)
    t.grad_own[...] = t.down_own[...]
    t.grad_stream[...] = t.down_stream[...]
    walk.finish()
    wires.finish()
    moves.finish()


def third_body(t, moves, wires):
    y, e, z, others, turn = prepare(t, moves, wires, (0, t.route))
    order = ("shares", "w", "gud", "ret", "ffn_in", "ed", "gue", "eg", "eu", "middle", "probs", "kv", "queries", "attended", "normed")

    def source(n):
        if n in SAVED or n == "w":
            return getattr(t, n + "_in")
        return getattr(t, n + "_all").at[0]

    need = fetcher(moves, [(n, source(n), getattr(t, n)) for n in order] + [("grads1", t.grads1, t.acc.at[1])])
    one, feed, attn = [
        Scatter(wires, columns, t.acc.at[n], t.pool.at[n], t.total.at[n], t.other.at[n], t.sums.at[n])
        for n, columns in ((1, slice(0, HALF)), (0, FEED), (0, ATTN))
    ]
    t.own0[...] = t.inputs[:, z].astype(F32).reshape(64, 768)
    moves.need(turn)
    met(others)
    coming = backward_start(wires, t, t.w, need, t.incoming)
    pump = pumper(
        [
            (lambda: need("grads1"), one.step0),
            (),
            (one.step1, feed.step0),
            (one.step2, feed.step1),
            (one.step3, feed.step2),
            (one.step4, feed.step3),
            (one.step5, feed.step4),
        ]
    )
    walk = backward_block(
        wires, moves, t, t.w, need, t.incoming, t.grad_own, t.own0, coming, pump, t.back0, t.acc.at[0]
    )
    attn.step0()
    t.input_grad[...] = t.down_stream[...]
    t.input_own[...] = t.down_own[...]
    attn.step1()
    feed.step5()
    one.step6()
    attn.step2()
    attn.step3()
    feed.step6()
    attn.step4()
    attn.step5()
    attn.step6()
    walk.finish()
    wires.finish()
    moves.finish()


def last_kernel(rows0, rows1, back0, back1, eg, eu, ed, sums, outputs, own, input_grad, own_grad, *rest):
    rows, grads, hidden, gu, sems = rest[-5:]
    g_gate, g_up, g_down, o_out, o_in, o_router, o_again, o_fgain, *o_parts = rest[:-5]
    at = pl.program_id(0) * 2 + pl.program_id(1)
    sources = [(src, back, i) for src, back in ((rows1, back1), (rows0, back0)) for i in range(2)]

    def copies(n):
        src, back, i = sources[n]
        return (
            pltpu.make_async_copy(src.at[i], rows.at[n % 2], sems.at[n % 2, 0]),
            pltpu.make_async_copy(back.at[i], grads.at[n % 2], sems.at[n % 2, 1]),
        )

    for n in range(4):

        @pl.when(at == n)
        def _():
            if n == 0:
                for copy in copies(0):
                    copy.start()
            if n < 3:
                for copy in copies(n + 1):
                    copy.start()
            for copy in copies(n):
                copy.wait()

    slot = at % 2
    for n in range(4):
        some = slice(n * 256, n * 256 + 256)
        mine = rows[slot, n]
        gate, up, hidden_grad = mm(mine, eg[...]), mm(mine, eu[...]), mm_t(grads[slot, n], ed[...])
        s = sigmoid(gate)
        silu = gate * s
        hidden[some] = (silu * up).astype(BF)
        gu[some, :512] = (hidden_grad * up * (s * (1.0 + gate * (1.0 - s)))).astype(BF)
        gu[some, 512:] = (hidden_grad * silu).astype(BF)
    both = t_mm(rows[slot].reshape(1024, 768), gu[...])
    g_gate[...] = both[:, :512]
    g_up[...] = both[:, 512:]
    g_down[...] = t_mm(hidden[...], grads[slot].reshape(1024, 768))

    @pl.when(at == 0)
    def _():
        z = lax.axis_index("tp")
        o_out[...] = outputs[...].astype(F32)
        o_out[:, z] = own[...].reshape(2, 32, 768)
        o_in[...] = input_grad[...].astype(F32)
        o_in[:, z] = own_grad[...].reshape(2, 32, 768)
        pick = (lanes((24, 128)) == lax.broadcasted_iota(jnp.int32, (24, 128), 0) + ROUTER).astype(F32)
        for layer in range(2):
            left, right = sums[layer, 0], sums[layer, 1]
            o_o, o_k, o_v, o_q, o_gate, o_up, o_down = [ref.at[layer] for ref in o_parts]
            o_o[...] = left[:, OUT]
            o_k[...] = left[:, 256:448]
            o_v[:, :64] = left[:, 448:512]
            o_v[:, 64:] = right[:, :128]
            o_q[...] = right[:, 128:320]
            o_gate[...] = left[:, 512:1024]
            o_up[:, :256] = left[:, 1024:]
            o_up[:, 256:] = right[:, 512:768]
            o_down[...] = right[:, 768:]
            small = lax.dot_general(
                pick,
                left[:, SMALL],
                (((1,), (1,)), ((), ())),
                precision=lax.Precision.HIGHEST,
                preferred_element_type=F32,
            )
            o_router[layer] = small[:16]
            o_again[layer : layer + 1] = small[16:17]
            o_fgain[layer : layer + 1] = small[17:18]


def last_results(rows, experts, others):
    wide = pl.BlockSpec((None, None, 768, 512), lambda n, i: (1 - n, i, 0, 0))
    tall = pl.BlockSpec((None, None, 512, 768), lambda n, i: (1 - n, i, 0, 0))
    fixed = lambda shape: pl.BlockSpec(shape, lambda n, i: (0,) * len(shape))
    more = [ROWS, ROWS, (2, 16, 24), (2, 24), (2, 24)] + [(2, 24, n) for n in (192, 192, 192, 192, 512, 512, 512)]
    shapes = [(2, 2, 768, 512), (2, 2, 768, 512), (2, 2, 512, 768), *more]
    return pl.pallas_call(
        last_kernel,
        grid=(2, 2),
        out_shape=[jax.ShapeDtypeStruct(shape, F32) for shape in shapes],
        in_specs=[ANY] * 4 + [wide, wide, tall] + [fixed(other.shape) for other in others],
        out_specs=[wide, wide, tall] + [fixed(shape) for shape in more],
        scratch_shapes=[
            pltpu.VMEM((2, 4, 256, 768), BF),
            pltpu.VMEM((2, 4, 256, 768), BF),
            pltpu.VMEM((1024, 512), BF),
            pltpu.VMEM((1024, 1024), BF),
            pltpu.SemaphoreType.DMA((2, 2)),
        ],
        compiler_params=pltpu.CompilerParams(vmem_limit_bytes=60 * 2**20),
        cost_estimate=pl.CostEstimate(flops=19_400_000_000, bytes_accessed=40_000_000, transcendentals=4_000_000),
        name="expert_grads",
    )(*rows, *experts, *others)


def rotation_table():
    half = HD // 2
    frequency = np.exp(-np.log(10000.0) * np.arange(half) / half)
    angles = np.arange(1024)[:, None] * frequency[None, :]
    cosine, sine = np.cos(angles), np.sin(angles)
    return np.concatenate([cosine, cosine, cosine, cosine, -sine, sine, -sine, sine], axis=1).astype(np.float32)


def shards(
    inputs, lengths, expert_ids, slot_ids, attn_gain, query_weight, key_weight, value_weight, out_weight, ffn_gain, router_weight,
    dense_gate, dense_up, dense_down, expert_gate, expert_up, expert_down, cotangent,
):
    ids, slots = jnp.swapaxes(expert_ids, 2, 3), jnp.swapaxes(slot_ids, 2, 3)
    stream = inputs.reshape(ROWS)
    experts = (expert_gate, expert_up, expert_down)
    common = {"ids": VM, "slots": VM, "table": ANY, "eg_all": ANY, "eu_all": ANY, "ed_all": ANY}
    given = (ids, slots, rotation_table(), *experts)
    always = {"route": ((256, 4), jnp.int32), "turn": ((128, 256), F32)}
    ins = ("stream", "cotangent", "again", "q", "k", "v", "o", "fgain", "router", "g", "u", "d")
    again = ("kv", "ffn_in", "arrived", "ret", "part", "own_out", "stream_out", "sent", "made")
    both = dict(SAVED, **FORWARD)
    *saved, w, last, last_own, grads1, rows0, rows1, back1, grad_own, grad_stream = launch(
        first_body,
        0,
        "forward_backward",
        dict(common, lengths=SMEM, **{n: VM for n in ins}),
        dict(
            {n + "_out": (shape, ANY) for n, shape in SAVED.items()}, w_out=(WEIGHTS["w"], ANY),
            outputs=((ROWS, BF), VM), outputs_own=(((64, 768), F32), VM), grads1=(GRADS, ANY), rows0=(DP_ROWS, ANY),
            rows1=(DP_ROWS, ANY), back1=(DP_ROWS, ANY), grad_own=(((64, 768), F32), VM), grad_stream=((ROWS, BF), VM),
        ),
        dict(
            both, **WEIGHTS, **BACKWARD, **always, **{n + "1": both[n] for n in again}, land_f1=FORWARD["land"],
            route1=always["route"], w1=WEIGHTS["w"], land0=GRADS, land1=GRADS,
            own0=((64, 768), F32), stage=((24, WIDE), F32), cot_own=((64, 768), F32),
        ),
        (
            *given, lengths, stream, cotangent.reshape(ROWS), attn_gain, query_weight, key_weight, value_weight,
            out_weight, ffn_gain, jnp.swapaxes(router_weight, 1, 2), dense_gate, dense_up, dense_down,
        ),
    )
    sums, first, first_own, back0 = launch(
        third_body,
        2,
        "backward_0_scatter",
        dict(common, incoming=VM, grad_own=VM, inputs=VM, **{n + "_in": ANY for n in SAVED}, w_in=ANY, grads1=ANY),
        dict(
            sums=(((2, 2, 24, HALF), F32), VM), input_grad=((ROWS, BF), VM), input_own=(((64, 768), F32), VM), back0=(DP_ROWS, ANY)
        ),
        dict(SAVED, **WEIGHTS, **BACKWARD, **SCATTER, **always, own0=((64, 768), F32)),
        (*given, grad_stream, grad_own, stream, *saved, w, grads1),
    )
    g_eg, g_eu, g_ed, o_out, o_in, g_router, g_again, g_fgain, g_o, g_k, g_v, g_q, g_gate, g_up, g_down = last_results(
        (rows0, rows1, back0, back1), experts, (sums, last, last_own, first, first_own)
    )
    return (
        o_out.reshape(2, 128, 768),
        o_in.reshape(2, 128, 768),
        g_again,
        g_q,
        g_k,
        g_v,
        g_o,
        g_fgain,
        jnp.swapaxes(g_router, 1, 2),
        g_gate,
        g_up,
        g_down,
        g_eg,
        g_eu,
        g_ed,
    )


def solution(mesh):
    return jax.shard_map(
        shards,
        mesh=mesh,
        in_specs=(
            P("dp", "ep", None),
            P("dp"),
            P(None, "dp", "ep", None),
            P(None, "dp", "ep", None),
            P(None, ("dp", "ep")),
            P(None, ("dp", "ep"), "tp"),
            P(None, ("dp", "ep"), "tp"),
            P(None, ("dp", "ep"), "tp"),
            P(None, ("dp", "ep"), "tp"),
            P(None, ("dp", "ep")),
            P(None, ("dp", "ep"), None),
            P(None, ("dp", "ep"), "tp"),
            P(None, ("dp", "ep"), "tp"),
            P(None, ("dp", "ep"), "tp"),
            P(None, "ep", None, "tp"),
            P(None, "ep", None, "tp"),
            P(None, "ep", "tp", None),
            P("dp", "ep", None),
        ),
        out_specs=(
            P("dp", "ep", None),
            P("dp", "ep", None),
            P(None, ("dp", "ep")),
            P(None, ("dp", "ep"), "tp"),
            P(None, ("dp", "ep"), "tp"),
            P(None, ("dp", "ep"), "tp"),
            P(None, ("dp", "ep"), "tp"),
            P(None, ("dp", "ep")),
            P(None, ("dp", "ep"), None),
            P(None, ("dp", "ep"), "tp"),
            P(None, ("dp", "ep"), "tp"),
            P(None, ("dp", "ep"), "tp"),
            P(None, "ep", None, "tp"),
            P(None, "ep", None, "tp"),
            P(None, "ep", "tp", None),
        ),
        check_vma=False,
    )
```
